128 devices in a mesh: dp: 8 (over z, core), expert: 16 (over y, x).
Axes of the slice: x: 4, y: 4, z: 4, core: 2. Of those that a mesh axis runs over, the one named last changes fastest.
Arguments:
- tokens: bfloat16 [16384, 1536], P(('dp', 'expert')), may hold values from -6 to 6
- cotangent: bfloat16 [16384, 1536], P(('dp', 'expert')), may hold values from -6 to 6
- lengths: int32 [128, 4], P(('dp', 'expert')), may hold values from 1 to 64, 128 in all within a row
- routes: int32 [2, 16384, 4], P(None, ('dp', 'expert')), may hold values from 0 to 15, all different within a row; in each aligned block of 128 rows (0 to 127, 128 to 255, ..., all dimensions but the last counted through in order) at most 48 rows name the same one
- norm_attn: bfloat16 [2, 1536], P(None, 'dp'), may hold values from 0.5 to 1.5
- w_query: bfloat16 [2, 1536, 1536], P(None, 'dp'), may hold values from -0.15625 to 0.15625
- key_projection: bfloat16 [2, 1536, 256], P(None, 'dp'), may hold values from -0.15625 to 0.15625
- value_projection: bfloat16 [2, 1536, 256], P(None, 'dp'), may hold values from -0.15625 to 0.15625
- w_out: bfloat16 [2, 1536, 1536], P(None, 'dp'), may hold values from -0.625 to 0.625
- norm_ffn: bfloat16 [2, 1536], P(None, 'dp'), may hold values from 0.5 to 1.5
- w_router: bfloat16 [2, 1536, 16], P(None, 'dp'), may hold values from -0.078125 to 0.078125
- w_gate: bfloat16 [2, 16, 1536, 768], P(None, 'expert'), may hold values from -0.15625 to 0.15625
- w_up: bfloat16 [2, 16, 1536, 768], P(None, 'expert'), may hold values from -0.15625 to 0.15625
- w_down: bfloat16 [2, 16, 768, 1536], P(None, 'expert'), may hold values from -0.875 to 0.875
Outputs:
- mixed: bfloat16 [16384, 1536], P(('dp', 'expert'))
- grad_tokens: float32 [16384, 1536], P(('dp', 'expert'))
- grad_norm_attn: float32 [2, 1536], P(None, 'dp')
- grad_query: float32 [2, 1536, 1536], P(None, 'dp')
- grad_key: float32 [2, 1536, 256], P(None, 'dp')
- grad_value: float32 [2, 1536, 256], P(None, 'dp')
- grad_out: float32 [2, 1536, 1536], P(None, 'dp')
- grad_norm_ffn: float32 [2, 1536], P(None, 'dp')
- grad_router: float32 [2, 1536, 16], P(None, 'dp')
- grad_gate: float32 [2, 16, 1536, 768], P(None, 'expert', 'dp')
- grad_up: float32 [2, 16, 1536, 768], P(None, 'expert', 'dp')
- grad_down: float32 [2, 16, 768, 1536], P(None, 'expert', 'dp')
The draws below stay inside these ranges and needn't reach their ends.
Inputs may be any that keep to these rules, and one draw needn't show every extreme that they name: `lengths`: each device's row sums to 128 and its longest sequence has 64 tokens. `routes`: each token names 4 different experts; in each layer, among one device's 128 tokens no expert is named more than 48 times, a bound that some block reaches.
All inputs are finite; a program needn't handle non-finite values.
Results may differ from the reference program's by a relative error of at most 0.025.
Values may be sent and summed in bfloat16 or wider, within the bound.
No kernel may reach another device: no remote copies, remote signals or barrier semaphores. Data moves between devices by JAX's collectives and lax.ppermute only.
A program may use at most 192 MiB of HBM per device.

```python
import math
import jax
import jax.numpy as jnp
import numpy as np
from jax import lax

MODEL_WIDTH = 1536
QUERY_HEADS = 12
KEY_VALUE_HEADS = 2
HEAD_SIZE = 128
FF = 768
TOP = 4
LAYER_COUNT = 2
SEQ_DEV = 4
TOK_DEV = 128
EXPERTS = 16
CAP = 48
TOKENS = 16384
N_DP = 8
N_EXPERT = 16


def levels(rng, dims, split, low, top_value):
    level, own = 1.0, jax.random.fold_in(rng, 6)
    for axis_at, parts in split:
        draws = jnp.exp(jax.random.uniform(jax.random.fold_in(own, axis_at), (parts,), jnp.float32, low / len(split), top_value / len(split)))
        level = level * jnp.repeat(draws, dims[axis_at] // parts).reshape([-1 if axis == axis_at else 1 for axis in range(len(dims))])
    return level


def split_up(count, total, most, lean):
    loads = [(1 << 20) // math.isqrt(grade ** lean) + 1 for grade in range(2, count + 1)]
    spare, holding = total - most - (count - 1), [1] * (count - 1)
    while spare > 0:
        movable = [i for i in range(count - 1) if holding[i] < most]
        mass, left = sum([loads[i] for i in movable]), spare
        for i in movable:
            extra = min(most - holding[i], max(1, left * loads[i] // mass), spare)
            holding[i] = holding[i] + extra
            spare = spare - extra
    return np.array([most] + holding)


def uneven(stream_key, count, total, bound, skew):
    if count == 2:
        one = jax.random.randint(stream_key, (), max(1, total - bound), min(bound, total - 1) + 1)
        return jnp.stack([one, total - one])
    sizes = jnp.asarray(split_up(count, total, bound, skew), jnp.int32)
    twos = (count - 1) // 2
    donor, receiver = sizes[1:1 + 2 * twos:2], sizes[2:2 + 2 * twos:2]
    room = jnp.minimum(donor - 1, bound - receiver)
    moved = jax.random.randint(jax.random.fold_in(stream_key, 1), (twos,), 0, 1 << 20) % (room + 1)
    sizes = sizes.at[1:1 + 2 * twos:2].set(donor - moved).at[2:2 + 2 * twos:2].set(receiver + moved)
    return sizes[jax.random.permutation(jax.random.fold_in(stream_key, 2), count)]


def routed_block(own_key, own, number, rows, number_of, top, most, slope):
    ranking = jax.random.permutation(own_key, number_of)
    heavy_load, common = portions_of(number_of, rows * top, most, slope, True), portions_of(number_of, rows * top, most, slope, False)
    places = jnp.arange(number_of)

    def named(tallies, turn):
        used = int((tallies > 0).sum())
        fixed = max(1, used // 4)
        shifted = fixed + (places - fixed + turn * (used - fixed)) % max(1, number_of - fixed)
        return jnp.zeros((number_of,), jnp.int32).at[ranking[jnp.where(places < fixed, places, shifted)]].set(jnp.asarray(tallies, jnp.int32))

    tallies = jnp.where(number % 4 == 0, named(heavy_load, number // 4), named(common, number - number // 4 - 1))
    mixed = jax.random.permutation(jax.random.fold_in(own, 3), number_of)
    giver, receiver = mixed[0:number_of // 2 * 2:2], mixed[1:number_of // 2 * 2:2]
    slack = jnp.minimum(tallies[giver] - 1, most - tallies[receiver]) // 2
    slack = jnp.where((giver == ranking[0]) | (receiver == ranking[0]) | (tallies[receiver] == 0), 0, jnp.maximum(slack, 0))
    shifted = jax.random.randint(jax.random.fold_in(own, 4), (number_of // 2,), 0, 1 << 20) % (slack + 1)
    tallies = tallies.at[giver].add(-shifted).at[receiver].add(shifted)
    labels = jnp.searchsorted(jnp.cumsum(tallies), jnp.arange(rows * top), side="right").astype(jnp.int32)
    table = labels.reshape(top, rows).T
    table = table[jax.random.permutation(jax.random.fold_in(own, 1), rows)]
    turn = jax.random.randint(jax.random.fold_in(own, 2), (rows, 1), 0, top)
    return jnp.take_along_axis(table, (jnp.arange(top)[None, :] + turn) % top, axis=1)


def portions_of(number_of, total, reach, lean, full):
    weights = [(1 << 20) // math.isqrt(standing ** lean) + 1 for standing in range(1, number_of + 1)]
    largest = reach if full else min(reach, max(-(-total // number_of), total * weights[0] // sum(weights)))
    least = 1 if total - largest >= number_of - 1 else 0
    given, surplus = [largest] + [least] * (number_of - 1), total - largest - least * (number_of - 1)
    while surplus > 0:
        candidates = [i for i in range(1, number_of) if given[i] < largest] or [i for i in range(1, number_of) if given[i] < reach]
        whole, remaining = sum([weights[i] for i in candidates]), surplus
        for i in candidates:
            more = min(reach - given[i], max(1, remaining * weights[i] // whole), surplus)
            given[i] = given[i] + more
            surplus = surplus - more
    return np.array(given)


def noise(stream_key, dims, width, bound, split=(), kind=jnp.bfloat16):
    loudness = levels(stream_key, dims, split, -0.22, 0.18) if split else 1.0
    values = jax.random.normal(stream_key, dims, jnp.float32) * width * loudness
    return jnp.minimum(jnp.maximum(values, -bound), bound).astype(kind)


def setup_inputs(seed: int = 0) -> dict:
    seeds = jax.random.split(jax.random.key(seed), 15)
    tokens = noise(seeds[0], (TOKENS, MODEL_WIDTH), 1.0, 6.0, ((0, 128),))
    cotangent = noise(seeds[1], (TOKENS, MODEL_WIDTH), 1.0, 6.0, ((0, 128),))
    lengths = jax.vmap(lambda own: uneven(own, SEQ_DEV, TOK_DEV, TOK_DEV // 2, 2))(jax.random.split(seeds[2], (N_DP * N_EXPERT))).reshape((N_DP * N_EXPERT, SEQ_DEV)).astype(jnp.int32)
    routes_keys = jax.random.split(jax.random.fold_in(seeds[3], 1), LAYER_COUNT * TOKENS // TOK_DEV)
    routes_turns = jax.random.permutation(jax.random.fold_in(seeds[3], 3), LAYER_COUNT * TOKENS // TOK_DEV)
    routes = jax.vmap(lambda own, number: routed_block(jax.random.fold_in(seeds[3], 2), own, number, TOK_DEV, EXPERTS, TOP, CAP, 2))(routes_keys, routes_turns).reshape((LAYER_COUNT, TOKENS, TOP))
    norm_attn = jnp.clip(1.0 + 0.1 * jax.random.normal(seeds[4], (LAYER_COUNT, MODEL_WIDTH), jnp.float32), 0.5, 1.5).astype(jnp.bfloat16)
    w_query = noise(seeds[5], (LAYER_COUNT, MODEL_WIDTH, QUERY_HEADS * HEAD_SIZE), MODEL_WIDTH ** -0.5, 0.15625, ((1, 8),))
    key_projection = noise(seeds[6], (LAYER_COUNT, MODEL_WIDTH, KEY_VALUE_HEADS * HEAD_SIZE), MODEL_WIDTH ** -0.5, 0.15625, ((1, 8),))
    value_projection = noise(seeds[7], (LAYER_COUNT, MODEL_WIDTH, KEY_VALUE_HEADS * HEAD_SIZE), MODEL_WIDTH ** -0.5, 0.15625, ((1, 8),))
    w_out = noise(seeds[8], (LAYER_COUNT, QUERY_HEADS * HEAD_SIZE, MODEL_WIDTH), (QUERY_HEADS * HEAD_SIZE // 16) ** -0.5, 0.625, ((1, 8),))
    norm_ffn = jnp.clip(1.0 + 0.1 * jax.random.normal(seeds[9], (LAYER_COUNT, MODEL_WIDTH), jnp.float32), 0.5, 1.5).astype(jnp.bfloat16)
    w_router = noise(seeds[10], (LAYER_COUNT, MODEL_WIDTH, EXPERTS), (4 * MODEL_WIDTH) ** -0.5, 0.078125, ((1, 8),))
    w_gate = noise(seeds[11], (LAYER_COUNT, EXPERTS, MODEL_WIDTH, FF), MODEL_WIDTH ** -0.5, 0.15625, ((1, 16),))
    w_up = noise(seeds[12], (LAYER_COUNT, EXPERTS, MODEL_WIDTH, FF), MODEL_WIDTH ** -0.5, 0.15625, ((1, 16),))
    w_down = noise(seeds[13], (LAYER_COUNT, EXPERTS, FF, MODEL_WIDTH), (FF // 16) ** -0.5, 0.875, ((1, 16),))
    return dict(tokens=tokens, cotangent=cotangent, lengths=lengths, routes=routes, norm_attn=norm_attn, w_query=w_query, key_projection=key_projection, value_projection=value_projection, w_out=w_out, norm_ffn=norm_ffn, w_router=w_router, w_gate=w_gate, w_up=w_up, w_down=w_down)


@jax.custom_vjp
def reduced_dtype(v):
    return lax.optimization_barrier(v.astype(jnp.bfloat16)).astype(jnp.float32)

@jax.custom_vjp
def reduced_backward(v):
    return v

def low_keep(v):
    return (reduced_dtype(v), None)

def low_pass(kept, grad):
    return (grad,)

def back_keep(v):
    return (v, None)

def back_low(kept, grad):
    return (reduced_dtype(grad),)
reduced_dtype.defvjp(low_keep, low_pass)
reduced_backward.defvjp(back_keep, back_low)
epsilon = 1e-06
rope_base = 1000000.0
highest_precision = lax.Precision.HIGHEST

def rms_norm(values, gain):
    return values * lax.rsqrt(lax.optimization_barrier(jnp.mean(values * values, axis=-1, keepdims=True)) + epsilon) * gain

def rotate(values, cosine, sine):
    half_size = values.shape[-1] // 2
    first_half = values[..., :half_size]
    second_half = values[..., half_size:]
    return jnp.concatenate([first_half * cosine - second_half * sine, second_half * cosine + first_half * sine], axis=-1)

def seq_tables(counts, row_number):
    ends = jnp.cumsum(counts).astype(jnp.int32)
    starts = (ends - counts).astype(jnp.int32)
    place = jnp.arange(row_number, dtype=jnp.int32)
    member = (place[:, None] >= starts[None, :]) & (place[:, None] < ends[None, :])
    segment = lax.optimization_barrier(jnp.sum(jnp.where(member, jnp.arange(counts.shape[0], dtype=jnp.int32)[None, :], 0), axis=1))
    position = place - lax.optimization_barrier(jnp.sum(jnp.where(member, starts[None, :], 0), axis=1))
    allowed = (segment[:, None] == segment[None, :]) & (place[:, None] >= place[None, :])
    half_size = HEAD_SIZE // 2
    freqs = rope_base ** (-2.0 * jnp.arange(half_size, dtype=jnp.float32) / HEAD_SIZE)
    angle = position.astype(jnp.float32)[:, None] * freqs[None, :]
    return (jnp.cos(angle), jnp.sin(angle), allowed)

def route_tables(choices, expert_count, capacity):
    entries = choices.shape[0] * choices.shape[1]
    flat_routes = choices.reshape(entries)
    onehot = (flat_routes[:, None] == jnp.arange(expert_count, dtype=jnp.int32)[None, :]).astype(jnp.int32)
    before = jnp.cumsum(onehot, axis=0) - onehot
    ranked = lax.optimization_barrier(jnp.sum(before * onehot, axis=1))
    dest = (flat_routes * capacity + ranked).astype(jnp.int32)
    source = jnp.full((expert_count * capacity,), entries, jnp.int32).at[dest].set(jnp.arange(entries, dtype=jnp.int32))
    valid = source < entries
    pick = jnp.minimum(source, entries - 1).astype(jnp.int32)
    return (dest, valid, pick)

def gate_values(logits, choices):
    router = jax.nn.softmax(logits, axis=-1)
    chosen = choices[:, :, None] == jnp.arange(logits.shape[-1], dtype=jnp.int32)[None, None, :]
    return lax.optimization_barrier(jnp.sum(jnp.where(chosen, router[:, None, :], 0.0), axis=-1))

def layer_apply(resid, params, cosine, sine, allowed, choices, dest, valid, pick):
    gain_one, query_weight, key_weight, value_weight, output_weight, gain_two, router_w, gate_w, up_w, down_w = params
    device_total = resid.shape[0]
    row_number = resid.shape[1]
    activations = reduced_dtype(rms_norm(resid, gain_one))
    query_matrix = reduced_backward(jnp.einsum('lmq,qy->lmy', activations, query_weight, precision=highest_precision)).reshape(device_total, row_number, KEY_VALUE_HEADS, QUERY_HEADS // KEY_VALUE_HEADS, HEAD_SIZE)
    key_matrix = reduced_backward(jnp.einsum('lmq,qy->lmy', activations, key_weight, precision=highest_precision)).reshape(device_total, row_number, KEY_VALUE_HEADS, HEAD_SIZE)
    value_matrix = reduced_dtype(reduced_backward(jnp.einsum('lmq,qy->lmy', activations, value_weight, precision=highest_precision))).reshape(device_total, row_number, KEY_VALUE_HEADS, HEAD_SIZE)
    query_matrix = reduced_dtype(rotate(query_matrix, cosine[:, :, None, None, :], sine[:, :, None, None, :]))
    key_matrix = reduced_dtype(rotate(key_matrix, cosine[:, :, None, :], sine[:, :, None, :]))
    scores = reduced_backward(jnp.einsum('nthgd,nshd->nhgts', query_matrix, key_matrix, precision=highest_precision) * HEAD_SIZE ** (-0.5))
    scores = jnp.where(allowed[:, None, None], scores, -1000000000.0)
    weights = reduced_dtype(jax.nn.softmax(scores, axis=-1))
    attended = jnp.einsum('nhgts,nshd->nthgd', weights, value_matrix, precision=highest_precision).reshape(device_total, row_number, QUERY_HEADS * HEAD_SIZE)
    attended = reduced_dtype(reduced_backward(attended))
    after = resid + reduced_backward(jnp.einsum('ntf,fd->ntd', attended, output_weight, precision=highest_precision))
    acts_two = reduced_dtype(rms_norm(after, gain_two))
    logits = reduced_backward(jnp.einsum('ntd,de->nte', acts_two, router_w, precision=highest_precision))
    gate_rows = jax.vmap(gate_values)(logits, choices)
    slot_rows = jnp.take_along_axis(acts_two, (pick // TOP)[:, :, None], axis=1)
    slot_rows = reduced_backward(jnp.where(valid[:, :, None], slot_rows, 0.0)).reshape(device_total, EXPERTS, CAP, MODEL_WIDTH)
    gate_pre = reduced_backward(jnp.einsum('necd,edf->necf', slot_rows, gate_w, precision=highest_precision))
    up_pre = reduced_backward(jnp.einsum('necd,edf->necf', slot_rows, up_w, precision=highest_precision))
    hidden = reduced_dtype(jax.nn.gelu(gate_pre) * up_pre)
    slot_out = reduced_dtype(reduced_backward(jnp.einsum('necf,efd->necd', hidden, down_w, precision=highest_precision)))
    slot_out = slot_out.reshape(device_total, EXPERTS * CAP, MODEL_WIDTH)
    returned = jnp.take_along_axis(slot_out, dest[:, :, None], axis=1).reshape(device_total, row_number, TOP, MODEL_WIDTH)
    return after + lax.optimization_barrier(jnp.sum(gate_rows[:, :, :, None] * returned, axis=2))

def reference(tokens, cotangent, lengths, routes, norm_attn, w_query, key_projection, value_projection, w_out, norm_ffn, w_router, w_gate, w_up, w_down):
    device_total = N_DP * N_EXPERT
    cosine, sine, allowed = jax.vmap(lambda counts: seq_tables(counts, TOK_DEV))(lengths)
    tables = []
    for layer_index in range(LAYER_COUNT):
        choices = routes[layer_index].reshape(device_total, TOK_DEV, TOP)
        dest, valid, pick = jax.vmap(lambda group_routes: route_tables(group_routes, EXPERTS, CAP))(choices)
        tables.append((choices, dest, valid, pick))
    params = tuple((element.astype(jnp.float32) for element in (norm_attn, w_query, key_projection, value_projection, w_out, norm_ffn, w_router, w_gate, w_up, w_down)))

    def forward(resid, weight_set):
        for layer_index in range(LAYER_COUNT):
            choices, dest, valid, pick = tables[layer_index]
            layer_params = tuple((element[layer_index] for element in weight_set))
            resid = layer_apply(resid, layer_params, cosine, sine, allowed, choices, dest, valid, pick)
        return resid
    start = tokens.astype(jnp.float32).reshape(device_total, TOK_DEV, MODEL_WIDTH)
    result, pullback = jax.vjp(forward, start, params)
    grad_start, grads = pullback(cotangent.astype(jnp.float32).reshape(device_total, TOK_DEV, MODEL_WIDTH))
    return (result.reshape(TOKENS, MODEL_WIDTH).astype(jnp.bfloat16), grad_start.reshape(TOKENS, MODEL_WIDTH), grads[0], grads[1], grads[2], grads[3], grads[4], grads[5], grads[6], grads[7], grads[8], grads[9])
```

```python
import jax
import jax.numpy as jnp
from jax import lax
from jax.sharding import PartitionSpec as P

QUERY_HEADS = 12
KEY_VALUE_HEADS = 2
GROUPS = QUERY_HEADS // KEY_VALUE_HEADS
HEAD = 128
TOP = 4
LAYERS = 2
WIDTH = 1536
FF = 768
ROWS = 128
EXPERTS = 16
CAP = 48
SLOTS = EXPERTS * CAP
DP = 8
SHARD = WIDTH // DP
Q_END = QUERY_HEADS * HEAD
K_END = Q_END + KEY_VALUE_HEADS * HEAD
V_END = K_END + KEY_VALUE_HEADS * HEAD
EPSILON = 1e-06
ROPE_BASE = 1000000.0
SCALE = HEAD ** (-0.5)
BF = jnp.bfloat16
F32 = jnp.float32


def dot(left, right, left_dim=1, right_dim=0):
    return lax.dot_general(
        left, right, (((left_dim,), (right_dim,)), ((), ())), preferred_element_type=F32
    )


def split(values):
    high = values.astype(BF)
    return high, (values - high.astype(F32)).astype(BF)


def rotate(values, cosine, sine):
    first, second = values[..., : HEAD // 2], values[..., HEAD // 2 :]
    return jnp.concatenate(
        [first * cosine - second * sine, second * cosine + first * sine], axis=-1
    )


def seq_tables(counts):
    ends = jnp.cumsum(counts)
    starts = ends - counts
    place = jnp.arange(ROWS, dtype=jnp.int32)
    member = (place[:, None] >= starts[None, :]) & (place[:, None] < ends[None, :])
    index = jnp.arange(counts.shape[0], dtype=jnp.int32)
    segment = jnp.sum(jnp.where(member, index[None, :], 0), axis=1)
    position = place - jnp.sum(jnp.where(member, starts[None, :], 0), axis=1)
    allowed = (segment[:, None] == segment[None, :]) & (place[:, None] >= place[None, :])
    freqs = ROPE_BASE ** (-2.0 * jnp.arange(HEAD // 2, dtype=F32) / HEAD)
    angle = position.astype(F32)[:, None] * freqs[None, :]
    return jnp.cos(angle), jnp.sin(angle), allowed


def expand_matrix():
    expert = lax.broadcasted_iota(jnp.int32, (EXPERTS, SLOTS), 0)
    slot = lax.broadcasted_iota(jnp.int32, (EXPERTS, SLOTS), 1)
    return (slot // CAP == expert).astype(BF)


def slot_matrix(choices, expand):
    experts = jnp.arange(EXPERTS, dtype=jnp.int32)
    member = jnp.any(choices[:, :, None] == experts[None, None, :], axis=1).astype(BF)
    row = lax.broadcasted_iota(jnp.int32, (ROWS, ROWS), 0)
    column = lax.broadcasted_iota(jnp.int32, (ROWS, ROWS), 1)
    rank = dot((column < row).astype(BF), member).astype(BF)
    slot = lax.broadcasted_iota(jnp.int32, (ROWS, SLOTS), 1)
    held = dot(member, expand) > 0.5
    return (held & (dot(rank, expand) == (slot % CAP).astype(F32))).astype(BF)


def unit(values):
    return lax.rsqrt(jnp.mean(values * values, axis=-1, keepdims=True) + EPSILON)


def norm_back(grad, gain, values):
    scale = unit(values)
    inner = grad * gain
    return scale * inner - values * (scale * scale * scale) * jnp.mean(
        inner * values, axis=-1, keepdims=True
    )


def exchange(rows):
    width = rows.shape[-1]
    moved = lax.all_to_all(
        rows.reshape(EXPERTS, CAP, width), "expert", split_axis=0, concat_axis=0, tiled=True
    )
    return moved.reshape(SLOTS, width)


def dispatch(slots, rows):
    return exchange(dot(slots, rows, 0, 0).astype(BF))


def attn_forward(x, weights, tables):
    cosine, sine, allowed = tables
    acts = (x * unit(x) * weights["gain_attn"]).astype(BF)
    qkv = dot(acts, weights["qkv"])
    query = qkv[:, :Q_END].reshape(ROWS, KEY_VALUE_HEADS, GROUPS, HEAD)
    key = qkv[:, Q_END:K_END].reshape(ROWS, KEY_VALUE_HEADS, HEAD)
    value = qkv[:, K_END:V_END].astype(BF).reshape(ROWS, KEY_VALUE_HEADS, HEAD)
    qrot = rotate(query, cosine[:, None, None, :], sine[:, None, None, :]).astype(BF)
    krot = rotate(key, cosine[:, None, :], sine[:, None, :]).astype(BF)
    scores = jnp.einsum("thgd,shd->hgts", qrot, krot, preferred_element_type=F32) * SCALE
    scores = jnp.where(allowed[None, None], scores, -1000000000.0)
    probs = jax.nn.softmax(scores, axis=-1)
    attended = jnp.einsum(
        "hgts,shd->thgd", probs.astype(BF), value, preferred_element_type=F32
    )
    attended = attended.reshape(ROWS, Q_END).astype(BF)
    after = x + dot(attended, weights["out"])
    acts_two = (after * unit(after) * weights["gain_ffn"]).astype(BF)
    router = jax.nn.softmax(dot(acts_two, weights["router"]), axis=-1)
    return dict(
        x=x, acts=acts, value=value, qrot=qrot, krot=krot, probs=probs, attended=attended,
        after=after, acts_two=acts_two, router=router,
    )


def attn_backward(dx, dacts_two, kept, weights, tables):
    cosine, sine, allowed = tables
    dafter = dx + norm_back(dacts_two, weights["gain_ffn"], kept["after"])
    dbranch = dafter.astype(BF)
    dattended = dot(dbranch, weights["out"], 1, 1).astype(BF)
    dattended = dattended.reshape(ROWS, KEY_VALUE_HEADS, GROUPS, HEAD)
    probs = kept["probs"]
    dprobs = jnp.einsum("thgd,shd->hgts", dattended, kept["value"], preferred_element_type=F32)
    dvalue = jnp.einsum(
        "hgts,thgd->shd", probs.astype(BF), dattended, preferred_element_type=F32
    ).astype(BF)
    dscores = probs * (dprobs - jnp.sum(dprobs * probs, axis=-1, keepdims=True))
    dscores = dscores.astype(BF)
    dqrot = jnp.einsum("hgts,shd->thgd", dscores, kept["krot"], preferred_element_type=F32)
    dkrot = jnp.einsum("hgts,thgd->shd", dscores, kept["qrot"], preferred_element_type=F32)
    dquery = rotate(dqrot * SCALE, cosine[:, None, None, :], -sine[:, None, None, :])
    dkey = rotate(dkrot * SCALE, cosine[:, None, :], -sine[:, None, :])
    dqkv = jnp.concatenate(
        [
            dquery.astype(BF).reshape(ROWS, -1),
            dkey.astype(BF).reshape(ROWS, -1),
            dvalue.reshape(ROWS, -1),
        ],
        axis=1,
    )
    dacts = dot(dqkv, weights["qkv"], 1, 1)
    dx_below = dafter + norm_back(dacts, weights["gain_attn"], kept["x"])
    return dx_below, dbranch, dqkv


def gated(pre):
    return jax.nn.gelu(pre[:, :FF]) * pre[:, FF:]


def experts_forward(received, gate_up, down):
    pre = dot(received, gate_up)
    hidden = gated(pre).astype(BF)
    return pre, hidden, dot(hidden, down).astype(BF)


def experts_backward(dslot, pre, hidden, received, gate_up, down):
    dhidden = dot(dslot, down, 1, 1)
    _, pull = jax.vjp(gated, pre)
    dpre = pull(dhidden)[0].astype(BF)
    back = dot(dpre, gate_up, 1, 1).astype(BF)
    grad_gate_up = dot(received, dpre, 0, 0).astype(BF)
    grad_down = dot(hidden, dslot, 0, 0).astype(BF)
    return back, grad_gate_up, grad_down


def expert_shares(grad_gate_up, grad_down):
    packed = jnp.concatenate(
        [grad_gate_up.reshape(DP, SHARD, WIDTH), grad_down.reshape(DP, FF // DP, WIDTH)], axis=1
    )
    return lax.psum_scatter(
        packed.reshape(-1, WIDTH), "dp", scatter_dimension=0, tiled=True
    ).astype(F32)


def columns_to_owners(arrays):
    packed = jnp.stack([a.reshape(ROWS, DP, SHARD) for a in arrays], axis=2)
    packed = packed.transpose(1, 0, 2, 3).reshape(DP, ROWS, len(arrays) * SHARD)
    moved = lax.all_to_all(packed, "dp", split_axis=0, concat_axis=0, tiled=True)
    moved = moved.reshape(DP * ROWS, len(arrays), SHARD)
    return [moved[:, i] for i in range(len(arrays))]


def sum_experts(values):
    width = values.shape[1] // EXPERTS
    pieces = values.astype(BF).reshape(SHARD, EXPERTS, width).transpose(1, 0, 2)
    pieces = lax.all_to_all(pieces, "expert", split_axis=0, concat_axis=0, tiled=True)
    mine = jnp.sum(pieces.astype(F32), axis=0).astype(BF)
    whole = lax.all_to_all(
        jnp.broadcast_to(mine[None], (EXPERTS, SHARD, width)),
        "expert", split_axis=0, concat_axis=0, tiled=True,
    )
    return whole.transpose(1, 0, 2).reshape(SHARD, EXPERTS * width).astype(F32)


def local(
    tokens, cotangent, lengths, routes, norm_attn, w_query, key_projection, value_projection,
    w_out, norm_ffn, w_router, w_gate, w_up, w_down,
):
    me_dp = lax.axis_index("dp")
    me_expert = lax.axis_index("expert")
    tables = seq_tables(lengths[0])
    expand = expand_matrix()
    slots = [slot_matrix(routes[l], expand) for l in range(LAYERS)]

    shard_qkv = [
        jnp.concatenate([w_query[l], key_projection[l], value_projection[l]], axis=1)
        for l in range(LAYERS)
    ]
    small = jnp.concatenate(
        [norm_attn.T, norm_ffn.T, w_router[0], w_router[1], jnp.zeros((SHARD, 92), BF)], axis=1
    )
    whole_a = lax.all_gather(
        jnp.concatenate([shard_qkv[0], small], axis=1), "dp", axis=0, tiled=True
    )
    whole_b = lax.all_gather(w_out[0], "dp", axis=0, tiled=True)
    whole_c = lax.all_gather(
        jnp.concatenate([shard_qkv[1], w_out[1]], axis=1), "dp", axis=0, tiled=True
    )
    small_all = whole_a[:, V_END:]
    gains = small_all[:, :4].T.astype(F32)
    weights = [
        dict(qkv=whole_a[:, :V_END], out=whole_b, gain_attn=gains[0], gain_ffn=gains[2],
             router=small_all[:, 4:20]),
        dict(qkv=whole_c[:, :V_END], out=whole_c[:, V_END:], gain_attn=gains[1],
             gain_ffn=gains[3], router=small_all[:, 20:36]),
    ]
    gate_up = [jnp.concatenate([w_gate[l, 0], w_up[l, 0]], axis=1) for l in range(LAYERS)]
    down = [w_down[l, 0] for l in range(LAYERS)]

    dx_rows = dispatch(slots[1], cotangent)

    kept0 = attn_forward(tokens.astype(F32), weights[0], tables)
    received0 = dispatch(slots[0], kept0["acts_two"])
    pre0, hidden0, out0 = experts_forward(received0, gate_up[0], down[0])
    returned0 = exchange(out0)
    router_slots0 = lax.dot(kept0["router"], expand.astype(F32), precision=lax.Precision.HIGHEST)
    gate0 = slots[0].astype(F32) * router_slots0
    gate0_high, gate0_low = split(gate0)
    x1 = kept0["after"] + dot(gate0_high, returned0) + dot(gate0_low, returned0)

    kept1 = attn_forward(x1, weights[1], tables)
    received1 = dispatch(slots[1], kept1["acts_two"])
    pre1, hidden1, out1 = experts_forward(received1, gate_up[1], down[1])
    router_here = jax.nn.softmax(dot(received1, weights[1]["router"]), axis=-1)
    mine = jnp.arange(EXPERTS, dtype=jnp.int32)[None, :] == me_expert
    gate_here = jnp.sum(jnp.where(mine, router_here, 0.0), axis=1, keepdims=True)
    dx_rows_wide = dx_rows.astype(F32)
    dslot1 = (gate_here * dx_rows_wide).astype(BF)
    dgate_here = jnp.sum(dx_rows_wide * out1.astype(F32), axis=1, keepdims=True)
    back1, grad_gate_up1, grad_down1 = experts_backward(
        dslot1, pre1, hidden1, received1, gate_up[1], down[1]
    )
    dgate_high, dgate_low = split(dgate_here)
    back1 = exchange(
        jnp.concatenate(
            [back1, dgate_high, dgate_low, jnp.zeros((SLOTS, 126), BF)], axis=1
        )
    )
    shares1 = expert_shares(grad_gate_up1, grad_down1)
    returned1 = exchange(out1)
    router_slots1 = lax.dot(kept1["router"], expand.astype(F32), precision=lax.Precision.HIGHEST)
    gate1_high, gate1_low = split(slots[1].astype(F32) * router_slots1)
    mixed = kept1["after"] + dot(gate1_high, returned1) + dot(gate1_low, returned1)

    def logits_back(drouter, router):
        inner = jnp.sum(drouter * router, axis=-1, keepdims=True)
        return (router * (drouter - inner)).astype(BF)

    drouter1 = dot(slots[1], back1[:, WIDTH : WIDTH + 1] * expand.T) + dot(
        slots[1], back1[:, WIDTH + 1 : WIDTH + 2] * expand.T
    )
    dlogits1 = logits_back(drouter1, kept1["router"])
    dacts_two1 = dot(dlogits1, weights[1]["router"], 1, 1) + dot(slots[1], back1[:, :WIDTH])
    dx0, dbranch1, dqkv1 = attn_backward(
        cotangent.astype(F32), dacts_two1, kept1, weights[1], tables
    )

    dslot0 = exchange(
        (dot(gate0_high, dx0.astype(BF), 0, 0) + dot(gate0_low, dx0.astype(BF), 0, 0)).astype(BF)
    )
    back0, grad_gate_up0, grad_down0 = experts_backward(
        dslot0, pre0, hidden0, received0, gate_up[0], down[0]
    )
    back0 = exchange(back0)
    shares0 = expert_shares(grad_gate_up0, grad_down0)
    dgate0 = dot(dx0.astype(BF), returned0, 1, 1) * slots[0].astype(F32)
    drouter0 = lax.dot_general(
        dgate0, expand.astype(F32), (((1,), (1,)), ((), ())), precision=lax.Precision.HIGHEST
    )
    dlogits0 = logits_back(drouter0, kept0["router"])
    dacts_two0 = dot(dlogits0, weights[0]["router"], 1, 1) + dot(slots[0], back0)
    grad_tokens, dbranch0, dqkv0 = attn_backward(dx0, dacts_two0, kept0, weights[0], tables)

    def pad(values, width):
        return jnp.pad(values, ((0, 0), (0, width - values.shape[1])))

    def gain_share(l, shares):
        rows = lax.dynamic_slice_in_dim(gate_up[l], me_dp * SHARD, SHARD, 0).astype(F32)
        return jnp.sum(shares[:SHARD] * rows, axis=1, keepdims=True)

    def tail(l, shares, router_sum, qkv_sum, gain_sum):
        grad_norm_attn = jnp.sum(qkv_sum * shard_qkv[l].astype(F32), axis=1)
        grad_norm_attn = grad_norm_attn / norm_attn[l].astype(F32)
        grad_norm_ffn = gain_sum + jnp.sum(router_sum * w_router[l].astype(F32), axis=1)
        return grad_norm_attn, grad_norm_ffn / norm_ffn[l].astype(F32)

    acts1, attended1, acts_two1 = columns_to_owners(
        [kept1["acts"], kept1["attended"], kept1["acts_two"]]
    )
    rows1 = lax.all_gather(
        jnp.concatenate([dqkv1, dbranch1, pad(dlogits1, HEAD)], axis=1), "dp", axis=0, tiled=True
    )
    grad_qkv1 = dot(acts1, rows1[:, :V_END], 0, 0)
    grad_out1 = dot(attended1, rows1[:, V_END : V_END + WIDTH], 0, 0)
    grad_router1 = dot(acts_two1, rows1[:, V_END + WIDTH :], 0, 0)[:, :EXPERTS]
    gain_high, gain_low = split(gain_share(1, shares1))
    sums1 = sum_experts(
        pad(jnp.concatenate(
            [grad_qkv1, grad_out1, grad_router1, gain_high.astype(F32), gain_low.astype(F32)],
            axis=1,
        ), 4096)
    )

    acts0, attended0, acts_two0 = columns_to_owners(
        [kept0["acts"], kept0["attended"], kept0["acts_two"]]
    )
    rows0 = lax.all_gather(
        jnp.concatenate([dbranch0, pad(dlogits0, HEAD)], axis=1), "dp", axis=0, tiled=True
    )
    grad_out0 = dot(attended0, rows0[:, :WIDTH], 0, 0)
    grad_router0 = dot(acts_two0, rows0[:, WIDTH:], 0, 0)[:, :EXPERTS]
    gain_high, gain_low = split(gain_share(0, shares0))
    sums0 = sum_experts(
        pad(jnp.concatenate(
            [grad_out0, grad_router0, gain_high.astype(F32), gain_low.astype(F32)], axis=1
        ), 2048)
    )
    rows0 = lax.all_gather(dqkv0, "dp", axis=0, tiled=True)
    qkv_sum0 = sum_experts(dot(acts0, rows0, 0, 0))

    qkv_sums = [qkv_sum0, sums1[:, :V_END]]
    out_sums = [sums0[:, :WIDTH], sums1[:, V_END : V_END + WIDTH]]
    ends = [sums0[:, WIDTH:], sums1[:, V_END + WIDTH :]]
    router_sums = [end[:, :EXPERTS] for end in ends]
    shares = [shares0, shares1]
    norms = [
        tail(l, shares[l], router_sums[l], qkv_sums[l], ends[l][:, EXPERTS] + ends[l][:, EXPERTS + 1])
        for l in range(LAYERS)
    ]
    return (
        mixed.astype(BF),
        grad_tokens,
        jnp.stack([n[0] for n in norms]),
        jnp.stack([s[:, :Q_END] for s in qkv_sums]),
        jnp.stack([s[:, Q_END:K_END] for s in qkv_sums]),
        jnp.stack([s[:, K_END:] for s in qkv_sums]),
        jnp.stack(out_sums),
        jnp.stack([n[1] for n in norms]),
        jnp.stack(router_sums),
        jnp.stack([s[:SHARD, :FF] for s in shares])[:, None],
        jnp.stack([s[:SHARD, FF:] for s in shares])[:, None],
        jnp.stack([s[SHARD:] for s in shares])[:, None],
    )


def solution(mesh):
    placed = (
        P(("dp", "expert"), None),
        P(("dp", "expert"), None),
        P(("dp", "expert"), None),
        P(None, ("dp", "expert"), None),
        P(None, "dp"),
        P(None, "dp", None),
        P(None, "dp", None),
        P(None, "dp", None),
        P(None, "dp", None),
        P(None, "dp"),
        P(None, "dp", None),
        P(None, "expert", None, None),
        P(None, "expert", None, None),
        P(None, "expert", None, None),
    )
    return jax.shard_map(
        local,
        mesh=mesh,
        in_specs=placed,
        out_specs=(
            P(("dp", "expert"), None),
            P(("dp", "expert"), None),
            P(None, "dp"),
            P(None, "dp", None),
            P(None, "dp", None),
            P(None, "dp", None),
            P(None, "dp", None),
            P(None, "dp"),
            P(None, "dp", None),
            P(None, "expert", "dp", None),
            P(None, "expert", "dp", None),
            P(None, "expert", "dp", None),
        ),
        check_vma=False,
    )
```

```python
import jax
import jax.numpy as jnp
from jax import lax
from jax.experimental import pallas as pl
from jax.experimental.pallas import tpu as pltpu
from jax.sharding import PartitionSpec as P

QUERY_HEADS = 12
KEY_VALUE_HEADS = 2
GROUPS = QUERY_HEADS // KEY_VALUE_HEADS
HEAD = 128
LAYERS = 2
WIDTH = 1536
FF = 768
ROWS = 128
EXPERTS = 16
CAP = 48
SLOTS = EXPERTS * CAP
DP = 8
SHARD = WIDTH // DP
Q_END = QUERY_HEADS * HEAD
K_END = Q_END + KEY_VALUE_HEADS * HEAD
QKV = K_END + KEY_VALUE_HEADS * HEAD
SMALL = QKV + WIDTH
PACKED = SMALL + HEAD
GAIN_ATTN, GAIN_FFN = 16, 17
GAIN_HIGH, GAIN_LOW = 16, 32
PIECES = WIDTH // HEAD
TILE = 256
BLOCK = 256
EPSILON = 1e-06
ROPE_BASE = 1000000.0
SCALE = HEAD ** (-0.5)
GELU_A = 0.7978845608028654
GELU_B = 0.044715
VMEM_BYTES = 56 << 20
BF = jnp.bfloat16
F32 = jnp.float32
ANY = pl.BlockSpec(memory_space=pl.ANY)


def dot(left, right, left_dim=1, right_dim=0):
    return lax.dot_general(
        left, right, (((left_dim,), (right_dim,)), ((), ())), preferred_element_type=F32
    )


def split(values):
    high = values.astype(BF)
    return high, (values - high.astype(F32)).astype(BF)


def unit(values):
    return lax.rsqrt(jnp.mean(values * values, axis=-1, keepdims=True) + EPSILON)


def turn(values, cosine, sine):
    return values * cosine + pltpu.roll(values, HEAD // 2, 1) * sine


def expert_lanes(transposed=False):
    shape = (SLOTS, HEAD) if transposed else (HEAD, SLOTS)
    slot = lax.broadcasted_iota(jnp.int32, shape, 0 if transposed else 1)
    first = lax.broadcasted_iota(jnp.int32, shape, 1 if transposed else 0) * CAP
    return ((slot >= first) & (slot < first + CAP)).astype(F32).astype(BF)


def gain_rows(small):
    row = lax.broadcasted_iota(jnp.int32, (8, HEAD), 0)
    lane = lax.broadcasted_iota(jnp.int32, (8, HEAD), 1)
    pick = ((lane == row + GAIN_ATTN) & (row < 2)).astype(F32).astype(BF)
    rows = dot(pick, small, 1, 1)
    return rows[0:1], rows[1:2]


def router_probs(rows, small):
    logits = dot(rows, small)
    lane = lax.broadcasted_iota(jnp.int32, logits.shape, 1)
    logits = jnp.where(lane < EXPERTS, logits, -1e30)
    powers = jnp.exp(logits - jnp.max(logits, axis=-1, keepdims=True))
    return powers / jnp.sum(powers, axis=-1, keepdims=True)


def start_all(pairs, sems):
    copies = [
        pltpu.make_async_copy(source, target, sems.at[i]) for i, (source, target) in enumerate(pairs)
    ]
    for copy in copies:
        copy.start()
    return copies


def attn_forward_kernel(first, refs):
    refs = iter(refs)
    x_in = next(refs)
    if not first:
        returned_hbm, high_in, low_in = next(refs), next(refs), next(refs)
    w_hbm, cosine, sine, allowed, take, give = (next(refs) for _ in range(6))
    next(refs)
    (x_out, acts, qrot, krot, value, probs, attended, after, acts_two, router, high, low, rows,
     w, returned, sems) = refs
    pairs = []
    if not first:
        pairs += [(returned_hbm, returned)]
    pairs += [(w_hbm.at[:, pl.ds(SMALL, HEAD)], w.at[:, pl.ds(SMALL, HEAD)])]
    pairs += [
        (w_hbm.at[:, pl.ds(at, TILE)], w.at[:, pl.ds(at, TILE)]) for at in range(0, SMALL, TILE)
    ]
    copies = start_all(pairs, sems)
    if first:
        x = x_in[...].astype(F32)
    else:
        copies.pop(0).wait()
        x = x_in[...] + dot(high_in[...], returned[...]) + dot(low_in[...], returned[...])
    x_out[...] = x
    copies.pop(0).wait()
    small = w[:, SMALL:]
    gain_attn, gain_ffn = gain_rows(small)
    acts[...] = (x * unit(x) * gain_attn).astype(BF)
    for tile in range(QKV // TILE):
        copies[tile].wait()
        wide = dot(acts[...], w[:, tile * TILE : (tile + 1) * TILE])
        for half in range(TILE // HEAD):
            head = tile * (TILE // HEAD) + half
            part = wide[:, half * HEAD : (half + 1) * HEAD]
            if head < QUERY_HEADS:
                qrot[head] = turn(part, cosine[...], sine[...]).astype(BF)
            elif head < QUERY_HEADS + KEY_VALUE_HEADS:
                krot[head - QUERY_HEADS] = turn(part, cosine[...], sine[...]).astype(BF)
            else:
                value[head - QUERY_HEADS - KEY_VALUE_HEADS] = part.astype(BF)
    open_scores = (allowed[...] > 0.5)[None]
    for k in range(KEY_VALUE_HEADS):
        heads = slice(k * GROUPS, (k + 1) * GROUPS)
        scores = dot(qrot[heads].reshape(GROUPS * ROWS, HEAD), krot[k], 1, 1) * SCALE
        scores = jnp.where(open_scores, scores.reshape(GROUPS, ROWS, ROWS), -1000000000.0)
        powers = jnp.exp(scores - jnp.max(scores, axis=-1, keepdims=True))
        shares = powers / jnp.sum(powers, axis=-1, keepdims=True)
        probs[heads] = shares
        mixed = dot(shares.astype(BF).reshape(GROUPS * ROWS, ROWS), value[k]).astype(BF)
        for group in range(GROUPS):
            at = (k * GROUPS + group) * HEAD
            attended[:, at : at + HEAD] = mixed[group * ROWS : (group + 1) * ROWS]
    for tile in range(WIDTH // TILE):
        copies[QKV // TILE + tile].wait()
        at = tile * TILE
        after[:, at : at + TILE] = x_out[:, at : at + TILE] + dot(
            attended[...], w[:, QKV + at : QKV + at + TILE]
        )
    total = after[...]
    acts_two[...] = (total * unit(total) * gain_ffn).astype(BF)
    rows[...] = dot(take[...], acts_two[...]).astype(BF)
    shares = router_probs(acts_two[...], small)
    router[...] = shares
    share_high, share_low = split(shares)
    spread = expert_lanes()
    high[...] = dot(share_high, spread).astype(BF) * give[...]
    low[...] = dot(share_low, spread).astype(BF) * give[...]


def attn_forward(x, combine, w, tables, take, give, order):
    first = combine is None
    sd = jax.ShapeDtypeStruct
    outs = [
        sd((ROWS, WIDTH), F32), sd((ROWS, WIDTH), BF), sd((QUERY_HEADS, ROWS, HEAD), BF),
        sd((KEY_VALUE_HEADS, ROWS, HEAD), BF), sd((KEY_VALUE_HEADS, ROWS, HEAD), BF),
        sd((QUERY_HEADS, ROWS, ROWS), F32), sd((ROWS, WIDTH), BF), sd((ROWS, WIDTH), F32),
        sd((ROWS, WIDTH), BF), sd((ROWS, HEAD), F32), sd((ROWS, SLOTS), BF), sd((ROWS, SLOTS), BF),
        sd((SLOTS, WIDTH), BF),
    ]
    ins = [x] + ([] if first else list(combine)) + [w, *tables, take, give, order]
    vmem = pl.BlockSpec(memory_space=pltpu.VMEM)
    specs = [vmem] + ([] if first else [ANY, vmem, vmem]) + [ANY] + [vmem] * 5 + [ANY]
    returned_shape = (16, HEAD) if first else (SLOTS, WIDTH)
    result = pl.pallas_call(
        lambda *refs: attn_forward_kernel(first, refs),
        out_shape=outs,
        in_specs=specs,
        out_specs=[vmem] * len(outs),
        scratch_shapes=[
            pltpu.VMEM((WIDTH, PACKED), BF),
            pltpu.VMEM(returned_shape, BF),
            pltpu.SemaphoreType.DMA((2 + SMALL // TILE,)),
        ],
        compiler_params=pltpu.CompilerParams(vmem_limit_bytes=VMEM_BYTES),
        cost_estimate=pl.CostEstimate(
            flops=2 * ROWS * WIDTH * PACKED, bytes_accessed=20 << 20, transcendentals=200000
        ),
        name="attn_forward",
    )(*ins)
    names = (
        "x", "acts", "qrot", "krot", "value", "probs", "attended", "after", "acts_two", "router",
        "high", "low", "rows",
    )
    return dict(zip(names, result))


def norm_back(grad, gain, values):
    scale = unit(values)
    inner = grad * gain
    return scale * inner - values * (scale * scale * scale) * jnp.mean(
        inner * values, axis=-1, keepdims=True
    )


def attn_backward_kernel(last, refs):
    refs = iter(refs)
    (dx_in, back_hbm, w_hbm, cosine, sine, give, router, after, x_in, probs, qrot, krot,
     value) = (next(refs) for _ in range(13))
    if last:
        take_below, router_below = next(refs), next(refs)
    else:
        returned_hbm = next(refs)
    next(refs)
    dx_out, packed = next(refs), next(refs)
    if last:
        rows = next(refs)
    w, back, returned, datt, sems = refs
    pairs = [(back_hbm, back)]
    if not last:
        pairs += [(returned_hbm, returned)]
    pairs += [(w_hbm.at[:, pl.ds(SMALL, HEAD)], w.at[:, pl.ds(SMALL, HEAD)])]
    for start, width in ((QKV, WIDTH), (0, QKV)):
        for at in range(0, WIDTH, TILE):
            block = (pl.ds(at, TILE), pl.ds(start, width))
            pairs += [(w_hbm.at[block], w.at[block])]
    copies = start_all(pairs, sems)
    dx = dx_in[...].astype(F32)
    copies.pop(0).wait()
    spread = expert_lanes(True)
    if last:
        dgate = back[:, WIDTH:].astype(F32)
        drouter = dot(give[...], (dgate[:, 0:1] * spread).astype(BF))
        drouter += dot(give[...], (dgate[:, 1:2] * spread).astype(BF))
    else:
        copies.pop(0).wait()
        dgate = dot(dx.astype(BF), returned[...], 1, 1) * give[...]
        dgate_high, dgate_low = split(dgate)
        drouter = dot(dgate_high, spread) + dot(dgate_low, spread)
    copies.pop(0).wait()
    small = w[:, SMALL:]
    gain_attn, gain_ffn = gain_rows(small)
    shares = router[...]
    dlogits = shares * (drouter - jnp.sum(drouter * shares, axis=-1, keepdims=True))
    dlogits = dlogits.astype(BF)
    dacts_two = dot(dlogits, small, 1, 1) + dot(give[...], back[:, :WIDTH])
    total = after[...]
    scale = unit(total)
    dgain = jnp.sum(dacts_two * total * scale, axis=0, keepdims=True)
    dgain_high, dgain_low = split(dgain)
    pieces = [jnp.zeros((GAIN_HIGH, HEAD), F32)]
    for part in (dgain_high.astype(F32), dgain_low.astype(F32)):
        pieces += [part[:, at : at + HEAD] for at in range(0, WIDTH, HEAD)]
        pieces += [jnp.zeros((GAIN_LOW - GAIN_HIGH - PIECES, HEAD), F32)]
    pieces += [jnp.zeros((HEAD - 2 * GAIN_LOW + GAIN_HIGH, HEAD), F32)]
    packed[:, SMALL:] = (dlogits.astype(F32) + jnp.concatenate(pieces, axis=0).T).astype(BF)
    dafter = dx + norm_back(dacts_two, gain_ffn, total)
    dx_out[...] = dafter
    packed[:, QKV:SMALL] = dafter.astype(BF)
    for tile in range(WIDTH // TILE):
        copies[tile].wait()
        wide = dot(
            packed[:, QKV:SMALL], w[tile * TILE : (tile + 1) * TILE, QKV:SMALL], 1, 1
        ).astype(BF)
        for half in range(TILE // HEAD):
            datt[tile * (TILE // HEAD) + half] = wide[:, half * HEAD : (half + 1) * HEAD]
    for k in range(KEY_VALUE_HEADS):
        heads = slice(k * GROUPS, (k + 1) * GROUPS)
        datt_k = datt[heads].reshape(GROUPS * ROWS, HEAD)
        p = probs[heads].reshape(GROUPS * ROWS, ROWS)
        dprobs = dot(datt_k, value[k], 1, 1)
        dvalue = dot(p.astype(BF), datt_k, 0, 0)
        dscores = (p * (dprobs - jnp.sum(dprobs * p, axis=-1, keepdims=True))).astype(BF)
        dqrot = dot(dscores, krot[k]) * SCALE
        dkrot = dot(dscores, qrot[heads].reshape(GROUPS * ROWS, HEAD), 0, 0) * SCALE
        for group in range(GROUPS):
            at = (k * GROUPS + group) * HEAD
            part = dqrot[group * ROWS : (group + 1) * ROWS]
            packed[:, at : at + HEAD] = turn(part, cosine[...], -sine[...]).astype(BF)
        at = Q_END + k * HEAD
        packed[:, at : at + HEAD] = turn(dkrot, cosine[...], -sine[...]).astype(BF)
        at = K_END + k * HEAD
        packed[:, at : at + HEAD] = dvalue.astype(BF)
    parts = []
    for tile in range(WIDTH // TILE):
        copies[WIDTH // TILE + tile].wait()
        parts += [dot(packed[:, :QKV], w[tile * TILE : (tile + 1) * TILE, :QKV], 1, 1)]
    dacts = jnp.concatenate(parts, axis=1)
    dx = dx_out[...] + norm_back(dacts, gain_attn, x_in[...].astype(F32))
    dx_out[...] = dx
    if last:
        dx_low = dx.astype(BF)
        below_high, below_low = split(router_below[...])
        gates = dot(spread, below_high, 1, 1).astype(BF) * take_below[...]
        gates_low = dot(spread, below_low, 1, 1).astype(BF) * take_below[...]
        rows[...] = (dot(gates, dx_low) + dot(gates_low, dx_low)).astype(BF)


def attn_backward(dx, back, kept, w, tables, give, below, returned, order):
    last = below is not None
    sd = jax.ShapeDtypeStruct
    outs = [sd((ROWS, WIDTH), F32), sd((ROWS, PACKED), BF)]
    if last:
        outs += [sd((SLOTS, WIDTH), BF)]
    vmem = pl.BlockSpec(memory_space=pltpu.VMEM)
    ins = [dx, back, w, tables[0], tables[1], give]
    ins += [kept[n] for n in ("router", "after", "x", "probs", "qrot", "krot", "value")]
    specs = [vmem, ANY, ANY] + [vmem] * 10
    if last:
        ins += list(below)
        specs += [vmem] * 2
    else:
        ins += [returned]
        specs += [ANY]
    return pl.pallas_call(
        lambda *refs: attn_backward_kernel(last, refs),
        out_shape=outs,
        in_specs=specs + [ANY],
        out_specs=[vmem] * len(outs),
        scratch_shapes=[
            pltpu.VMEM((WIDTH, PACKED), BF),
            pltpu.VMEM(back.shape, BF),
            pltpu.VMEM((16, HEAD) if last else (SLOTS, WIDTH), BF),
            pltpu.VMEM((QUERY_HEADS, ROWS, HEAD), BF),
            pltpu.SemaphoreType.DMA((3 + 2 * WIDTH // TILE,)),
        ],
        compiler_params=pltpu.CompilerParams(vmem_limit_bytes=VMEM_BYTES),
        cost_estimate=pl.CostEstimate(
            flops=2 * ROWS * WIDTH * PACKED, bytes_accessed=20 << 20, transcendentals=0
        ),
        name="attn_backward",
    )(*ins, order)


def gelu_parts(gate):
    square = gate * gate
    bend = jnp.tanh(GELU_A * gate * (1.0 + GELU_B * square))
    return bend, square


def gelu(gate):
    bend, _ = gelu_parts(gate)
    return 0.5 * gate * (1.0 + bend)


def gelu_both(gate):
    bend, square = gelu_parts(gate)
    slope = 0.5 * (1.0 + bend) + 0.5 * gate * (1.0 - bend * bend) * GELU_A * (
        1.0 + 3.0 * GELU_B * square
    )
    return 0.5 * gate * (1.0 + bend), slope


def row_block(width):
    return pl.BlockSpec((BLOCK, width), lambda i: (i, 0))


def expert_block(l, rows, columns):
    return pl.BlockSpec((None, None, rows, columns), lambda i: (l, 0, 0, 0))


def experts_forward_kernel(received, gate_w, up_w, down_w, _, gate_pre, up_pre, hidden, out):
    gate = dot(received[...], gate_w[...])
    up = dot(received[...], up_w[...])
    gate_pre[...] = gate
    up_pre[...] = up
    hidden[...] = (gelu(gate) * up).astype(BF)
    out[...] = dot(hidden[...], down_w[...]).astype(BF)


def experts_forward(l, received, weights, order):
    sd = jax.ShapeDtypeStruct
    return pl.pallas_call(
        experts_forward_kernel,
        grid=(SLOTS // BLOCK,),
        out_shape=[
            sd((SLOTS, FF), F32), sd((SLOTS, FF), F32), sd((SLOTS, FF), BF), sd((SLOTS, WIDTH), BF)
        ],
        in_specs=[
            row_block(WIDTH), expert_block(l, WIDTH, FF), expert_block(l, WIDTH, FF),
            expert_block(l, FF, WIDTH), ANY,
        ],
        out_specs=[row_block(FF), row_block(FF), row_block(FF), row_block(WIDTH)],
        compiler_params=pltpu.CompilerParams(vmem_limit_bytes=VMEM_BYTES),
        cost_estimate=pl.CostEstimate(
            flops=6 * SLOTS * WIDTH * FF, bytes_accessed=20 << 20, transcendentals=SLOTS * FF
        ),
        name="experts_forward",
    )(received, *weights, order)


def experts_both_kernel(
    me, received, dx, small, gate_w, up_w, down_w, _,
    hidden, out, dslot, dgate_pre, dup_pre, back,
):
    gate = dot(received[...], gate_w[...])
    up = dot(received[...], up_w[...])
    act, slope = gelu_both(gate)
    hidden[...] = (act * up).astype(BF)
    out_low = dot(hidden[...], down_w[...]).astype(BF)
    out[...] = out_low
    shares = router_probs(received[...], small[...])
    lane = lax.broadcasted_iota(jnp.int32, shares.shape, 1)
    weight = jnp.sum(jnp.where(lane == me[0], shares, 0.0), axis=-1, keepdims=True)
    dx_wide = dx[...].astype(F32)
    dslot[...] = (weight * dx_wide).astype(BF)
    dgate = jnp.sum(dx_wide * out_low.astype(F32), axis=-1, keepdims=True)
    dgate_high, dgate_low = split(dgate)
    back[:, WIDTH:] = jnp.where(
        lane == 0, dgate_high.astype(F32), jnp.where(lane == 1, dgate_low.astype(F32), 0.0)
    ).astype(BF)
    dhidden = dot(dslot[...], down_w[...], 1, 1)
    dgate_pre[...] = (dhidden * up * slope).astype(BF)
    dup_pre[...] = (dhidden * act).astype(BF)
    back[:, :WIDTH] = (
        dot(dgate_pre[...], gate_w[...], 1, 1) + dot(dup_pre[...], up_w[...], 1, 1)
    ).astype(BF)


def experts_both(l, me, received, dx, w, weights, order):
    sd = jax.ShapeDtypeStruct
    return pl.pallas_call(
        experts_both_kernel,
        grid=(SLOTS // BLOCK,),
        out_shape=[
            sd((SLOTS, FF), BF), sd((SLOTS, WIDTH), BF), sd((SLOTS, WIDTH), BF),
            sd((SLOTS, FF), BF), sd((SLOTS, FF), BF), sd((SLOTS, WIDTH + HEAD), BF),
        ],
        in_specs=[
            pl.BlockSpec(memory_space=pltpu.SMEM), row_block(WIDTH), row_block(WIDTH),
            pl.BlockSpec((WIDTH, HEAD), lambda i: (0, SMALL // HEAD)),
            expert_block(l, WIDTH, FF), expert_block(l, WIDTH, FF), expert_block(l, FF, WIDTH), ANY,
        ],
        out_specs=[
            row_block(FF), row_block(WIDTH), row_block(WIDTH), row_block(FF), row_block(FF),
            row_block(WIDTH + HEAD),
        ],
        compiler_params=pltpu.CompilerParams(vmem_limit_bytes=VMEM_BYTES),
        cost_estimate=pl.CostEstimate(
            flops=12 * SLOTS * WIDTH * FF, bytes_accessed=24 << 20, transcendentals=SLOTS * FF
        ),
        name="experts_both",
    )(me, received, dx, w, *weights, order)


def experts_backward_kernel(
    dslot, gate_pre, up_pre, gate_w, up_w, down_w, _, dgate_pre, dup_pre, back
):
    dhidden = dot(dslot[...], down_w[...], 1, 1)
    act, slope = gelu_both(gate_pre[...])
    dgate_pre[...] = (dhidden * up_pre[...] * slope).astype(BF)
    dup_pre[...] = (dhidden * act).astype(BF)
    back[...] = (
        dot(dgate_pre[...], gate_w[...], 1, 1) + dot(dup_pre[...], up_w[...], 1, 1)
    ).astype(BF)


def experts_backward(l, dslot, gate_pre, up_pre, weights, order):
    sd = jax.ShapeDtypeStruct
    return pl.pallas_call(
        experts_backward_kernel,
        grid=(SLOTS // BLOCK,),
        out_shape=[sd((SLOTS, FF), BF), sd((SLOTS, FF), BF), sd((SLOTS, WIDTH), BF)],
        in_specs=[
            row_block(WIDTH), row_block(FF), row_block(FF),
            expert_block(l, WIDTH, FF), expert_block(l, WIDTH, FF), expert_block(l, FF, WIDTH), ANY,
        ],
        out_specs=[row_block(FF), row_block(FF), row_block(WIDTH)],
        compiler_params=pltpu.CompilerParams(vmem_limit_bytes=VMEM_BYTES),
        cost_estimate=pl.CostEstimate(
            flops=6 * SLOTS * WIDTH * FF, bytes_accessed=20 << 20, transcendentals=SLOTS * FF
        ),
        name="experts_backward",
    )(dslot, gate_pre, up_pre, *weights, order)


def expert_grads_kernel(received, dgate_pre, dup_pre, hidden, dslot, _, packed):
    gate = dot(received[...], dgate_pre[...], 0, 0).astype(BF)
    up = dot(received[...], dup_pre[...], 0, 0).astype(BF)
    down = dot(hidden[...], dslot[...], 0, 0).astype(BF)
    for part in range(DP // 2):
        packed[part, :SHARD, :FF] = gate[part * SHARD : (part + 1) * SHARD]
        packed[part, :SHARD, FF:] = up[part * SHARD : (part + 1) * SHARD]
        packed[part, SHARD:] = down[part * FF // DP : (part + 1) * FF // DP]


def expert_grads(received, dgate_pre, dup_pre, hidden, dslot, order):
    rows = SHARD + FF // DP
    whole = lambda width: pl.BlockSpec((SLOTS, width), lambda i: (0, 0))
    part = lambda width: pl.BlockSpec((SLOTS, width), lambda i: (0, i))
    return pl.pallas_call(
        expert_grads_kernel,
        grid=(2,),
        out_shape=jax.ShapeDtypeStruct((DP, rows, WIDTH), BF),
        in_specs=[part(WIDTH // 2), whole(FF), whole(FF), part(FF // 2), whole(WIDTH), ANY],
        out_specs=pl.BlockSpec((DP // 2, rows, WIDTH), lambda i: (i, 0, 0)),
        compiler_params=pltpu.CompilerParams(vmem_limit_bytes=VMEM_BYTES),
        cost_estimate=pl.CostEstimate(
            flops=6 * SLOTS * WIDTH * FF, bytes_accessed=14 << 20, transcendentals=0
        ),
        name="expert_grads",
    )(received, dgate_pre, dup_pre, hidden, dslot, order).reshape(DP * rows, WIDTH)


def seq_tables(counts):
    ends = jnp.cumsum(counts)
    starts = ends - counts
    place = jnp.arange(ROWS, dtype=jnp.int32)
    member = (place[:, None] >= starts[None, :]) & (place[:, None] < ends[None, :])
    index = jnp.arange(counts.shape[0], dtype=jnp.int32)
    segment = jnp.sum(jnp.where(member, index[None, :], 0), axis=1)
    position = place - jnp.sum(jnp.where(member, starts[None, :], 0), axis=1)
    allowed = (segment[:, None] == segment[None, :]) & (place[:, None] >= place[None, :])
    freqs = ROPE_BASE ** (-2.0 * jnp.arange(HEAD // 2, dtype=F32) / HEAD)
    angle = position.astype(F32)[:, None] * freqs[None, :]
    cosine, sine = jnp.cos(angle), jnp.sin(angle)
    return (
        jnp.concatenate([cosine, cosine], axis=1),
        jnp.concatenate([-sine, sine], axis=1),
        allowed.astype(F32),
    )


def slot_matrix(choices):
    experts = jnp.arange(EXPERTS, dtype=jnp.int32)
    member = jnp.any(choices[:, :, None] == experts[None, None, :], axis=1).astype(BF)
    row = lax.broadcasted_iota(jnp.int32, (ROWS, ROWS), 0)
    column = lax.broadcasted_iota(jnp.int32, (ROWS, ROWS), 1)
    rank = dot((column < row).astype(BF), member).astype(BF)
    expert = lax.broadcasted_iota(jnp.int32, (EXPERTS, SLOTS), 0)
    slot = lax.broadcasted_iota(jnp.int32, (EXPERTS, SLOTS), 1)
    expand = (slot // CAP == expert).astype(BF)
    place = (lax.broadcasted_iota(jnp.int32, (ROWS, SLOTS), 1) % CAP).astype(F32)
    return ((dot(member, expand) > 0.5) & (dot(rank, expand) == place)).astype(BF)


def exchange(rows):
    width = rows.shape[-1]
    moved = lax.all_to_all(
        rows.reshape(EXPERTS, CAP, width), "expert", split_axis=0, concat_axis=0, tiled=True
    )
    return moved.reshape(SLOTS, width)


def columns_to_owners(arrays):
    packed = jnp.stack([a.reshape(ROWS, DP, SHARD) for a in arrays], axis=2)
    packed = packed.transpose(1, 0, 2, 3).reshape(DP, ROWS, len(arrays) * SHARD)
    moved = lax.all_to_all(packed, "dp", split_axis=0, concat_axis=0, tiled=True)
    return moved.reshape(DP * ROWS, len(arrays) * SHARD)


def sum_experts(values):
    width = values.shape[1] // EXPERTS
    pieces = values.astype(BF).reshape(SHARD, EXPERTS, width).transpose(1, 0, 2)
    pieces = lax.all_to_all(pieces, "expert", split_axis=0, concat_axis=0, tiled=True)
    mine = jnp.sum(pieces.astype(F32), axis=0).astype(BF)
    whole = lax.all_to_all(
        jnp.broadcast_to(mine[None], (EXPERTS, SHARD, width)),
        "expert", split_axis=0, concat_axis=0, tiled=True,
    )
    return whole.transpose(1, 0, 2).reshape(SHARD, EXPERTS * width).astype(F32)


def dense_grads(columns, rows, me_dp):
    part = lambda i: columns[:, i * SHARD : (i + 1) * SHARD]
    grad_qkv = dot(part(0), rows[:, :QKV], 0, 0)
    grad_out = dot(part(1), rows[:, QKV:SMALL], 0, 0)
    grad_router = dot(part(2), rows[:, SMALL:], 0, 0)[:, :EXPERTS]
    ends = jnp.sum(rows[:, SMALL:].astype(F32).reshape(DP, ROWS, HEAD), axis=0)
    gain = ends[:, GAIN_HIGH : GAIN_HIGH + PIECES] + ends[:, GAIN_LOW : GAIN_LOW + PIECES]
    gain = lax.dynamic_slice_in_dim(gain.T.reshape(WIDTH), me_dp * SHARD, SHARD, 0)
    gain_high, gain_low = split(gain[:, None])
    wide = jnp.concatenate(
        [grad_qkv, grad_out, grad_router, gain_high.astype(F32), gain_low.astype(F32)], axis=1
    )
    return sum_experts(jnp.pad(wide, ((0, 0), (0, 4096 - wide.shape[1]))))


def local(
    tokens, cotangent, lengths, routes, norm_attn, w_query, key_projection, value_projection,
    w_out, norm_ffn, w_router, w_gate, w_up, w_down,
):
    me_dp = lax.axis_index("dp")
    me_expert = lax.axis_index("expert").astype(jnp.int32).reshape(1)
    tables = seq_tables(lengths[0])
    give = [slot_matrix(routes[l]) for l in range(LAYERS)]
    take = [g.T for g in give]
    experts = (w_gate, w_up, w_down)

    shard_qkv = [
        jnp.concatenate([w_query[l], key_projection[l], value_projection[l]], axis=1)
        for l in range(LAYERS)
    ]
    w = []
    for l in range(LAYERS):
        shard = jnp.concatenate(
            [shard_qkv[l], w_out[l], w_router[l], norm_attn[l][:, None], norm_ffn[l][:, None],
             jnp.zeros((SHARD, HEAD - EXPERTS - 2), BF)],
            axis=1,
        )
        w.append(lax.all_gather(shard, "dp", axis=0, tiled=True))

    dx_rows = exchange(dot(take[1], cotangent).astype(BF))

    kept0 = attn_forward(tokens, None, w[0], tables, take[0], give[0], dx_rows)
    received0 = exchange(kept0["rows"])
    gate_pre0, up_pre0, hidden0, out0 = experts_forward(0, received0, experts, me_expert)
    returned0 = exchange(out0)
    columns0 = columns_to_owners([kept0["acts"], kept0["attended"], kept0["acts_two"]])

    kept1 = attn_forward(
        kept0["after"], (returned0, kept0["high"], kept0["low"]), w[1], tables, take[1], give[1],
        columns0,
    )
    received1 = exchange(kept1["rows"])
    columns1 = columns_to_owners([kept1["acts"], kept1["attended"], kept1["acts_two"]])
    hidden1, out1, dslot1, dgate_pre1, dup_pre1, back1 = experts_both(
        1, me_expert, received1, dx_rows, w[1], experts, columns1
    )
    back1 = exchange(back1)
    shares1 = lax.psum_scatter(
        expert_grads(received1, dgate_pre1, dup_pre1, hidden1, dslot1, me_expert),
        "dp", scatter_dimension=0, tiled=True,
    )
    returned1 = exchange(out1)
    mixed = kept1["after"] + dot(kept1["high"], returned1) + dot(kept1["low"], returned1)

    dx0, packed1, rows0 = attn_backward(
        cotangent, back1, kept1, w[1], tables, give[1], (take[0], kept0["router"]), None,
        me_expert,
    )
    dslot0 = exchange(rows0)
    factors1 = lax.all_gather(packed1, "dp", axis=0, tiled=True)
    dgate_pre0, dup_pre0, back0 = experts_backward(
        0, dslot0, gate_pre0, up_pre0, experts, me_expert
    )
    back0 = exchange(back0)
    grad_tokens, packed0 = attn_backward(
        dx0, back0, kept0, w[0], tables, give[0], None, returned0, factors1
    )
    factors0 = lax.all_gather(packed0, "dp", axis=0, tiled=True)
    sums1 = dense_grads(columns1, factors1, me_dp)
    shares0 = lax.psum_scatter(
        expert_grads(received0, dgate_pre0, dup_pre0, hidden0, dslot0, packed0),
        "dp", scatter_dimension=0, tiled=True,
    )
    sums0 = dense_grads(columns0, factors0, me_dp)

    sums = [sums0, sums1]
    shares = [shares0.astype(F32), shares1.astype(F32)]
    grad_norm_attn = [
        jnp.sum(sums[l][:, :QKV] * shard_qkv[l].astype(F32), axis=1) / norm_attn[l].astype(F32)
        for l in range(LAYERS)
    ]
    gain_at = SMALL + EXPERTS
    return (
        mixed.astype(BF),
        grad_tokens,
        jnp.stack(grad_norm_attn),
        jnp.stack([s[:, :Q_END] for s in sums]),
        jnp.stack([s[:, Q_END:K_END] for s in sums]),
        jnp.stack([s[:, K_END:QKV] for s in sums]),
        jnp.stack([s[:, QKV:SMALL] for s in sums]),
        jnp.stack([s[:, gain_at] + s[:, gain_at + 1] for s in sums]),
        jnp.stack([s[:, SMALL:gain_at] for s in sums]),
        jnp.stack([s[:SHARD, :FF] for s in shares])[:, None],
        jnp.stack([s[:SHARD, FF:] for s in shares])[:, None],
        jnp.stack([s[SHARD:] for s in shares])[:, None],
    )


def solution(mesh):
    placed = (
        P(("dp", "expert"), None),
        P(("dp", "expert"), None),
        P(("dp", "expert"), None),
        P(None, ("dp", "expert"), None),
        P(None, "dp"),
        P(None, "dp", None),
        P(None, "dp", None),
        P(None, "dp", None),
        P(None, "dp", None),
        P(None, "dp"),
        P(None, "dp", None),
        P(None, "expert", None, None),
        P(None, "expert", None, None),
        P(None, "expert", None, None),
    )
    return jax.shard_map(
        local,
        mesh=mesh,
        in_specs=placed,
        out_specs=(
            P(("dp", "expert"), None),
            P(("dp", "expert"), None),
            P(None, "dp"),
            P(None, "dp", None),
            P(None, "dp", None),
            P(None, "dp", None),
            P(None, "dp", None),
            P(None, "dp"),
            P(None, "dp", None),
            P(None, "expert", "dp", None),
            P(None, "expert", "dp", None),
            P(None, "expert", "dp", None),
        ),
        check_vma=False,
    )
```

```python
import jax
import jax.numpy as jnp
from jax import lax
from jax.experimental import pallas as pl
from jax.experimental.pallas import tpu as pltpu
from jax.sharding import PartitionSpec as P

QUERY_HEADS = 12
KEY_VALUE_HEADS = 2
GROUPS = QUERY_HEADS // KEY_VALUE_HEADS
HEAD = 128
LAYERS = 2
WIDTH = 1536
FF = 768
ROWS = 128
EXPERTS = 16
CAP = 48
SLOTS = EXPERTS * CAP
DP = 8
SHARD = WIDTH // DP
Q_END = QUERY_HEADS * HEAD
K_END = Q_END + KEY_VALUE_HEADS * HEAD
QKV = K_END + KEY_VALUE_HEADS * HEAD
SMALL = QKV + WIDTH
PACKED = SMALL + HEAD
GAIN_ATTN, GAIN_FFN = 16, 17
GAIN_HIGH, GAIN_LOW = 16, 32
PIECES = WIDTH // HEAD
TILE = 256
PARTS = 3
PART = SLOTS // PARTS
PART_ROWS = CAP // PARTS
CHUNKS, CHUNK = 16, 256
COLUMNS = 3 * WIDTH
EPSILON = 1e-06
ROPE_BASE = 1000000.0
SCALE = HEAD ** (-0.5)
GELU_A = 0.7978845608028654
GELU_B = 0.044715
VMEM_BYTES = 56 << 20
BF = jnp.bfloat16
F32 = jnp.float32
ANY = pl.BlockSpec(memory_space=pl.ANY)


def dot(left, right, left_dim=1, right_dim=0):
    return lax.dot_general(
        left, right, (((left_dim,), (right_dim,)), ((), ())), preferred_element_type=F32
    )


def split(values):
    high = values.astype(BF)
    return high, (values - high.astype(F32)).astype(BF)


def unit(values):
    return lax.rsqrt(jnp.mean(values * values, axis=-1, keepdims=True) + EPSILON)


def turn(values, cosine, sine):
    return values * cosine + pltpu.roll(values, HEAD // 2, 1) * sine


def expert_lanes(transposed=False, in_parts=False):
    shape = (SLOTS, HEAD) if transposed else (HEAD, SLOTS)
    slot = lax.broadcasted_iota(jnp.int32, shape, 0 if transposed else 1)
    expert = lax.broadcasted_iota(jnp.int32, shape, 1 if transposed else 0)
    if in_parts:
        held = ((slot & (PART - 1)) >> 4) == expert
    else:
        held = (slot >= expert * CAP) & (slot < expert * CAP + CAP)
    return held.astype(F32).astype(BF)


def gain_rows(small):
    row = lax.broadcasted_iota(jnp.int32, (8, HEAD), 0)
    lane = lax.broadcasted_iota(jnp.int32, (8, HEAD), 1)
    pick = ((lane == row + GAIN_ATTN) & (row < 2)).astype(F32).astype(BF)
    rows = dot(pick, small, 1, 1)
    return rows[0:1], rows[1:2]


def router_probs(rows, small):
    logits = dot(rows, small)
    lane = lax.broadcasted_iota(jnp.int32, logits.shape, 1)
    logits = jnp.where(lane < EXPERTS, logits, -1e30)
    powers = jnp.exp(logits - jnp.max(logits, axis=-1, keepdims=True))
    return powers / jnp.sum(powers, axis=-1, keepdims=True)


def start_all(pairs, sems):
    copies = [
        pltpu.make_async_copy(source, target, sems.at[i]) for i, (source, target) in enumerate(pairs)
    ]
    for copy in copies:
        copy.start()
    return copies


def attn_forward_kernel(first, order_count, refs):
    refs = iter(refs)
    x_in = next(refs)
    if not first:
        returned_hbm, high_in, low_in = next(refs), next(refs), next(refs)
    w_hbm, cosine, sine, allowed, take, give = (next(refs) for _ in range(6))
    for _ in range(order_count):
        next(refs)
    (x_out, columns, qrot, krot, value, probs, after, router, high, low, rows,
     w, returned, sems) = refs
    acts = columns.at[:, :WIDTH]
    attended = columns.at[:, WIDTH : 2 * WIDTH]
    acts_two = columns.at[:, 2 * WIDTH :]
    pairs = []
    if not first:
        pairs += [(returned_hbm, returned)]
    pairs += [(w_hbm.at[:, pl.ds(SMALL, HEAD)], w.at[:, pl.ds(SMALL, HEAD)])]
    pairs += [
        (w_hbm.at[:, pl.ds(at, TILE)], w.at[:, pl.ds(at, TILE)]) for at in range(0, SMALL, TILE)
    ]
    copies = start_all(pairs, sems)
    if first:
        x = x_in[...].astype(F32)
    else:
        copies.pop(0).wait()
        x = x_in[...] + dot(high_in[...], returned[...]) + dot(low_in[...], returned[...])
    x_out[...] = x
    copies.pop(0).wait()
    small = w[:, SMALL:]
    gain_attn, gain_ffn = gain_rows(small)
    acts[...] = (x * unit(x) * gain_attn).astype(BF)
    for tile in range(QKV // TILE):
        copies[tile].wait()
        wide = dot(acts[...], w[:, tile * TILE : (tile + 1) * TILE])
        for half in range(TILE // HEAD):
            head = tile * (TILE // HEAD) + half
            part = wide[:, half * HEAD : (half + 1) * HEAD]
            if head < QUERY_HEADS:
                qrot[head] = turn(part, cosine[...], sine[...]).astype(BF)
            elif head < QUERY_HEADS + KEY_VALUE_HEADS:
                krot[head - QUERY_HEADS] = turn(part, cosine[...], sine[...]).astype(BF)
            else:
                value[head - QUERY_HEADS - KEY_VALUE_HEADS] = part.astype(BF)
    open_scores = (allowed[...] > 0.5)[None]
    for k in range(KEY_VALUE_HEADS):
        heads = slice(k * GROUPS, (k + 1) * GROUPS)
        scores = dot(qrot[heads].reshape(GROUPS * ROWS, HEAD), krot[k], 1, 1) * SCALE
        scores = jnp.where(open_scores, scores.reshape(GROUPS, ROWS, ROWS), -1000000000.0)
        powers = jnp.exp(scores - jnp.max(scores, axis=-1, keepdims=True))
        shares = powers / jnp.sum(powers, axis=-1, keepdims=True)
        probs[heads] = shares
        mixed = dot(shares.astype(BF).reshape(GROUPS * ROWS, ROWS), value[k]).astype(BF)
        for group in range(GROUPS):
            at = (k * GROUPS + group) * HEAD
            attended[:, at : at + HEAD] = mixed[group * ROWS : (group + 1) * ROWS]
    for tile in range(WIDTH // TILE):
        copies[QKV // TILE + tile].wait()
        at = tile * TILE
        after[:, at : at + TILE] = x_out[:, at : at + TILE] + dot(
            attended[...], w[:, QKV + at : QKV + at + TILE]
        )
    total = after[...]
    acts_two[...] = (total * unit(total) * gain_ffn).astype(BF)
    rows[...] = dot(take[...], acts_two[...]).astype(BF)
    shares = router_probs(acts_two[...], small)
    router[...] = shares
    share_high, share_low = split(shares)
    spread = expert_lanes(in_parts=not first)
    high[...] = dot(share_high, spread).astype(BF) * give[...]
    low[...] = dot(share_low, spread).astype(BF) * give[...]


def attn_forward(x, combine, w, tables, take, give, order):
    first = combine is None
    sd = jax.ShapeDtypeStruct
    outs = [
        sd((ROWS, WIDTH), F32), sd((ROWS, COLUMNS), BF), sd((QUERY_HEADS, ROWS, HEAD), BF),
        sd((KEY_VALUE_HEADS, ROWS, HEAD), BF), sd((KEY_VALUE_HEADS, ROWS, HEAD), BF),
        sd((QUERY_HEADS, ROWS, ROWS), F32), sd((ROWS, WIDTH), F32), sd((ROWS, HEAD), F32),
        sd((ROWS, SLOTS), BF), sd((ROWS, SLOTS), BF), sd((SLOTS, WIDTH), BF),
    ]
    ins = [x] + ([] if first else list(combine)) + [w, *tables, take, give, *order]
    vmem = pl.BlockSpec(memory_space=pltpu.VMEM)
    specs = [vmem] + ([] if first else [ANY, vmem, vmem]) + [ANY] + [vmem] * 5
    specs += [ANY] * len(order)
    returned_shape = (16, HEAD) if first else (SLOTS, WIDTH)
    result = pl.pallas_call(
        lambda *refs: attn_forward_kernel(first, len(order), refs),
        out_shape=outs,
        in_specs=specs,
        out_specs=[vmem] * len(outs),
        scratch_shapes=[
            pltpu.VMEM((WIDTH, PACKED), BF),
            pltpu.VMEM(returned_shape, BF),
            pltpu.SemaphoreType.DMA((2 + SMALL // TILE,)),
        ],
        compiler_params=pltpu.CompilerParams(vmem_limit_bytes=VMEM_BYTES),
        cost_estimate=pl.CostEstimate(
            flops=2 * ROWS * WIDTH * PACKED, bytes_accessed=20 << 20, transcendentals=200000
        ),
        name="attn_forward",
    )(*ins)
    names = (
        "x", "columns", "qrot", "krot", "value", "probs", "after", "router", "high", "low", "rows",
    )
    return dict(zip(names, result))


def norm_back(grad, gain, values):
    scale = unit(values)
    inner = grad * gain
    return scale * inner - values * (scale * scale * scale) * jnp.mean(
        inner * values, axis=-1, keepdims=True
    )


def attn_backward_kernel(last, order_count, refs):
    refs = iter(refs)
    (dx_in, back_hbm, w_hbm, cosine, sine, give, router, after, x_in, probs, qrot, krot,
     value) = (next(refs) for _ in range(13))
    if last:
        take_below, router_below = next(refs), next(refs)
    else:
        returned_hbm = next(refs)
    for _ in range(order_count):
        next(refs)
    dx_out, packed = next(refs), next(refs)
    if last:
        rows = next(refs)
    w, back, returned, datt, sems = refs
    pairs = [(back_hbm, back)]
    if not last:
        pairs += [(returned_hbm, returned)]
    pairs += [(w_hbm.at[:, pl.ds(SMALL, HEAD)], w.at[:, pl.ds(SMALL, HEAD)])]
    for start, width in ((QKV, WIDTH), (0, QKV)):
        for at in range(0, WIDTH, TILE):
            block = (pl.ds(at, TILE), pl.ds(start, width))
            pairs += [(w_hbm.at[block], w.at[block])]
    copies = start_all(pairs, sems)
    dx = dx_in[...].astype(F32)
    copies.pop(0).wait()
    spread = expert_lanes(True)
    if last:
        dgate = back[:, WIDTH:].astype(F32)
        drouter = dot(give[...], (dgate[:, 0:1] * spread).astype(BF))
        drouter += dot(give[...], (dgate[:, 1:2] * spread).astype(BF))
    else:
        copies.pop(0).wait()
        dgate = dot(dx.astype(BF), returned[...], 1, 1) * give[...]
        dgate_high, dgate_low = split(dgate)
        drouter = dot(dgate_high, spread) + dot(dgate_low, spread)
    copies.pop(0).wait()
    small = w[:, SMALL:]
    gain_attn, gain_ffn = gain_rows(small)
    shares = router[...]
    dlogits = shares * (drouter - jnp.sum(drouter * shares, axis=-1, keepdims=True))
    dlogits = dlogits.astype(BF)
    dacts_two = dot(dlogits, small, 1, 1) + dot(give[...], back[:, :WIDTH])
    total = after[...]
    scale = unit(total)
    dgain = jnp.sum(dacts_two * total * scale, axis=0, keepdims=True)
    dgain_high, dgain_low = split(dgain)
    pieces = [jnp.zeros((GAIN_HIGH, HEAD), F32)]
    for part in (dgain_high.astype(F32), dgain_low.astype(F32)):
        pieces += [part[:, at : at + HEAD] for at in range(0, WIDTH, HEAD)]
        pieces += [jnp.zeros((GAIN_LOW - GAIN_HIGH - PIECES, HEAD), F32)]
    pieces += [jnp.zeros((HEAD - 2 * GAIN_LOW + GAIN_HIGH, HEAD), F32)]
    packed[:, SMALL:] = (dlogits.astype(F32) + jnp.concatenate(pieces, axis=0).T).astype(BF)
    dafter = dx + norm_back(dacts_two, gain_ffn, total)
    dx_out[...] = dafter
    packed[:, QKV:SMALL] = dafter.astype(BF)
    for tile in range(WIDTH // TILE):
        copies[tile].wait()
        wide = dot(
            packed[:, QKV:SMALL], w[tile * TILE : (tile + 1) * TILE, QKV:SMALL], 1, 1
        ).astype(BF)
        for half in range(TILE // HEAD):
            datt[tile * (TILE // HEAD) + half] = wide[:, half * HEAD : (half + 1) * HEAD]
    for k in range(KEY_VALUE_HEADS):
        heads = slice(k * GROUPS, (k + 1) * GROUPS)
        datt_k = datt[heads].reshape(GROUPS * ROWS, HEAD)
        p = probs[heads].reshape(GROUPS * ROWS, ROWS)
        dprobs = dot(datt_k, value[k], 1, 1)
        dvalue = dot(p.astype(BF), datt_k, 0, 0)
        dscores = (p * (dprobs - jnp.sum(dprobs * p, axis=-1, keepdims=True))).astype(BF)
        dqrot = dot(dscores, krot[k]) * SCALE
        dkrot = dot(dscores, qrot[heads].reshape(GROUPS * ROWS, HEAD), 0, 0) * SCALE
        for group in range(GROUPS):
            at = (k * GROUPS + group) * HEAD
            part = dqrot[group * ROWS : (group + 1) * ROWS]
            packed[:, at : at + HEAD] = turn(part, cosine[...], -sine[...]).astype(BF)
        at = Q_END + k * HEAD
        packed[:, at : at + HEAD] = turn(dkrot, cosine[...], -sine[...]).astype(BF)
        at = K_END + k * HEAD
        packed[:, at : at + HEAD] = dvalue.astype(BF)
    parts = []
    for tile in range(WIDTH // TILE):
        copies[WIDTH // TILE + tile].wait()
        parts += [dot(packed[:, :QKV], w[tile * TILE : (tile + 1) * TILE, :QKV], 1, 1)]
    dacts = jnp.concatenate(parts, axis=1)
    dx = dx_out[...] + norm_back(dacts, gain_attn, x_in[...].astype(F32))
    dx_out[...] = dx
    if last:
        dx_low = dx.astype(BF)
        below_high, below_low = split(router_below[...])
        gates = dot(spread, below_high, 1, 1).astype(BF) * take_below[...]
        gates_low = dot(spread, below_low, 1, 1).astype(BF) * take_below[...]
        rows[...] = (dot(gates, dx_low) + dot(gates_low, dx_low)).astype(BF)


def attn_backward(dx, back, kept, w, tables, give, below, returned, order):
    last = below is not None
    sd = jax.ShapeDtypeStruct
    outs = [sd((ROWS, WIDTH), F32), sd((ROWS, PACKED), BF)]
    if last:
        outs += [sd((SLOTS, WIDTH), BF)]
    vmem = pl.BlockSpec(memory_space=pltpu.VMEM)
    ins = [dx, back, w, tables[0], tables[1], give]
    ins += [kept[n] for n in ("router", "after", "x", "probs", "qrot", "krot", "value")]
    specs = [vmem, ANY, ANY] + [vmem] * 10
    if last:
        ins += list(below)
        specs += [vmem] * 2
    else:
        ins += [returned]
        specs += [ANY]
    return pl.pallas_call(
        lambda *refs: attn_backward_kernel(last, len(order), refs),
        out_shape=outs,
        in_specs=specs + [ANY] * len(order),
        out_specs=[vmem] * len(outs),
        scratch_shapes=[
            pltpu.VMEM((WIDTH, PACKED), BF),
            pltpu.VMEM(back.shape, BF),
            pltpu.VMEM((16, HEAD) if last else (SLOTS, WIDTH), BF),
            pltpu.VMEM((QUERY_HEADS, ROWS, HEAD), BF),
            pltpu.SemaphoreType.DMA((3 + 2 * WIDTH // TILE,)),
        ],
        compiler_params=pltpu.CompilerParams(vmem_limit_bytes=VMEM_BYTES),
        cost_estimate=pl.CostEstimate(
            flops=2 * ROWS * WIDTH * PACKED, bytes_accessed=20 << 20, transcendentals=0
        ),
        name="attn_backward",
    )(*ins, *order)


def gelu_parts(gate):
    square = gate * gate
    bend = jnp.tanh(GELU_A * gate * (1.0 + GELU_B * square))
    return bend, square


def gelu(gate):
    bend, _ = gelu_parts(gate)
    return 0.5 * gate * (1.0 + bend)


def gelu_both(gate):
    bend, square = gelu_parts(gate)
    slope = 0.5 * (1.0 + bend) + 0.5 * gate * (1.0 - bend * bend) * GELU_A * (
        1.0 + 3.0 * GELU_B * square
    )
    return 0.5 * gate * (1.0 + bend), slope


def weight_pairs(l, gate_hbm, up_hbm, down_hbm, gate_w, up_w, down_w):
    gate_up = []
    for at in range(0, FF, TILE):
        block = (slice(None), pl.ds(at, TILE))
        gate_up += [(gate_hbm.at[l, 0].at[block], gate_w.at[block])]
        gate_up += [(up_hbm.at[l, 0].at[block], up_w.at[block])]
    down = [(down_hbm.at[l, 0], down_w)]
    return gate_up, down


def tiles(width):
    return [slice(at, at + TILE) for at in range(0, width, TILE)]


def run_experts(kernel, name, ins, order, outs, scratch, in_copies, flops):
    sd = jax.ShapeDtypeStruct
    count = len(ins) + len(order)
    specs = [
        pl.BlockSpec(memory_space=pltpu.SMEM if a.dtype == jnp.int32 else pl.ANY) for a in ins
    ]

    def body(*refs):
        kernel(*refs[: len(ins)], *refs[count:])

    return pl.pallas_call(
        body,
        out_shape=[sd(shape, BF) for shape in outs],
        in_specs=specs + [ANY] * len(order),
        out_specs=[ANY] * len(outs),
        scratch_shapes=[pltpu.VMEM(shape, kind) for shape, kind in scratch]
        + [pltpu.SemaphoreType.DMA((in_copies,)), pltpu.SemaphoreType.DMA((40,))],
        compiler_params=pltpu.CompilerParams(vmem_limit_bytes=VMEM_BYTES),
        cost_estimate=pl.CostEstimate(
            flops=flops, bytes_accessed=20 << 20, transcendentals=SLOTS * FF
        ),
        name=name,
    )(*ins, *order)


class Writer:
    def __init__(self, sems):
        self.sems, self.copies = sems, []

    def send(self, source, target):
        copy = pltpu.make_async_copy(source, target, self.sems.at[len(self.copies)])
        copy.start()
        self.copies.append(copy)

    def finish(self):
        for copy in self.copies:
            copy.wait()


def experts_forward_kernel(
    received_hbm, gate_hbm, up_hbm, down_hbm, act_hbm, slope_hbm, hidden_hbm, out_hbm,
    received, gate_w, up_w, down_w, act_s, slope_s, hidden, out, in_sems, out_sems,
):
    gate_up, down = weight_pairs(0, gate_hbm, up_hbm, down_hbm, gate_w, up_w, down_w)
    copies = start_all([(received_hbm, received)] + gate_up + down, in_sems)
    writer = Writer(out_sems)
    copies.pop(0).wait()
    for tile in tiles(FF):
        copies.pop(0).wait()
        copies.pop(0).wait()
        gate = dot(received[...], gate_w[:, tile])
        up = dot(received[...], up_w[:, tile])
        act, slope = gelu_both(gate)
        act_s[:, tile] = act.astype(BF)
        slope_s[:, tile] = (slope * up).astype(BF)
        hidden[:, tile] = (act * up).astype(BF)
    copies.pop(0).wait()
    writer.send(act_s, act_hbm)
    writer.send(slope_s, slope_hbm)
    writer.send(hidden, hidden_hbm)
    for tile in tiles(WIDTH):
        out[:, tile] = dot(hidden[...], down_w[:, tile]).astype(BF)
        writer.send(out.at[:, tile], out_hbm.at[:, tile])
    writer.finish()


EXPERT_SCRATCH = [((WIDTH, FF), BF), ((WIDTH, FF), BF), ((FF, WIDTH), BF)]


def experts_forward(received, weights, order):
    small = (SLOTS, FF)
    wide = (SLOTS, WIDTH)
    return run_experts(
        experts_forward_kernel, "experts_forward", [received, *weights], order,
        [small, small, small, wide],
        [(wide, BF)] + EXPERT_SCRATCH + [(small, BF)] * 3 + [(wide, BF)],
        8, 6 * SLOTS * WIDTH * FF,
    )


def back_tiles(dgate, dup, gate_w, up_w, back, back_hbm, writer):
    for tile in tiles(WIDTH):
        back[:, tile] = (
            dot(dgate[...], gate_w[tile], 1, 1) + dot(dup[...], up_w[tile], 1, 1)
        ).astype(BF)
        writer.send(back.at[:, tile], back_hbm.at[:, tile])


def experts_both_kernel(
    me, received_hbm, dx_hbm, w_hbm, gate_hbm, up_hbm, down_hbm,
    hidden_hbm, out_hbm, dslot_hbm, dgate_hbm, dup_hbm, back_hbm,
    received, dx, small, gate_w, up_w, down_w, act_s, slope_s, hidden, out, dslot, dgate, dup,
    back, in_sems, out_sems,
):
    gate_up, down = weight_pairs(1, gate_hbm, up_hbm, down_hbm, gate_w, up_w, down_w)
    pairs = [(received_hbm, received)] + gate_up
    pairs += [(w_hbm.at[:, pl.ds(SMALL, HEAD)], small), (dx_hbm, dx)] + down
    copies = start_all(pairs, in_sems)
    writer = Writer(out_sems)
    copies.pop(0).wait()
    for tile in tiles(FF):
        copies.pop(0).wait()
        copies.pop(0).wait()
        gate = dot(received[...], gate_w[:, tile])
        up = dot(received[...], up_w[:, tile])
        act, slope = gelu_both(gate)
        act_s[:, tile] = act
        slope_s[:, tile] = slope * up
        hidden[:, tile] = (act * up).astype(BF)
    for copy in copies:
        copy.wait()
    writer.send(hidden, hidden_hbm)
    shares = router_probs(received[...], small[...])
    lane = lax.broadcasted_iota(jnp.int32, shares.shape, 1)
    weight = jnp.sum(jnp.where(lane == me[0], shares, 0.0), axis=-1, keepdims=True)
    total = jnp.zeros((SLOTS, 1), F32)
    for tile in tiles(WIDTH):
        part = dot(hidden[...], down_w[:, tile]).astype(BF)
        for expert in range(EXPERTS):
            for p in range(PARTS):
                at = expert * CAP + p * PART_ROWS
                out[p, expert, :, tile] = part[at : at + PART_ROWS]
        wide = dx[:, tile].astype(F32)
        total += jnp.sum(wide * part.astype(F32), axis=-1, keepdims=True)
        dslot[:, tile] = (weight * wide).astype(BF)
    writer.send(out, out_hbm)
    writer.send(dslot, dslot_hbm)
    high, low = split(total)
    back[:, WIDTH:] = jnp.where(
        lane == 0, high.astype(F32), jnp.where(lane == 1, low.astype(F32), 0.0)
    ).astype(BF)
    writer.send(back.at[:, WIDTH:], back_hbm.at[:, WIDTH:])
    for tile in tiles(FF):
        dhidden = dot(dslot[...], down_w[tile], 1, 1)
        dgate[:, tile] = (dhidden * slope_s[:, tile]).astype(BF)
        dup[:, tile] = (dhidden * act_s[:, tile]).astype(BF)
    writer.send(dgate, dgate_hbm)
    writer.send(dup, dup_hbm)
    back_tiles(dgate, dup, gate_w, up_w, back, back_hbm, writer)
    writer.finish()


def experts_both(me, received, dx, w, weights, order):
    small = (SLOTS, FF)
    wide = (SLOTS, WIDTH)
    parts = (PARTS, EXPERTS, PART_ROWS, WIDTH)
    back = (SLOTS, WIDTH + HEAD)
    return run_experts(
        experts_both_kernel, "experts_both", [me, received, dx, w, *weights], order,
        [small, parts, wide, small, small, back],
        [(wide, BF), (wide, BF), ((WIDTH, HEAD), BF)] + EXPERT_SCRATCH
        + [(small, F32), (small, F32), (small, BF), (parts, BF), (wide, BF), (small, BF),
           (small, BF), (back, BF)],
        10, 12 * SLOTS * WIDTH * FF,
    )


def experts_backward_kernel(
    dslot_hbm, act_hbm, slope_hbm, gate_hbm, up_hbm, down_hbm, dgate_hbm, dup_hbm, back_hbm,
    dslot, act_s, slope_s, gate_w, up_w, down_w, dgate, dup, back, in_sems, out_sems,
):
    pairs = [(dslot_hbm, dslot)]
    for tile in tiles(FF):
        block = pl.ds(tile.start, TILE)
        pairs += [(down_hbm.at[0, 0].at[block], down_w.at[block])]
    pairs += [(slope_hbm, slope_s), (act_hbm, act_s)]
    for tile in tiles(WIDTH):
        block = pl.ds(tile.start, TILE)
        pairs += [(gate_hbm.at[0, 0].at[block], gate_w.at[block])]
        pairs += [(up_hbm.at[0, 0].at[block], up_w.at[block])]
    copies = start_all(pairs, in_sems)
    writer = Writer(out_sems)
    copies.pop(0).wait()
    dhidden = []
    for tile in tiles(FF):
        copies.pop(0).wait()
        dhidden += [dot(dslot[...], down_w[tile], 1, 1)]
    copies.pop(0).wait()
    copies.pop(0).wait()
    for tile, part in zip(tiles(FF), dhidden):
        dgate[:, tile] = (part * slope_s[:, tile].astype(F32)).astype(BF)
        dup[:, tile] = (part * act_s[:, tile].astype(F32)).astype(BF)
    writer.send(dgate, dgate_hbm)
    writer.send(dup, dup_hbm)
    for copy in copies:
        copy.wait()
    back_tiles(dgate, dup, gate_w, up_w, back, back_hbm, writer)
    writer.finish()


def experts_backward(dslot, act, slope, weights, order):
    small = (SLOTS, FF)
    wide = (SLOTS, WIDTH)
    return run_experts(
        experts_backward_kernel, "experts_backward", [dslot, act, slope, *weights], order,
        [small, small, wide],
        [(wide, BF), (small, BF), (small, BF)] + EXPERT_SCRATCH
        + [(small, BF), (small, BF), (wide, BF)],
        6 + 2 * WIDTH // TILE, 6 * SLOTS * WIDTH * FF,
    )


def expert_grads_kernel(received, dgate_pre, dup_pre, hidden, dslot, packed):
    gate = dot(received[...], dgate_pre[...], 0, 0).astype(BF)
    up = dot(received[...], dup_pre[...], 0, 0).astype(BF)
    down = dot(hidden[...], dslot[...], 0, 0).astype(BF)
    for part in range(DP // 2):
        packed[part, :SHARD, :FF] = gate[part * SHARD : (part + 1) * SHARD]
        packed[part, :SHARD, FF:] = up[part * SHARD : (part + 1) * SHARD]
        packed[part, SHARD:] = down[part * FF // DP : (part + 1) * FF // DP]


def expert_grads(received, dgate_pre, dup_pre, hidden, dslot):
    rows = SHARD + FF // DP
    whole = lambda width: pl.BlockSpec((SLOTS, width), lambda i: (0, 0))
    part = lambda width: pl.BlockSpec((SLOTS, width), lambda i: (0, i))
    return pl.pallas_call(
        expert_grads_kernel,
        grid=(2,),
        out_shape=jax.ShapeDtypeStruct((DP, rows, WIDTH), BF),
        in_specs=[part(WIDTH // 2), whole(FF), whole(FF), part(FF // 2), whole(WIDTH)],
        out_specs=pl.BlockSpec((DP // 2, rows, WIDTH), lambda i: (i, 0, 0)),
        compiler_params=pltpu.CompilerParams(vmem_limit_bytes=VMEM_BYTES),
        cost_estimate=pl.CostEstimate(
            flops=6 * SLOTS * WIDTH * FF, bytes_accessed=14 << 20, transcendentals=0
        ),
        name="expert_grads",
    )(received, dgate_pre, dup_pre, hidden, dslot).reshape(DP * rows, WIDTH)


def seq_tables(counts):
    ends = jnp.cumsum(counts)
    starts = ends - counts
    place = jnp.arange(ROWS, dtype=jnp.int32)
    member = (place[:, None] >= starts[None, :]) & (place[:, None] < ends[None, :])
    index = jnp.arange(counts.shape[0], dtype=jnp.int32)
    segment = jnp.sum(jnp.where(member, index[None, :], 0), axis=1)
    position = place - jnp.sum(jnp.where(member, starts[None, :], 0), axis=1)
    allowed = (segment[:, None] == segment[None, :]) & (place[:, None] >= place[None, :])
    freqs = ROPE_BASE ** (-2.0 * jnp.arange(HEAD // 2, dtype=F32) / HEAD)
    angle = position.astype(F32)[:, None] * freqs[None, :]
    cosine, sine = jnp.cos(angle), jnp.sin(angle)
    return (
        jnp.concatenate([cosine, cosine], axis=1),
        jnp.concatenate([-sine, sine], axis=1),
        allowed.astype(F32),
    )


def slot_matrix(choices, in_parts=False):
    experts = jnp.arange(EXPERTS, dtype=jnp.int32)
    member = jnp.any(choices[:, :, None] == experts[None, None, :], axis=1).astype(BF)
    row = lax.broadcasted_iota(jnp.int32, (ROWS, ROWS), 0)
    column = lax.broadcasted_iota(jnp.int32, (ROWS, ROWS), 1)
    rank = dot((column < row).astype(BF), member).astype(BF)
    slot = jnp.arange(SLOTS, dtype=jnp.int32)[None, :]
    if in_parts:
        owner, place = slot % PART // PART_ROWS, slot // PART * PART_ROWS + slot % PART_ROWS
    else:
        owner, place = slot // CAP, slot % CAP
    expand = (owner == experts[:, None]).astype(BF)
    return ((dot(member, expand) > 0.5) & (dot(rank, expand) == place.astype(F32))).astype(BF)


def exchange(rows):
    width = rows.shape[-1]
    moved = lax.all_to_all(
        rows.reshape(EXPERTS, -1, width), "expert", split_axis=0, concat_axis=0, tiled=True
    )
    return moved.reshape(-1, width)


def after(values, order):
    return pl.pallas_call(
        lambda *refs: None,
        out_shape=jax.ShapeDtypeStruct(values.shape, values.dtype),
        in_specs=[ANY, ANY],
        out_specs=ANY,
        input_output_aliases={0: 0},
        name="after",
    )(values, order)


def dense_grads_kernel(me, columns_hbm, factors_hbm, pieces_hbm, columns, turned, factors, total,
                       pieces, in_sems, out_sems):
    start = me[0] * SHARD
    shift = start % HEAD
    base = start - shift
    pairs = []
    for i in range(3):
        at = pl.multiple_of(base + i * WIDTH, HEAD)
        pairs += [(columns_hbm.at[:, pl.ds(at, TILE)], columns.at[:, pl.ds(i * TILE, TILE)])]
    for at in range(0, PACKED, CHUNK):
        block = (slice(None), pl.ds(at, min(CHUNK, PACKED - at)))
        pairs += [(factors_hbm.at[block], factors.at[block])]
    copies = start_all(pairs, in_sems)
    writer = Writer(out_sems)
    for i in range(3):
        copies.pop(0).wait()
        turned[i] = columns[:, i * TILE : (i + 1) * TILE].T
    for chunk in range(SMALL // CHUNK):
        copies.pop(0).wait()
        total[...] = dot(
            turned[0 if chunk < QKV // CHUNK else 1],
            factors[:, chunk * CHUNK : (chunk + 1) * CHUNK],
        )
        pieces[chunk] = total[pl.ds(pl.multiple_of(shift, 64), SHARD), :].astype(BF)
        writer.send(pieces.at[chunk], pieces_hbm.at[chunk])
    copies.pop(0).wait()
    ends = jnp.zeros((ROWS, HEAD), F32)
    for source in range(DP):
        ends += factors[source * ROWS : (source + 1) * ROWS, SMALL:].astype(F32)
    lane = lax.broadcasted_iota(jnp.int32, (ROWS, HEAD), 1)

    def gain_piece(piece):
        held = (lane == piece + GAIN_HIGH) | (lane == piece + GAIN_LOW)
        return jnp.sum(jnp.where(held, ends, 0.0), axis=1, keepdims=True)

    first, second = gain_piece(base // HEAD), gain_piece(base // HEAD + 1)
    gain = jnp.where(
        shift == 0,
        jnp.concatenate([first, second[: SHARD - ROWS]], axis=0),
        jnp.concatenate([first[ROWS // 2 :], second], axis=0),
    )
    gain_high, gain_low = split(gain)
    total[:, :HEAD] = dot(turned[2], factors[:, SMALL:])
    router = total[pl.ds(pl.multiple_of(shift, 64), SHARD), :HEAD]
    lane = lax.broadcasted_iota(jnp.int32, (SHARD, HEAD), 1)
    router = jnp.where(lane < EXPERTS, router, 0.0)
    router = jnp.where(lane == EXPERTS, gain_high.astype(F32), router)
    router = jnp.where(lane == EXPERTS + 1, gain_low.astype(F32), router)
    pieces[CHUNKS - 2] = jnp.concatenate([router, jnp.zeros_like(router)], axis=1).astype(BF)
    pieces[CHUNKS - 1] = jnp.zeros((SHARD, CHUNK), BF)
    writer.send(pieces.at[CHUNKS - 2], pieces_hbm.at[CHUNKS - 2])
    writer.send(pieces.at[CHUNKS - 1], pieces_hbm.at[CHUNKS - 1])
    writer.finish()


def dense_grads(me, columns, factors, order):
    tokens = DP * ROWS

    def body(*refs):
        dense_grads_kernel(*refs[:3], *refs[3 + len(order) :])

    return pl.pallas_call(
        body,
        out_shape=jax.ShapeDtypeStruct((CHUNKS, SHARD, CHUNK), BF),
        in_specs=[pl.BlockSpec(memory_space=pltpu.SMEM), ANY, ANY] + [ANY] * len(order),
        out_specs=ANY,
        scratch_shapes=[
            pltpu.VMEM((tokens, 3 * TILE), BF),
            pltpu.VMEM((3, TILE, tokens), BF),
            pltpu.VMEM((tokens, PACKED), BF),
            pltpu.VMEM((TILE, CHUNK), F32),
            pltpu.VMEM((CHUNKS, SHARD, CHUNK), BF),
            pltpu.SemaphoreType.DMA((3 + CHUNKS,)),
            pltpu.SemaphoreType.DMA((CHUNKS,)),
        ],
        compiler_params=pltpu.CompilerParams(vmem_limit_bytes=VMEM_BYTES),
        cost_estimate=pl.CostEstimate(
            flops=2 * tokens * TILE * PACKED, bytes_accessed=10 << 20, transcendentals=0
        ),
        name="dense_grads",
    )(me, columns, factors, *order)


def sum_pieces_kernel(pieces, out):
    total = pieces[0].astype(F32)
    for i in range(1, CHUNKS):
        total += pieces[i].astype(F32)
    out[...] = jnp.broadcast_to(total.astype(BF)[None], out.shape)


def sum_experts(pieces):
    pieces = lax.all_to_all(pieces, "expert", split_axis=0, concat_axis=0, tiled=True)
    vmem = pl.BlockSpec(memory_space=pltpu.VMEM)
    whole = pl.pallas_call(
        sum_pieces_kernel,
        out_shape=jax.ShapeDtypeStruct(pieces.shape, BF),
        in_specs=[vmem],
        out_specs=vmem,
        compiler_params=pltpu.CompilerParams(vmem_limit_bytes=VMEM_BYTES),
        name="sum_pieces",
    )(pieces)
    return lax.all_to_all(whole, "expert", split_axis=0, concat_axis=0, tiled=True)


def finish_kernel(
    pieces0, pieces1, w_query, key_projection, value_projection, norm_attn, norm_ffn,
    gain_attn, query, key, value, out, gain_ffn, router,
):
    for l, pieces in enumerate((pieces0, pieces1)):
        rows = jnp.zeros((SHARD, 1), F32)
        for chunk in range(SMALL // CHUNK):
            part = pieces[chunk].astype(F32)
            at = slice(chunk * CHUNK, (chunk + 1) * CHUNK)
            if chunk < Q_END // CHUNK:
                weight = w_query[l, :, at]
                query[l, :, at] = part
            elif chunk < QKV // CHUNK:
                weight, target = ((key_projection, key), (value_projection, value))[
                    chunk - Q_END // CHUNK
                ]
                weight = weight[l]
                target[l] = part
            else:
                at = slice(chunk * CHUNK - QKV, (chunk + 1) * CHUNK - QKV)
                out[l, :, at] = part
                continue
            rows += jnp.sum(part * weight.astype(F32), axis=1, keepdims=True)
        ends = pieces[CHUNKS - 2, :, :HEAD].astype(F32)
        router[l] = ends[:, :EXPERTS]
        ffn = ends[:, EXPERTS : EXPERTS + 1] + ends[:, EXPERTS + 1 : EXPERTS + 2]
        lane = lax.broadcasted_iota(jnp.int32, (SHARD, HEAD), 1)
        both = jnp.where(lane == 0, rows, jnp.where(lane == 1, ffn, 0.0))
        both = jnp.concatenate([both, jnp.zeros((TILE - SHARD, HEAD), F32)], axis=0).T
        gain_attn[l : l + 1] = both[0:1, :SHARD] / norm_attn[l : l + 1].astype(F32)
        gain_ffn[l : l + 1] = both[1:2, :SHARD]


def finish(pieces0, pieces1, w_query, key_projection, value_projection, norm_attn, norm_ffn):
    sd = jax.ShapeDtypeStruct
    vmem = pl.BlockSpec(memory_space=pltpu.VMEM)
    keys = (LAYERS, SHARD, KEY_VALUE_HEADS * HEAD)
    return pl.pallas_call(
        finish_kernel,
        out_shape=[
            sd((LAYERS, SHARD), F32), sd((LAYERS, SHARD, Q_END), F32), sd(keys, F32), sd(keys, F32),
            sd((LAYERS, SHARD, WIDTH), F32), sd((LAYERS, SHARD), F32),
            sd((LAYERS, SHARD, EXPERTS), F32),
        ],
        in_specs=[vmem] * 7,
        out_specs=[vmem] * 7,
        compiler_params=pltpu.CompilerParams(vmem_limit_bytes=VMEM_BYTES),
        name="finish",
    )(pieces0, pieces1, w_query, key_projection, value_projection, norm_attn, norm_ffn)


def finish_experts_kernel(shares0, shares1, gate, up, down):
    for l, shares in enumerate((shares0, shares1)):
        gate[l, 0] = shares[:SHARD, :FF].astype(F32)
        up[l, 0] = shares[:SHARD, FF:].astype(F32)
        down[l, 0] = shares[SHARD:].astype(F32)


def finish_experts(shares0, shares1):
    sd = jax.ShapeDtypeStruct
    vmem = pl.BlockSpec(memory_space=pltpu.VMEM)
    return pl.pallas_call(
        finish_experts_kernel,
        out_shape=[
            sd((LAYERS, 1, SHARD, FF), F32), sd((LAYERS, 1, SHARD, FF), F32),
            sd((LAYERS, 1, FF // DP, WIDTH), F32),
        ],
        in_specs=[vmem] * 2,
        out_specs=[vmem] * 3,
        compiler_params=pltpu.CompilerParams(vmem_limit_bytes=VMEM_BYTES),
        name="finish_experts",
    )(shares0, shares1)


def mixed_kernel(x, high, low, part0, part1, part2, out):
    total = x[...]
    for p, part in enumerate((part0, part1, part2)):
        at = slice(p * PART, (p + 1) * PART)
        total += dot(high[:, at], part[...]) + dot(low[:, at], part[...])
    out[...] = total.astype(BF)


def mixed_rows(x, high, low, parts):
    vmem = pl.BlockSpec(memory_space=pltpu.VMEM)
    return pl.pallas_call(
        mixed_kernel,
        out_shape=jax.ShapeDtypeStruct((ROWS, WIDTH), BF),
        in_specs=[vmem] * 6,
        out_specs=vmem,
        compiler_params=pltpu.CompilerParams(vmem_limit_bytes=VMEM_BYTES),
        name="mixed",
    )(x, high, low, *parts)


def local(
    tokens, cotangent, lengths, routes, norm_attn, w_query, key_projection, value_projection,
    w_out, norm_ffn, w_router, w_gate, w_up, w_down,
):
    me_dp = lax.axis_index("dp").astype(jnp.int32).reshape(1)
    me_expert = lax.axis_index("expert").astype(jnp.int32).reshape(1)
    tables = seq_tables(lengths[0])
    give = [slot_matrix(routes[l]) for l in range(LAYERS)]
    take = [g.T for g in give]
    give_parts = slot_matrix(routes[1], True)
    experts = (w_gate, w_up, w_down)

    def gather(values):
        return lax.all_gather(values, "dp", axis=0, tiled=True)

    w = [
        gather(
            jnp.concatenate(
                [w_query[l], key_projection[l], value_projection[l], w_out[l], w_router[l],
                 norm_attn[l][:, None], norm_ffn[l][:, None],
                 jnp.zeros((SHARD, HEAD - EXPERTS - 2), BF)],
                axis=1,
            )
        )
        for l in range(LAYERS)
    ]

    dx_rows = exchange(dot(take[1], cotangent).astype(BF))

    kept0 = attn_forward(tokens, None, w[0], tables, take[0], give[0], (dx_rows,))
    received0 = exchange(kept0["rows"])
    act0, slope0, hidden0, out0 = experts_forward(received0, experts, ())
    returned0 = exchange(out0)
    columns0 = gather(kept0["columns"])

    kept1 = attn_forward(
        kept0["after"], (returned0, kept0["high"], kept0["low"]), w[1], tables, take[1],
        give_parts, (),
    )
    received1 = exchange(kept1["rows"])
    columns1 = gather(kept1["columns"])
    hidden1, out1, dslot1, dgate1, dup1, back1 = experts_both(
        me_expert, received1, dx_rows, w[1], experts, ()
    )
    back1 = exchange(back1)
    grads1 = expert_grads(received1, dgate1, dup1, hidden1, dslot1)
    shares1 = lax.psum_scatter(grads1, "dp", scatter_dimension=0, tiled=True)
    parts = [exchange(out1[p]) for p in range(PARTS)]

    dx0, packed1, rows0 = attn_backward(
        cotangent, back1, kept1, w[1], tables, give[1], (take[0], kept0["router"]), None,
        (grads1, columns0, columns1),
    )
    dslot0 = exchange(rows0)
    factors1 = gather(packed1)
    dgate0, dup0, back0 = experts_backward(dslot0, act0, slope0, experts, (parts[0],))
    back0 = exchange(back0)
    grads0 = expert_grads(received0, dgate0, dup0, hidden0, dslot0)
    grad_tokens, packed0 = attn_backward(
        dx0, back0, kept0, w[0], tables, give[0], None, returned0,
        (factors1, shares1, grads0, parts[1]),
    )
    factors0 = gather(packed0)
    pieces1 = sum_experts(dense_grads(me_dp, columns1, factors1, ()))
    mixed = mixed_rows(kept1["after"], kept1["high"], kept1["low"], parts)
    pieces0 = sum_experts(dense_grads(me_dp, columns0, factors0, (pieces1, parts[2])))
    shares0 = lax.psum_scatter(after(grads0, factors0), "dp", scatter_dimension=0, tiled=True)

    gain_attn, query, key, value, out, gain_ffn, router = finish(
        pieces0, pieces1, w_query, key_projection, value_projection, norm_attn, norm_ffn
    )
    gate, up, down = finish_experts(shares0, shares1)
    return (
        mixed, grad_tokens, gain_attn, query, key, value, out, gain_ffn, router, gate, up, down
    )


def solution(mesh):
    placed = (
        P(("dp", "expert"), None),
        P(("dp", "expert"), None),
        P(("dp", "expert"), None),
        P(None, ("dp", "expert"), None),
        P(None, "dp"),
        P(None, "dp", None),
        P(None, "dp", None),
        P(None, "dp", None),
        P(None, "dp", None),
        P(None, "dp"),
        P(None, "dp", None),
        P(None, "expert", None, None),
        P(None, "expert", None, None),
        P(None, "expert", None, None),
    )
    return jax.shard_map(
        local,
        mesh=mesh,
        in_specs=placed,
        out_specs=(
            P(("dp", "expert"), None),
            P(("dp", "expert"), None),
            P(None, "dp"),
            P(None, "dp", None),
            P(None, "dp", None),
            P(None, "dp", None),
            P(None, "dp", None),
            P(None, "dp"),
            P(None, "dp", None),
            P(None, "expert", "dp", None),
            P(None, "expert", "dp", None),
            P(None, "expert", "dp", None),
        ),
        check_vma=False,
    )
```

```python
import jax
import jax.numpy as jnp
from jax import lax
from jax.experimental import pallas as pl
from jax.experimental.pallas import tpu as pltpu
from jax.sharding import PartitionSpec as P

QUERY_HEADS = 12
KEY_VALUE_HEADS = 2
GROUPS = QUERY_HEADS // KEY_VALUE_HEADS
HEAD = 128
LAYERS = 2
WIDTH = 1536
FF = 768
ROWS = 128
EXPERTS = 16
CAP = 48
SLOTS = EXPERTS * CAP
DP = 8
SHARD = WIDTH // DP
Q_END = QUERY_HEADS * HEAD
K_END = Q_END + KEY_VALUE_HEADS * HEAD
QKV = K_END + KEY_VALUE_HEADS * HEAD
SMALL = QKV + WIDTH
PACKED = SMALL + HEAD
GAIN_ATTN, GAIN_FFN = 16, 17
GAIN_HIGH, GAIN_LOW = 16, 32
PIECES = WIDTH // HEAD
TILE = 256
PART_ROWS = (16, 32)
PART_ENDS = (EXPERTS * 16, SLOTS)
CHUNKS, CHUNK = 16, 256
COLUMNS = 3 * WIDTH
EPSILON = 1e-06
ROPE_BASE = 1000000.0
SCALE = HEAD ** (-0.5)
GELU_A = 0.7978845608028654
GELU_B = 0.044715
VMEM_BYTES = 56 << 20
BF = jnp.bfloat16
F32 = jnp.float32
ANY = pl.BlockSpec(memory_space=pl.ANY)


def dot(left, right, left_dim=1, right_dim=0):
    return lax.dot_general(
        left, right, (((left_dim,), (right_dim,)), ((), ())), preferred_element_type=F32
    )


def split(values):
    high = values.astype(BF)
    return high, (values - high.astype(F32)).astype(BF)


def unit(values):
    return lax.rsqrt(jnp.mean(values * values, axis=-1, keepdims=True) + EPSILON)


def turn(values, cosine, sine):
    return values * cosine + pltpu.roll(values, HEAD // 2, 1) * sine


def expert_lanes(transposed=False, in_parts=False):
    shape = (SLOTS, HEAD) if transposed else (HEAD, SLOTS)
    slot = lax.broadcasted_iota(jnp.int32, shape, 0 if transposed else 1)
    expert = lax.broadcasted_iota(jnp.int32, shape, 1 if transposed else 0)
    if in_parts:
        first = (slot >> 4) == expert
        held = first | ((slot >= PART_ENDS[0]) & (((slot - PART_ENDS[0]) >> 5) == expert))
    else:
        held = (slot >= expert * CAP) & (slot < expert * CAP + CAP)
    return held.astype(F32).astype(BF)


def gain_rows(small):
    row = lax.broadcasted_iota(jnp.int32, (8, HEAD), 0)
    lane = lax.broadcasted_iota(jnp.int32, (8, HEAD), 1)
    pick = ((lane == row + GAIN_ATTN) & (row < 2)).astype(F32).astype(BF)
    rows = dot(pick, small, 1, 1)
    return rows[0:1], rows[1:2]


def router_probs(rows, small):
    logits = dot(rows, small)
    lane = lax.broadcasted_iota(jnp.int32, logits.shape, 1)
    logits = jnp.where(lane < EXPERTS, logits, -1e30)
    powers = jnp.exp(logits - jnp.max(logits, axis=-1, keepdims=True))
    return powers / jnp.sum(powers, axis=-1, keepdims=True)


def start_all(pairs, sems):
    copies = [
        pltpu.make_async_copy(source, target, sems.at[i]) for i, (source, target) in enumerate(pairs)
    ]
    for copy in copies:
        copy.start()
    return copies


def attn_forward_kernel(first, order_count, refs):
    refs = iter(refs)
    x_in = next(refs)
    if not first:
        returned_hbm, high_in, low_in = next(refs), next(refs), next(refs)
    w_hbm, cosine, sine, allowed, take, give = (next(refs) for _ in range(6))
    for _ in range(order_count):
        next(refs)
    (x_out, columns, qrot, krot, value, probs, after, router, high, low, rows,
     w, returned, sems) = refs
    acts = columns.at[:, :WIDTH]
    attended = columns.at[:, WIDTH : 2 * WIDTH]
    acts_two = columns.at[:, 2 * WIDTH :]
    pairs = []
    if not first:
        pairs += [(returned_hbm, returned)]
    pairs += [(w_hbm.at[:, pl.ds(SMALL, HEAD)], w.at[:, pl.ds(SMALL, HEAD)])]
    pairs += [
        (w_hbm.at[:, pl.ds(at, TILE)], w.at[:, pl.ds(at, TILE)]) for at in range(0, SMALL, TILE)
    ]
    copies = start_all(pairs, sems)
    if first:
        x = x_in[...].astype(F32)
    else:
        copies.pop(0).wait()
        x = x_in[...] + dot(high_in[...], returned[...]) + dot(low_in[...], returned[...])
    x_out[...] = x
    copies.pop(0).wait()
    small = w[:, SMALL:]
    gain_attn, gain_ffn = gain_rows(small)
    acts[...] = (x * unit(x) * gain_attn).astype(BF)
    for tile in range(QKV // TILE):
        copies[tile].wait()
        wide = dot(acts[...], w[:, tile * TILE : (tile + 1) * TILE])
        for half in range(TILE // HEAD):
            head = tile * (TILE // HEAD) + half
            part = wide[:, half * HEAD : (half + 1) * HEAD]
            if head < QUERY_HEADS:
                qrot[head] = turn(part, cosine[...], sine[...]).astype(BF)
            elif head < QUERY_HEADS + KEY_VALUE_HEADS:
                krot[head - QUERY_HEADS] = turn(part, cosine[...], sine[...]).astype(BF)
            else:
                value[head - QUERY_HEADS - KEY_VALUE_HEADS] = part.astype(BF)
    open_scores = (allowed[...] > 0.5)[None]
    for k in range(KEY_VALUE_HEADS):
        heads = slice(k * GROUPS, (k + 1) * GROUPS)
        scores = dot(qrot[heads].reshape(GROUPS * ROWS, HEAD), krot[k], 1, 1) * SCALE
        scores = jnp.where(open_scores, scores.reshape(GROUPS, ROWS, ROWS), -1000000000.0)
        powers = jnp.exp(scores - jnp.max(scores, axis=-1, keepdims=True))
        shares = powers / jnp.sum(powers, axis=-1, keepdims=True)
        probs[heads] = shares
        mixed = dot(shares.astype(BF).reshape(GROUPS * ROWS, ROWS), value[k]).astype(BF)
        for group in range(GROUPS):
            at = (k * GROUPS + group) * HEAD
            attended[:, at : at + HEAD] = mixed[group * ROWS : (group + 1) * ROWS]
    for tile in range(WIDTH // TILE):
        copies[QKV // TILE + tile].wait()
        at = tile * TILE
        after[:, at : at + TILE] = x_out[:, at : at + TILE] + dot(
            attended[...], w[:, QKV + at : QKV + at + TILE]
        )
    total = after[...]
    acts_two[...] = (total * unit(total) * gain_ffn).astype(BF)
    rows[...] = dot(take[...], acts_two[...]).astype(BF)
    shares = router_probs(acts_two[...], small)
    router[...] = shares
    share_high, share_low = split(shares)
    spread = expert_lanes(in_parts=not first)
    high[...] = dot(share_high, spread).astype(BF) * give[...]
    low[...] = dot(share_low, spread).astype(BF) * give[...]


def attn_forward(x, combine, w, tables, take, give, order):
    first = combine is None
    sd = jax.ShapeDtypeStruct
    outs = [
        sd((ROWS, WIDTH), F32), sd((ROWS, COLUMNS), BF), sd((QUERY_HEADS, ROWS, HEAD), BF),
        sd((KEY_VALUE_HEADS, ROWS, HEAD), BF), sd((KEY_VALUE_HEADS, ROWS, HEAD), BF),
        sd((QUERY_HEADS, ROWS, ROWS), F32), sd((ROWS, WIDTH), F32), sd((ROWS, HEAD), F32),
        sd((ROWS, SLOTS), BF), sd((ROWS, SLOTS), BF), sd((SLOTS, WIDTH), BF),
    ]
    ins = [x] + ([] if first else list(combine)) + [w, *tables, take, give, *order]
    vmem = pl.BlockSpec(memory_space=pltpu.VMEM)
    specs = [vmem] + ([] if first else [ANY, vmem, vmem]) + [ANY] + [vmem] * 5
    specs += [ANY] * len(order)
    returned_shape = (16, HEAD) if first else (SLOTS, WIDTH)
    result = pl.pallas_call(
        lambda *refs: attn_forward_kernel(first, len(order), refs),
        out_shape=outs,
        in_specs=specs,
        out_specs=[vmem] * len(outs),
        scratch_shapes=[
            pltpu.VMEM((WIDTH, PACKED), BF),
            pltpu.VMEM(returned_shape, BF),
            pltpu.SemaphoreType.DMA((2 + SMALL // TILE,)),
        ],
        compiler_params=pltpu.CompilerParams(vmem_limit_bytes=VMEM_BYTES),
        cost_estimate=pl.CostEstimate(
            flops=2 * ROWS * WIDTH * PACKED, bytes_accessed=20 << 20, transcendentals=200000
        ),
        name="attn_forward",
    )(*ins)
    names = (
        "x", "columns", "qrot", "krot", "value", "probs", "after", "router", "high", "low", "rows",
    )
    return dict(zip(names, result))


def norm_back(grad, gain, values):
    scale = unit(values)
    inner = grad * gain
    return scale * inner - values * (scale * scale * scale) * jnp.mean(
        inner * values, axis=-1, keepdims=True
    )


def attn_backward_kernel(last, order_count, refs):
    refs = iter(refs)
    (dx_in, back_hbm, w_hbm, cosine, sine, give, router, after, x_in, probs, qrot, krot,
     value) = (next(refs) for _ in range(13))
    if last:
        take_below, router_below = next(refs), next(refs)
    else:
        returned_hbm = next(refs)
    for _ in range(order_count):
        next(refs)
    dx_out, packed = next(refs), next(refs)
    if last:
        rows = next(refs)
    w, back, returned, datt, sems = refs
    pairs = [(back_hbm, back)]
    if not last:
        pairs += [(returned_hbm, returned)]
    pairs += [(w_hbm.at[:, pl.ds(SMALL, HEAD)], w.at[:, pl.ds(SMALL, HEAD)])]
    for start, width in ((QKV, WIDTH), (0, QKV)):
        for at in range(0, WIDTH, TILE):
            block = (pl.ds(at, TILE), pl.ds(start, width))
            pairs += [(w_hbm.at[block], w.at[block])]
    copies = start_all(pairs, sems)
    dx = dx_in[...].astype(F32)
    copies.pop(0).wait()
    spread = expert_lanes(True)
    if last:
        dgate = back[:, WIDTH:].astype(F32)
        drouter = dot(give[...], (dgate[:, 0:1] * spread).astype(BF))
        drouter += dot(give[...], (dgate[:, 1:2] * spread).astype(BF))
    else:
        copies.pop(0).wait()
        dgate = dot(dx.astype(BF), returned[...], 1, 1) * give[...]
        dgate_high, dgate_low = split(dgate)
        drouter = dot(dgate_high, spread) + dot(dgate_low, spread)
    copies.pop(0).wait()
    small = w[:, SMALL:]
    gain_attn, gain_ffn = gain_rows(small)
    shares = router[...]
    dlogits = shares * (drouter - jnp.sum(drouter * shares, axis=-1, keepdims=True))
    dlogits = dlogits.astype(BF)
    dacts_two = dot(dlogits, small, 1, 1) + dot(give[...], back[:, :WIDTH])
    total = after[...]
    scale = unit(total)
    dgain = jnp.sum(dacts_two * total * scale, axis=0, keepdims=True)
    dgain_high, dgain_low = split(dgain)
    pieces = [jnp.zeros((GAIN_HIGH, HEAD), F32)]
    for part in (dgain_high.astype(F32), dgain_low.astype(F32)):
        pieces += [part[:, at : at + HEAD] for at in range(0, WIDTH, HEAD)]
        pieces += [jnp.zeros((GAIN_LOW - GAIN_HIGH - PIECES, HEAD), F32)]
    pieces += [jnp.zeros((HEAD - 2 * GAIN_LOW + GAIN_HIGH, HEAD), F32)]
    packed[:, SMALL:] = (dlogits.astype(F32) + jnp.concatenate(pieces, axis=0).T).astype(BF)
    dafter = dx + norm_back(dacts_two, gain_ffn, total)
    dx_out[...] = dafter
    packed[:, QKV:SMALL] = dafter.astype(BF)
    for tile in range(WIDTH // TILE):
        copies[tile].wait()
        wide = dot(
            packed[:, QKV:SMALL], w[tile * TILE : (tile + 1) * TILE, QKV:SMALL], 1, 1
        ).astype(BF)
        for half in range(TILE // HEAD):
            datt[tile * (TILE // HEAD) + half] = wide[:, half * HEAD : (half + 1) * HEAD]
    for k in range(KEY_VALUE_HEADS):
        heads = slice(k * GROUPS, (k + 1) * GROUPS)
        datt_k = datt[heads].reshape(GROUPS * ROWS, HEAD)
        p = probs[heads].reshape(GROUPS * ROWS, ROWS)
        dprobs = dot(datt_k, value[k], 1, 1)
        dvalue = dot(p.astype(BF), datt_k, 0, 0)
        dscores = (p * (dprobs - jnp.sum(dprobs * p, axis=-1, keepdims=True))).astype(BF)
        dqrot = dot(dscores, krot[k]) * SCALE
        dkrot = dot(dscores, qrot[heads].reshape(GROUPS * ROWS, HEAD), 0, 0) * SCALE
        for group in range(GROUPS):
            at = (k * GROUPS + group) * HEAD
            part = dqrot[group * ROWS : (group + 1) * ROWS]
            packed[:, at : at + HEAD] = turn(part, cosine[...], -sine[...]).astype(BF)
        at = Q_END + k * HEAD
        packed[:, at : at + HEAD] = turn(dkrot, cosine[...], -sine[...]).astype(BF)
        at = K_END + k * HEAD
        packed[:, at : at + HEAD] = dvalue.astype(BF)
    parts = []
    for tile in range(WIDTH // TILE):
        copies[WIDTH // TILE + tile].wait()
        parts += [dot(packed[:, :QKV], w[tile * TILE : (tile + 1) * TILE, :QKV], 1, 1)]
    dacts = jnp.concatenate(parts, axis=1)
    dx = dx_out[...] + norm_back(dacts, gain_attn, x_in[...].astype(F32))
    dx_out[...] = dx
    if last:
        dx_low = dx.astype(BF)
        below_high, below_low = split(router_below[...])
        gates = dot(spread, below_high, 1, 1).astype(BF) * take_below[...]
        gates_low = dot(spread, below_low, 1, 1).astype(BF) * take_below[...]
        rows[...] = (dot(gates, dx_low) + dot(gates_low, dx_low)).astype(BF)


def attn_backward(dx, back, kept, w, tables, give, below, returned, order):
    last = below is not None
    sd = jax.ShapeDtypeStruct
    outs = [sd((ROWS, WIDTH), F32), sd((ROWS, PACKED), BF)]
    if last:
        outs += [sd((SLOTS, WIDTH), BF)]
    vmem = pl.BlockSpec(memory_space=pltpu.VMEM)
    ins = [dx, back, w, tables[0], tables[1], give]
    ins += [kept[n] for n in ("router", "after", "x", "probs", "qrot", "krot", "value")]
    specs = [vmem, ANY, ANY] + [vmem] * 10
    if last:
        ins += list(below)
        specs += [vmem] * 2
    else:
        ins += [returned]
        specs += [ANY]
    return pl.pallas_call(
        lambda *refs: attn_backward_kernel(last, len(order), refs),
        out_shape=outs,
        in_specs=specs + [ANY] * len(order),
        out_specs=[vmem] * len(outs),
        scratch_shapes=[
            pltpu.VMEM((WIDTH, PACKED), BF),
            pltpu.VMEM(back.shape, BF),
            pltpu.VMEM((16, HEAD) if last else (SLOTS, WIDTH), BF),
            pltpu.VMEM((QUERY_HEADS, ROWS, HEAD), BF),
            pltpu.SemaphoreType.DMA((3 + 2 * WIDTH // TILE,)),
        ],
        compiler_params=pltpu.CompilerParams(vmem_limit_bytes=VMEM_BYTES),
        cost_estimate=pl.CostEstimate(
            flops=2 * ROWS * WIDTH * PACKED, bytes_accessed=20 << 20, transcendentals=0
        ),
        name="attn_backward",
    )(*ins, *order)


def gelu_parts(gate):
    square = gate * gate
    bend = jnp.tanh(GELU_A * gate * (1.0 + GELU_B * square))
    return bend, square


def gelu(gate):
    bend, _ = gelu_parts(gate)
    return 0.5 * gate * (1.0 + bend)


def gelu_both(gate):
    bend, square = gelu_parts(gate)
    slope = 0.5 * (1.0 + bend) + 0.5 * gate * (1.0 - bend * bend) * GELU_A * (
        1.0 + 3.0 * GELU_B * square
    )
    return 0.5 * gate * (1.0 + bend), slope


def weight_pairs(l, gate_hbm, up_hbm, down_hbm, gate_w, up_w, down_w):
    gate_up = []
    for at in range(0, FF, TILE):
        block = (slice(None), pl.ds(at, TILE))
        gate_up += [(gate_hbm.at[l, 0].at[block], gate_w.at[block])]
        gate_up += [(up_hbm.at[l, 0].at[block], up_w.at[block])]
    down = [(down_hbm.at[l, 0], down_w)]
    return gate_up, down


def tiles(width):
    return [slice(at, at + TILE) for at in range(0, width, TILE)]


def run_experts(kernel, name, ins, order, outs, scratch, in_copies, flops):
    sd = jax.ShapeDtypeStruct
    count = len(ins) + len(order)
    specs = [
        pl.BlockSpec(memory_space=pltpu.SMEM if a.dtype == jnp.int32 else pl.ANY) for a in ins
    ]

    def body(*refs):
        kernel(*refs[: len(ins)], *refs[count:])

    return pl.pallas_call(
        body,
        out_shape=[sd(shape, BF) for shape in outs],
        in_specs=specs + [ANY] * len(order),
        out_specs=[ANY] * len(outs),
        scratch_shapes=[pltpu.VMEM(shape, kind) for shape, kind in scratch]
        + [pltpu.SemaphoreType.DMA((in_copies,)), pltpu.SemaphoreType.DMA((40,))],
        compiler_params=pltpu.CompilerParams(vmem_limit_bytes=VMEM_BYTES),
        cost_estimate=pl.CostEstimate(
            flops=flops, bytes_accessed=20 << 20, transcendentals=SLOTS * FF
        ),
        name=name,
    )(*ins, *order)


class Writer:
    def __init__(self, sems):
        self.sems, self.copies = sems, []

    def send(self, source, target):
        copy = pltpu.make_async_copy(source, target, self.sems.at[len(self.copies)])
        copy.start()
        self.copies.append(copy)

    def finish(self):
        for copy in self.copies:
            copy.wait()


def experts_forward_kernel(
    received_hbm, gate_hbm, up_hbm, down_hbm, act_hbm, slope_hbm, hidden_hbm, out_hbm,
    received, gate_w, up_w, down_w, act_s, slope_s, hidden, out, in_sems, out_sems,
):
    gate_up, down = weight_pairs(0, gate_hbm, up_hbm, down_hbm, gate_w, up_w, down_w)
    copies = start_all([(received_hbm, received)] + gate_up + down, in_sems)
    writer = Writer(out_sems)
    copies.pop(0).wait()
    for tile in tiles(FF):
        copies.pop(0).wait()
        copies.pop(0).wait()
        gate = dot(received[...], gate_w[:, tile])
        up = dot(received[...], up_w[:, tile])
        act, slope = gelu_both(gate)
        act_s[:, tile] = act.astype(BF)
        slope_s[:, tile] = (slope * up).astype(BF)
        hidden[:, tile] = (act * up).astype(BF)
    copies.pop(0).wait()
    writer.send(act_s, act_hbm)
    writer.send(slope_s, slope_hbm)
    writer.send(hidden, hidden_hbm)
    for tile in tiles(WIDTH):
        out[:, tile] = dot(hidden[...], down_w[:, tile]).astype(BF)
        writer.send(out.at[:, tile], out_hbm.at[:, tile])
    writer.finish()


EXPERT_SCRATCH = [((WIDTH, FF), BF), ((WIDTH, FF), BF), ((FF, WIDTH), BF)]


def experts_forward(received, weights, order):
    small = (SLOTS, FF)
    wide = (SLOTS, WIDTH)
    return run_experts(
        experts_forward_kernel, "experts_forward", [received, *weights], order,
        [small, small, small, wide],
        [(wide, BF)] + EXPERT_SCRATCH + [(small, BF)] * 3 + [(wide, BF)],
        8, 6 * SLOTS * WIDTH * FF,
    )


def back_tiles(dgate, dup, gate_w, up_w, back, back_hbm, writer):
    for tile in tiles(WIDTH):
        back[:, tile] = (
            dot(dgate[...], gate_w[tile], 1, 1) + dot(dup[...], up_w[tile], 1, 1)
        ).astype(BF)
        writer.send(back.at[:, tile], back_hbm.at[:, tile])


def experts_both_kernel(
    me, received_hbm, dx_hbm, w_hbm, gate_hbm, up_hbm, down_hbm,
    hidden_hbm, early_hbm, late_hbm, dslot_hbm, dgate_hbm, dup_hbm, back_hbm,
    received, dx, small, gate_w, up_w, down_w, act_s, slope_s, hidden, early, late, dslot, dgate, dup,
    back, in_sems, out_sems,
):
    gate_up, down = weight_pairs(1, gate_hbm, up_hbm, down_hbm, gate_w, up_w, down_w)
    pairs = [(received_hbm, received)] + gate_up
    pairs += [(w_hbm.at[:, pl.ds(SMALL, HEAD)], small), (dx_hbm, dx)] + down
    copies = start_all(pairs, in_sems)
    writer = Writer(out_sems)
    copies.pop(0).wait()
    for tile in tiles(FF):
        copies.pop(0).wait()
        copies.pop(0).wait()
        gate = dot(received[...], gate_w[:, tile])
        up = dot(received[...], up_w[:, tile])
        act, slope = gelu_both(gate)
        act_s[:, tile] = act
        slope_s[:, tile] = slope * up
        hidden[:, tile] = (act * up).astype(BF)
    for copy in copies:
        copy.wait()
    writer.send(hidden, hidden_hbm)
    shares = router_probs(received[...], small[...])
    lane = lax.broadcasted_iota(jnp.int32, shares.shape, 1)
    weight = jnp.sum(jnp.where(lane == me[0], shares, 0.0), axis=-1, keepdims=True)
    total = jnp.zeros((SLOTS, 1), F32)
    for tile in tiles(WIDTH):
        part = dot(hidden[...], down_w[:, tile]).astype(BF)
        for expert in range(EXPERTS):
            at = expert * CAP
            early[expert, :, tile] = part[at : at + PART_ROWS[0]]
            late[expert, :, tile] = part[at + PART_ROWS[0] : at + CAP]
        wide = dx[:, tile].astype(F32)
        total += jnp.sum(wide * part.astype(F32), axis=-1, keepdims=True)
        dslot[:, tile] = (weight * wide).astype(BF)
    writer.send(early, early_hbm)
    writer.send(late, late_hbm)
    writer.send(dslot, dslot_hbm)
    high, low = split(total)
    back[:, WIDTH:] = jnp.where(
        lane == 0, high.astype(F32), jnp.where(lane == 1, low.astype(F32), 0.0)
    ).astype(BF)
    writer.send(back.at[:, WIDTH:], back_hbm.at[:, WIDTH:])
    for tile in tiles(FF):
        dhidden = dot(dslot[...], down_w[tile], 1, 1)
        dgate[:, tile] = (dhidden * slope_s[:, tile]).astype(BF)
        dup[:, tile] = (dhidden * act_s[:, tile]).astype(BF)
    writer.send(dgate, dgate_hbm)
    writer.send(dup, dup_hbm)
    back_tiles(dgate, dup, gate_w, up_w, back, back_hbm, writer)
    writer.finish()


def experts_both(me, received, dx, w, weights, order):
    small = (SLOTS, FF)
    wide = (SLOTS, WIDTH)
    early, late = ((EXPERTS, rows, WIDTH) for rows in PART_ROWS)
    back = (SLOTS, WIDTH + HEAD)
    return run_experts(
        experts_both_kernel, "experts_both", [me, received, dx, w, *weights], order,
        [small, early, late, wide, small, small, back],
        [(wide, BF), (wide, BF), ((WIDTH, HEAD), BF)] + EXPERT_SCRATCH
        + [(small, F32), (small, F32), (small, BF), (early, BF), (late, BF), (wide, BF),
           (small, BF), (small, BF), (back, BF)],
        10, 12 * SLOTS * WIDTH * FF,
    )


def experts_backward_kernel(
    dslot_hbm, act_hbm, slope_hbm, gate_hbm, up_hbm, down_hbm, dgate_hbm, dup_hbm, back_hbm,
    dslot, act_s, slope_s, gate_w, up_w, down_w, dgate, dup, back, in_sems, out_sems,
):
    pairs = [(dslot_hbm, dslot)]
    for tile in tiles(FF):
        block = pl.ds(tile.start, TILE)
        pairs += [(down_hbm.at[0, 0].at[block], down_w.at[block])]
    pairs += [(slope_hbm, slope_s), (act_hbm, act_s)]
    for tile in tiles(WIDTH):
        block = pl.ds(tile.start, TILE)
        pairs += [(gate_hbm.at[0, 0].at[block], gate_w.at[block])]
        pairs += [(up_hbm.at[0, 0].at[block], up_w.at[block])]
    copies = start_all(pairs, in_sems)
    writer = Writer(out_sems)
    copies.pop(0).wait()
    dhidden = []
    for tile in tiles(FF):
        copies.pop(0).wait()
        dhidden += [dot(dslot[...], down_w[tile], 1, 1)]
    copies.pop(0).wait()
    copies.pop(0).wait()
    for tile, part in zip(tiles(FF), dhidden):
        dgate[:, tile] = (part * slope_s[:, tile].astype(F32)).astype(BF)
        dup[:, tile] = (part * act_s[:, tile].astype(F32)).astype(BF)
    writer.send(dgate, dgate_hbm)
    writer.send(dup, dup_hbm)
    for copy in copies:
        copy.wait()
    back_tiles(dgate, dup, gate_w, up_w, back, back_hbm, writer)
    writer.finish()


def experts_backward(dslot, act, slope, weights, order):
    small = (SLOTS, FF)
    wide = (SLOTS, WIDTH)
    return run_experts(
        experts_backward_kernel, "experts_backward", [dslot, act, slope, *weights], order,
        [small, small, wide],
        [(wide, BF), (small, BF), (small, BF)] + EXPERT_SCRATCH
        + [(small, BF), (small, BF), (wide, BF)],
        6 + 2 * WIDTH // TILE, 6 * SLOTS * WIDTH * FF,
    )


def expert_grads_kernel(received, dgate_pre, dup_pre, hidden, dslot, packed):
    gate = dot(received[...], dgate_pre[...], 0, 0).astype(BF)
    up = dot(received[...], dup_pre[...], 0, 0).astype(BF)
    down = dot(hidden[...], dslot[...], 0, 0).astype(BF)
    for part in range(DP // 2):
        packed[part, :SHARD, :FF] = gate[part * SHARD : (part + 1) * SHARD]
        packed[part, :SHARD, FF:] = up[part * SHARD : (part + 1) * SHARD]
        packed[part, SHARD:] = down[part * FF // DP : (part + 1) * FF // DP]


def expert_grads(received, dgate_pre, dup_pre, hidden, dslot):
    rows = SHARD + FF // DP
    whole = lambda width: pl.BlockSpec((SLOTS, width), lambda i: (0, 0))
    part = lambda width: pl.BlockSpec((SLOTS, width), lambda i: (0, i))
    return pl.pallas_call(
        expert_grads_kernel,
        grid=(2,),
        out_shape=jax.ShapeDtypeStruct((DP, rows, WIDTH), BF),
        in_specs=[part(WIDTH // 2), whole(FF), whole(FF), part(FF // 2), whole(WIDTH)],
        out_specs=pl.BlockSpec((DP // 2, rows, WIDTH), lambda i: (i, 0, 0)),
        compiler_params=pltpu.CompilerParams(vmem_limit_bytes=VMEM_BYTES),
        cost_estimate=pl.CostEstimate(
            flops=6 * SLOTS * WIDTH * FF, bytes_accessed=14 << 20, transcendentals=0
        ),
        name="expert_grads",
    )(received, dgate_pre, dup_pre, hidden, dslot).reshape(DP * rows, WIDTH)


def seq_tables(counts):
    ends = jnp.cumsum(counts)
    starts = ends - counts
    place = jnp.arange(ROWS, dtype=jnp.int32)
    member = (place[:, None] >= starts[None, :]) & (place[:, None] < ends[None, :])
    index = jnp.arange(counts.shape[0], dtype=jnp.int32)
    segment = jnp.sum(jnp.where(member, index[None, :], 0), axis=1)
    position = place - jnp.sum(jnp.where(member, starts[None, :], 0), axis=1)
    allowed = (segment[:, None] == segment[None, :]) & (place[:, None] >= place[None, :])
    freqs = ROPE_BASE ** (-2.0 * jnp.arange(HEAD // 2, dtype=F32) / HEAD)
    angle = position.astype(F32)[:, None] * freqs[None, :]
    cosine, sine = jnp.cos(angle), jnp.sin(angle)
    return (
        jnp.concatenate([cosine, cosine], axis=1),
        jnp.concatenate([-sine, sine], axis=1),
        allowed.astype(F32),
    )


def slot_matrix(choices, in_parts=False):
    experts = jnp.arange(EXPERTS, dtype=jnp.int32)
    member = jnp.any(choices[:, :, None] == experts[None, None, :], axis=1).astype(BF)
    row = lax.broadcasted_iota(jnp.int32, (ROWS, ROWS), 0)
    column = lax.broadcasted_iota(jnp.int32, (ROWS, ROWS), 1)
    rank = dot((column < row).astype(BF), member).astype(BF)
    slot = jnp.arange(SLOTS, dtype=jnp.int32)[None, :]
    if in_parts:
        later = slot - PART_ENDS[0]
        owner = jnp.where(later < 0, slot // 16, later // 32)
        place = jnp.where(later < 0, slot % 16, 16 + later % 32)
    else:
        owner, place = slot // CAP, slot % CAP
    expand = (owner == experts[:, None]).astype(BF)
    return ((dot(member, expand) > 0.5) & (dot(rank, expand) == place.astype(F32))).astype(BF)


def exchange(rows):
    width = rows.shape[-1]
    moved = lax.all_to_all(
        rows.reshape(EXPERTS, -1, width), "expert", split_axis=0, concat_axis=0, tiled=True
    )
    return moved.reshape(-1, width)


def after(values, order):
    return pl.pallas_call(
        lambda *refs: None,
        out_shape=jax.ShapeDtypeStruct(values.shape, values.dtype),
        in_specs=[ANY, ANY],
        out_specs=ANY,
        input_output_aliases={0: 0},
        name="after",
    )(values, order)


def dense_grads_kernel(me, columns_hbm, factors_hbm, extra, pieces_hbm, columns, turned, factors,
                       total, pieces, in_sems, out_sems):
    start = me[0] * SHARD
    shift = start % HEAD
    base = start - shift
    pairs = []
    for i in range(3):
        at = pl.multiple_of(base + i * WIDTH, HEAD)
        pairs += [(columns_hbm.at[:, pl.ds(at, TILE)], columns.at[:, pl.ds(i * TILE, TILE)])]
    for at in range(0, PACKED, CHUNK):
        block = (slice(None), pl.ds(at, min(CHUNK, PACKED - at)))
        pairs += [(factors_hbm.at[block], factors.at[block])]
    copies = start_all(pairs, in_sems)
    writer = Writer(out_sems)
    for i in range(3):
        copies.pop(0).wait()
        turned[i] = columns[:, i * TILE : (i + 1) * TILE].T

    def put(chunk, values):
        pieces[chunk, :, :CHUNK] = values.astype(BF)
        if extra is not None:
            pieces[chunk, :, CHUNK:] = extra[...]
        writer.send(pieces.at[chunk], pieces_hbm.at[chunk])

    for chunk in range(SMALL // CHUNK):
        copies.pop(0).wait()
        total[...] = dot(
            turned[0 if chunk < QKV // CHUNK else 1],
            factors[:, chunk * CHUNK : (chunk + 1) * CHUNK],
        )
        put(chunk, total[pl.ds(pl.multiple_of(shift, 64), SHARD), :])
    copies.pop(0).wait()
    ends = jnp.zeros((ROWS, HEAD), F32)
    for source in range(DP):
        ends += factors[source * ROWS : (source + 1) * ROWS, SMALL:].astype(F32)
    lane = lax.broadcasted_iota(jnp.int32, (ROWS, HEAD), 1)

    def gain_piece(piece):
        held = (lane == piece + GAIN_HIGH) | (lane == piece + GAIN_LOW)
        return jnp.sum(jnp.where(held, ends, 0.0), axis=1, keepdims=True)

    first, second = gain_piece(base // HEAD), gain_piece(base // HEAD + 1)
    gain = jnp.where(
        shift == 0,
        jnp.concatenate([first, second[: SHARD - ROWS]], axis=0),
        jnp.concatenate([first[ROWS // 2 :], second], axis=0),
    )
    gain_high, gain_low = split(gain)
    total[:, :HEAD] = dot(turned[2], factors[:, SMALL:])
    router = total[pl.ds(pl.multiple_of(shift, 64), SHARD), :HEAD]
    lane = lax.broadcasted_iota(jnp.int32, (SHARD, HEAD), 1)
    router = jnp.where(lane < EXPERTS, router, 0.0)
    router = jnp.where(lane == EXPERTS, gain_high.astype(F32), router)
    router = jnp.where(lane == EXPERTS + 1, gain_low.astype(F32), router)
    put(CHUNKS - 2, jnp.concatenate([router, jnp.zeros_like(router)], axis=1))
    put(CHUNKS - 1, jnp.zeros((SHARD, CHUNK), F32))
    writer.finish()


def dense_grads(me, columns, factors, extra, order):
    tokens = DP * ROWS
    held = [] if extra is None else [extra]
    width = CHUNK * (1 + len(held))

    def body(*refs):
        rest = refs[3 + len(held) + len(order) :]
        dense_grads_kernel(*refs[:3], refs[3] if held else None, *rest)

    return pl.pallas_call(
        body,
        out_shape=jax.ShapeDtypeStruct((CHUNKS, SHARD, width), BF),
        in_specs=[pl.BlockSpec(memory_space=pltpu.SMEM), ANY, ANY]
        + [pl.BlockSpec(memory_space=pltpu.VMEM)] * len(held)
        + [ANY] * len(order),
        out_specs=ANY,
        scratch_shapes=[
            pltpu.VMEM((tokens, 3 * TILE), BF),
            pltpu.VMEM((3, TILE, tokens), BF),
            pltpu.VMEM((tokens, PACKED), BF),
            pltpu.VMEM((TILE, CHUNK), F32),
            pltpu.VMEM((CHUNKS, SHARD, width), BF),
            pltpu.SemaphoreType.DMA((3 + CHUNKS,)),
            pltpu.SemaphoreType.DMA((CHUNKS,)),
        ],
        compiler_params=pltpu.CompilerParams(vmem_limit_bytes=VMEM_BYTES),
        cost_estimate=pl.CostEstimate(
            flops=2 * tokens * TILE * PACKED, bytes_accessed=10 << 20, transcendentals=0
        ),
        name="dense_grads",
    )(me, columns, factors, *held, *order)


def to_expert_peers(pieces):
    return lax.all_to_all(pieces, "expert", split_axis=0, concat_axis=0, tiled=True)


def sum_pieces_kernel(pieces, out):
    total = pieces[0, :, :CHUNK].astype(F32)
    for i in range(1, CHUNKS):
        total += pieces[i, :, :CHUNK].astype(F32)
    if len(out.shape) == 3:
        out[...] = jnp.broadcast_to(total.astype(BF)[None], out.shape)
    else:
        out[...] = total.astype(BF)


def sum_pieces(pieces, copies):
    vmem = pl.BlockSpec(memory_space=pltpu.VMEM)
    return pl.pallas_call(
        sum_pieces_kernel,
        out_shape=jax.ShapeDtypeStruct((copies,) * (copies > 1) + (SHARD, CHUNK), BF),
        in_specs=[vmem],
        out_specs=vmem,
        compiler_params=pltpu.CompilerParams(vmem_limit_bytes=VMEM_BYTES),
        name="sum_pieces",
    )(pieces)


def finish_kernel(l, at, refs):
    (pieces, w_query, key_projection, value_projection, norm_attn), refs = refs[:5], refs[5:]
    if l == 0:
        ends_above, refs = refs[0], refs[5:]
        (query_hbm, key_hbm, value_hbm, out_hbm, gain_attn, gain_ffn, router) = refs[:7]
        query, key, value, out, sems = refs[7:]
    else:
        query_hbm, key_hbm, value_hbm, out_hbm, ends_out, query, key, value, out, sems = refs
    writer = Writer(sems)
    rows = jnp.zeros((SHARD, 1), F32)
    for chunk in range(SMALL // CHUNK):
        part = pieces[chunk, :, at : at + CHUNK].astype(F32)
        lanes = slice(chunk * CHUNK, (chunk + 1) * CHUNK)
        if chunk < Q_END // CHUNK:
            query[:, lanes] = part
            weight = w_query[l, :, lanes]
        elif chunk == Q_END // CHUNK:
            key[...] = part
            weight = key_projection[l]
            writer.send(query, query_hbm.at[l])
            writer.send(key, key_hbm.at[l])
        elif chunk < QKV // CHUNK:
            value[...] = part
            weight = value_projection[l]
            writer.send(value, value_hbm.at[l])
        else:
            out[:, lanes.start - QKV : lanes.stop - QKV] = part
            continue
        rows += jnp.sum(part * weight.astype(F32), axis=1, keepdims=True)
    writer.send(out, out_hbm.at[l])
    ends = pieces[CHUNKS - 2, :, at : at + HEAD].astype(F32)
    ffn = ends[:, EXPERTS : EXPERTS + 1] + ends[:, EXPERTS + 1 : EXPERTS + 2]
    lane = lax.broadcasted_iota(jnp.int32, (SHARD, HEAD), 1)
    ends = jnp.where(lane == EXPERTS, rows, jnp.where(lane == EXPERTS + 1, ffn, ends))
    if l > 0:
        ends_out[...] = ends
    else:
        for layer, part in enumerate((ends, ends_above[...])):
            router[layer] = part[:, :EXPERTS]
            wide = jnp.concatenate([part, jnp.zeros((TILE - SHARD, HEAD), F32)], axis=0).T
            gain = norm_attn[layer : layer + 1].astype(F32)
            gain_attn[layer : layer + 1] = wide[EXPERTS : EXPERTS + 1, :SHARD] / gain
            gain_ffn[layer : layer + 1] = wide[EXPERTS + 1 : EXPERTS + 2, :SHARD]
    writer.finish()


def finish(l, pieces, at, weights, norm_attn, above):
    sd = jax.ShapeDtypeStruct
    vmem = pl.BlockSpec(memory_space=pltpu.VMEM)
    keys = (SHARD, KEY_VALUE_HEADS * HEAD)
    slabs = [(SHARD, Q_END), keys, keys, (SHARD, WIDTH)]
    outs = [sd((LAYERS,) + shape, F32) for shape in slabs]
    if above is None:
        outs += [sd((SHARD, HEAD), F32)]
        ins, in_specs, aliases = [], [], {}
    else:
        outs += [sd((LAYERS, SHARD), F32)] * 2 + [sd((LAYERS, SHARD, EXPERTS), F32)]
        ins, in_specs = [above[4], *above[:4]], [vmem] + [ANY] * 4
        aliases = {6 + i: i for i in range(4)}
    return pl.pallas_call(
        lambda *refs: finish_kernel(l, at, refs),
        out_shape=outs,
        in_specs=[vmem] * 5 + in_specs,
        out_specs=[ANY] * 4 + [vmem] * (len(outs) - 4),
        input_output_aliases=aliases,
        scratch_shapes=[pltpu.VMEM(shape, F32) for shape in slabs]
        + [pltpu.SemaphoreType.DMA((4,))],
        compiler_params=pltpu.CompilerParams(vmem_limit_bytes=VMEM_BYTES),
        name="finish",
    )(pieces, *weights, norm_attn, *ins)


def finish_experts_kernel(shares0, shares1, gate, up, down):
    for l, shares in enumerate((shares0, shares1)):
        gate[l, 0] = shares[:SHARD, :FF].astype(F32)
        up[l, 0] = shares[:SHARD, FF:].astype(F32)
        down[l, 0] = shares[SHARD:].astype(F32)


def finish_experts(shares0, shares1):
    sd = jax.ShapeDtypeStruct
    vmem = pl.BlockSpec(memory_space=pltpu.VMEM)
    return pl.pallas_call(
        finish_experts_kernel,
        out_shape=[
            sd((LAYERS, 1, SHARD, FF), F32), sd((LAYERS, 1, SHARD, FF), F32),
            sd((LAYERS, 1, FF // DP, WIDTH), F32),
        ],
        in_specs=[vmem] * 2,
        out_specs=[vmem] * 3,
        compiler_params=pltpu.CompilerParams(vmem_limit_bytes=VMEM_BYTES),
        name="finish_experts",
    )(shares0, shares1)


def mixed_kernel(x, high, low, early, late, out):
    total = x[...]
    for at, part in ((slice(0, PART_ENDS[0]), early), (slice(*PART_ENDS), late)):
        total += dot(high[:, at], part[...]) + dot(low[:, at], part[...])
    out[...] = total.astype(BF)


def mixed_rows(x, high, low, parts):
    vmem = pl.BlockSpec(memory_space=pltpu.VMEM)
    return pl.pallas_call(
        mixed_kernel,
        out_shape=jax.ShapeDtypeStruct((ROWS, WIDTH), BF),
        in_specs=[vmem] * 5,
        out_specs=vmem,
        compiler_params=pltpu.CompilerParams(vmem_limit_bytes=VMEM_BYTES),
        name="mixed",
    )(x, high, low, *parts)


def local(
    tokens, cotangent, lengths, routes, norm_attn, w_query, key_projection, value_projection,
    w_out, norm_ffn, w_router, w_gate, w_up, w_down,
):
    me_dp = lax.axis_index("dp").astype(jnp.int32).reshape(1)
    me_expert = lax.axis_index("expert").astype(jnp.int32).reshape(1)
    tables = seq_tables(lengths[0])
    give = [slot_matrix(routes[l]) for l in range(LAYERS)]
    take = [g.T for g in give]
    give_parts = slot_matrix(routes[1], True)
    experts = (w_gate, w_up, w_down)

    def gather(values):
        return lax.all_gather(values, "dp", axis=0, tiled=True)

    w = [
        gather(
            jnp.concatenate(
                [w_query[l], key_projection[l], value_projection[l], w_out[l], w_router[l],
                 norm_attn[l][:, None], norm_ffn[l][:, None],
                 jnp.zeros((SHARD, HEAD - EXPERTS - 2), BF)],
                axis=1,
            )
        )
        for l in range(LAYERS)
    ]

    dx_rows = exchange(dot(take[1], cotangent).astype(BF))

    kept0 = attn_forward(tokens, None, w[0], tables, take[0], give[0], (dx_rows,))
    received0 = exchange(kept0["rows"])
    act0, slope0, hidden0, out0 = experts_forward(received0, experts, ())
    returned0 = exchange(out0)
    columns0 = gather(kept0["columns"])

    kept1 = attn_forward(
        kept0["after"], (returned0, kept0["high"], kept0["low"]), w[1], tables, take[1],
        give_parts, (),
    )
    received1 = exchange(kept1["rows"])
    columns1 = gather(kept1["columns"])
    hidden1, early1, late1, dslot1, dgate1, dup1, back1 = experts_both(
        me_expert, received1, dx_rows, w[1], experts, ()
    )
    back1 = exchange(back1)
    grads1 = expert_grads(received1, dgate1, dup1, hidden1, dslot1)
    early1 = exchange(early1)
    late1 = exchange(late1)

    dx0, packed1, rows0 = attn_backward(
        cotangent, back1, kept1, w[1], tables, give[1], (take[0], kept0["router"]), None,
        (grads1, columns0, columns1),
    )
    dslot0 = exchange(rows0)
    factors1 = gather(packed1)
    shares1 = lax.psum_scatter(after(grads1, packed1), "dp", scatter_dimension=0, tiled=True)
    dgate0, dup0, back0 = experts_backward(dslot0, act0, slope0, experts, ())
    back0 = exchange(back0)
    grads0 = expert_grads(received0, dgate0, dup0, hidden0, dslot0)
    pieces1 = dense_grads(me_dp, columns1, factors1, None, (early1,))
    grad_tokens, packed0 = attn_backward(
        dx0, back0, kept0, w[0], tables, give[0], None, returned0, (shares1, grads0, pieces1)
    )
    factors0 = gather(packed0)
    summed1 = sum_pieces(to_expert_peers(after(pieces1, late1)), 1)
    shares0 = lax.psum_scatter(after(grads0, summed1), "dp", scatter_dimension=0, tiled=True)
    mixed = mixed_rows(kept1["after"], kept1["high"], kept1["low"], (early1, late1))
    pieces = to_expert_peers(dense_grads(me_dp, columns0, factors0, summed1, ()))
    pieces0 = to_expert_peers(sum_pieces(pieces, CHUNKS))

    dense = (w_query, key_projection, value_projection)
    above = finish(1, pieces, CHUNK, dense, norm_attn, None)
    query, key, value, out, gain_attn, gain_ffn, router = finish(
        0, pieces0, 0, dense, norm_attn, above
    )
    gate, up, down = finish_experts(shares0, shares1)
    return (
        mixed, grad_tokens, gain_attn, query, key, value, out, gain_ffn, router, gate, up, down
    )


def solution(mesh):
    placed = (
        P(("dp", "expert"), None),
        P(("dp", "expert"), None),
        P(("dp", "expert"), None),
        P(None, ("dp", "expert"), None),
        P(None, "dp"),
        P(None, "dp", None),
        P(None, "dp", None),
        P(None, "dp", None),
        P(None, "dp", None),
        P(None, "dp"),
        P(None, "dp", None),
        P(None, "expert", None, None),
        P(None, "expert", None, None),
        P(None, "expert", None, None),
    )
    return jax.shard_map(
        local,
        mesh=mesh,
        in_specs=placed,
        out_specs=(
            P(("dp", "expert"), None),
            P(("dp", "expert"), None),
            P(None, "dp"),
            P(None, "dp", None),
            P(None, "dp", None),
            P(None, "dp", None),
            P(None, "dp", None),
            P(None, "dp"),
            P(None, "dp", None),
            P(None, "expert", "dp", None),
            P(None, "expert", "dp", None),
            P(None, "expert", "dp", None),
        ),
        check_vma=False,
    )
```

```python
import jax
import jax.numpy as jnp
from jax import lax
from jax.experimental import pallas as pl
from jax.experimental.pallas import tpu as pltpu
from jax.sharding import PartitionSpec as P

QUERY_HEADS = 12
KEY_VALUE_HEADS = 2
GROUPS = QUERY_HEADS // KEY_VALUE_HEADS
HEAD = 128
LAYERS = 2
WIDTH = 1536
FF = 768
ROWS = 128
EXPERTS = 16
CAP = 48
SLOTS = EXPERTS * CAP
DP = 8
SHARD = WIDTH // DP
Q_END = QUERY_HEADS * HEAD
K_END = Q_END + KEY_VALUE_HEADS * HEAD
QKV = K_END + KEY_VALUE_HEADS * HEAD
SMALL = QKV + WIDTH
PACKED = SMALL + HEAD
GAIN_ATTN, GAIN_FFN = 16, 17
GAIN_HIGH, GAIN_LOW = 16, 32
PIECES = WIDTH // HEAD
TILE = 256
PART_ROWS = (16, 32)
PART_ENDS = (EXPERTS * 16, SLOTS)
CHUNKS, CHUNK = 16, 256
COLUMNS = 3 * WIDTH
EPSILON = 1e-06
ROPE_BASE = 1000000.0
SCALE = HEAD ** (-0.5)
GELU_A = 0.7978845608028654
GELU_B = 0.044715
VMEM_BYTES = 56 << 20
BF = jnp.bfloat16
F32 = jnp.float32
ANY = pl.BlockSpec(memory_space=pl.ANY)


def dot(left, right, left_dim=1, right_dim=0):
    return lax.dot_general(
        left, right, (((left_dim,), (right_dim,)), ((), ())), preferred_element_type=F32
    )


def split(values):
    high = values.astype(BF)
    return high, (values - high.astype(F32)).astype(BF)


def unit(values):
    return lax.rsqrt(jnp.mean(values * values, axis=-1, keepdims=True) + EPSILON)


def turn(values, cosine, sine):
    return values * cosine + pltpu.roll(values, HEAD // 2, 1) * sine


def expert_lanes(transposed=False, in_parts=False):
    shape = (SLOTS, HEAD) if transposed else (HEAD, SLOTS)
    slot = lax.broadcasted_iota(jnp.int32, shape, 0 if transposed else 1)
    expert = lax.broadcasted_iota(jnp.int32, shape, 1 if transposed else 0)
    if in_parts:
        first = (slot >> 4) == expert
        held = first | ((slot >= PART_ENDS[0]) & (((slot - PART_ENDS[0]) >> 5) == expert))
    else:
        held = (slot >= expert * CAP) & (slot < expert * CAP + CAP)
    return held.astype(F32).astype(BF)


def gain_rows(small):
    row = lax.broadcasted_iota(jnp.int32, (8, HEAD), 0)
    lane = lax.broadcasted_iota(jnp.int32, (8, HEAD), 1)
    pick = ((lane == row + GAIN_ATTN) & (row < 2)).astype(F32).astype(BF)
    rows = dot(pick, small, 1, 1)
    return rows[0:1], rows[1:2]


def router_probs(rows, small):
    logits = dot(rows, small)
    lane = lax.broadcasted_iota(jnp.int32, logits.shape, 1)
    logits = jnp.where(lane < EXPERTS, logits, -1e30)
    powers = jnp.exp(logits - jnp.max(logits, axis=-1, keepdims=True))
    return powers / jnp.sum(powers, axis=-1, keepdims=True)


def start_all(pairs, sems):
    copies = [
        pltpu.make_async_copy(source, target, sems.at[i]) for i, (source, target) in enumerate(pairs)
    ]
    for copy in copies:
        copy.start()
    return copies


class Writer:
    def __init__(self, sems):
        self.sems, self.copies = sems, []

    def send(self, source, target):
        copy = pltpu.make_async_copy(source, target, self.sems.at[len(self.copies)])
        copy.start()
        self.copies.append(copy)

    def finish(self):
        for copy in self.copies:
            copy.wait()


class Reader:
    def __init__(self, sems, pairs):
        self.copies = start_all(pairs, sems)

    def take(self, count=1):
        for _ in range(count):
            self.copies.pop(0).wait()


def tiles(width):
    return [slice(at, at + TILE) for at in range(0, width, TILE)]


def small_block(w_hbm, w):
    return (w_hbm.at[:, pl.ds(SMALL, HEAD)], w.at[:, pl.ds(SMALL, HEAD)])


def column_block(w_hbm, w, at):
    return (w_hbm.at[:, pl.ds(at, TILE)], w.at[:, pl.ds(at, TILE)])


def attn_forward_kernel(first, ins, outs, scratch):
    (x_hbm, w_hbm, cosine_hbm, sine_hbm, allowed_hbm, take_hbm, give_hbm), ins = ins[:7], ins[7:]
    (columns_hbm, qrot_hbm, krot_hbm, value_hbm, probs_hbm, after_hbm, router_hbm, high_hbm, low_hbm,
     rows_hbm), outs = outs[:10], outs[10:]
    (x_in, w, cosine, sine, allowed, take, give, returned, gates, x, columns, qrot, krot, value, probs,
     after, router, high, low, rows, in_sems, out_sems) = scratch
    acts = columns.at[:, :WIDTH]
    attended = columns.at[:, WIDTH : 2 * WIDTH]
    acts_two = columns.at[:, 2 * WIDTH :]
    pairs = []
    if not first:
        high_below, low_below, returned_hbm = ins
        pairs += [(high_below, gates.at[:ROWS]), (low_below, gates.at[ROWS:])]
        pairs += [(returned_hbm, returned)]
    pairs += [(x_hbm, x_in), small_block(w_hbm, w)]
    pairs += [column_block(w_hbm, w, at) for at in range(0, QKV, TILE)]
    pairs += [(cosine_hbm, cosine), (sine_hbm, sine), (allowed_hbm, allowed)]
    pairs += [column_block(w_hbm, w, at) for at in range(QKV, SMALL, TILE)]
    pairs += [(take_hbm, take), (give_hbm, give)]
    reader, writer = Reader(in_sems, pairs), Writer(out_sems)
    if first:
        reader.take()
        x[...] = x_in[...].astype(F32)
    else:
        reader.take(4)
        for tile in tiles(WIDTH):
            both = dot(gates[...], returned[:, tile])
            x[:, tile] = x_in[:, tile] + both[:ROWS] + both[ROWS:]
        writer.send(x, outs[0])
    reader.take()
    small = w[:, SMALL:]
    gain_attn, gain_ffn = gain_rows(small)
    total = x[...]
    acts[...] = (total * unit(total) * gain_attn).astype(BF)
    wide = []
    for tile in tiles(QKV):
        reader.take()
        wide += [dot(acts[...], w[:, tile])]
    reader.take(3)
    for tile in range(QKV // TILE):
        for half in range(TILE // HEAD):
            head = tile * (TILE // HEAD) + half
            part = wide[tile][:, half * HEAD : (half + 1) * HEAD]
            if head < QUERY_HEADS:
                qrot[head] = turn(part, cosine[...], sine[...]).astype(BF)
            elif head < QUERY_HEADS + KEY_VALUE_HEADS:
                krot[head - QUERY_HEADS] = turn(part, cosine[...], sine[...]).astype(BF)
            else:
                value[head - QUERY_HEADS - KEY_VALUE_HEADS] = part.astype(BF)
    writer.send(qrot, qrot_hbm)
    writer.send(krot, krot_hbm)
    writer.send(value, value_hbm)
    open_scores = (allowed[...] > 0.5)[None]
    for k in range(KEY_VALUE_HEADS):
        heads = slice(k * GROUPS, (k + 1) * GROUPS)
        scores = dot(qrot[heads].reshape(GROUPS * ROWS, HEAD), krot[k], 1, 1) * SCALE
        scores = jnp.where(open_scores, scores.reshape(GROUPS, ROWS, ROWS), -1000000000.0)
        powers = jnp.exp(scores - jnp.max(scores, axis=-1, keepdims=True))
        shares = powers / jnp.sum(powers, axis=-1, keepdims=True)
        probs[heads] = shares
        mixed = dot(shares.astype(BF).reshape(GROUPS * ROWS, ROWS), value[k]).astype(BF)
        for group in range(GROUPS):
            at = (k * GROUPS + group) * HEAD
            attended[:, at : at + HEAD] = mixed[group * ROWS : (group + 1) * ROWS]
    writer.send(probs, probs_hbm)
    for tile in tiles(WIDTH):
        reader.take()
        after[:, tile] = x[:, tile] + dot(
            attended[...], w[:, QKV + tile.start : QKV + tile.stop]
        )
    writer.send(after, after_hbm)
    total = after[...]
    acts_two[...] = (total * unit(total) * gain_ffn).astype(BF)
    writer.send(columns, columns_hbm)
    reader.take(2)
    for tile in tiles(WIDTH):
        rows[:, tile] = dot(take[...], acts_two[:, tile]).astype(BF)
        writer.send(rows.at[:, tile], rows_hbm.at[:, tile])
    shares = router_probs(acts_two[...], small)
    router[...] = shares
    spread = expert_lanes(in_parts=not first)
    both = dot(jnp.concatenate(split(shares), axis=0), spread).astype(BF)
    high[...] = both[:ROWS] * give[...]
    low[...] = both[ROWS:] * give[...]
    writer.send(router, router_hbm)
    writer.send(high, high_hbm)
    writer.send(low, low_hbm)
    writer.finish()


HEADS = (QUERY_HEADS, ROWS, HEAD)
KEYS = (KEY_VALUE_HEADS, ROWS, HEAD)
TABLE = (ROWS, HEAD)
TOKENS = (ROWS, WIDTH)
WIDE = (SLOTS, WIDTH)


def run_attn(kernel, name, ins, order, outs, scratch, in_copies, out_copies, vmem):
    sd = jax.ShapeDtypeStruct

    def body(*refs):
        first_out = len(ins) + len(order)
        first_scratch = first_out + len(outs)
        kernel(refs[: len(ins)], refs[first_out:first_scratch], refs[first_scratch:])

    return pl.pallas_call(
        body,
        out_shape=[sd(shape, kind) for shape, kind in outs],
        in_specs=[ANY] * (len(ins) + len(order)),
        out_specs=[ANY] * len(outs),
        scratch_shapes=[pltpu.VMEM(shape, kind) for shape, kind in scratch]
        + [pltpu.SemaphoreType.DMA((in_copies,)), pltpu.SemaphoreType.DMA((out_copies,))],
        compiler_params=pltpu.CompilerParams(vmem_limit_bytes=vmem),
        cost_estimate=pl.CostEstimate(
            flops=2 * ROWS * WIDTH * PACKED, bytes_accessed=20 << 20, transcendentals=200000
        ),
        name=name,
    )(*ins, *order)


def attn_forward(x, combine, w, tables, take, give, order):
    first = combine is None
    outs = [
        ((ROWS, COLUMNS), BF), (HEADS, BF), (KEYS, BF), (KEYS, BF), ((QUERY_HEADS, ROWS, ROWS), F32),
        (TOKENS, F32), (TABLE, F32), ((ROWS, SLOTS), BF), ((ROWS, SLOTS), BF), (WIDE, BF),
    ]
    names = [
        "columns", "qrot", "krot", "value", "probs", "after", "router", "high", "low", "rows"
    ]
    scratch = [(TOKENS, x.dtype), ((WIDTH, PACKED), BF)] + [(TABLE, F32)] * 3
    scratch += [((SLOTS, ROWS), BF), ((ROWS, SLOTS), BF)]
    scratch += [((16, HEAD), BF)] * 2 if first else [(WIDE, BF), ((2 * ROWS, SLOTS), BF)]
    scratch += [(TOKENS, F32)] + outs
    ins = [x, w, *tables, take, give]
    if not first:
        high, low, returned = combine
        ins += [high, low, returned]
        outs = outs + [(TOKENS, F32)]
        names += ["x"]
    result = run_attn(
        lambda *refs: attn_forward_kernel(first, *refs), "attn_forward", ins, order, outs, scratch,
        10 + SMALL // TILE, 20, VMEM_BYTES,
    )
    return dict(zip(names, result))


def norm_back(grad, gain, values):
    scale = unit(values)
    inner = grad * gain
    return scale * inner - values * (scale * scale * scale) * jnp.mean(
        inner * values, axis=-1, keepdims=True
    )


def attn_backward_kernel(last, ins, outs, scratch):
    (dx_hbm, back_hbm, w_hbm, cosine_hbm, sine_hbm, give_hbm, router_hbm, after_hbm, x_hbm, probs_hbm,
     qrot_hbm, krot_hbm, value_hbm), ins = ins[:13], ins[13:]
    (dx_in, back, w, cosine, sine, give, router, after, x_in, probs, qrot, krot, value, wide_in,
     small_in, datt, dx_out, packed), scratch = scratch[:18], scratch[18:]
    if last:
        rows, scratch = scratch[0], scratch[1:]
    in_sems, out_sems = scratch
    pairs = [(give_hbm, give), (back_hbm, back), (router_hbm, router), (dx_hbm, dx_in)]
    if not last:
        pairs += [(ins[0], wide_in)]
    pairs += [small_block(w_hbm, w), (after_hbm, after)]
    for at in range(0, WIDTH, TILE):
        block = (pl.ds(at, TILE), pl.ds(QKV, WIDTH))
        pairs += [(w_hbm.at[block], w.at[block])]
    pairs += [(probs_hbm, probs), (value_hbm, value), (krot_hbm, krot), (qrot_hbm, qrot)]
    pairs += [(cosine_hbm, cosine), (sine_hbm, sine)]
    for at in range(0, WIDTH, TILE):
        block = (pl.ds(at, TILE), pl.ds(0, QKV))
        pairs += [(w_hbm.at[block], w.at[block])]
    pairs += [(x_hbm, x_in)]
    if last:
        pairs += [(ins[0], wide_in), (ins[1], small_in)]
    reader, writer = Reader(in_sems, pairs), Writer(out_sems)
    reader.take(4)
    dx = dx_in[...].astype(F32)
    spread = expert_lanes(True)
    if last:
        dgate = back[:, WIDTH:].astype(F32)
        drouter = dot(give[...], (dgate[:, 0:1] * spread).astype(BF))
        drouter += dot(give[...], (dgate[:, 1:2] * spread).astype(BF))
    else:
        reader.take()
        dgate = dot(dx.astype(BF), wide_in[...], 1, 1) * give[...]
        both = dot(jnp.concatenate(split(dgate), axis=0), spread)
        drouter = both[:ROWS] + both[ROWS:]
    reader.take(2)
    small = w[:, SMALL:]
    gain_attn, gain_ffn = gain_rows(small)
    shares = router[...]
    dlogits = shares * (drouter - jnp.sum(drouter * shares, axis=-1, keepdims=True))
    dlogits = dlogits.astype(BF)
    dacts_two = dot(dlogits, small, 1, 1) + dot(give[...], back[:, :WIDTH])
    total = after[...]
    scale = unit(total)
    dafter = dx + norm_back(dacts_two, gain_ffn, total)
    dx_out[...] = dafter
    packed[:, QKV:SMALL] = dafter.astype(BF)
    dgain = jnp.sum(dacts_two * total * scale, axis=0, keepdims=True)
    dgain_high, dgain_low = split(dgain)
    pieces = [jnp.zeros((GAIN_HIGH, HEAD), F32)]
    for part in (dgain_high.astype(F32), dgain_low.astype(F32)):
        pieces += [part[:, at : at + HEAD] for at in range(0, WIDTH, HEAD)]
        pieces += [jnp.zeros((GAIN_LOW - GAIN_HIGH - PIECES, HEAD), F32)]
    pieces += [jnp.zeros((HEAD - 2 * GAIN_LOW + GAIN_HIGH, HEAD), F32)]
    packed[:, SMALL:] = (dlogits.astype(F32) + jnp.concatenate(pieces, axis=0).T).astype(BF)
    writer.send(packed.at[:, QKV:], outs[1].at[:, QKV:])
    for tile in tiles(WIDTH):
        reader.take()
        wide = dot(packed[:, QKV:SMALL], w[tile, QKV:SMALL], 1, 1).astype(BF)
        for half in range(TILE // HEAD):
            datt[tile.start // HEAD + half] = wide[:, half * HEAD : (half + 1) * HEAD]
    reader.take(6)
    for k in range(KEY_VALUE_HEADS):
        heads = slice(k * GROUPS, (k + 1) * GROUPS)
        datt_k = datt[heads].reshape(GROUPS * ROWS, HEAD)
        p = probs[heads].reshape(GROUPS * ROWS, ROWS)
        dprobs = dot(datt_k, value[k], 1, 1)
        dvalue = dot(p.astype(BF), datt_k, 0, 0)
        dscores = (p * (dprobs - jnp.sum(dprobs * p, axis=-1, keepdims=True))).astype(BF)
        dqrot = dot(dscores, krot[k]) * SCALE
        dkrot = dot(dscores, qrot[heads].reshape(GROUPS * ROWS, HEAD), 0, 0) * SCALE
        for group in range(GROUPS):
            at = (k * GROUPS + group) * HEAD
            part = dqrot[group * ROWS : (group + 1) * ROWS]
            packed[:, at : at + HEAD] = turn(part, cosine[...], -sine[...]).astype(BF)
        at = Q_END + k * HEAD
        packed[:, at : at + HEAD] = turn(dkrot, cosine[...], -sine[...]).astype(BF)
        at = K_END + k * HEAD
        packed[:, at : at + HEAD] = dvalue.astype(BF)
    writer.send(packed.at[:, :QKV], outs[1].at[:, :QKV])
    parts = []
    for tile in tiles(WIDTH):
        reader.take()
        parts += [dot(packed[:, :QKV], w[tile, :QKV], 1, 1)]
    dacts = jnp.concatenate(parts, axis=1)
    reader.take()
    dx = dx_out[...] + norm_back(dacts, gain_attn, x_in[...].astype(F32))
    dx_out[...] = dx
    writer.send(dx_out, outs[0])
    if last:
        reader.take(2)
        dx_low = dx.astype(BF)
        both = dot(spread, jnp.concatenate(split(small_in[...]), axis=0), 1, 1).astype(BF)
        gates = jnp.concatenate([both[:, :ROWS] * wide_in[...], both[:, ROWS:] * wide_in[...]], axis=1)
        twice = jnp.concatenate([dx_low, dx_low], axis=0)
        for tile in tiles(WIDTH):
            rows[:, tile] = dot(gates, twice[:, tile]).astype(BF)
            writer.send(rows.at[:, tile], outs[2].at[:, tile])
    writer.finish()


def attn_backward(dx, back, x, kept, w, tables, give, below, returned, order):
    last = below is not None
    outs = [(TOKENS, F32), ((ROWS, PACKED), BF)]
    if last:
        outs += [(WIDE, BF)]
    ins = [dx, back, w, tables[0], tables[1], give, kept["router"], kept["after"], x]
    ins += [kept[n] for n in ("probs", "qrot", "krot", "value")]
    ins += list(below) if last else [returned]
    scratch = [
        (TOKENS, dx.dtype), (back.shape, BF), ((WIDTH, PACKED), BF), (TABLE, F32), (TABLE, F32),
        ((ROWS, SLOTS), BF), (TABLE, F32), (TOKENS, F32), (TOKENS, x.dtype),
        ((QUERY_HEADS, ROWS, ROWS), F32), (HEADS, BF), (KEYS, BF), (KEYS, BF),
        ((SLOTS, ROWS), BF) if last else (WIDE, BF), (TABLE, F32), (HEADS, BF),
    ] + outs
    return run_attn(
        lambda *refs: attn_backward_kernel(last, *refs), "attn_backward", ins, order, outs, scratch,
        16 + 2 * WIDTH // TILE, 12, VMEM_BYTES,
    )


def gelu_parts(gate):
    square = gate * gate
    bend = jnp.tanh(GELU_A * gate * (1.0 + GELU_B * square))
    return bend, square


def gelu(gate):
    bend, _ = gelu_parts(gate)
    return 0.5 * gate * (1.0 + bend)


def gelu_both(gate):
    bend, square = gelu_parts(gate)
    slope = 0.5 * (1.0 + bend) + 0.5 * gate * (1.0 - bend * bend) * GELU_A * (
        1.0 + 3.0 * GELU_B * square
    )
    return 0.5 * gate * (1.0 + bend), slope


def weight_pairs(l, gate_hbm, up_hbm, down_hbm, gate_w, up_w, down_w):
    gate_up = []
    for at in range(0, FF, TILE):
        block = (slice(None), pl.ds(at, TILE))
        gate_up += [(gate_hbm.at[l, 0].at[block], gate_w.at[block])]
        gate_up += [(up_hbm.at[l, 0].at[block], up_w.at[block])]
    down = [(down_hbm.at[l, 0], down_w)]
    return gate_up, down


def run_experts(kernel, name, ins, order, outs, scratch, in_copies, flops):
    sd = jax.ShapeDtypeStruct
    count = len(ins) + len(order)
    specs = [
        pl.BlockSpec(memory_space=pltpu.SMEM if a.dtype == jnp.int32 else pl.ANY) for a in ins
    ]

    def body(*refs):
        kernel(*refs[: len(ins)], *refs[count:])

    return pl.pallas_call(
        body,
        out_shape=[sd(shape, BF) for shape in outs],
        in_specs=specs + [ANY] * len(order),
        out_specs=[ANY] * len(outs),
        scratch_shapes=[pltpu.VMEM(shape, kind) for shape, kind in scratch]
        + [pltpu.SemaphoreType.DMA((in_copies,)), pltpu.SemaphoreType.DMA((40,))],
        compiler_params=pltpu.CompilerParams(vmem_limit_bytes=VMEM_BYTES),
        cost_estimate=pl.CostEstimate(
            flops=flops, bytes_accessed=20 << 20, transcendentals=SLOTS * FF
        ),
        name=name,
    )(*ins, *order)


def experts_forward_kernel(
    received_hbm, gate_hbm, up_hbm, down_hbm, act_hbm, slope_hbm, hidden_hbm, out_hbm,
    received, gate_w, up_w, down_w, act_s, slope_s, hidden, out, in_sems, out_sems,
):
    gate_up, down = weight_pairs(0, gate_hbm, up_hbm, down_hbm, gate_w, up_w, down_w)
    copies = start_all([(received_hbm, received)] + gate_up + down, in_sems)
    writer = Writer(out_sems)
    copies.pop(0).wait()
    for tile in tiles(FF):
        copies.pop(0).wait()
        copies.pop(0).wait()
        gate = dot(received[...], gate_w[:, tile])
        up = dot(received[...], up_w[:, tile])
        act, slope = gelu_both(gate)
        act_s[:, tile] = act.astype(BF)
        slope_s[:, tile] = (slope * up).astype(BF)
        hidden[:, tile] = (act * up).astype(BF)
    copies.pop(0).wait()
    writer.send(act_s, act_hbm)
    writer.send(slope_s, slope_hbm)
    writer.send(hidden, hidden_hbm)
    for tile in tiles(WIDTH):
        out[:, tile] = dot(hidden[...], down_w[:, tile]).astype(BF)
        writer.send(out.at[:, tile], out_hbm.at[:, tile])
    writer.finish()


EXPERT_SCRATCH = [((WIDTH, FF), BF), ((WIDTH, FF), BF), ((FF, WIDTH), BF)]


def experts_forward(received, weights, order):
    small = (SLOTS, FF)
    wide = (SLOTS, WIDTH)
    return run_experts(
        experts_forward_kernel, "experts_forward", [received, *weights], order,
        [small, small, small, wide],
        [(wide, BF)] + EXPERT_SCRATCH + [(small, BF)] * 3 + [(wide, BF)],
        8, 6 * SLOTS * WIDTH * FF,
    )


def back_tiles(dgate, dup, gate_w, up_w, back, back_hbm, writer):
    for tile in tiles(WIDTH):
        back[:, tile] = (
            dot(dgate[...], gate_w[tile], 1, 1) + dot(dup[...], up_w[tile], 1, 1)
        ).astype(BF)
        writer.send(back.at[:, tile], back_hbm.at[:, tile])


def experts_both_kernel(
    me, received_hbm, dx_hbm, w_hbm, gate_hbm, up_hbm, down_hbm,
    hidden_hbm, early_hbm, late_hbm, dslot_hbm, dgate_hbm, dup_hbm, back_hbm,
    received, dx, small, gate_w, up_w, down_w, act_s, slope_s, hidden, early, late, dslot, dgate, dup,
    back, in_sems, out_sems,
):
    gate_up, down = weight_pairs(1, gate_hbm, up_hbm, down_hbm, gate_w, up_w, down_w)
    pairs = [(received_hbm, received)] + gate_up
    pairs += [(w_hbm.at[:, pl.ds(SMALL, HEAD)], small), (dx_hbm, dx)] + down
    copies = start_all(pairs, in_sems)
    writer = Writer(out_sems)
    copies.pop(0).wait()
    for tile in tiles(FF):
        copies.pop(0).wait()
        copies.pop(0).wait()
        gate = dot(received[...], gate_w[:, tile])
        up = dot(received[...], up_w[:, tile])
        act, slope = gelu_both(gate)
        act_s[:, tile] = act
        slope_s[:, tile] = slope * up
        hidden[:, tile] = (act * up).astype(BF)
    for copy in copies:
        copy.wait()
    writer.send(hidden, hidden_hbm)
    shares = router_probs(received[...], small[...])
    lane = lax.broadcasted_iota(jnp.int32, shares.shape, 1)
    weight = jnp.sum(jnp.where(lane == me[0], shares, 0.0), axis=-1, keepdims=True)
    total = jnp.zeros((SLOTS, 1), F32)
    for tile in tiles(WIDTH):
        part = dot(hidden[...], down_w[:, tile]).astype(BF)
        for expert in range(EXPERTS):
            at = expert * CAP
            early[expert, :, tile] = part[at : at + PART_ROWS[0]]
            row = tile.start // TILE * PART_ROWS[1]
            late[expert, row : row + PART_ROWS[1]] = part[at + PART_ROWS[0] : at + CAP]
        wide = dx[:, tile].astype(F32)
        total += jnp.sum(wide * part.astype(F32), axis=-1, keepdims=True)
        dslot[:, tile] = (weight * wide).astype(BF)
    writer.send(early, early_hbm)
    writer.send(late, late_hbm)
    writer.send(dslot, dslot_hbm)
    high, low = split(total)
    back[:, WIDTH:] = jnp.where(
        lane == 0, high.astype(F32), jnp.where(lane == 1, low.astype(F32), 0.0)
    ).astype(BF)
    writer.send(back.at[:, WIDTH:], back_hbm.at[:, WIDTH:])
    for tile in tiles(FF):
        dhidden = dot(dslot[...], down_w[tile], 1, 1)
        dgate[:, tile] = (dhidden * slope_s[:, tile]).astype(BF)
        dup[:, tile] = (dhidden * act_s[:, tile]).astype(BF)
    writer.send(dgate, dgate_hbm)
    writer.send(dup, dup_hbm)
    back_tiles(dgate, dup, gate_w, up_w, back, back_hbm, writer)
    writer.finish()


def experts_both(me, received, dx, w, weights, order):
    small = (SLOTS, FF)
    wide = (SLOTS, WIDTH)
    early = (EXPERTS, PART_ROWS[0], WIDTH)
    late = (EXPERTS, SHARD, CHUNK)
    back = (SLOTS, WIDTH + HEAD)
    return run_experts(
        experts_both_kernel, "experts_both", [me, received, dx, w, *weights], order,
        [small, early, late, wide, small, small, back],
        [(wide, BF), (wide, BF), ((WIDTH, HEAD), BF)] + EXPERT_SCRATCH
        + [(small, F32), (small, F32), (small, BF), (early, BF), (late, BF), (wide, BF),
           (small, BF), (small, BF), (back, BF)],
        10, 12 * SLOTS * WIDTH * FF,
    )


def experts_backward_kernel(
    dslot_hbm, act_hbm, slope_hbm, gate_hbm, up_hbm, down_hbm, dgate_hbm, dup_hbm, back_hbm,
    dslot, act_s, slope_s, gate_w, up_w, down_w, dgate, dup, back, in_sems, out_sems,
):
    pairs = [(dslot_hbm, dslot)]
    for tile in tiles(FF):
        block = pl.ds(tile.start, TILE)
        pairs += [(down_hbm.at[0, 0].at[block], down_w.at[block])]
    pairs += [(slope_hbm, slope_s), (act_hbm, act_s)]
    for tile in tiles(WIDTH):
        block = pl.ds(tile.start, TILE)
        pairs += [(gate_hbm.at[0, 0].at[block], gate_w.at[block])]
        pairs += [(up_hbm.at[0, 0].at[block], up_w.at[block])]
    copies = start_all(pairs, in_sems)
    writer = Writer(out_sems)
    copies.pop(0).wait()
    dhidden = []
    for tile in tiles(FF):
        copies.pop(0).wait()
        dhidden += [dot(dslot[...], down_w[tile], 1, 1)]
    copies.pop(0).wait()
    copies.pop(0).wait()
    for tile, part in zip(tiles(FF), dhidden):
        dgate[:, tile] = (part * slope_s[:, tile].astype(F32)).astype(BF)
        dup[:, tile] = (part * act_s[:, tile].astype(F32)).astype(BF)
    writer.send(dgate, dgate_hbm)
    writer.send(dup, dup_hbm)
    for copy in copies:
        copy.wait()
    back_tiles(dgate, dup, gate_w, up_w, back, back_hbm, writer)
    writer.finish()


def experts_backward(dslot, act, slope, weights, order):
    small = (SLOTS, FF)
    wide = (SLOTS, WIDTH)
    return run_experts(
        experts_backward_kernel, "experts_backward", [dslot, act, slope, *weights], order,
        [small, small, wide],
        [(wide, BF), (small, BF), (small, BF)] + EXPERT_SCRATCH
        + [(small, BF), (small, BF), (wide, BF)],
        6 + 2 * WIDTH // TILE, 6 * SLOTS * WIDTH * FF,
    )


def expert_grads_kernel(received, dgate_pre, dup_pre, hidden, dslot, packed):
    gate = dot(received[...], dgate_pre[...], 0, 0).astype(BF)
    up = dot(received[...], dup_pre[...], 0, 0).astype(BF)
    down = dot(hidden[...], dslot[...], 0, 0).astype(BF)
    for part in range(DP // 2):
        packed[part, :SHARD, :FF] = gate[part * SHARD : (part + 1) * SHARD]
        packed[part, :SHARD, FF:] = up[part * SHARD : (part + 1) * SHARD]
        packed[part, SHARD:] = down[part * FF // DP : (part + 1) * FF // DP]


def expert_grads(received, dgate_pre, dup_pre, hidden, dslot):
    rows = SHARD + FF // DP
    whole = lambda width: pl.BlockSpec((SLOTS, width), lambda i: (0, 0))
    part = lambda width: pl.BlockSpec((SLOTS, width), lambda i: (0, i))
    return pl.pallas_call(
        expert_grads_kernel,
        grid=(2,),
        out_shape=jax.ShapeDtypeStruct((DP, rows, WIDTH), BF),
        in_specs=[part(WIDTH // 2), whole(FF), whole(FF), part(FF // 2), whole(WIDTH)],
        out_specs=pl.BlockSpec((DP // 2, rows, WIDTH), lambda i: (i, 0, 0)),
        compiler_params=pltpu.CompilerParams(vmem_limit_bytes=VMEM_BYTES),
        cost_estimate=pl.CostEstimate(
            flops=6 * SLOTS * WIDTH * FF, bytes_accessed=14 << 20, transcendentals=0
        ),
        name="expert_grads",
    )(received, dgate_pre, dup_pre, hidden, dslot).reshape(DP * rows, WIDTH)


def seq_tables(counts):
    ends = jnp.cumsum(counts)
    starts = ends - counts
    place = jnp.arange(ROWS, dtype=jnp.int32)
    member = (place[:, None] >= starts[None, :]) & (place[:, None] < ends[None, :])
    index = jnp.arange(counts.shape[0], dtype=jnp.int32)
    segment = jnp.sum(jnp.where(member, index[None, :], 0), axis=1)
    position = place - jnp.sum(jnp.where(member, starts[None, :], 0), axis=1)
    allowed = (segment[:, None] == segment[None, :]) & (place[:, None] >= place[None, :])
    freqs = ROPE_BASE ** (-2.0 * jnp.arange(HEAD // 2, dtype=F32) / HEAD)
    angle = position.astype(F32)[:, None] * freqs[None, :]
    cosine, sine = jnp.cos(angle), jnp.sin(angle)
    return (
        jnp.concatenate([cosine, cosine], axis=1),
        jnp.concatenate([-sine, sine], axis=1),
        allowed.astype(F32),
    )


def slot_matrix(choices, in_parts=False):
    experts = jnp.arange(EXPERTS, dtype=jnp.int32)
    member = jnp.any(choices[:, :, None] == experts[None, None, :], axis=1).astype(BF)
    row = lax.broadcasted_iota(jnp.int32, (ROWS, ROWS), 0)
    column = lax.broadcasted_iota(jnp.int32, (ROWS, ROWS), 1)
    rank = dot((column < row).astype(BF), member).astype(BF)
    slot = jnp.arange(SLOTS, dtype=jnp.int32)[None, :]
    if in_parts:
        later = slot - PART_ENDS[0]
        owner = jnp.where(later < 0, slot // 16, later // 32)
        place = jnp.where(later < 0, slot % 16, 16 + later % 32)
    else:
        owner, place = slot // CAP, slot % CAP
    expand = (owner == experts[:, None]).astype(BF)
    return ((dot(member, expand) > 0.5) & (dot(rank, expand) == place.astype(F32))).astype(BF)


def exchange(rows):
    width = rows.shape[-1]
    moved = lax.all_to_all(
        rows.reshape(EXPERTS, -1, width), "expert", split_axis=0, concat_axis=0, tiled=True
    )
    return moved.reshape(-1, width)


def after(values, order):
    return pl.pallas_call(
        lambda *refs: None,
        out_shape=jax.ShapeDtypeStruct(values.shape, values.dtype),
        in_specs=[ANY, ANY],
        out_specs=ANY,
        input_output_aliases={0: 0},
        name="after",
    )(values, order)


def turn_columns_kernel(me, columns_hbm, turned_hbm, columns, turned, in_sems, out_sems):
    base = me[0] * SHARD // HEAD * HEAD
    pairs = []
    for i in range(3):
        at = pl.multiple_of(base + i * WIDTH, HEAD)
        pairs += [(columns_hbm.at[:, pl.ds(at, TILE)], columns.at[:, pl.ds(i * TILE, TILE)])]
    reader, writer = Reader(in_sems, pairs), Writer(out_sems)
    for i in range(3):
        reader.take()
        turned[i] = columns[:, i * TILE : (i + 1) * TILE].T
        writer.send(turned.at[i], turned_hbm.at[i])
    writer.finish()


def turn_columns(me, columns):
    tokens = DP * ROWS
    return pl.pallas_call(
        turn_columns_kernel,
        out_shape=jax.ShapeDtypeStruct((3, TILE, tokens), BF),
        in_specs=[pl.BlockSpec(memory_space=pltpu.SMEM), ANY],
        out_specs=ANY,
        scratch_shapes=[
            pltpu.VMEM((tokens, 3 * TILE), BF),
            pltpu.VMEM((3, TILE, tokens), BF),
            pltpu.SemaphoreType.DMA((3,)),
            pltpu.SemaphoreType.DMA((3,)),
        ],
        compiler_params=pltpu.CompilerParams(vmem_limit_bytes=VMEM_BYTES),
        cost_estimate=pl.CostEstimate(flops=0, bytes_accessed=4 << 20, transcendentals=0),
        name="turn_columns",
    )(me, columns)


def dense_grads_kernel(me, turned_hbm, factors_hbm, extra, pieces_hbm, turned, factors, total,
                       pieces, in_sems, out_sems):
    start = me[0] * SHARD
    shift = start % HEAD
    base = start - shift
    copies = Writer(out_sems)
    if len(extra.shape) == 3:
        copies.send(extra, pieces_hbm.at[:, :, pl.ds(CHUNK, CHUNK)])
    else:
        for chunk in range(CHUNKS):
            copies.send(extra, pieces_hbm.at[chunk, :, pl.ds(CHUNK, CHUNK)])
    pairs = [(turned_hbm, turned)]
    for at in range(0, PACKED, CHUNK):
        block = (slice(None), pl.ds(at, min(CHUNK, PACKED - at)))
        pairs += [(factors_hbm.at[block], factors.at[block])]
    reader = Reader(in_sems, pairs)
    reader.take()

    def put(chunk, values):
        pieces[chunk] = values.astype(BF)
        copies.send(pieces.at[chunk], pieces_hbm.at[chunk, :, pl.ds(0, CHUNK)])

    for chunk in range(SMALL // CHUNK):
        reader.take()
        total[chunk % 2] = dot(
            turned[0 if chunk < QKV // CHUNK else 1],
            factors[:, chunk * CHUNK : (chunk + 1) * CHUNK],
        )
        put(chunk, total[chunk % 2, pl.ds(pl.multiple_of(shift, 64), SHARD), :])
    reader.take()
    ends = jnp.zeros((ROWS, HEAD), F32)
    for source in range(DP):
        ends += factors[source * ROWS : (source + 1) * ROWS, SMALL:].astype(F32)
    lane = lax.broadcasted_iota(jnp.int32, (ROWS, HEAD), 1)

    def gain_piece(piece):
        held = (lane == piece + GAIN_HIGH) | (lane == piece + GAIN_LOW)
        return jnp.sum(jnp.where(held, ends, 0.0), axis=1, keepdims=True)

    first, second = gain_piece(base // HEAD), gain_piece(base // HEAD + 1)
    gain = jnp.where(
        shift == 0,
        jnp.concatenate([first, second[: SHARD - ROWS]], axis=0),
        jnp.concatenate([first[ROWS // 2 :], second], axis=0),
    )
    gain_high, gain_low = split(gain)
    total[0, :, :HEAD] = dot(turned[2], factors[:, SMALL:])
    router = total[0, pl.ds(pl.multiple_of(shift, 64), SHARD), :HEAD]
    lane = lax.broadcasted_iota(jnp.int32, (SHARD, HEAD), 1)
    router = jnp.where(lane < EXPERTS, router, 0.0)
    router = jnp.where(lane == EXPERTS, gain_high.astype(F32), router)
    router = jnp.where(lane == EXPERTS + 1, gain_low.astype(F32), router)
    put(CHUNKS - 2, jnp.concatenate([router, jnp.zeros_like(router)], axis=1))
    put(CHUNKS - 1, jnp.zeros((SHARD, CHUNK), F32))
    copies.finish()


def dense_grads(me, turned, factors, extra, order):
    tokens = DP * ROWS

    def body(*refs):
        dense_grads_kernel(*refs[:4], *refs[4 + len(order) :])

    return pl.pallas_call(
        body,
        out_shape=jax.ShapeDtypeStruct((CHUNKS, SHARD, 2 * CHUNK), BF),
        in_specs=[pl.BlockSpec(memory_space=pltpu.SMEM)] + [ANY] * (3 + len(order)),
        out_specs=ANY,
        scratch_shapes=[
            pltpu.VMEM((3, TILE, tokens), BF),
            pltpu.VMEM((tokens, PACKED), BF),
            pltpu.VMEM((2, TILE, CHUNK), F32),
            pltpu.VMEM((CHUNKS, SHARD, CHUNK), BF),
            pltpu.SemaphoreType.DMA((1 + CHUNKS,)),
            pltpu.SemaphoreType.DMA((2 * CHUNKS,)),
        ],
        compiler_params=pltpu.CompilerParams(vmem_limit_bytes=VMEM_BYTES),
        cost_estimate=pl.CostEstimate(
            flops=2 * tokens * TILE * PACKED, bytes_accessed=10 << 20, transcendentals=0
        ),
        name="dense_grads",
    )(me, turned, factors, extra, *order)


def to_expert_peers(pieces):
    return lax.all_to_all(pieces, "expert", split_axis=0, concat_axis=0, tiled=True)


def sum_pieces_kernel(pieces_hbm, out_hbm, pieces, out, in_sems, out_sems):
    half = CHUNKS // 2
    pairs = []
    for at in (0, half):
        block = pl.ds(at, half)
        pairs += [(pieces_hbm.at[block, :, pl.ds(0, CHUNK)], pieces.at[block])]
    reader, writer = Reader(in_sems, pairs), Writer(out_sems)
    reader.take()
    total = pieces[0].astype(F32)
    for i in range(1, half):
        total += pieces[i].astype(F32)
    reader.take()
    for i in range(half, CHUNKS):
        total += pieces[i].astype(F32)
    out[...] = total.astype(BF)
    if len(out_hbm.shape) == 3:
        for i in range(CHUNKS):
            writer.send(out, out_hbm.at[i])
    else:
        writer.send(out, out_hbm)
    writer.finish()


def sum_pieces(pieces, copies):
    return pl.pallas_call(
        sum_pieces_kernel,
        out_shape=jax.ShapeDtypeStruct((copies,) * (copies > 1) + (SHARD, CHUNK), BF),
        in_specs=[ANY],
        out_specs=ANY,
        scratch_shapes=[
            pltpu.VMEM((CHUNKS, SHARD, CHUNK), BF),
            pltpu.VMEM((SHARD, CHUNK), BF),
            pltpu.SemaphoreType.DMA((2,)),
            pltpu.SemaphoreType.DMA((CHUNKS,)),
        ],
        compiler_params=pltpu.CompilerParams(vmem_limit_bytes=VMEM_BYTES),
        name="sum_pieces",
    )(pieces)


def finish_kernel(l, at, refs):
    (pieces, w_query, key_projection, value_projection, norm_attn), refs = refs[:5], refs[5:]
    if l == 0:
        ends_above, refs = refs[0], refs[5:]
        (query_hbm, key_hbm, value_hbm, out_hbm, gain_attn, gain_ffn, router) = refs[:7]
        query, key, value, out, sems = refs[7:]
    else:
        query_hbm, key_hbm, value_hbm, out_hbm, ends_out, query, key, value, out, sems = refs
    writer = Writer(sems)
    rows = jnp.zeros((SHARD, 1), F32)
    for chunk in range(SMALL // CHUNK):
        part = pieces[chunk, :, at : at + CHUNK].astype(F32)
        lanes = slice(chunk * CHUNK, (chunk + 1) * CHUNK)
        if chunk < Q_END // CHUNK:
            query[:, lanes] = part
            weight = w_query[l, :, lanes]
        elif chunk == Q_END // CHUNK:
            key[...] = part
            weight = key_projection[l]
            writer.send(query, query_hbm.at[l])
            writer.send(key, key_hbm.at[l])
        elif chunk < QKV // CHUNK:
            value[...] = part
            weight = value_projection[l]
            writer.send(value, value_hbm.at[l])
        else:
            out[:, lanes.start - QKV : lanes.stop - QKV] = part
            continue
        rows += jnp.sum(part * weight.astype(F32), axis=1, keepdims=True)
    writer.send(out, out_hbm.at[l])
    ends = pieces[CHUNKS - 2, :, at : at + HEAD].astype(F32)
    ffn = ends[:, EXPERTS : EXPERTS + 1] + ends[:, EXPERTS + 1 : EXPERTS + 2]
    lane = lax.broadcasted_iota(jnp.int32, (SHARD, HEAD), 1)
    ends = jnp.where(lane == EXPERTS, rows, jnp.where(lane == EXPERTS + 1, ffn, ends))
    if l > 0:
        ends_out[...] = ends
    else:
        for layer, part in enumerate((ends, ends_above[...])):
            wide = jnp.concatenate([part, jnp.zeros((TILE - SHARD, HEAD), F32)], axis=0).T
            router[layer] = wide[:EXPERTS, :SHARD]
            gain = norm_attn[layer : layer + 1].astype(F32)
            gain_attn[layer : layer + 1] = wide[EXPERTS : EXPERTS + 1, :SHARD] / gain
            gain_ffn[layer : layer + 1] = wide[EXPERTS + 1 : EXPERTS + 2, :SHARD]
    writer.finish()


def finish(l, pieces, at, weights, norm_attn, above):
    sd = jax.ShapeDtypeStruct
    vmem = pl.BlockSpec(memory_space=pltpu.VMEM)
    keys = (SHARD, KEY_VALUE_HEADS * HEAD)
    slabs = [(SHARD, Q_END), keys, keys, (SHARD, WIDTH)]
    outs = [sd((LAYERS,) + shape, F32) for shape in slabs]
    if above is None:
        outs += [sd((SHARD, HEAD), F32)]
        ins, in_specs, aliases = [], [], {}
    else:
        outs += [sd((LAYERS, SHARD), F32)] * 2 + [sd((LAYERS, EXPERTS, SHARD), F32)]
        ins, in_specs = [above[4], *above[:4]], [vmem] + [ANY] * 4
        aliases = {6 + i: i for i in range(4)}
    return pl.pallas_call(
        lambda *refs: finish_kernel(l, at, refs),
        out_shape=outs,
        in_specs=[vmem] * 5 + in_specs,
        out_specs=[ANY] * 4 + [vmem] * (len(outs) - 4),
        input_output_aliases=aliases,
        scratch_shapes=[pltpu.VMEM(shape, F32) for shape in slabs]
        + [pltpu.SemaphoreType.DMA((4,))],
        compiler_params=pltpu.CompilerParams(vmem_limit_bytes=VMEM_BYTES),
        name="finish",
    )(pieces, *weights, norm_attn, *ins)


def finish_experts_kernel(shares0, shares1, gate, up, down):
    for l, shares in enumerate((shares0, shares1)):
        gate[l, 0] = shares[:SHARD, :FF].astype(F32)
        up[l, 0] = shares[:SHARD, FF:].astype(F32)
        down[l, 0] = shares[SHARD:].astype(F32)


def finish_experts(shares0, shares1):
    sd = jax.ShapeDtypeStruct
    vmem = pl.BlockSpec(memory_space=pltpu.VMEM)
    return pl.pallas_call(
        finish_experts_kernel,
        out_shape=[
            sd((LAYERS, 1, SHARD, FF), F32), sd((LAYERS, 1, SHARD, FF), F32),
            sd((LAYERS, 1, FF // DP, WIDTH), F32),
        ],
        in_specs=[vmem] * 2,
        out_specs=[vmem] * 3,
        compiler_params=pltpu.CompilerParams(vmem_limit_bytes=VMEM_BYTES),
        name="finish_experts",
    )(shares0, shares1)


def mixed_kernel(x_hbm, high, low, early_hbm, got_hbm, out, x, gates, early, got, late, sems):
    pairs = [
        (high, gates.at[:ROWS]), (low, gates.at[ROWS:]), (x_hbm, x), (early_hbm, early),
        (got_hbm.at[:, :, pl.ds(CHUNK, CHUNK)], got),
    ]
    Reader(sems, pairs).take(len(pairs))
    for expert in range(EXPERTS):
        rows = slice(expert * PART_ROWS[1], (expert + 1) * PART_ROWS[1])
        for tile in tiles(WIDTH):
            at = tile.start // TILE * PART_ROWS[1]
            late[rows, tile] = got[expert, at : at + PART_ROWS[1]]
    for tile in tiles(WIDTH):
        both = dot(gates[:, : PART_ENDS[0]], early[:, tile])
        both += dot(gates[:, PART_ENDS[0] :], late[:, tile])
        out[:, tile] = (x[:, tile] + both[:ROWS] + both[ROWS:]).astype(BF)


def mixed_rows(x, high, low, early, got):
    return pl.pallas_call(
        mixed_kernel,
        out_shape=jax.ShapeDtypeStruct(TOKENS, BF),
        in_specs=[ANY] * 5,
        out_specs=pl.BlockSpec(memory_space=pltpu.VMEM),
        scratch_shapes=[
            pltpu.VMEM(TOKENS, F32),
            pltpu.VMEM((2 * ROWS, SLOTS), BF),
            pltpu.VMEM((PART_ENDS[0], WIDTH), BF),
            pltpu.VMEM((EXPERTS, SHARD, CHUNK), BF),
            pltpu.VMEM((SLOTS - PART_ENDS[0], WIDTH), BF),
            pltpu.SemaphoreType.DMA((5,)),
        ],
        compiler_params=pltpu.CompilerParams(vmem_limit_bytes=VMEM_BYTES),
        name="mixed",
    )(x, high, low, early, got)


def local(
    tokens, cotangent, lengths, routes, norm_attn, w_query, key_projection, value_projection,
    w_out, norm_ffn, w_router, w_gate, w_up, w_down,
):
    me_dp = lax.axis_index("dp").astype(jnp.int32).reshape(1)
    me_expert = lax.axis_index("expert").astype(jnp.int32).reshape(1)
    tables = seq_tables(lengths[0])
    give = [slot_matrix(routes[l]) for l in range(LAYERS)]
    take = [g.T for g in give]
    give_parts = slot_matrix(routes[1], True)
    experts = (w_gate, w_up, w_down)

    def gather(values):
        return lax.all_gather(values, "dp", axis=0, tiled=True)

    w = [
        gather(
            jnp.concatenate(
                [w_query[l], key_projection[l], value_projection[l], w_out[l], w_router[l],
                 norm_attn[l][:, None], norm_ffn[l][:, None],
                 jnp.zeros((SHARD, HEAD - EXPERTS - 2), BF)],
                axis=1,
            )
        )
        for l in range(LAYERS)
    ]

    dx_rows = exchange(dot(take[1], cotangent).astype(BF))

    kept0 = attn_forward(
        tokens, None, w[0], tables, take[0], give[0],
        (dx_rows, give[1], give_parts, me_dp, me_expert),
    )
    received0 = exchange(kept0["rows"])
    act0, slope0, hidden0, out0 = experts_forward(received0, experts, ())
    returned0 = exchange(out0)
    columns0 = gather(kept0["columns"])

    kept1 = attn_forward(
        kept0["after"], (kept0["high"], kept0["low"], returned0), w[1], tables, take[1],
        give_parts, (),
    )
    received1 = exchange(kept1["rows"])
    columns1 = gather(kept1["columns"])
    hidden1, early1, late1, dslot1, dgate1, dup1, back1 = experts_both(
        me_expert, received1, dx_rows, w[1], experts, ()
    )
    back1 = exchange(back1)
    grads1 = expert_grads(received1, dgate1, dup1, hidden1, dslot1)
    turned0, turned1 = turn_columns(me_dp, columns0), turn_columns(me_dp, columns1)
    early1 = exchange(early1)

    dx0, packed1, rows0 = attn_backward(
        cotangent, back1, kept1["x"], kept1, w[1], tables, give[1], (take[0], kept0["router"]),
        None, (grads1, turned0, turned1),
    )
    dslot0 = exchange(rows0)
    factors1 = gather(packed1)
    shares1 = lax.psum_scatter(after(grads1, packed1), "dp", scatter_dimension=0, tiled=True)
    dgate0, dup0, back0 = experts_backward(dslot0, act0, slope0, experts, ())
    back0 = exchange(back0)
    grads0 = expert_grads(received0, dgate0, dup0, hidden0, dslot0)
    pieces1 = dense_grads(me_dp, turned1, factors1, late1, (early1,))
    grad_tokens, packed0 = attn_backward(
        dx0, back0, tokens, kept0, w[0], tables, give[0], None, returned0,
        (shares1, grads0, pieces1),
    )
    factors0 = gather(packed0)
    got = to_expert_peers(pieces1)
    summed1 = sum_pieces(got, 1)
    shares0 = lax.psum_scatter(after(grads0, summed1), "dp", scatter_dimension=0, tiled=True)
    mixed = mixed_rows(kept1["after"], kept1["high"], kept1["low"], early1, got)
    pieces = to_expert_peers(dense_grads(me_dp, turned0, factors0, summed1, ()))
    pieces0 = to_expert_peers(sum_pieces(pieces, CHUNKS))

    dense = (w_query, key_projection, value_projection)
    above = finish(1, pieces, CHUNK, dense, norm_attn, None)
    query, key, value, out, gain_attn, gain_ffn, router = finish(
        0, pieces0, 0, dense, norm_attn, above
    )
    gate, up, down = finish_experts(shares0, shares1)
    return (
        mixed, grad_tokens, gain_attn, query, key, value, out, gain_ffn,
        router.transpose(0, 2, 1), gate, up, down,
    )


def solution(mesh):
    placed = (
        P(("dp", "expert"), None),
        P(("dp", "expert"), None),
        P(("dp", "expert"), None),
        P(None, ("dp", "expert"), None),
        P(None, "dp"),
        P(None, "dp", None),
        P(None, "dp", None),
        P(None, "dp", None),
        P(None, "dp", None),
        P(None, "dp"),
        P(None, "dp", None),
        P(None, "expert", None, None),
        P(None, "expert", None, None),
        P(None, "expert", None, None),
    )
    return jax.shard_map(
        local,
        mesh=mesh,
        in_specs=placed,
        out_specs=(
            P(("dp", "expert"), None),
            P(("dp", "expert"), None),
            P(None, "dp"),
            P(None, "dp", None),
            P(None, "dp", None),
            P(None, "dp", None),
            P(None, "dp", None),
            P(None, "dp"),
            P(None, "dp", None),
            P(None, "expert", "dp", None),
            P(None, "expert", "dp", None),
            P(None, "expert", "dp", None),
        ),
        check_vma=False,
    )
```

```python
import jax
import jax.numpy as jnp
from jax import lax
from jax.experimental import pallas as pl
from jax.experimental.pallas import tpu as pltpu
from jax.sharding import PartitionSpec as P

QUERY_HEADS = 12
KEY_VALUE_HEADS = 2
GROUPS = QUERY_HEADS // KEY_VALUE_HEADS
HEAD = 128
LAYERS = 2
WIDTH = 1536
FF = 768
ROWS = 128
EXPERTS = 16
CAP = 48
SLOTS = EXPERTS * CAP
DP = 8
SHARD = WIDTH // DP
Q_END = QUERY_HEADS * HEAD
K_END = Q_END + KEY_VALUE_HEADS * HEAD
QKV = K_END + KEY_VALUE_HEADS * HEAD
SMALL = QKV + WIDTH
PACKED = SMALL + HEAD
GAIN_ATTN, GAIN_FFN = 16, 17
GAIN_HIGH, GAIN_LOW = 16, 32
PIECES = WIDTH // HEAD
TILE = 256
PART_ROWS = (16, 32)
PART_ENDS = (EXPERTS * 16, SLOTS)
CHUNKS, CHUNK = 16, 256
COLUMNS = 3 * WIDTH
EPSILON = 1e-06
ROPE_BASE = 1000000.0
SCALE = HEAD ** (-0.5)
GELU_A = 0.7978845608028654
GELU_B = 0.044715
VMEM_BYTES = 56 << 20
BF = jnp.bfloat16
F32 = jnp.float32
ANY = pl.BlockSpec(memory_space=pl.ANY)


def dot(left, right, left_dim=1, right_dim=0):
    return lax.dot_general(
        left, right, (((left_dim,), (right_dim,)), ((), ())), preferred_element_type=F32
    )


def split(values):
    high = values.astype(BF)
    return high, (values - high.astype(F32)).astype(BF)


def unit(values):
    return lax.rsqrt(jnp.mean(values * values, axis=-1, keepdims=True) + EPSILON)


def turn(values, cosine, sine):
    return values * cosine + pltpu.roll(values, HEAD // 2, 1) * sine


def expert_lanes(transposed=False, in_parts=False):
    shape = (SLOTS, HEAD) if transposed else (HEAD, SLOTS)
    slot = lax.broadcasted_iota(jnp.int32, shape, 0 if transposed else 1)
    expert = lax.broadcasted_iota(jnp.int32, shape, 1 if transposed else 0)
    if in_parts:
        first = (slot >> 4) == expert
        held = first | ((slot >= PART_ENDS[0]) & (((slot - PART_ENDS[0]) >> 5) == expert))
    else:
        held = (slot >= expert * CAP) & (slot < expert * CAP + CAP)
    return held.astype(F32).astype(BF)


def gain_rows(small):
    row = lax.broadcasted_iota(jnp.int32, (8, HEAD), 0)
    lane = lax.broadcasted_iota(jnp.int32, (8, HEAD), 1)
    pick = ((lane == row + GAIN_ATTN) & (row < 2)).astype(F32).astype(BF)
    rows = dot(pick, small, 1, 1)
    return rows[0:1], rows[1:2]


def router_probs(rows, small):
    logits = dot(rows, small)
    lane = lax.broadcasted_iota(jnp.int32, logits.shape, 1)
    logits = jnp.where(lane < EXPERTS, logits, -1e30)
    powers = jnp.exp(logits - jnp.max(logits, axis=-1, keepdims=True))
    return powers / jnp.sum(powers, axis=-1, keepdims=True)


def start_all(pairs, sems):
    copies = [
        pltpu.make_async_copy(source, target, sems.at[i]) for i, (source, target) in enumerate(pairs)
    ]
    for copy in copies:
        copy.start()
    return copies


class Writer:
    def __init__(self, sems):
        self.sems, self.copies = sems, []

    def send(self, source, target):
        copy = pltpu.make_async_copy(source, target, self.sems.at[len(self.copies)])
        copy.start()
        self.copies.append(copy)

    def finish(self):
        for copy in self.copies:
            copy.wait()


class Reader:
    def __init__(self, sems, pairs):
        self.copies = start_all(pairs, sems)

    def take(self, count=1):
        for _ in range(count):
            self.copies.pop(0).wait()


def tiles(width):
    return [slice(at, at + TILE) for at in range(0, width, TILE)]


def small_block(w_hbm, w):
    last = w_hbm.shape[1] - HEAD
    return (w_hbm.at[:, pl.ds(last, HEAD)], w.at[:, pl.ds(SMALL, HEAD)])


def column_block(w_hbm, w, at):
    return (w_hbm.at[:, pl.ds(at, TILE)], w.at[:, pl.ds(at, TILE)])


def ring_blocks(me, blocks, w):
    pairs = []
    for core in range(2):
        start = me if core == 0 else me + 1 - 2 * (me % 2)
        for block, step in enumerate((0, DP - 2, 2, 4, 4)):
            ref = blocks[core * 5 + block]
            at = (start + step) % DP * SHARD + (SHARD // 2 if block == 4 else 0)
            at = pl.multiple_of(at, SHARD // 2)
            pairs += [(ref, w.at[pl.ds(at, ref.shape[0]), pl.ds(QKV, WIDTH)])]
    return pairs


def attn_forward_kernel(first, ins, outs, scratch):
    (x_hbm, w_hbm, cosine_hbm, sine_hbm, allowed_hbm, take_hbm, give_hbm), ins = ins[:7], ins[7:]
    (columns_hbm, qrot_hbm, krot_hbm, value_hbm, probs_hbm, after_hbm, router_hbm, high_hbm, low_hbm,
     rows_hbm), outs = outs[:10], outs[10:]
    (x_in, w, cosine, sine, allowed, take, give, returned, gates, x, columns, qrot, krot, value, probs,
     after, router, high, low, rows, in_sems, out_sems) = scratch
    acts = columns.at[:, :WIDTH]
    attended = columns.at[:, WIDTH : 2 * WIDTH]
    acts_two = columns.at[:, 2 * WIDTH :]
    pairs = []
    if first:
        out_pairs = ring_blocks(ins[0][0], ins[1:], w)
    else:
        out_pairs = [column_block(w_hbm, w, at) for at in range(QKV, SMALL, TILE)]
        high_below, low_below, returned_hbm = ins
        pairs += [(high_below, gates.at[:ROWS]), (low_below, gates.at[ROWS:])]
        pairs += [(returned_hbm, returned)]
    pairs += [(x_hbm, x_in), small_block(w_hbm, w)]
    pairs += [column_block(w_hbm, w, at) for at in range(0, QKV, TILE)]
    pairs += [(cosine_hbm, cosine), (sine_hbm, sine), (allowed_hbm, allowed)]
    pairs += out_pairs + [(take_hbm, take), (give_hbm, give)]
    reader, writer = Reader(in_sems, pairs), Writer(out_sems)
    if first:
        reader.take()
        x[...] = x_in[...].astype(F32)
    else:
        reader.take(4)
        for tile in tiles(WIDTH):
            both = dot(gates[...], returned[:, tile])
            x[:, tile] = x_in[:, tile] + both[:ROWS] + both[ROWS:]
        writer.send(x, outs[0])
    reader.take()
    small = w[:, SMALL:]
    gain_attn, gain_ffn = gain_rows(small)
    total = x[...]
    acts[...] = (total * unit(total) * gain_attn).astype(BF)
    wide = []
    for tile in tiles(QKV):
        reader.take()
        wide += [dot(acts[...], w[:, tile])]
    reader.take(3)
    for tile in range(QKV // TILE):
        for half in range(TILE // HEAD):
            head = tile * (TILE // HEAD) + half
            part = wide[tile][:, half * HEAD : (half + 1) * HEAD]
            if head < QUERY_HEADS:
                qrot[head] = turn(part, cosine[...], sine[...]).astype(BF)
            elif head < QUERY_HEADS + KEY_VALUE_HEADS:
                krot[head - QUERY_HEADS] = turn(part, cosine[...], sine[...]).astype(BF)
            else:
                value[head - QUERY_HEADS - KEY_VALUE_HEADS] = part.astype(BF)
    writer.send(qrot, qrot_hbm)
    writer.send(krot, krot_hbm)
    writer.send(value, value_hbm)
    open_scores = (allowed[...] > 0.5)[None]
    for k in range(KEY_VALUE_HEADS):
        heads = slice(k * GROUPS, (k + 1) * GROUPS)
        scores = dot(qrot[heads].reshape(GROUPS * ROWS, HEAD), krot[k], 1, 1) * SCALE
        scores = jnp.where(open_scores, scores.reshape(GROUPS, ROWS, ROWS), -1000000000.0)
        powers = jnp.exp(scores - jnp.max(scores, axis=-1, keepdims=True))
        shares = powers / jnp.sum(powers, axis=-1, keepdims=True)
        probs[heads] = shares
        mixed = dot(shares.astype(BF).reshape(GROUPS * ROWS, ROWS), value[k]).astype(BF)
        for group in range(GROUPS):
            at = (k * GROUPS + group) * HEAD
            attended[:, at : at + HEAD] = mixed[group * ROWS : (group + 1) * ROWS]
    writer.send(probs, probs_hbm)
    if first:
        reader.take(len(out_pairs))
    for tile in tiles(WIDTH):
        if not first:
            reader.take()
        after[:, tile] = x[:, tile] + dot(
            attended[...], w[:, QKV + tile.start : QKV + tile.stop]
        )
    writer.send(after, after_hbm)
    total = after[...]
    acts_two[...] = (total * unit(total) * gain_ffn).astype(BF)
    writer.send(columns, columns_hbm)
    reader.take(2)
    for tile in tiles(WIDTH):
        rows[:, tile] = dot(take[...], acts_two[:, tile]).astype(BF)
        writer.send(rows.at[:, tile], rows_hbm.at[:, tile])
    shares = router_probs(acts_two[...], small)
    router[...] = shares
    spread = expert_lanes(in_parts=not first)
    both = dot(jnp.concatenate(split(shares), axis=0), spread).astype(BF)
    high[...] = both[:ROWS] * give[...]
    low[...] = both[ROWS:] * give[...]
    writer.send(router, router_hbm)
    writer.send(high, high_hbm)
    writer.send(low, low_hbm)
    writer.finish()


HEADS = (QUERY_HEADS, ROWS, HEAD)
KEYS = (KEY_VALUE_HEADS, ROWS, HEAD)
TABLE = (ROWS, HEAD)
TOKENS = (ROWS, WIDTH)
WIDE = (SLOTS, WIDTH)


def specs_of(ins):
    return [pl.BlockSpec(memory_space=pltpu.SMEM if a.dtype == jnp.int32 else pl.ANY) for a in ins]


def run_attn(kernel, name, ins, order, outs, scratch, in_copies, out_copies, vmem):
    sd = jax.ShapeDtypeStruct

    def body(*refs):
        first_out = len(ins) + len(order)
        first_scratch = first_out + len(outs)
        kernel(refs[: len(ins)], refs[first_out:first_scratch], refs[first_scratch:])

    return pl.pallas_call(
        body,
        out_shape=[sd(shape, kind) for shape, kind in outs],
        in_specs=specs_of(ins) + [ANY] * len(order),
        out_specs=[ANY] * len(outs),
        scratch_shapes=[pltpu.VMEM(shape, kind) for shape, kind in scratch]
        + [pltpu.SemaphoreType.DMA((in_copies,)), pltpu.SemaphoreType.DMA((out_copies,))],
        compiler_params=pltpu.CompilerParams(vmem_limit_bytes=vmem),
        cost_estimate=pl.CostEstimate(
            flops=2 * ROWS * WIDTH * PACKED, bytes_accessed=20 << 20, transcendentals=200000
        ),
        name=name,
    )(*ins, *order)


def attn_forward(x, combine, w, ring, tables, take, give, order):
    first = combine is None
    outs = [
        ((ROWS, COLUMNS), BF), (HEADS, BF), (KEYS, BF), (KEYS, BF), ((QUERY_HEADS, ROWS, ROWS), F32),
        (TOKENS, F32), (TABLE, F32), ((ROWS, SLOTS), BF), ((ROWS, SLOTS), BF), (WIDE, BF),
    ]
    names = [
        "columns", "qrot", "krot", "value", "probs", "after", "router", "high", "low", "rows"
    ]
    scratch = [(TOKENS, x.dtype), ((WIDTH, PACKED), BF)] + [(TABLE, F32)] * 3
    scratch += [((SLOTS, ROWS), BF), ((ROWS, SLOTS), BF)]
    scratch += [((16, HEAD), BF)] * 2 if first else [(WIDE, BF), ((2 * ROWS, SLOTS), BF)]
    scratch += [(TOKENS, F32)] + outs
    ins = [x, w, *tables, take, give]
    if first:
        ins += ring
    else:
        high, low, returned = combine
        ins += [high, low, returned]
        outs = outs + [(TOKENS, F32)]
        names += ["x"]
    result = run_attn(
        lambda *refs: attn_forward_kernel(first, *refs), "attn_forward", ins, order, outs, scratch,
        20 + QKV // TILE, 20, VMEM_BYTES,
    )
    return dict(zip(names, result))


def norm_back(grad, gain, values):
    scale = unit(values)
    inner = grad * gain
    return scale * inner - values * (scale * scale * scale) * jnp.mean(
        inner * values, axis=-1, keepdims=True
    )


def attn_backward_kernel(last, ins, outs, scratch):
    (dx_hbm, back_hbm, w_hbm, cosine_hbm, sine_hbm, give_hbm, router_hbm, after_hbm, x_hbm, probs_hbm,
     qrot_hbm, krot_hbm, value_hbm), ins = ins[:13], ins[13:]
    (dx_in, back, w, cosine, sine, give, router, after, x_in, probs, qrot, krot, value, wide_in,
     small_in, datt, dx_out, packed), scratch = scratch[:18], scratch[18:]
    if last:
        rows, scratch = scratch[0], scratch[1:]
    in_sems, out_sems = scratch
    pairs = [(give_hbm, give), (back_hbm, back), (router_hbm, router), (dx_hbm, dx_in)]
    if not last:
        pairs += [(ins[0], wide_in)]
    pairs += [small_block(w_hbm, w), (after_hbm, after)]
    if last:
        for at in range(0, WIDTH, TILE):
            block = (pl.ds(at, TILE), pl.ds(QKV, WIDTH))
            pairs += [(w_hbm.at[block], w.at[block])]
    else:
        pairs += ring_blocks(ins[1][0], ins[2:], w)
    pairs += [(probs_hbm, probs), (value_hbm, value), (krot_hbm, krot), (qrot_hbm, qrot)]
    pairs += [(cosine_hbm, cosine), (sine_hbm, sine)]
    for at in range(0, WIDTH, TILE):
        block = (pl.ds(at, TILE), pl.ds(0, QKV))
        pairs += [(w_hbm.at[block], w.at[block])]
    pairs += [(x_hbm, x_in)]
    if last:
        pairs += [(ins[0], wide_in), (ins[1], small_in)]
    reader, writer = Reader(in_sems, pairs), Writer(out_sems)
    reader.take(4)
    dx = dx_in[...].astype(F32)
    spread = expert_lanes(True)
    if last:
        dgate = back[:, WIDTH:].astype(F32)
        drouter = dot(give[...], (dgate[:, 0:1] * spread).astype(BF))
        drouter += dot(give[...], (dgate[:, 1:2] * spread).astype(BF))
    else:
        reader.take()
        dgate = dot(dx.astype(BF), wide_in[...], 1, 1) * give[...]
        both = dot(jnp.concatenate(split(dgate), axis=0), spread)
        drouter = both[:ROWS] + both[ROWS:]
    reader.take(2)
    small = w[:, SMALL:]
    gain_attn, gain_ffn = gain_rows(small)
    shares = router[...]
    dlogits = shares * (drouter - jnp.sum(drouter * shares, axis=-1, keepdims=True))
    dlogits = dlogits.astype(BF)
    dacts_two = dot(dlogits, small, 1, 1) + dot(give[...], back[:, :WIDTH])
    total = after[...]
    scale = unit(total)
    dafter = dx + norm_back(dacts_two, gain_ffn, total)
    dx_out[...] = dafter
    packed[:, QKV:SMALL] = dafter.astype(BF)
    dgain = jnp.sum(dacts_two * total * scale, axis=0, keepdims=True)
    dgain_high, dgain_low = split(dgain)
    pieces = [jnp.zeros((GAIN_HIGH, HEAD), F32)]
    for part in (dgain_high.astype(F32), dgain_low.astype(F32)):
        pieces += [part[:, at : at + HEAD] for at in range(0, WIDTH, HEAD)]
        pieces += [jnp.zeros((GAIN_LOW - GAIN_HIGH - PIECES, HEAD), F32)]
    pieces += [jnp.zeros((HEAD - 2 * GAIN_LOW + GAIN_HIGH, HEAD), F32)]
    packed[:, SMALL:] = (dlogits.astype(F32) + jnp.concatenate(pieces, axis=0).T).astype(BF)
    writer.send(packed.at[:, QKV:], outs[1].at[:, QKV:])
    if not last:
        reader.take(len(ins) - 2)
    for tile in tiles(WIDTH):
        if last:
            reader.take()
        wide = dot(packed[:, QKV:SMALL], w[tile, QKV:SMALL], 1, 1).astype(BF)
        for half in range(TILE // HEAD):
            datt[tile.start // HEAD + half] = wide[:, half * HEAD : (half + 1) * HEAD]
    reader.take(6)
    for k in range(KEY_VALUE_HEADS):
        heads = slice(k * GROUPS, (k + 1) * GROUPS)
        datt_k = datt[heads].reshape(GROUPS * ROWS, HEAD)
        p = probs[heads].reshape(GROUPS * ROWS, ROWS)
        dprobs = dot(datt_k, value[k], 1, 1)
        dvalue = dot(p.astype(BF), datt_k, 0, 0)
        dscores = (p * (dprobs - jnp.sum(dprobs * p, axis=-1, keepdims=True))).astype(BF)
        dqrot = dot(dscores, krot[k]) * SCALE
        dkrot = dot(dscores, qrot[heads].reshape(GROUPS * ROWS, HEAD), 0, 0) * SCALE
        for group in range(GROUPS):
            at = (k * GROUPS + group) * HEAD
            part = dqrot[group * ROWS : (group + 1) * ROWS]
            packed[:, at : at + HEAD] = turn(part, cosine[...], -sine[...]).astype(BF)
        at = Q_END + k * HEAD
        packed[:, at : at + HEAD] = turn(dkrot, cosine[...], -sine[...]).astype(BF)
        at = K_END + k * HEAD
        packed[:, at : at + HEAD] = dvalue.astype(BF)
    writer.send(packed.at[:, :QKV], outs[1].at[:, :QKV])
    parts = []
    for tile in tiles(WIDTH):
        reader.take()
        parts += [dot(packed[:, :QKV], w[tile, :QKV], 1, 1)]
    dacts = jnp.concatenate(parts, axis=1)
    reader.take()
    dx = dx_out[...] + norm_back(dacts, gain_attn, x_in[...].astype(F32))
    dx_out[...] = dx
    writer.send(dx_out, outs[0])
    if last:
        reader.take(2)
        dx_low = dx.astype(BF)
        both = dot(spread, jnp.concatenate(split(small_in[...]), axis=0), 1, 1).astype(BF)
        gates = jnp.concatenate([both[:, :ROWS] * wide_in[...], both[:, ROWS:] * wide_in[...]], axis=1)
        twice = jnp.concatenate([dx_low, dx_low], axis=0)
        for tile in tiles(WIDTH):
            rows[:, tile] = dot(gates, twice[:, tile]).astype(BF)
            writer.send(rows.at[:, tile], outs[2].at[:, tile])
    writer.finish()


def attn_backward(dx, back, x, kept, w, ring, tables, give, below, returned, order):
    last = below is not None
    outs = [(TOKENS, F32), ((ROWS, PACKED), BF)]
    if last:
        outs += [(WIDE, BF)]
    ins = [dx, back, w, tables[0], tables[1], give, kept["router"], kept["after"], x]
    ins += [kept[n] for n in ("probs", "qrot", "krot", "value")]
    ins += list(below) if last else [returned, *ring]
    scratch = [
        (TOKENS, dx.dtype), (back.shape, BF), ((WIDTH, PACKED), BF), (TABLE, F32), (TABLE, F32),
        ((ROWS, SLOTS), BF), (TABLE, F32), (TOKENS, F32), (TOKENS, x.dtype),
        ((QUERY_HEADS, ROWS, ROWS), F32), (HEADS, BF), (KEYS, BF), (KEYS, BF),
        ((SLOTS, ROWS), BF) if last else (WIDE, BF), (TABLE, F32), (HEADS, BF),
    ] + outs
    return run_attn(
        lambda *refs: attn_backward_kernel(last, *refs), "attn_backward", ins, order, outs, scratch,
        24 + WIDTH // TILE, 12, VMEM_BYTES,
    )


def gelu_parts(gate):
    square = gate * gate
    bend = jnp.tanh(GELU_A * gate * (1.0 + GELU_B * square))
    return bend, square


def gelu(gate):
    bend, _ = gelu_parts(gate)
    return 0.5 * gate * (1.0 + bend)


def gelu_both(gate):
    bend, square = gelu_parts(gate)
    slope = 0.5 * (1.0 + bend) + 0.5 * gate * (1.0 - bend * bend) * GELU_A * (
        1.0 + 3.0 * GELU_B * square
    )
    return 0.5 * gate * (1.0 + bend), slope


def weight_pairs(l, gate_hbm, up_hbm, down_hbm, gate_w, up_w, down_w):
    gate_up = []
    for at in range(0, FF, TILE):
        block = (slice(None), pl.ds(at, TILE))
        gate_up += [(gate_hbm.at[l, 0].at[block], gate_w.at[block])]
        gate_up += [(up_hbm.at[l, 0].at[block], up_w.at[block])]
    down = [(down_hbm.at[l, 0], down_w)]
    return gate_up, down


def run_experts(kernel, name, ins, order, outs, scratch, in_copies, flops):
    sd = jax.ShapeDtypeStruct
    count = len(ins) + len(order)

    def body(*refs):
        kernel(*refs[: len(ins)], *refs[count:])

    return pl.pallas_call(
        body,
        out_shape=[sd(shape, BF) for shape in outs],
        in_specs=specs_of(ins) + [ANY] * len(order),
        out_specs=[ANY] * len(outs),
        scratch_shapes=[pltpu.VMEM(shape, kind) for shape, kind in scratch]
        + [pltpu.SemaphoreType.DMA((in_copies,)), pltpu.SemaphoreType.DMA((40,))],
        compiler_params=pltpu.CompilerParams(vmem_limit_bytes=VMEM_BYTES),
        cost_estimate=pl.CostEstimate(
            flops=flops, bytes_accessed=20 << 20, transcendentals=SLOTS * FF
        ),
        name=name,
    )(*ins, *order)


def experts_forward_kernel(
    received_hbm, gate_hbm, up_hbm, down_hbm, act_hbm, slope_hbm, hidden_hbm, out_hbm,
    received, gate_w, up_w, down_w, act_s, slope_s, hidden, out, in_sems, out_sems,
):
    gate_up, down = weight_pairs(0, gate_hbm, up_hbm, down_hbm, gate_w, up_w, down_w)
    copies = start_all([(received_hbm, received)] + gate_up + down, in_sems)
    writer = Writer(out_sems)
    copies.pop(0).wait()
    for tile in tiles(FF):
        copies.pop(0).wait()
        copies.pop(0).wait()
        gate = dot(received[...], gate_w[:, tile])
        up = dot(received[...], up_w[:, tile])
        act, slope = gelu_both(gate)
        act_s[:, tile] = act.astype(BF)
        slope_s[:, tile] = (slope * up).astype(BF)
        hidden[:, tile] = (act * up).astype(BF)
    copies.pop(0).wait()
    writer.send(act_s, act_hbm)
    writer.send(slope_s, slope_hbm)
    writer.send(hidden, hidden_hbm)
    for tile in tiles(WIDTH):
        out[:, tile] = dot(hidden[...], down_w[:, tile]).astype(BF)
        writer.send(out.at[:, tile], out_hbm.at[:, tile])
    writer.finish()


EXPERT_SCRATCH = [((WIDTH, FF), BF), ((WIDTH, FF), BF), ((FF, WIDTH), BF)]


def experts_forward(received, weights, order):
    small = (SLOTS, FF)
    wide = (SLOTS, WIDTH)
    return run_experts(
        experts_forward_kernel, "experts_forward", [received, *weights], order,
        [small, small, small, wide],
        [(wide, BF)] + EXPERT_SCRATCH + [(small, BF)] * 3 + [(wide, BF)],
        8, 6 * SLOTS * WIDTH * FF,
    )


def back_tiles(dgate, dup, gate_w, up_w, back, back_hbm, writer):
    for tile in tiles(WIDTH):
        back[:, tile] = (
            dot(dgate[...], gate_w[tile], 1, 1) + dot(dup[...], up_w[tile], 1, 1)
        ).astype(BF)
        writer.send(back.at[:, tile], back_hbm.at[:, tile])


def experts_both_kernel(
    me, received_hbm, dx_hbm, w_hbm, gate_hbm, up_hbm, down_hbm,
    hidden_hbm, early_hbm, late_hbm, dslot_hbm, dgate_hbm, dup_hbm, back_hbm,
    received, dx, small, gate_w, up_w, down_w, act_s, slope_s, hidden, early, late, dslot, dgate, dup,
    back, in_sems, out_sems,
):
    gate_up, down = weight_pairs(1, gate_hbm, up_hbm, down_hbm, gate_w, up_w, down_w)
    pairs = [(received_hbm, received)] + gate_up
    pairs += [(w_hbm.at[:, pl.ds(SMALL, HEAD)], small), (dx_hbm, dx)] + down
    copies = start_all(pairs, in_sems)
    writer = Writer(out_sems)
    copies.pop(0).wait()
    for tile in tiles(FF):
        copies.pop(0).wait()
        copies.pop(0).wait()
        gate = dot(received[...], gate_w[:, tile])
        up = dot(received[...], up_w[:, tile])
        act, slope = gelu_both(gate)
        act_s[:, tile] = act
        slope_s[:, tile] = slope * up
        hidden[:, tile] = (act * up).astype(BF)
    for copy in copies:
        copy.wait()
    writer.send(hidden, hidden_hbm)
    shares = router_probs(received[...], small[...])
    lane = lax.broadcasted_iota(jnp.int32, shares.shape, 1)
    weight = jnp.sum(jnp.where(lane == me[0], shares, 0.0), axis=-1, keepdims=True)
    total = jnp.zeros((SLOTS, 1), F32)
    for tile in tiles(WIDTH):
        part = dot(hidden[...], down_w[:, tile]).astype(BF)
        for expert in range(EXPERTS):
            at = expert * CAP
            early[expert, :, tile] = part[at : at + PART_ROWS[0]]
            row = tile.start // TILE * PART_ROWS[1]
            late[expert, row : row + PART_ROWS[1]] = part[at + PART_ROWS[0] : at + CAP]
        wide = dx[:, tile].astype(F32)
        total += jnp.sum(wide * part.astype(F32), axis=-1, keepdims=True)
        dslot[:, tile] = (weight * wide).astype(BF)
    writer.send(early, early_hbm)
    writer.send(late, late_hbm)
    writer.send(dslot, dslot_hbm)
    high, low = split(total)
    back[:, WIDTH:] = jnp.where(
        lane == 0, high.astype(F32), jnp.where(lane == 1, low.astype(F32), 0.0)
    ).astype(BF)
    writer.send(back.at[:, WIDTH:], back_hbm.at[:, WIDTH:])
    for tile in tiles(FF):
        dhidden = dot(dslot[...], down_w[tile], 1, 1)
        dgate[:, tile] = (dhidden * slope_s[:, tile]).astype(BF)
        dup[:, tile] = (dhidden * act_s[:, tile]).astype(BF)
    writer.send(dgate, dgate_hbm)
    writer.send(dup, dup_hbm)
    back_tiles(dgate, dup, gate_w, up_w, back, back_hbm, writer)
    writer.finish()


def experts_both(me, received, dx, w, weights, order):
    small = (SLOTS, FF)
    wide = (SLOTS, WIDTH)
    early = (EXPERTS, PART_ROWS[0], WIDTH)
    late = (EXPERTS, SHARD, CHUNK)
    back = (SLOTS, WIDTH + HEAD)
    return run_experts(
        experts_both_kernel, "experts_both", [me, received, dx, w, *weights], order,
        [small, early, late, wide, small, small, back],
        [(wide, BF), (wide, BF), ((WIDTH, HEAD), BF)] + EXPERT_SCRATCH
        + [(small, F32), (small, F32), (small, BF), (early, BF), (late, BF), (wide, BF),
           (small, BF), (small, BF), (back, BF)],
        10, 12 * SLOTS * WIDTH * FF,
    )


def experts_backward_kernel(
    dslot_hbm, act_hbm, slope_hbm, gate_hbm, up_hbm, down_hbm, dgate_hbm, dup_hbm, back_hbm,
    dslot, act_s, slope_s, gate_w, up_w, down_w, dgate, dup, back, in_sems, out_sems,
):
    pairs = [(dslot_hbm, dslot)]
    for tile in tiles(FF):
        block = pl.ds(tile.start, TILE)
        pairs += [(down_hbm.at[0, 0].at[block], down_w.at[block])]
    pairs += [(slope_hbm, slope_s), (act_hbm, act_s)]
    for tile in tiles(WIDTH):
        block = pl.ds(tile.start, TILE)
        pairs += [(gate_hbm.at[0, 0].at[block], gate_w.at[block])]
        pairs += [(up_hbm.at[0, 0].at[block], up_w.at[block])]
    copies = start_all(pairs, in_sems)
    writer = Writer(out_sems)
    copies.pop(0).wait()
    dhidden = []
    for tile in tiles(FF):
        copies.pop(0).wait()
        dhidden += [dot(dslot[...], down_w[tile], 1, 1)]
    copies.pop(0).wait()
    copies.pop(0).wait()
    for tile, part in zip(tiles(FF), dhidden):
        dgate[:, tile] = (part * slope_s[:, tile].astype(F32)).astype(BF)
        dup[:, tile] = (part * act_s[:, tile].astype(F32)).astype(BF)
    writer.send(dgate, dgate_hbm)
    writer.send(dup, dup_hbm)
    for copy in copies:
        copy.wait()
    back_tiles(dgate, dup, gate_w, up_w, back, back_hbm, writer)
    writer.finish()


def experts_backward(dslot, act, slope, weights, order):
    small = (SLOTS, FF)
    wide = (SLOTS, WIDTH)
    return run_experts(
        experts_backward_kernel, "experts_backward", [dslot, act, slope, *weights], order,
        [small, small, wide],
        [(wide, BF), (small, BF), (small, BF)] + EXPERT_SCRATCH
        + [(small, BF), (small, BF), (wide, BF)],
        6 + 2 * WIDTH // TILE, 6 * SLOTS * WIDTH * FF,
    )


def expert_grads_kernel(received, dgate_pre, dup_pre, hidden, dslot, packed):
    gate = dot(received[...], dgate_pre[...], 0, 0).astype(BF)
    up = dot(received[...], dup_pre[...], 0, 0).astype(BF)
    down = dot(hidden[...], dslot[...], 0, 0).astype(BF)
    for part in range(DP // 2):
        packed[part, :SHARD, :FF] = gate[part * SHARD : (part + 1) * SHARD]
        packed[part, :SHARD, FF:] = up[part * SHARD : (part + 1) * SHARD]
        packed[part, SHARD:] = down[part * FF // DP : (part + 1) * FF // DP]


def expert_grads(received, dgate_pre, dup_pre, hidden, dslot):
    rows = SHARD + FF // DP
    whole = lambda width: pl.BlockSpec((SLOTS, width), lambda i: (0, 0))
    part = lambda width: pl.BlockSpec((SLOTS, width), lambda i: (0, i))
    return pl.pallas_call(
        expert_grads_kernel,
        grid=(2,),
        out_shape=jax.ShapeDtypeStruct((DP, rows, WIDTH), BF),
        in_specs=[part(WIDTH // 2), whole(FF), whole(FF), part(FF // 2), whole(WIDTH)],
        out_specs=pl.BlockSpec((DP // 2, rows, WIDTH), lambda i: (i, 0, 0)),
        compiler_params=pltpu.CompilerParams(vmem_limit_bytes=VMEM_BYTES),
        cost_estimate=pl.CostEstimate(
            flops=6 * SLOTS * WIDTH * FF, bytes_accessed=14 << 20, transcendentals=0
        ),
        name="expert_grads",
    )(received, dgate_pre, dup_pre, hidden, dslot).reshape(DP * rows, WIDTH)


def pack_kernel(
    l, query_hbm, key_hbm, value_hbm, out_hbm, router_hbm, gain_attn, gain_ffn, packed_hbm, *rest
):
    if l == 0:
        out_copy, packed, out, router, sems, out_sems = rest
    else:
        packed, router, sems, out_sems = rest
        out = packed.at[:, pl.ds(QKV, WIDTH)]
    pairs = [
        (router_hbm.at[l], router),
        (query_hbm.at[l], packed.at[:, pl.ds(0, Q_END)]),
        (key_hbm.at[l], packed.at[:, pl.ds(Q_END, K_END - Q_END)]),
        (value_hbm.at[l], packed.at[:, pl.ds(K_END, QKV - K_END)]),
        (out_hbm.at[l], out),
    ]
    reader, writer = Reader(sems, pairs), Writer(out_sems)
    reader.take()
    small = [router[...].astype(F32), gain_attn[l : l + 1].astype(F32)]
    small += [gain_ffn[l : l + 1].astype(F32), jnp.zeros((HEAD - EXPERTS - 2, SHARD), F32)]
    small = jnp.concatenate(small, axis=0)
    small = jnp.concatenate([small, jnp.zeros((HEAD, TILE - SHARD), F32)], axis=1).T
    packed[:, packed.shape[1] - HEAD :] = small[:SHARD].astype(BF)
    reader.take(3)
    if l == 0:
        writer.send(packed, packed_hbm)
        reader.take()
        writer.send(out, out_copy)
    else:
        reader.take()
        writer.send(packed, packed_hbm)
    writer.finish()


def pack(l, query, key, value, out, router, gain_attn, gain_ffn):
    sd = jax.ShapeDtypeStruct
    vmem = pl.BlockSpec(memory_space=pltpu.VMEM)
    packed = (SHARD, QKV + HEAD) if l == 0 else (SHARD, PACKED)
    outs = [packed] + [(SHARD, WIDTH)] * (l == 0)
    return pl.pallas_call(
        lambda *refs: pack_kernel(l, *refs),
        out_shape=[sd(shape, BF) for shape in outs],
        in_specs=[ANY] * 5 + [vmem] * 2,
        out_specs=[ANY] * len(outs),
        scratch_shapes=[pltpu.VMEM(shape, BF) for shape in outs]
        + [pltpu.VMEM((EXPERTS, SHARD), BF)]
        + [pltpu.SemaphoreType.DMA((5,)), pltpu.SemaphoreType.DMA((2,))],
        compiler_params=pltpu.CompilerParams(vmem_limit_bytes=VMEM_BYTES),
        name="pack",
    )(query, key, value, out, router.transpose(0, 2, 1), gain_attn, gain_ffn)


def ring(block):
    def move(values, step):
        return lax.ppermute(values, "dp", [(i, (i + step) % DP) for i in range(DP)])

    half = block.shape[0] // 2
    previous, following = move(block, 2), move(block, -2)
    far = [move(previous[:half], 2), move(following[half:], -2)]
    mine = [block, previous, following, *far]
    swap = [(i, i ^ 1) for i in range(DP)]
    return mine + [lax.ppermute(values, "dp", swap) for values in mine]


def seq_tables(counts):
    ends = jnp.cumsum(counts)
    starts = ends - counts
    place = jnp.arange(ROWS, dtype=jnp.int32)
    member = (place[:, None] >= starts[None, :]) & (place[:, None] < ends[None, :])
    index = jnp.arange(counts.shape[0], dtype=jnp.int32)
    segment = jnp.sum(jnp.where(member, index[None, :], 0), axis=1)
    position = place - jnp.sum(jnp.where(member, starts[None, :], 0), axis=1)
    allowed = (segment[:, None] == segment[None, :]) & (place[:, None] >= place[None, :])
    freqs = ROPE_BASE ** (-2.0 * jnp.arange(HEAD // 2, dtype=F32) / HEAD)
    angle = position.astype(F32)[:, None] * freqs[None, :]
    cosine, sine = jnp.cos(angle), jnp.sin(angle)
    return (
        jnp.concatenate([cosine, cosine], axis=1),
        jnp.concatenate([-sine, sine], axis=1),
        allowed.astype(F32),
    )


def slot_matrix(choices, in_parts=False):
    experts = jnp.arange(EXPERTS, dtype=jnp.int32)
    member = jnp.any(choices[:, :, None] == experts[None, None, :], axis=1).astype(BF)
    row = lax.broadcasted_iota(jnp.int32, (ROWS, ROWS), 0)
    column = lax.broadcasted_iota(jnp.int32, (ROWS, ROWS), 1)
    rank = dot((column < row).astype(BF), member).astype(BF)
    slot = jnp.arange(SLOTS, dtype=jnp.int32)[None, :]
    if in_parts:
        later = slot - PART_ENDS[0]
        owner = jnp.where(later < 0, slot // 16, later // 32)
        place = jnp.where(later < 0, slot % 16, 16 + later % 32)
    else:
        owner, place = slot // CAP, slot % CAP
    expand = (owner == experts[:, None]).astype(BF)
    return ((dot(member, expand) > 0.5) & (dot(rank, expand) == place.astype(F32))).astype(BF)


def exchange(rows):
    width = rows.shape[-1]
    moved = lax.all_to_all(
        rows.reshape(EXPERTS, -1, width), "expert", split_axis=0, concat_axis=0, tiled=True
    )
    return moved.reshape(-1, width)


def after(values, order):
    return pl.pallas_call(
        lambda *refs: None,
        out_shape=jax.ShapeDtypeStruct(values.shape, values.dtype),
        in_specs=[ANY, ANY],
        out_specs=ANY,
        input_output_aliases={0: 0},
        name="after",
    )(values, order)


def turn_columns_kernel(me, columns_hbm, turned_hbm, columns, turned, in_sems, out_sems):
    base = me[0] * SHARD // HEAD * HEAD
    pairs = []
    for i in range(3):
        at = pl.multiple_of(base + i * WIDTH, HEAD)
        pairs += [(columns_hbm.at[:, pl.ds(at, TILE)], columns.at[:, pl.ds(i * TILE, TILE)])]
    reader, writer = Reader(in_sems, pairs), Writer(out_sems)
    for i in range(3):
        reader.take()
        turned[i] = columns[:, i * TILE : (i + 1) * TILE].T
        writer.send(turned.at[i], turned_hbm.at[i])
    writer.finish()


def turn_columns(me, columns):
    tokens = DP * ROWS
    return pl.pallas_call(
        turn_columns_kernel,
        out_shape=jax.ShapeDtypeStruct((3, TILE, tokens), BF),
        in_specs=[pl.BlockSpec(memory_space=pltpu.SMEM), ANY],
        out_specs=ANY,
        scratch_shapes=[
            pltpu.VMEM((tokens, 3 * TILE), BF),
            pltpu.VMEM((3, TILE, tokens), BF),
            pltpu.SemaphoreType.DMA((3,)),
            pltpu.SemaphoreType.DMA((3,)),
        ],
        compiler_params=pltpu.CompilerParams(vmem_limit_bytes=VMEM_BYTES),
        cost_estimate=pl.CostEstimate(flops=0, bytes_accessed=4 << 20, transcendentals=0),
        name="turn_columns",
    )(me, columns)


def dense_grads_kernel(me, turned_hbm, factors_hbm, extra, pieces_hbm, turned, factors, total,
                       held, pieces, in_sems, out_sems):
    start = me[0] * SHARD
    shift = start % HEAD
    base = start - shift
    copies = Writer(out_sems)
    shared = len(extra.shape) == 2
    if shared:
        pairs = [(extra, held)]
    else:
        pairs = [(extra, pieces.at[:, :, pl.ds(CHUNK, CHUNK)])]
    pairs += [(turned_hbm, turned)]
    for at in range(0, PACKED, CHUNK):
        block = (slice(None), pl.ds(at, min(CHUNK, PACKED - at)))
        pairs += [(factors_hbm.at[block], factors.at[block])]
    reader = Reader(in_sems, pairs)
    reader.take(2)

    def put(chunk, values):
        pieces[chunk, :, :CHUNK] = values.astype(BF)
        if shared:
            pieces[chunk, :, CHUNK:] = held[...]
        copies.send(pieces.at[chunk], pieces_hbm.at[chunk])

    for chunk in range(SMALL // CHUNK):
        reader.take()
        total[chunk % 2] = dot(
            turned[0 if chunk < QKV // CHUNK else 1],
            factors[:, chunk * CHUNK : (chunk + 1) * CHUNK],
        )
        put(chunk, total[chunk % 2, pl.ds(pl.multiple_of(shift, 64), SHARD), :])
    reader.take()
    ends = jnp.zeros((ROWS, HEAD), F32)
    for source in range(DP):
        ends += factors[source * ROWS : (source + 1) * ROWS, SMALL:].astype(F32)
    lane = lax.broadcasted_iota(jnp.int32, (ROWS, HEAD), 1)

    def gain_piece(piece):
        held = (lane == piece + GAIN_HIGH) | (lane == piece + GAIN_LOW)
        return jnp.sum(jnp.where(held, ends, 0.0), axis=1, keepdims=True)

    first, second = gain_piece(base // HEAD), gain_piece(base // HEAD + 1)
    gain = jnp.where(
        shift == 0,
        jnp.concatenate([first, second[: SHARD - ROWS]], axis=0),
        jnp.concatenate([first[ROWS // 2 :], second], axis=0),
    )
    gain_high, gain_low = split(gain)
    total[0, :, :HEAD] = dot(turned[2], factors[:, SMALL:])
    router = total[0, pl.ds(pl.multiple_of(shift, 64), SHARD), :HEAD]
    lane = lax.broadcasted_iota(jnp.int32, (SHARD, HEAD), 1)
    router = jnp.where(lane < EXPERTS, router, 0.0)
    router = jnp.where(lane == EXPERTS, gain_high.astype(F32), router)
    router = jnp.where(lane == EXPERTS + 1, gain_low.astype(F32), router)
    put(CHUNKS - 2, jnp.concatenate([router, jnp.zeros_like(router)], axis=1))
    put(CHUNKS - 1, jnp.zeros((SHARD, CHUNK), F32))
    copies.finish()


def dense_grads(me, turned, factors, extra, order):
    tokens = DP * ROWS

    def body(*refs):
        dense_grads_kernel(*refs[:4], *refs[4 + len(order) :])

    return pl.pallas_call(
        body,
        out_shape=jax.ShapeDtypeStruct((CHUNKS, SHARD, 2 * CHUNK), BF),
        in_specs=[pl.BlockSpec(memory_space=pltpu.SMEM)] + [ANY] * (3 + len(order)),
        out_specs=ANY,
        scratch_shapes=[
            pltpu.VMEM((3, TILE, tokens), BF),
            pltpu.VMEM((tokens, PACKED), BF),
            pltpu.VMEM((2, TILE, CHUNK), F32),
            pltpu.VMEM((SHARD, CHUNK), BF),
            pltpu.VMEM((CHUNKS, SHARD, 2 * CHUNK), BF),
            pltpu.SemaphoreType.DMA((2 + CHUNKS,)),
            pltpu.SemaphoreType.DMA((CHUNKS,)),
        ],
        compiler_params=pltpu.CompilerParams(vmem_limit_bytes=VMEM_BYTES),
        cost_estimate=pl.CostEstimate(
            flops=2 * tokens * TILE * PACKED, bytes_accessed=10 << 20, transcendentals=0
        ),
        name="dense_grads",
    )(me, turned, factors, extra, *order)


def to_expert_peers(pieces):
    return lax.all_to_all(pieces, "expert", split_axis=0, concat_axis=0, tiled=True)


def sum_pieces_kernel(pieces_hbm, out_hbm, pieces, out, in_sems, out_sems):
    half = CHUNKS // 2
    pairs = []
    for at in (0, half):
        block = pl.ds(at, half)
        pairs += [(pieces_hbm.at[block, :, pl.ds(0, CHUNK)], pieces.at[block])]
    reader, writer = Reader(in_sems, pairs), Writer(out_sems)
    reader.take()
    total = pieces[0].astype(F32)
    for i in range(1, half):
        total += pieces[i].astype(F32)
    reader.take()
    for i in range(half, CHUNKS):
        total += pieces[i].astype(F32)
    out[...] = total.astype(BF)
    if len(out_hbm.shape) == 3:
        for i in range(CHUNKS):
            writer.send(out, out_hbm.at[i])
    else:
        writer.send(out, out_hbm)
    writer.finish()


def sum_pieces(pieces, copies):
    return pl.pallas_call(
        sum_pieces_kernel,
        out_shape=jax.ShapeDtypeStruct((copies,) * (copies > 1) + (SHARD, CHUNK), BF),
        in_specs=[ANY],
        out_specs=ANY,
        scratch_shapes=[
            pltpu.VMEM((CHUNKS, SHARD, CHUNK), BF),
            pltpu.VMEM((SHARD, CHUNK), BF),
            pltpu.SemaphoreType.DMA((2,)),
            pltpu.SemaphoreType.DMA((CHUNKS,)),
        ],
        compiler_params=pltpu.CompilerParams(vmem_limit_bytes=VMEM_BYTES),
        name="sum_pieces",
    )(pieces)


def finish_kernel(l, at, refs):
    (pieces, w_query, key_projection, value_projection, norm_attn), refs = refs[:5], refs[5:]
    if l == 0:
        ends_above, refs = refs[0], refs[5:]
        (query_hbm, key_hbm, value_hbm, out_hbm, gain_attn, gain_ffn, router) = refs[:7]
        query, key, value, out, sems = refs[7:]
    else:
        query_hbm, key_hbm, value_hbm, out_hbm, ends_out, query, key, value, out, sems = refs
    writer = Writer(sems)
    rows = jnp.zeros((SHARD, 1), F32)
    for chunk in range(SMALL // CHUNK):
        part = pieces[chunk, :, at : at + CHUNK].astype(F32)
        lanes = slice(chunk * CHUNK, (chunk + 1) * CHUNK)
        if chunk < Q_END // CHUNK:
            query[:, lanes] = part
            weight = w_query[l, :, lanes]
        elif chunk == Q_END // CHUNK:
            key[...] = part
            weight = key_projection[l]
            writer.send(query, query_hbm.at[l])
            writer.send(key, key_hbm.at[l])
        elif chunk < QKV // CHUNK:
            value[...] = part
            weight = value_projection[l]
            writer.send(value, value_hbm.at[l])
        else:
            out[:, lanes.start - QKV : lanes.stop - QKV] = part
            continue
        rows += jnp.sum(part * weight.astype(F32), axis=1, keepdims=True)
    writer.send(out, out_hbm.at[l])
    ends = pieces[CHUNKS - 2, :, at : at + HEAD].astype(F32)
    ffn = ends[:, EXPERTS : EXPERTS + 1] + ends[:, EXPERTS + 1 : EXPERTS + 2]
    lane = lax.broadcasted_iota(jnp.int32, (SHARD, HEAD), 1)
    ends = jnp.where(lane == EXPERTS, rows, jnp.where(lane == EXPERTS + 1, ffn, ends))
    if l > 0:
        ends_out[...] = ends
    else:
        for layer, part in enumerate((ends, ends_above[...])):
            wide = jnp.concatenate([part, jnp.zeros((TILE - SHARD, HEAD), F32)], axis=0).T
            router[layer] = wide[:EXPERTS, :SHARD]
            gain = norm_attn[layer : layer + 1].astype(F32)
            gain_attn[layer : layer + 1] = wide[EXPERTS : EXPERTS + 1, :SHARD] / gain
            gain_ffn[layer : layer + 1] = wide[EXPERTS + 1 : EXPERTS + 2, :SHARD]
    writer.finish()


def finish(l, pieces, at, weights, norm_attn, above):
    sd = jax.ShapeDtypeStruct
    vmem = pl.BlockSpec(memory_space=pltpu.VMEM)
    keys = (SHARD, KEY_VALUE_HEADS * HEAD)
    slabs = [(SHARD, Q_END), keys, keys, (SHARD, WIDTH)]
    outs = [sd((LAYERS,) + shape, F32) for shape in slabs]
    if above is None:
        outs += [sd((SHARD, HEAD), F32)]
        ins, in_specs, aliases = [], [], {}
    else:
        outs += [sd((LAYERS, SHARD), F32)] * 2 + [sd((LAYERS, EXPERTS, SHARD), F32)]
        ins, in_specs = [above[4], *above[:4]], [vmem] + [ANY] * 4
        aliases = {6 + i: i for i in range(4)}
    return pl.pallas_call(
        lambda *refs: finish_kernel(l, at, refs),
        out_shape=outs,
        in_specs=[vmem] * 5 + in_specs,
        out_specs=[ANY] * 4 + [vmem] * (len(outs) - 4),
        input_output_aliases=aliases,
        scratch_shapes=[pltpu.VMEM(shape, F32) for shape in slabs]
        + [pltpu.SemaphoreType.DMA((4,))],
        compiler_params=pltpu.CompilerParams(vmem_limit_bytes=VMEM_BYTES),
        name="finish",
    )(pieces, *weights, norm_attn, *ins)


def finish_experts_kernel(shares0, shares1, gate, up, down):
    for l, shares in enumerate((shares0, shares1)):
        gate[l, 0] = shares[:SHARD, :FF].astype(F32)
        up[l, 0] = shares[:SHARD, FF:].astype(F32)
        down[l, 0] = shares[SHARD:].astype(F32)


def finish_experts(shares0, shares1):
    sd = jax.ShapeDtypeStruct
    vmem = pl.BlockSpec(memory_space=pltpu.VMEM)
    return pl.pallas_call(
        finish_experts_kernel,
        out_shape=[
            sd((LAYERS, 1, SHARD, FF), F32), sd((LAYERS, 1, SHARD, FF), F32),
            sd((LAYERS, 1, FF // DP, WIDTH), F32),
        ],
        in_specs=[vmem] * 2,
        out_specs=[vmem] * 3,
        compiler_params=pltpu.CompilerParams(vmem_limit_bytes=VMEM_BYTES),
        name="finish_experts",
    )(shares0, shares1)


def mixed_kernel(x_hbm, high, low, early_hbm, got_hbm, out, x, gates, early, got, late, sems):
    pairs = [
        (high, gates.at[:ROWS]), (low, gates.at[ROWS:]), (x_hbm, x), (early_hbm, early),
        (got_hbm.at[:, :, pl.ds(CHUNK, CHUNK)], got),
    ]
    Reader(sems, pairs).take(len(pairs))
    for expert in range(EXPERTS):
        rows = slice(expert * PART_ROWS[1], (expert + 1) * PART_ROWS[1])
        for tile in tiles(WIDTH):
            at = tile.start // TILE * PART_ROWS[1]
            late[rows, tile] = got[expert, at : at + PART_ROWS[1]]
    for tile in tiles(WIDTH):
        both = dot(gates[:, : PART_ENDS[0]], early[:, tile])
        both += dot(gates[:, PART_ENDS[0] :], late[:, tile])
        out[:, tile] = (x[:, tile] + both[:ROWS] + both[ROWS:]).astype(BF)


def mixed_rows(x, high, low, early, got):
    return pl.pallas_call(
        mixed_kernel,
        out_shape=jax.ShapeDtypeStruct(TOKENS, BF),
        in_specs=[ANY] * 5,
        out_specs=pl.BlockSpec(memory_space=pltpu.VMEM),
        scratch_shapes=[
            pltpu.VMEM(TOKENS, F32),
            pltpu.VMEM((2 * ROWS, SLOTS), BF),
            pltpu.VMEM((PART_ENDS[0], WIDTH), BF),
            pltpu.VMEM((EXPERTS, SHARD, CHUNK), BF),
            pltpu.VMEM((SLOTS - PART_ENDS[0], WIDTH), BF),
            pltpu.SemaphoreType.DMA((5,)),
        ],
        compiler_params=pltpu.CompilerParams(vmem_limit_bytes=VMEM_BYTES),
        name="mixed",
    )(x, high, low, early, got)


def local(
    tokens, cotangent, lengths, routes, norm_attn, w_query, key_projection, value_projection,
    w_out, norm_ffn, w_router, w_gate, w_up, w_down,
):
    me_dp = lax.axis_index("dp").astype(jnp.int32).reshape(1)
    me_expert = lax.axis_index("expert").astype(jnp.int32).reshape(1)
    tables = seq_tables(lengths[0])
    give = [slot_matrix(routes[l]) for l in range(LAYERS)]
    take = [g.T for g in give]
    give_parts = slot_matrix(routes[1], True)
    experts = (w_gate, w_up, w_down)

    def gather(values):
        return lax.all_gather(values, "dp", axis=0, tiled=True)

    weights = (w_query, key_projection, value_projection, w_out, w_router, norm_attn, norm_ffn)
    shard0, out_shard0 = pack(0, *weights)
    w = [gather(shard0), gather(pack(1, *weights)[0])]
    out_ring = [me_dp, *ring(out_shard0)]

    dx_rows = exchange(dot(take[1], cotangent).astype(BF))

    kept0 = attn_forward(
        tokens, None, w[0], out_ring, tables, take[0], give[0],
        (dx_rows, give[1], give_parts, me_expert),
    )
    received0 = exchange(kept0["rows"])
    act0, slope0, hidden0, out0 = experts_forward(received0, experts, ())
    returned0 = exchange(after(out0, w[1]))
    columns0 = gather(kept0["columns"])

    kept1 = attn_forward(
        kept0["after"], (kept0["high"], kept0["low"], returned0), w[1], None, tables, take[1],
        give_parts, (),
    )
    received1 = exchange(kept1["rows"])
    columns1 = gather(kept1["columns"])
    hidden1, early1, late1, dslot1, dgate1, dup1, back1 = experts_both(
        me_expert, received1, dx_rows, w[1], experts, ()
    )
    back1 = exchange(back1)
    grads1 = expert_grads(received1, dgate1, dup1, hidden1, dslot1)
    turned0, turned1 = turn_columns(me_dp, columns0), turn_columns(me_dp, columns1)
    early1 = exchange(early1)

    dx0, packed1, rows0 = attn_backward(
        cotangent, back1, kept1["x"], kept1, w[1], None, tables, give[1], (take[0], kept0["router"]),
        None, (grads1, turned0, turned1),
    )
    dslot0 = exchange(rows0)
    factors1 = gather(packed1)
    shares1 = lax.psum_scatter(after(grads1, packed1), "dp", scatter_dimension=0, tiled=True)
    dgate0, dup0, back0 = experts_backward(dslot0, act0, slope0, experts, ())
    back0 = exchange(back0)
    grads0 = expert_grads(received0, dgate0, dup0, hidden0, dslot0)
    pieces1 = dense_grads(me_dp, turned1, factors1, late1, (early1,))
    grad_tokens, packed0 = attn_backward(
        dx0, back0, tokens, kept0, w[0], out_ring, tables, give[0], None, returned0,
        (shares1, grads0, pieces1),
    )
    factors0 = gather(packed0)
    got = to_expert_peers(pieces1)
    summed1 = sum_pieces(got, 1)
    shares0 = lax.psum_scatter(after(grads0, summed1), "dp", scatter_dimension=0, tiled=True)
    mixed = mixed_rows(kept1["after"], kept1["high"], kept1["low"], early1, got)
    pieces = to_expert_peers(dense_grads(me_dp, turned0, factors0, summed1, ()))
    pieces0 = to_expert_peers(sum_pieces(pieces, CHUNKS))

    dense = (w_query, key_projection, value_projection)
    above = finish(1, pieces, CHUNK, dense, norm_attn, None)
    query, key, value, out, gain_attn, gain_ffn, router = finish(
        0, pieces0, 0, dense, norm_attn, above
    )
    gate, up, down = finish_experts(shares0, shares1)
    return (
        mixed, grad_tokens, gain_attn, query, key, value, out, gain_ffn,
        router.transpose(0, 2, 1), gate, up, down,
    )


def solution(mesh):
    placed = (
        P(("dp", "expert"), None),
        P(("dp", "expert"), None),
        P(("dp", "expert"), None),
        P(None, ("dp", "expert"), None),
        P(None, "dp"),
        P(None, "dp", None),
        P(None, "dp", None),
        P(None, "dp", None),
        P(None, "dp", None),
        P(None, "dp"),
        P(None, "dp", None),
        P(None, "expert", None, None),
        P(None, "expert", None, None),
        P(None, "expert", None, None),
    )
    return jax.shard_map(
        local,
        mesh=mesh,
        in_specs=placed,
        out_specs=(
            P(("dp", "expert"), None),
            P(("dp", "expert"), None),
            P(None, "dp"),
            P(None, "dp", None),
            P(None, "dp", None),
            P(None, "dp", None),
            P(None, "dp", None),
            P(None, "dp"),
            P(None, "dp", None),
            P(None, "expert", "dp", None),
            P(None, "expert", "dp", None),
            P(None, "expert", "dp", None),
        ),
        check_vma=False,
    )
```

```python
import jax
import jax.numpy as jnp
from jax import lax
from jax.experimental import pallas as pl
from jax.experimental.pallas import tpu as pltpu
from jax.sharding import PartitionSpec as P

QUERY_HEADS = 12
KEY_VALUE_HEADS = 2
GROUPS = QUERY_HEADS // KEY_VALUE_HEADS
HEAD = 128
LAYERS = 2
WIDTH = 1536
FF = 768
ROWS = 128
EXPERTS = 16
CAP = 48
SLOTS = EXPERTS * CAP
DP = 8
SHARD = WIDTH // DP
Q_END = QUERY_HEADS * HEAD
K_END = Q_END + KEY_VALUE_HEADS * HEAD
QKV = K_END + KEY_VALUE_HEADS * HEAD
SMALL = QKV + WIDTH
PACKED = SMALL + HEAD
GAIN_ATTN, GAIN_FFN = 16, 17
GAIN_HIGH, GAIN_LOW = 16, 32
PIECES = WIDTH // HEAD
TILE = 256
PARTS = 3
PART = SLOTS // PARTS
PART_ROWS = CAP // PARTS
CHUNKS, CHUNK = 16, 256
COLUMNS = 3 * WIDTH
EPSILON = 1e-06
ROPE_BASE = 1000000.0
SCALE = HEAD ** (-0.5)
GELU_A = 0.7978845608028654
GELU_B = 0.044715
VMEM_BYTES = 56 << 20
BF = jnp.bfloat16
F32 = jnp.float32
ANY = pl.BlockSpec(memory_space=pl.ANY)


def dot(left, right, left_dim=1, right_dim=0):
    return lax.dot_general(
        left, right, (((left_dim,), (right_dim,)), ((), ())), preferred_element_type=F32
    )


def split(values):
    high = values.astype(BF)
    return high, (values - high.astype(F32)).astype(BF)


def unit(values):
    return lax.rsqrt(jnp.mean(values * values, axis=-1, keepdims=True) + EPSILON)


def turn(values, cosine, sine):
    return values * cosine + pltpu.roll(values, HEAD // 2, 1) * sine


def expert_lanes(transposed=False, in_parts=False):
    shape = (SLOTS, HEAD) if transposed else (HEAD, SLOTS)
    slot = lax.broadcasted_iota(jnp.int32, shape, 0 if transposed else 1)
    expert = lax.broadcasted_iota(jnp.int32, shape, 1 if transposed else 0)
    if in_parts:
        held = ((slot & (PART - 1)) >> 4) == expert
    else:
        held = (slot >= expert * CAP) & (slot < expert * CAP + CAP)
    return held.astype(F32).astype(BF)


def gain_rows(small):
    row = lax.broadcasted_iota(jnp.int32, (8, HEAD), 0)
    lane = lax.broadcasted_iota(jnp.int32, (8, HEAD), 1)
    pick = ((lane == row + GAIN_ATTN) & (row < 2)).astype(F32).astype(BF)
    rows = dot(pick, small, 1, 1)
    return rows[0:1], rows[1:2]


def router_probs(rows, small):
    logits = dot(rows, small)
    lane = lax.broadcasted_iota(jnp.int32, logits.shape, 1)
    logits = jnp.where(lane < EXPERTS, logits, -1e30)
    powers = jnp.exp(logits - jnp.max(logits, axis=-1, keepdims=True))
    return powers / jnp.sum(powers, axis=-1, keepdims=True)


def start_all(pairs, sems):
    copies = [
        pltpu.make_async_copy(source, target, sems.at[i]) for i, (source, target) in enumerate(pairs)
    ]
    for copy in copies:
        copy.start()
    return copies


class Writer:
    def __init__(self, sems):
        self.sems, self.copies = sems, []

    def send(self, source, target):
        copy = pltpu.make_async_copy(source, target, self.sems.at[len(self.copies)])
        copy.start()
        self.copies.append(copy)

    def finish(self):
        for copy in self.copies:
            copy.wait()


class Reader:
    def __init__(self, sems, pairs):
        self.copies = start_all(pairs, sems)

    def take(self, count=1):
        for _ in range(count):
            self.copies.pop(0).wait()


def tiles(width):
    return [slice(at, at + TILE) for at in range(0, width, TILE)]


def small_block(w_hbm, w):
    last = w_hbm.shape[1] - HEAD
    return (w_hbm.at[:, pl.ds(last, HEAD)], w.at[:, pl.ds(SMALL, HEAD)])


def column_block(w_hbm, w, at):
    return (w_hbm.at[:, pl.ds(at, TILE)], w.at[:, pl.ds(at, TILE)])


def ring_blocks(me, blocks, w):
    pairs = []
    for core in range(2):
        start = me if core == 0 else me + 1 - 2 * (me % 2)
        for block, step in enumerate((0, DP - 2, 2, 4, 4)):
            ref = blocks[core * 5 + block]
            at = (start + step) % DP * SHARD + (SHARD // 2 if block == 4 else 0)
            at = pl.multiple_of(at, SHARD // 2)
            pairs += [(ref, w.at[pl.ds(at, ref.shape[0]), pl.ds(QKV, WIDTH)])]
    return pairs


def attn_forward_kernel(first, ins, outs, scratch):
    (x_hbm, w_hbm, cosine_hbm, sine_hbm, allowed_hbm, take_hbm, give_hbm), ins = ins[:7], ins[7:]
    (columns_hbm, qrot_hbm, krot_hbm, value_hbm, probs_hbm, after_hbm, router_hbm, high_hbm, low_hbm,
     rows_hbm), outs = outs[:10], outs[10:]
    (x_in, w, cosine, sine, allowed, take, give, returned, gates, x, columns, qrot, krot, value, probs,
     after, router, high, low, rows, in_sems, out_sems) = scratch
    acts = columns.at[:, :WIDTH]
    attended = columns.at[:, WIDTH : 2 * WIDTH]
    acts_two = columns.at[:, 2 * WIDTH :]
    pairs = []
    if first:
        out_pairs = ring_blocks(ins[0][0], ins[1:], w)
    else:
        out_pairs = [column_block(w_hbm, w, at) for at in range(QKV, SMALL, TILE)]
        high_below, low_below, returned_hbm = ins
        pairs += [(high_below, gates.at[:ROWS]), (low_below, gates.at[ROWS:])]
        pairs += [(returned_hbm, returned)]
    pairs += [(x_hbm, x_in), small_block(w_hbm, w)]
    pairs += [column_block(w_hbm, w, at) for at in range(0, QKV, TILE)]
    pairs += [(cosine_hbm, cosine), (sine_hbm, sine), (allowed_hbm, allowed)]
    pairs += out_pairs + [(take_hbm, take), (give_hbm, give)]
    reader, writer = Reader(in_sems, pairs), Writer(out_sems)
    if first:
        reader.take()
        x[...] = x_in[...].astype(F32)
    else:
        reader.take(4)
        for tile in tiles(WIDTH):
            both = dot(gates[...], returned[:, tile])
            x[:, tile] = x_in[:, tile] + both[:ROWS] + both[ROWS:]
        writer.send(x, outs[0])
    reader.take()
    small = w[:, SMALL:]
    gain_attn, gain_ffn = gain_rows(small)
    total = x[...]
    acts[...] = (total * unit(total) * gain_attn).astype(BF)
    wide = []
    for tile in tiles(QKV):
        reader.take()
        wide += [dot(acts[...], w[:, tile])]
    reader.take(3)
    for tile in range(QKV // TILE):
        for half in range(TILE // HEAD):
            head = tile * (TILE // HEAD) + half
            part = wide[tile][:, half * HEAD : (half + 1) * HEAD]
            if head < QUERY_HEADS:
                qrot[head] = turn(part, cosine[...], sine[...]).astype(BF)
            elif head < QUERY_HEADS + KEY_VALUE_HEADS:
                krot[head - QUERY_HEADS] = turn(part, cosine[...], sine[...]).astype(BF)
            else:
                value[head - QUERY_HEADS - KEY_VALUE_HEADS] = part.astype(BF)
    writer.send(qrot, qrot_hbm)
    writer.send(krot, krot_hbm)
    writer.send(value, value_hbm)
    open_scores = (allowed[...] > 0.5)[None]
    for k in range(KEY_VALUE_HEADS):
        heads = slice(k * GROUPS, (k + 1) * GROUPS)
        scores = dot(qrot[heads].reshape(GROUPS * ROWS, HEAD), krot[k], 1, 1) * SCALE
        scores = jnp.where(open_scores, scores.reshape(GROUPS, ROWS, ROWS), -1000000000.0)
        powers = jnp.exp(scores - jnp.max(scores, axis=-1, keepdims=True))
        shares = powers / jnp.sum(powers, axis=-1, keepdims=True)
        probs[heads] = shares
        mixed = dot(shares.astype(BF).reshape(GROUPS * ROWS, ROWS), value[k]).astype(BF)
        for group in range(GROUPS):
            at = (k * GROUPS + group) * HEAD
            attended[:, at : at + HEAD] = mixed[group * ROWS : (group + 1) * ROWS]
    writer.send(probs, probs_hbm)
    if first:
        reader.take(len(out_pairs))
    for tile in tiles(WIDTH):
        if not first:
            reader.take()
        after[:, tile] = x[:, tile] + dot(
            attended[...], w[:, QKV + tile.start : QKV + tile.stop]
        )
    writer.send(after, after_hbm)
    total = after[...]
    acts_two[...] = (total * unit(total) * gain_ffn).astype(BF)
    writer.send(columns, columns_hbm)
    reader.take(2)
    for tile in tiles(WIDTH):
        rows[:, tile] = dot(take[...], acts_two[:, tile]).astype(BF)
        writer.send(rows.at[:, tile], rows_hbm.at[:, tile])
    shares = router_probs(acts_two[...], small)
    router[...] = shares
    spread = expert_lanes(in_parts=not first)
    both = dot(jnp.concatenate(split(shares), axis=0), spread).astype(BF)
    high[...] = both[:ROWS] * give[...]
    low[...] = both[ROWS:] * give[...]
    writer.send(router, router_hbm)
    writer.send(high, high_hbm)
    writer.send(low, low_hbm)
    writer.finish()


HEADS = (QUERY_HEADS, ROWS, HEAD)
KEYS = (KEY_VALUE_HEADS, ROWS, HEAD)
TABLE = (ROWS, HEAD)
TOKENS = (ROWS, WIDTH)
WIDE = (SLOTS, WIDTH)


def specs_of(ins):
    return [pl.BlockSpec(memory_space=pltpu.SMEM if a.dtype == jnp.int32 else pl.ANY) for a in ins]


def run_attn(kernel, name, ins, order, outs, scratch, in_copies, out_copies, vmem):
    sd = jax.ShapeDtypeStruct

    def body(*refs):
        first_out = len(ins) + len(order)
        first_scratch = first_out + len(outs)
        kernel(refs[: len(ins)], refs[first_out:first_scratch], refs[first_scratch:])

    return pl.pallas_call(
        body,
        out_shape=[sd(shape, kind) for shape, kind in outs],
        in_specs=specs_of(ins) + [ANY] * len(order),
        out_specs=[ANY] * len(outs),
        scratch_shapes=[pltpu.VMEM(shape, kind) for shape, kind in scratch]
        + [pltpu.SemaphoreType.DMA((in_copies,)), pltpu.SemaphoreType.DMA((out_copies,))],
        compiler_params=pltpu.CompilerParams(vmem_limit_bytes=vmem),
        cost_estimate=pl.CostEstimate(
            flops=2 * ROWS * WIDTH * PACKED, bytes_accessed=20 << 20, transcendentals=200000
        ),
        name=name,
    )(*ins, *order)


def attn_forward(x, combine, w, ring, tables, take, give, order):
    first = combine is None
    outs = [
        ((ROWS, COLUMNS), BF), (HEADS, BF), (KEYS, BF), (KEYS, BF), ((QUERY_HEADS, ROWS, ROWS), F32),
        (TOKENS, F32), (TABLE, F32), ((ROWS, SLOTS), BF), ((ROWS, SLOTS), BF), (WIDE, BF),
    ]
    names = [
        "columns", "qrot", "krot", "value", "probs", "after", "router", "high", "low", "rows"
    ]
    scratch = [(TOKENS, x.dtype), ((WIDTH, PACKED), BF)] + [(TABLE, F32)] * 3
    scratch += [((SLOTS, ROWS), BF), ((ROWS, SLOTS), BF)]
    scratch += [((16, HEAD), BF)] * 2 if first else [(WIDE, BF), ((2 * ROWS, SLOTS), BF)]
    scratch += [(TOKENS, F32)] + outs
    ins = [x, w, *tables, take, give]
    if first:
        ins += ring
    else:
        high, low, returned = combine
        ins += [high, low, returned]
        outs = outs + [(TOKENS, F32)]
        names += ["x"]
    result = run_attn(
        lambda *refs: attn_forward_kernel(first, *refs), "attn_forward", ins, order, outs, scratch,
        20 + QKV // TILE, 20, VMEM_BYTES,
    )
    return dict(zip(names, result))


def norm_back(grad, gain, values):
    scale = unit(values)
    inner = grad * gain
    return scale * inner - values * (scale * scale * scale) * jnp.mean(
        inner * values, axis=-1, keepdims=True
    )


def attn_backward_kernel(last, ins, outs, scratch):
    (dx_hbm, back_hbm, w_hbm, cosine_hbm, sine_hbm, give_hbm, router_hbm, after_hbm, x_hbm, probs_hbm,
     qrot_hbm, krot_hbm, value_hbm), ins = ins[:13], ins[13:]
    (dx_in, back, w, cosine, sine, give, router, after, x_in, probs, qrot, krot, value, wide_in,
     small_in, datt, dx_out, packed), scratch = scratch[:18], scratch[18:]
    if last:
        rows, scratch = scratch[0], scratch[1:]
    in_sems, out_sems = scratch
    pairs = [(give_hbm, give), (back_hbm, back), (router_hbm, router), (dx_hbm, dx_in)]
    if not last:
        pairs += [(ins[0], wide_in)]
    pairs += [small_block(w_hbm, w), (after_hbm, after)]
    if last:
        for at in range(0, WIDTH, TILE):
            block = (pl.ds(at, TILE), pl.ds(QKV, WIDTH))
            pairs += [(w_hbm.at[block], w.at[block])]
    else:
        pairs += ring_blocks(ins[1][0], ins[2:], w)
    pairs += [(probs_hbm, probs), (value_hbm, value), (krot_hbm, krot), (qrot_hbm, qrot)]
    pairs += [(cosine_hbm, cosine), (sine_hbm, sine)]
    for at in range(0, WIDTH, TILE):
        block = (pl.ds(at, TILE), pl.ds(0, QKV))
        pairs += [(w_hbm.at[block], w.at[block])]
    pairs += [(x_hbm, x_in)]
    if last:
        pairs += [(ins[0], wide_in), (ins[1], small_in)]
    reader, writer = Reader(in_sems, pairs), Writer(out_sems)
    reader.take(4)
    dx = dx_in[...].astype(F32)
    spread = expert_lanes(True)
    if last:
        dgate = back[:, WIDTH:].astype(F32)
        drouter = dot(give[...], (dgate[:, 0:1] * spread).astype(BF))
        drouter += dot(give[...], (dgate[:, 1:2] * spread).astype(BF))
    else:
        reader.take()
        dgate = dot(dx.astype(BF), wide_in[...], 1, 1) * give[...]
        both = dot(jnp.concatenate(split(dgate), axis=0), spread)
        drouter = both[:ROWS] + both[ROWS:]
    reader.take(2)
    small = w[:, SMALL:]
    gain_attn, gain_ffn = gain_rows(small)
    shares = router[...]
    dlogits = shares * (drouter - jnp.sum(drouter * shares, axis=-1, keepdims=True))
    dlogits = dlogits.astype(BF)
    dacts_two = dot(dlogits, small, 1, 1) + dot(give[...], back[:, :WIDTH])
    total = after[...]
    scale = unit(total)
    dafter = dx + norm_back(dacts_two, gain_ffn, total)
    dx_out[...] = dafter
    packed[:, QKV:SMALL] = dafter.astype(BF)
    dgain = jnp.sum(dacts_two * total * scale, axis=0, keepdims=True)
    dgain_high, dgain_low = split(dgain)
    pieces = [jnp.zeros((GAIN_HIGH, HEAD), F32)]
    for part in (dgain_high.astype(F32), dgain_low.astype(F32)):
        pieces += [part[:, at : at + HEAD] for at in range(0, WIDTH, HEAD)]
        pieces += [jnp.zeros((GAIN_LOW - GAIN_HIGH - PIECES, HEAD), F32)]
    pieces += [jnp.zeros((HEAD - 2 * GAIN_LOW + GAIN_HIGH, HEAD), F32)]
    packed[:, SMALL:] = (dlogits.astype(F32) + jnp.concatenate(pieces, axis=0).T).astype(BF)
    writer.send(packed.at[:, QKV:], outs[1].at[:, QKV:])
    if not last:
        reader.take(len(ins) - 2)
    for tile in tiles(WIDTH):
        if last:
            reader.take()
        wide = dot(packed[:, QKV:SMALL], w[tile, QKV:SMALL], 1, 1).astype(BF)
        for half in range(TILE // HEAD):
            datt[tile.start // HEAD + half] = wide[:, half * HEAD : (half + 1) * HEAD]
    reader.take(6)
    for k in range(KEY_VALUE_HEADS):
        heads = slice(k * GROUPS, (k + 1) * GROUPS)
        datt_k = datt[heads].reshape(GROUPS * ROWS, HEAD)
        p = probs[heads].reshape(GROUPS * ROWS, ROWS)
        dprobs = dot(datt_k, value[k], 1, 1)
        dvalue = dot(p.astype(BF), datt_k, 0, 0)
        dscores = (p * (dprobs - jnp.sum(dprobs * p, axis=-1, keepdims=True))).astype(BF)
        dqrot = dot(dscores, krot[k]) * SCALE
        dkrot = dot(dscores, qrot[heads].reshape(GROUPS * ROWS, HEAD), 0, 0) * SCALE
        for group in range(GROUPS):
            at = (k * GROUPS + group) * HEAD
            part = dqrot[group * ROWS : (group + 1) * ROWS]
            packed[:, at : at + HEAD] = turn(part, cosine[...], -sine[...]).astype(BF)
        at = Q_END + k * HEAD
        packed[:, at : at + HEAD] = turn(dkrot, cosine[...], -sine[...]).astype(BF)
        at = K_END + k * HEAD
        packed[:, at : at + HEAD] = dvalue.astype(BF)
    writer.send(packed.at[:, :QKV], outs[1].at[:, :QKV])
    parts = []
    for tile in tiles(WIDTH):
        reader.take()
        parts += [dot(packed[:, :QKV], w[tile, :QKV], 1, 1)]
    dacts = jnp.concatenate(parts, axis=1)
    reader.take()
    dx = dx_out[...] + norm_back(dacts, gain_attn, x_in[...].astype(F32))
    dx_out[...] = dx
    writer.send(dx_out, outs[0])
    if last:
        reader.take(2)
        dx_low = dx.astype(BF)
        both = dot(spread, jnp.concatenate(split(small_in[...]), axis=0), 1, 1).astype(BF)
        gates = jnp.concatenate([both[:, :ROWS] * wide_in[...], both[:, ROWS:] * wide_in[...]], axis=1)
        twice = jnp.concatenate([dx_low, dx_low], axis=0)
        for tile in tiles(WIDTH):
            rows[:, tile] = dot(gates, twice[:, tile]).astype(BF)
            writer.send(rows.at[:, tile], outs[2].at[:, tile])
    writer.finish()


def attn_backward(dx, back, x, kept, w, ring, tables, give, below, returned, order):
    last = below is not None
    outs = [(TOKENS, F32), ((ROWS, PACKED), BF)]
    if last:
        outs += [(WIDE, BF)]
    ins = [dx, back, w, tables[0], tables[1], give, kept["router"], kept["after"], x]
    ins += [kept[n] for n in ("probs", "qrot", "krot", "value")]
    ins += list(below) if last else [returned, *ring]
    scratch = [
        (TOKENS, dx.dtype), (back.shape, BF), ((WIDTH, PACKED), BF), (TABLE, F32), (TABLE, F32),
        ((ROWS, SLOTS), BF), (TABLE, F32), (TOKENS, F32), (TOKENS, x.dtype),
        ((QUERY_HEADS, ROWS, ROWS), F32), (HEADS, BF), (KEYS, BF), (KEYS, BF),
        ((SLOTS, ROWS), BF) if last else (WIDE, BF), (TABLE, F32), (HEADS, BF),
    ] + outs
    return run_attn(
        lambda *refs: attn_backward_kernel(last, *refs), "attn_backward", ins, order, outs, scratch,
        24 + WIDTH // TILE, 12, VMEM_BYTES,
    )


def gelu_parts(gate):
    square = gate * gate
    bend = jnp.tanh(GELU_A * gate * (1.0 + GELU_B * square))
    return bend, square


def gelu(gate):
    bend, _ = gelu_parts(gate)
    return 0.5 * gate * (1.0 + bend)


def gelu_both(gate):
    bend, square = gelu_parts(gate)
    slope = 0.5 * (1.0 + bend) + 0.5 * gate * (1.0 - bend * bend) * GELU_A * (
        1.0 + 3.0 * GELU_B * square
    )
    return 0.5 * gate * (1.0 + bend), slope


def weight_pairs(l, gate_hbm, up_hbm, down_hbm, gate_w, up_w, down_w):
    gate_up = []
    for at in range(0, FF, TILE):
        block = (slice(None), pl.ds(at, TILE))
        gate_up += [(gate_hbm.at[l, 0].at[block], gate_w.at[block])]
        gate_up += [(up_hbm.at[l, 0].at[block], up_w.at[block])]
    down = [(down_hbm.at[l, 0], down_w)]
    return gate_up, down


def run_experts(kernel, name, ins, order, outs, scratch, in_copies, flops):
    sd = jax.ShapeDtypeStruct
    count = len(ins) + len(order)

    def body(*refs):
        kernel(*refs[: len(ins)], *refs[count:])

    return pl.pallas_call(
        body,
        out_shape=[sd(shape, BF) for shape in outs],
        in_specs=specs_of(ins) + [ANY] * len(order),
        out_specs=[ANY] * len(outs),
        scratch_shapes=[pltpu.VMEM(shape, kind) for shape, kind in scratch]
        + [pltpu.SemaphoreType.DMA((in_copies,)), pltpu.SemaphoreType.DMA((40,))],
        compiler_params=pltpu.CompilerParams(vmem_limit_bytes=VMEM_BYTES),
        cost_estimate=pl.CostEstimate(
            flops=flops, bytes_accessed=20 << 20, transcendentals=SLOTS * FF
        ),
        name=name,
    )(*ins, *order)


def experts_forward_kernel(
    received_hbm, gate_hbm, up_hbm, down_hbm, act_hbm, slope_hbm, hidden_hbm, out_hbm,
    received, gate_w, up_w, down_w, act_s, slope_s, hidden, out, in_sems, out_sems,
):
    gate_up, down = weight_pairs(0, gate_hbm, up_hbm, down_hbm, gate_w, up_w, down_w)
    copies = start_all([(received_hbm, received)] + gate_up + down, in_sems)
    writer = Writer(out_sems)
    copies.pop(0).wait()
    for tile in tiles(FF):
        copies.pop(0).wait()
        copies.pop(0).wait()
        gate = dot(received[...], gate_w[:, tile])
        up = dot(received[...], up_w[:, tile])
        act, slope = gelu_both(gate)
        act_s[:, tile] = act.astype(BF)
        slope_s[:, tile] = (slope * up).astype(BF)
        hidden[:, tile] = (act * up).astype(BF)
    copies.pop(0).wait()
    writer.send(act_s, act_hbm)
    writer.send(slope_s, slope_hbm)
    writer.send(hidden, hidden_hbm)
    for tile in tiles(WIDTH):
        out[:, tile] = dot(hidden[...], down_w[:, tile]).astype(BF)
        writer.send(out.at[:, tile], out_hbm.at[:, tile])
    writer.finish()


EXPERT_SCRATCH = [((WIDTH, FF), BF), ((WIDTH, FF), BF), ((FF, WIDTH), BF)]


def experts_forward(received, weights, order):
    small = (SLOTS, FF)
    wide = (SLOTS, WIDTH)
    return run_experts(
        experts_forward_kernel, "experts_forward", [received, *weights], order,
        [small, small, small, wide],
        [(wide, BF)] + EXPERT_SCRATCH + [(small, BF)] * 3 + [(wide, BF)],
        8, 6 * SLOTS * WIDTH * FF,
    )


def back_tiles(dgate, dup, gate_w, up_w, back, back_hbm, writer):
    for tile in tiles(WIDTH):
        back[:, tile] = (
            dot(dgate[...], gate_w[tile], 1, 1) + dot(dup[...], up_w[tile], 1, 1)
        ).astype(BF)
        writer.send(back.at[:, tile], back_hbm.at[:, tile])


def experts_both_kernel(
    me, received_hbm, dx_hbm, w_hbm, gate_hbm, up_hbm, down_hbm,
    hidden_hbm, part0_hbm, part1_hbm, part2_hbm, dslot_hbm, dgate_hbm, dup_hbm, back_hbm,
    received, dx, small, gate_w, up_w, down_w, act_s, slope_s, hidden, part0, part1, part2, dslot, dgate, dup,
    back, in_sems, out_sems,
):
    gate_up, down = weight_pairs(1, gate_hbm, up_hbm, down_hbm, gate_w, up_w, down_w)
    pairs = [(received_hbm, received)] + gate_up
    pairs += [(w_hbm.at[:, pl.ds(SMALL, HEAD)], small), (dx_hbm, dx)] + down
    copies = start_all(pairs, in_sems)
    writer = Writer(out_sems)
    copies.pop(0).wait()
    for tile in tiles(FF):
        copies.pop(0).wait()
        copies.pop(0).wait()
        gate = dot(received[...], gate_w[:, tile])
        up = dot(received[...], up_w[:, tile])
        act, slope = gelu_both(gate)
        act_s[:, tile] = act
        slope_s[:, tile] = slope * up
        hidden[:, tile] = (act * up).astype(BF)
    for copy in copies:
        copy.wait()
    writer.send(hidden, hidden_hbm)
    shares = router_probs(received[...], small[...])
    lane = lax.broadcasted_iota(jnp.int32, shares.shape, 1)
    weight = jnp.sum(jnp.where(lane == me[0], shares, 0.0), axis=-1, keepdims=True)
    total = jnp.zeros((SLOTS, 1), F32)
    for tile in tiles(WIDTH):
        part = dot(hidden[...], down_w[:, tile]).astype(BF)
        for expert in range(EXPERTS):
            for p, target in enumerate((part0, part1, part2)):
                at = expert * CAP + p * PART_ROWS
                target[expert, :, tile] = part[at : at + PART_ROWS]
        wide = dx[:, tile].astype(F32)
        total += jnp.sum(wide * part.astype(F32), axis=-1, keepdims=True)
        dslot[:, tile] = (weight * wide).astype(BF)
    writer.send(part0, part0_hbm)
    writer.send(part1, part1_hbm)
    writer.send(part2, part2_hbm)
    writer.send(dslot, dslot_hbm)
    high, low = split(total)
    back[:, WIDTH:] = jnp.where(
        lane == 0, high.astype(F32), jnp.where(lane == 1, low.astype(F32), 0.0)
    ).astype(BF)
    writer.send(back.at[:, WIDTH:], back_hbm.at[:, WIDTH:])
    for tile in tiles(FF):
        dhidden = dot(dslot[...], down_w[tile], 1, 1)
        dgate[:, tile] = (dhidden * slope_s[:, tile]).astype(BF)
        dup[:, tile] = (dhidden * act_s[:, tile]).astype(BF)
    writer.send(dgate, dgate_hbm)
    writer.send(dup, dup_hbm)
    back_tiles(dgate, dup, gate_w, up_w, back, back_hbm, writer)
    writer.finish()


def experts_both(me, received, dx, w, weights, order):
    small = (SLOTS, FF)
    wide = (SLOTS, WIDTH)
    part = (EXPERTS, PART_ROWS, WIDTH)
    back = (SLOTS, WIDTH + HEAD)
    return run_experts(
        experts_both_kernel, "experts_both", [me, received, dx, w, *weights], order,
        [small, part, part, part, wide, small, small, back],
        [(wide, BF), (wide, BF), ((WIDTH, HEAD), BF)] + EXPERT_SCRATCH
        + [(small, F32), (small, F32), (small, BF), (part, BF), (part, BF), (part, BF),
           (wide, BF), (small, BF), (small, BF), (back, BF)],
        10, 12 * SLOTS * WIDTH * FF,
    )


def experts_backward_kernel(
    dslot_hbm, act_hbm, slope_hbm, gate_hbm, up_hbm, down_hbm, dgate_hbm, dup_hbm, back_hbm,
    dslot, act_s, slope_s, gate_w, up_w, down_w, dgate, dup, back, in_sems, out_sems,
):
    pairs = [(dslot_hbm, dslot)]
    for tile in tiles(FF):
        block = pl.ds(tile.start, TILE)
        pairs += [(down_hbm.at[0, 0].at[block], down_w.at[block])]
    pairs += [(slope_hbm, slope_s), (act_hbm, act_s)]
    for tile in tiles(WIDTH):
        block = pl.ds(tile.start, TILE)
        pairs += [(gate_hbm.at[0, 0].at[block], gate_w.at[block])]
        pairs += [(up_hbm.at[0, 0].at[block], up_w.at[block])]
    copies = start_all(pairs, in_sems)
    writer = Writer(out_sems)
    copies.pop(0).wait()
    dhidden = []
    for tile in tiles(FF):
        copies.pop(0).wait()
        dhidden += [dot(dslot[...], down_w[tile], 1, 1)]
    copies.pop(0).wait()
    copies.pop(0).wait()
    for tile, part in zip(tiles(FF), dhidden):
        dgate[:, tile] = (part * slope_s[:, tile].astype(F32)).astype(BF)
        dup[:, tile] = (part * act_s[:, tile].astype(F32)).astype(BF)
    writer.send(dgate, dgate_hbm)
    writer.send(dup, dup_hbm)
    for copy in copies:
        copy.wait()
    back_tiles(dgate, dup, gate_w, up_w, back, back_hbm, writer)
    writer.finish()


def experts_backward(dslot, act, slope, weights, order):
    small = (SLOTS, FF)
    wide = (SLOTS, WIDTH)
    return run_experts(
        experts_backward_kernel, "experts_backward", [dslot, act, slope, *weights], order,
        [small, small, wide],
        [(wide, BF), (small, BF), (small, BF)] + EXPERT_SCRATCH
        + [(small, BF), (small, BF), (wide, BF)],
        6 + 2 * WIDTH // TILE, 6 * SLOTS * WIDTH * FF,
    )


def expert_grads_kernel(received, dgate_pre, dup_pre, hidden, dslot, packed):
    gate = dot(received[...], dgate_pre[...], 0, 0).astype(BF)
    up = dot(received[...], dup_pre[...], 0, 0).astype(BF)
    down = dot(hidden[...], dslot[...], 0, 0).astype(BF)
    for part in range(DP // 2):
        packed[part, :SHARD, :FF] = gate[part * SHARD : (part + 1) * SHARD]
        packed[part, :SHARD, FF:] = up[part * SHARD : (part + 1) * SHARD]
        packed[part, SHARD:] = down[part * FF // DP : (part + 1) * FF // DP]


def expert_grads(received, dgate_pre, dup_pre, hidden, dslot):
    rows = SHARD + FF // DP
    whole = lambda width: pl.BlockSpec((SLOTS, width), lambda i: (0, 0))
    part = lambda width: pl.BlockSpec((SLOTS, width), lambda i: (0, i))
    return pl.pallas_call(
        expert_grads_kernel,
        grid=(2,),
        out_shape=jax.ShapeDtypeStruct((DP, rows, WIDTH), BF),
        in_specs=[part(WIDTH // 2), whole(FF), whole(FF), part(FF // 2), whole(WIDTH)],
        out_specs=pl.BlockSpec((DP // 2, rows, WIDTH), lambda i: (i, 0, 0)),
        compiler_params=pltpu.CompilerParams(vmem_limit_bytes=VMEM_BYTES),
        cost_estimate=pl.CostEstimate(
            flops=6 * SLOTS * WIDTH * FF, bytes_accessed=14 << 20, transcendentals=0
        ),
        name="expert_grads",
    )(received, dgate_pre, dup_pre, hidden, dslot).reshape(DP * rows, WIDTH)


def pack_kernel(
    l, query_hbm, key_hbm, value_hbm, out_hbm, router_hbm, gain_attn, gain_ffn, packed_hbm, *rest
):
    if l == 0:
        out_copy, packed, out, router, sems, out_sems = rest
    else:
        packed, router, sems, out_sems = rest
        out = packed.at[:, pl.ds(QKV, WIDTH)]
    pairs = [
        (router_hbm.at[l], router),
        (query_hbm.at[l], packed.at[:, pl.ds(0, Q_END)]),
        (key_hbm.at[l], packed.at[:, pl.ds(Q_END, K_END - Q_END)]),
        (value_hbm.at[l], packed.at[:, pl.ds(K_END, QKV - K_END)]),
        (out_hbm.at[l], out),
    ]
    reader, writer = Reader(sems, pairs), Writer(out_sems)
    reader.take()
    small = [router[...].astype(F32), gain_attn[l : l + 1].astype(F32)]
    small += [gain_ffn[l : l + 1].astype(F32), jnp.zeros((HEAD - EXPERTS - 2, SHARD), F32)]
    small = jnp.concatenate(small, axis=0)
    small = jnp.concatenate([small, jnp.zeros((HEAD, TILE - SHARD), F32)], axis=1).T
    packed[:, packed.shape[1] - HEAD :] = small[:SHARD].astype(BF)
    reader.take(3)
    if l == 0:
        writer.send(packed, packed_hbm)
        reader.take()
        writer.send(out, out_copy)
    else:
        reader.take()
        writer.send(packed, packed_hbm)
    writer.finish()


def pack(l, query, key, value, out, router, gain_attn, gain_ffn):
    sd = jax.ShapeDtypeStruct
    vmem = pl.BlockSpec(memory_space=pltpu.VMEM)
    packed = (SHARD, QKV + HEAD) if l == 0 else (SHARD, PACKED)
    outs = [packed] + [(SHARD, WIDTH)] * (l == 0)
    return pl.pallas_call(
        lambda *refs: pack_kernel(l, *refs),
        out_shape=[sd(shape, BF) for shape in outs],
        in_specs=[ANY] * 5 + [vmem] * 2,
        out_specs=[ANY] * len(outs),
        scratch_shapes=[pltpu.VMEM(shape, BF) for shape in outs]
        + [pltpu.VMEM((EXPERTS, SHARD), BF)]
        + [pltpu.SemaphoreType.DMA((5,)), pltpu.SemaphoreType.DMA((2,))],
        compiler_params=pltpu.CompilerParams(vmem_limit_bytes=VMEM_BYTES),
        name="pack",
    )(query, key, value, out, router.transpose(0, 2, 1), gain_attn, gain_ffn)


def ring(block):
    def move(values, step):
        return lax.ppermute(values, "dp", [(i, (i + step) % DP) for i in range(DP)])

    half = block.shape[0] // 2
    previous, following = move(block, 2), move(block, -2)
    far = [move(previous[:half], 2), move(following[half:], -2)]
    mine = [block, previous, following, *far]
    swap = [(i, i ^ 1) for i in range(DP)]
    return mine + [lax.ppermute(values, "dp", swap) for values in mine]


def seq_tables(counts):
    ends = jnp.cumsum(counts)
    starts = ends - counts
    place = jnp.arange(ROWS, dtype=jnp.int32)
    member = (place[:, None] >= starts[None, :]) & (place[:, None] < ends[None, :])
    index = jnp.arange(counts.shape[0], dtype=jnp.int32)
    segment = jnp.sum(jnp.where(member, index[None, :], 0), axis=1)
    position = place - jnp.sum(jnp.where(member, starts[None, :], 0), axis=1)
    allowed = (segment[:, None] == segment[None, :]) & (place[:, None] >= place[None, :])
    freqs = ROPE_BASE ** (-2.0 * jnp.arange(HEAD // 2, dtype=F32) / HEAD)
    angle = position.astype(F32)[:, None] * freqs[None, :]
    cosine, sine = jnp.cos(angle), jnp.sin(angle)
    return (
        jnp.concatenate([cosine, cosine], axis=1),
        jnp.concatenate([-sine, sine], axis=1),
        allowed.astype(F32),
    )


def slot_matrix(choices, in_parts=False):
    experts = jnp.arange(EXPERTS, dtype=jnp.int32)
    member = jnp.any(choices[:, :, None] == experts[None, None, :], axis=1).astype(BF)
    row = lax.broadcasted_iota(jnp.int32, (ROWS, ROWS), 0)
    column = lax.broadcasted_iota(jnp.int32, (ROWS, ROWS), 1)
    rank = dot((column < row).astype(BF), member).astype(BF)
    slot = jnp.arange(SLOTS, dtype=jnp.int32)[None, :]
    if in_parts:
        owner, place = slot % PART // PART_ROWS, slot // PART * PART_ROWS + slot % PART_ROWS
    else:
        owner, place = slot // CAP, slot % CAP
    expand = (owner == experts[:, None]).astype(BF)
    return ((dot(member, expand) > 0.5) & (dot(rank, expand) == place.astype(F32))).astype(BF)


def exchange(rows):
    width = rows.shape[-1]
    moved = lax.all_to_all(
        rows.reshape(EXPERTS, -1, width), "expert", split_axis=0, concat_axis=0, tiled=True
    )
    return moved.reshape(-1, width)


def after(values, *order):
    return pl.pallas_call(
        lambda *refs: None,
        out_shape=jax.ShapeDtypeStruct(values.shape, values.dtype),
        in_specs=[ANY] * (1 + len(order)),
        out_specs=ANY,
        input_output_aliases={0: 0},
        name="after",
    )(values, *order)


def turn_columns_kernel(me, columns_hbm, turned_hbm, columns, turned, in_sems, out_sems):
    base = me[0] * SHARD // HEAD * HEAD
    pairs = []
    for i in range(3):
        at = pl.multiple_of(base + i * WIDTH, HEAD)
        pairs += [(columns_hbm.at[:, pl.ds(at, TILE)], columns.at[:, pl.ds(i * TILE, TILE)])]
    reader, writer = Reader(in_sems, pairs), Writer(out_sems)
    for i in range(3):
        reader.take()
        turned[i] = columns[:, i * TILE : (i + 1) * TILE].T
        writer.send(turned.at[i], turned_hbm.at[i])
    writer.finish()


def turn_columns(me, columns):
    tokens = DP * ROWS
    return pl.pallas_call(
        turn_columns_kernel,
        out_shape=jax.ShapeDtypeStruct((3, TILE, tokens), BF),
        in_specs=[pl.BlockSpec(memory_space=pltpu.SMEM), ANY],
        out_specs=ANY,
        scratch_shapes=[
            pltpu.VMEM((tokens, 3 * TILE), BF),
            pltpu.VMEM((3, TILE, tokens), BF),
            pltpu.SemaphoreType.DMA((3,)),
            pltpu.SemaphoreType.DMA((3,)),
        ],
        compiler_params=pltpu.CompilerParams(vmem_limit_bytes=VMEM_BYTES),
        cost_estimate=pl.CostEstimate(flops=0, bytes_accessed=4 << 20, transcendentals=0),
        name="turn_columns",
    )(me, columns)


def dense_grads_kernel(me, turned_hbm, factors_hbm, pieces_hbm, turned, factors, total, pieces,
                       in_sems, out_sems):
    start = me[0] * SHARD
    shift = start % HEAD
    base = start - shift
    copies = Writer(out_sems)
    pairs = [(turned_hbm, turned)]
    for at in range(0, PACKED, CHUNK):
        block = (slice(None), pl.ds(at, min(CHUNK, PACKED - at)))
        pairs += [(factors_hbm.at[block], factors.at[block])]
    reader = Reader(in_sems, pairs)
    reader.take()

    def put(chunk, values):
        pieces[chunk] = values.astype(BF)
        copies.send(pieces.at[chunk], pieces_hbm.at[chunk])

    for chunk in range(SMALL // CHUNK):
        reader.take()
        total[chunk % 2] = dot(
            turned[0 if chunk < QKV // CHUNK else 1],
            factors[:, chunk * CHUNK : (chunk + 1) * CHUNK],
        )
        put(chunk, total[chunk % 2, pl.ds(pl.multiple_of(shift, 64), SHARD), :])
    reader.take()
    ends = jnp.zeros((ROWS, HEAD), F32)
    for source in range(DP):
        ends += factors[source * ROWS : (source + 1) * ROWS, SMALL:].astype(F32)
    lane = lax.broadcasted_iota(jnp.int32, (ROWS, HEAD), 1)

    def gain_piece(piece):
        held = (lane == piece + GAIN_HIGH) | (lane == piece + GAIN_LOW)
        return jnp.sum(jnp.where(held, ends, 0.0), axis=1, keepdims=True)

    first, second = gain_piece(base // HEAD), gain_piece(base // HEAD + 1)
    gain = jnp.where(
        shift == 0,
        jnp.concatenate([first, second[: SHARD - ROWS]], axis=0),
        jnp.concatenate([first[ROWS // 2 :], second], axis=0),
    )
    gain_high, gain_low = split(gain)
    total[0, :, :HEAD] = dot(turned[2], factors[:, SMALL:])
    router = total[0, pl.ds(pl.multiple_of(shift, 64), SHARD), :HEAD]
    lane = lax.broadcasted_iota(jnp.int32, (SHARD, HEAD), 1)
    router = jnp.where(lane < EXPERTS, router, 0.0)
    router = jnp.where(lane == EXPERTS, gain_high.astype(F32), router)
    router = jnp.where(lane == EXPERTS + 1, gain_low.astype(F32), router)
    put(CHUNKS - 2, jnp.concatenate([router, jnp.zeros_like(router)], axis=1))
    put(CHUNKS - 1, jnp.zeros((SHARD, CHUNK), F32))
    copies.finish()


def dense_grads(me, turned, factors, order):
    tokens = DP * ROWS

    def body(*refs):
        dense_grads_kernel(*refs[:3], *refs[3 + len(order) :])

    return pl.pallas_call(
        body,
        out_shape=jax.ShapeDtypeStruct((CHUNKS, SHARD, CHUNK), BF),
        in_specs=[pl.BlockSpec(memory_space=pltpu.SMEM)] + [ANY] * (2 + len(order)),
        out_specs=ANY,
        scratch_shapes=[
            pltpu.VMEM((3, TILE, tokens), BF),
            pltpu.VMEM((tokens, PACKED), BF),
            pltpu.VMEM((2, TILE, CHUNK), F32),
            pltpu.VMEM((CHUNKS, SHARD, CHUNK), BF),
            pltpu.SemaphoreType.DMA((1 + CHUNKS,)),
            pltpu.SemaphoreType.DMA((CHUNKS,)),
        ],
        compiler_params=pltpu.CompilerParams(vmem_limit_bytes=VMEM_BYTES),
        cost_estimate=pl.CostEstimate(
            flops=2 * tokens * TILE * PACKED, bytes_accessed=10 << 20, transcendentals=0
        ),
        name="dense_grads",
    )(me, turned, factors, *order)


def to_expert_peers(pieces):
    return lax.all_to_all(pieces, "expert", split_axis=0, concat_axis=0, tiled=True)


def sum_pieces_kernel(pieces_hbm, out_hbm, pieces, out, in_sems, out_sems):
    half = CHUNKS // 2
    pairs = []
    for at in (0, half):
        block = pl.ds(at, half)
        pairs += [(pieces_hbm.at[block, :, pl.ds(0, CHUNK)], pieces.at[block])]
    reader, writer = Reader(in_sems, pairs), Writer(out_sems)
    reader.take()
    total = pieces[0].astype(F32)
    for i in range(1, half):
        total += pieces[i].astype(F32)
    reader.take()
    for i in range(half, CHUNKS):
        total += pieces[i].astype(F32)
    out[...] = total.astype(BF)
    if len(out_hbm.shape) == 3:
        for i in range(CHUNKS):
            writer.send(out, out_hbm.at[i])
    else:
        writer.send(out, out_hbm)
    writer.finish()


def sum_pieces(pieces, copies):
    return pl.pallas_call(
        sum_pieces_kernel,
        out_shape=jax.ShapeDtypeStruct((copies,) * (copies > 1) + (SHARD, CHUNK), BF),
        in_specs=[ANY],
        out_specs=ANY,
        scratch_shapes=[
            pltpu.VMEM((CHUNKS, SHARD, CHUNK), BF),
            pltpu.VMEM((SHARD, CHUNK), BF),
            pltpu.SemaphoreType.DMA((2,)),
            pltpu.SemaphoreType.DMA((CHUNKS,)),
        ],
        compiler_params=pltpu.CompilerParams(vmem_limit_bytes=VMEM_BYTES),
        name="sum_pieces",
    )(pieces)


def finish_kernel(l, refs):
    (pieces, w_query, key_projection, value_projection, norm_attn), refs = refs[:5], refs[5:]
    if l == 0:
        ends_above, refs = refs[0], refs[5:]
        (query_hbm, key_hbm, value_hbm, out_hbm, gain_attn, gain_ffn, router) = refs[:7]
        query, key, value, out, sems = refs[7:]
    else:
        query_hbm, key_hbm, value_hbm, out_hbm, ends_out, query, key, value, out, sems = refs
    writer = Writer(sems)
    rows = jnp.zeros((SHARD, 1), F32)
    for chunk in range(SMALL // CHUNK):
        part = pieces[chunk].astype(F32)
        lanes = slice(chunk * CHUNK, (chunk + 1) * CHUNK)
        if chunk < Q_END // CHUNK:
            query[:, lanes] = part
            weight = w_query[l, :, lanes]
        elif chunk == Q_END // CHUNK:
            key[...] = part
            weight = key_projection[l]
            writer.send(query, query_hbm.at[l])
            writer.send(key, key_hbm.at[l])
        elif chunk < QKV // CHUNK:
            value[...] = part
            weight = value_projection[l]
            writer.send(value, value_hbm.at[l])
        else:
            out[:, lanes.start - QKV : lanes.stop - QKV] = part
            continue
        rows += jnp.sum(part * weight.astype(F32), axis=1, keepdims=True)
    writer.send(out, out_hbm.at[l])
    ends = pieces[CHUNKS - 2, :, :HEAD].astype(F32)
    ffn = ends[:, EXPERTS : EXPERTS + 1] + ends[:, EXPERTS + 1 : EXPERTS + 2]
    lane = lax.broadcasted_iota(jnp.int32, (SHARD, HEAD), 1)
    ends = jnp.where(lane == EXPERTS, rows, jnp.where(lane == EXPERTS + 1, ffn, ends))
    if l > 0:
        ends_out[...] = ends
    else:
        for layer, part in enumerate((ends, ends_above[...])):
            wide = jnp.concatenate([part, jnp.zeros((TILE - SHARD, HEAD), F32)], axis=0).T
            router[layer] = wide[:EXPERTS, :SHARD]
            gain = norm_attn[layer : layer + 1].astype(F32)
            gain_attn[layer : layer + 1] = wide[EXPERTS : EXPERTS + 1, :SHARD] / gain
            gain_ffn[layer : layer + 1] = wide[EXPERTS + 1 : EXPERTS + 2, :SHARD]
    writer.finish()


def finish(l, pieces, weights, norm_attn, above):
    sd = jax.ShapeDtypeStruct
    vmem = pl.BlockSpec(memory_space=pltpu.VMEM)
    keys = (SHARD, KEY_VALUE_HEADS * HEAD)
    slabs = [(SHARD, Q_END), keys, keys, (SHARD, WIDTH)]
    outs = [sd((LAYERS,) + shape, F32) for shape in slabs]
    if above is None:
        outs += [sd((SHARD, HEAD), F32)]
        ins, in_specs, aliases = [], [], {}
    else:
        outs += [sd((LAYERS, SHARD), F32)] * 2 + [sd((LAYERS, EXPERTS, SHARD), F32)]
        ins, in_specs = [above[4], *above[:4]], [vmem] + [ANY] * 4
        aliases = {6 + i: i for i in range(4)}
    return pl.pallas_call(
        lambda *refs: finish_kernel(l, refs),
        out_shape=outs,
        in_specs=[vmem] * 5 + in_specs,
        out_specs=[ANY] * 4 + [vmem] * (len(outs) - 4),
        input_output_aliases=aliases,
        scratch_shapes=[pltpu.VMEM(shape, F32) for shape in slabs]
        + [pltpu.SemaphoreType.DMA((4,))],
        compiler_params=pltpu.CompilerParams(vmem_limit_bytes=VMEM_BYTES),
        name="finish",
    )(pieces, *weights, norm_attn, *ins)


def finish_experts_kernel(shares0, shares1, gate, up, down):
    for l, shares in enumerate((shares0, shares1)):
        gate[l, 0] = shares[:SHARD, :FF].astype(F32)
        up[l, 0] = shares[:SHARD, FF:].astype(F32)
        down[l, 0] = shares[SHARD:].astype(F32)


def finish_experts(shares0, shares1):
    sd = jax.ShapeDtypeStruct
    vmem = pl.BlockSpec(memory_space=pltpu.VMEM)
    return pl.pallas_call(
        finish_experts_kernel,
        out_shape=[
            sd((LAYERS, 1, SHARD, FF), F32), sd((LAYERS, 1, SHARD, FF), F32),
            sd((LAYERS, 1, FF // DP, WIDTH), F32),
        ],
        in_specs=[vmem] * 2,
        out_specs=[vmem] * 3,
        compiler_params=pltpu.CompilerParams(vmem_limit_bytes=VMEM_BYTES),
        name="finish_experts",
    )(shares0, shares1)


def mixed_kernel(x_hbm, high, low, part0, part1, part2, out, x, gates, returned, sems):
    pairs = [(high, gates.at[:ROWS]), (low, gates.at[ROWS:]), (x_hbm, x)]
    for p, part in enumerate((part0, part1, part2)):
        pairs += [(part, returned.at[pl.ds(p * PART, PART)])]
    Reader(sems, pairs).take(len(pairs))
    for tile in tiles(WIDTH):
        both = dot(gates[...], returned[:, tile])
        out[:, tile] = (x[:, tile] + both[:ROWS] + both[ROWS:]).astype(BF)


def mixed_rows(x, high, low, parts):
    return pl.pallas_call(
        mixed_kernel,
        out_shape=jax.ShapeDtypeStruct(TOKENS, BF),
        in_specs=[ANY] * 6,
        out_specs=pl.BlockSpec(memory_space=pltpu.VMEM),
        scratch_shapes=[
            pltpu.VMEM(TOKENS, F32),
            pltpu.VMEM((2 * ROWS, SLOTS), BF),
            pltpu.VMEM(WIDE, BF),
            pltpu.SemaphoreType.DMA((6,)),
        ],
        compiler_params=pltpu.CompilerParams(vmem_limit_bytes=VMEM_BYTES),
        name="mixed",
    )(x, high, low, *parts)


def local(
    tokens, cotangent, lengths, routes, norm_attn, w_query, key_projection, value_projection,
    w_out, norm_ffn, w_router, w_gate, w_up, w_down,
):
    me_dp = lax.axis_index("dp").astype(jnp.int32).reshape(1)
    me_expert = lax.axis_index("expert").astype(jnp.int32).reshape(1)
    tables = seq_tables(lengths[0])
    give = [slot_matrix(routes[l]) for l in range(LAYERS)]
    take = [g.T for g in give]
    give_parts = slot_matrix(routes[1], True)
    experts = (w_gate, w_up, w_down)

    def gather(values):
        return lax.all_gather(values, "dp", axis=0, tiled=True)

    weights = (w_query, key_projection, value_projection, w_out, w_router, norm_attn, norm_ffn)
    shard0, out_shard0 = pack(0, *weights)
    w = [gather(shard0), gather(pack(1, *weights)[0])]
    out_ring = [me_dp, *ring(out_shard0)]

    dx_rows = exchange(dot(take[1], cotangent).astype(BF))

    kept0 = attn_forward(
        tokens, None, w[0], out_ring, tables, take[0], give[0],
        (dx_rows, give[1], give_parts, me_expert),
    )
    received0 = exchange(kept0["rows"])
    act0, slope0, hidden0, out0 = experts_forward(received0, experts, ())
    returned0 = exchange(out0)
    columns0 = gather(kept0["columns"])

    kept1 = attn_forward(
        kept0["after"], (kept0["high"], kept0["low"], returned0), w[1], None, tables, take[1],
        give_parts, (),
    )
    received1 = exchange(kept1["rows"])
    columns1 = gather(kept1["columns"])
    hidden1, *parts, dslot1, dgate1, dup1, back1 = experts_both(
        me_expert, received1, dx_rows, w[1], experts, ()
    )
    back1 = exchange(back1)
    grads1 = expert_grads(received1, dgate1, dup1, hidden1, dslot1)
    turned0, turned1 = turn_columns(me_dp, columns0), turn_columns(me_dp, columns1)
    parts[0] = exchange(after(parts[0], grads1, turned0, turned1))

    dx0, packed1, rows0 = attn_backward(
        cotangent, back1, kept1["x"], kept1, w[1], None, tables, give[1], (take[0], kept0["router"]),
        None, (),
    )
    packed1 = after(packed1, parts[0])
    dslot0 = exchange(rows0)
    factors1 = gather(packed1)
    shares1 = lax.psum_scatter(after(grads1, packed1), "dp", scatter_dimension=0, tiled=True)
    dgate0, dup0, back0 = experts_backward(dslot0, act0, slope0, experts, ())
    back0 = exchange(back0)
    grads0 = expert_grads(received0, dgate0, dup0, hidden0, dslot0)
    parts[1] = exchange(parts[1])
    pieces1 = dense_grads(me_dp, turned1, factors1, (parts[1],))
    parts[2] = exchange(after(parts[2], grads0, pieces1))
    grad_tokens, packed0 = attn_backward(
        dx0, back0, tokens, kept0, w[0], out_ring, tables, give[0], None, returned0,
        (shares1,),
    )
    factors0 = gather(after(packed0, parts[2]))
    summed1 = sum_pieces(to_expert_peers(pieces1), CHUNKS)
    shares0 = lax.psum_scatter(after(grads0, summed1), "dp", scatter_dimension=0, tiled=True)
    mixed = mixed_rows(kept1["after"], kept1["high"], kept1["low"], parts)
    pieces1 = to_expert_peers(summed1)
    pieces0 = dense_grads(me_dp, turned0, factors0, ())
    pieces0 = to_expert_peers(after(pieces0, pieces1))
    pieces0 = to_expert_peers(sum_pieces(pieces0, CHUNKS))

    dense = (w_query, key_projection, value_projection)
    above = finish(1, pieces1, dense, norm_attn, None)
    query, key, value, out, gain_attn, gain_ffn, router = finish(
        0, pieces0, dense, norm_attn, above
    )
    gate, up, down = finish_experts(shares0, shares1)
    return (
        mixed, grad_tokens, gain_attn, query, key, value, out, gain_ffn,
        router.transpose(0, 2, 1), gate, up, down,
    )


def solution(mesh):
    placed = (
        P(("dp", "expert"), None),
        P(("dp", "expert"), None),
        P(("dp", "expert"), None),
        P(None, ("dp", "expert"), None),
        P(None, "dp"),
        P(None, "dp", None),
        P(None, "dp", None),
        P(None, "dp", None),
        P(None, "dp", None),
        P(None, "dp"),
        P(None, "dp", None),
        P(None, "expert", None, None),
        P(None, "expert", None, None),
        P(None, "expert", None, None),
    )
    return jax.shard_map(
        local,
        mesh=mesh,
        in_specs=placed,
        out_specs=(
            P(("dp", "expert"), None),
            P(("dp", "expert"), None),
            P(None, "dp"),
            P(None, "dp", None),
            P(None, "dp", None),
            P(None, "dp", None),
            P(None, "dp", None),
            P(None, "dp"),
            P(None, "dp", None),
            P(None, "expert", "dp", None),
            P(None, "expert", "dp", None),
            P(None, "expert", "dp", None),
        ),
        check_vma=False,
    )
```

```python
import jax
import jax.numpy as jnp
from jax import lax
from jax.experimental import pallas as pl
from jax.experimental.pallas import tpu as pltpu
from jax.sharding import PartitionSpec as P

QUERY_HEADS = 12
KEY_VALUE_HEADS = 2
GROUPS = QUERY_HEADS // KEY_VALUE_HEADS
HEAD = 128
LAYERS = 2
WIDTH = 1536
FF = 768
ROWS = 128
EXPERTS = 16
CAP = 48
SLOTS = EXPERTS * CAP
DP = 8
SHARD = WIDTH // DP
Q_END = QUERY_HEADS * HEAD
K_END = Q_END + KEY_VALUE_HEADS * HEAD
QKV = K_END + KEY_VALUE_HEADS * HEAD
SMALL = QKV + WIDTH
PACKED = SMALL + HEAD
GAIN_ATTN, GAIN_FFN = 16, 17
GAIN_HIGH, GAIN_LOW = 16, 32
PIECES = WIDTH // HEAD
TILE = 256
PARTS = 3
PART = SLOTS // PARTS
PART_ROWS = CAP // PARTS
CHUNKS, CHUNK = 16, 256
COLUMNS = 3 * WIDTH
EPSILON = 1e-06
ROPE_BASE = 1000000.0
SCALE = HEAD ** (-0.5)
GELU_A = 0.7978845608028654
GELU_B = 0.044715
VMEM_BYTES = 56 << 20
BF = jnp.bfloat16
F32 = jnp.float32
ANY = pl.BlockSpec(memory_space=pl.ANY)


def dot(left, right, left_dim=1, right_dim=0):
    return lax.dot_general(
        left, right, (((left_dim,), (right_dim,)), ((), ())), preferred_element_type=F32
    )


def split(values):
    high = values.astype(BF)
    return high, (values - high.astype(F32)).astype(BF)


def unit(values):
    return lax.rsqrt(jnp.mean(values * values, axis=-1, keepdims=True) + EPSILON)


def turn(values, cosine, sine):
    return values * cosine + pltpu.roll(values, HEAD // 2, 1) * sine


def expert_lanes(transposed=False, in_parts=False):
    shape = (SLOTS, HEAD) if transposed else (HEAD, SLOTS)
    slot = lax.broadcasted_iota(jnp.int32, shape, 0 if transposed else 1)
    expert = lax.broadcasted_iota(jnp.int32, shape, 1 if transposed else 0)
    if in_parts:
        held = ((slot & (PART - 1)) >> 4) == expert
    else:
        held = (slot >= expert * CAP) & (slot < expert * CAP + CAP)
    return held.astype(F32).astype(BF)


def gain_rows(small):
    row = lax.broadcasted_iota(jnp.int32, (8, HEAD), 0)
    lane = lax.broadcasted_iota(jnp.int32, (8, HEAD), 1)
    pick = ((lane == row + GAIN_ATTN) & (row < 2)).astype(F32).astype(BF)
    rows = dot(pick, small, 1, 1)
    return rows[0:1], rows[1:2]


def router_probs(rows, small):
    logits = dot(rows, small)
    lane = lax.broadcasted_iota(jnp.int32, logits.shape, 1)
    logits = jnp.where(lane < EXPERTS, logits, -1e30)
    powers = jnp.exp(logits - jnp.max(logits, axis=-1, keepdims=True))
    return powers / jnp.sum(powers, axis=-1, keepdims=True)


def start_all(pairs, sems):
    copies = [
        pltpu.make_async_copy(source, target, sems.at[i]) for i, (source, target) in enumerate(pairs)
    ]
    for copy in copies:
        copy.start()
    return copies


class Writer:
    def __init__(self, sems):
        self.sems, self.copies = sems, []

    def send(self, source, target):
        copy = pltpu.make_async_copy(source, target, self.sems.at[len(self.copies)])
        copy.start()
        self.copies.append(copy)

    def finish(self):
        for copy in self.copies:
            copy.wait()


class Reader:
    def __init__(self, sems, pairs):
        self.copies = start_all(pairs, sems)

    def take(self, count=1):
        for _ in range(count):
            self.copies.pop(0).wait()


def tiles(width):
    return [slice(at, at + TILE) for at in range(0, width, TILE)]


def small_block(w_hbm, w):
    last = w_hbm.shape[1] - HEAD
    return (w_hbm.at[:, pl.ds(last, HEAD)], w.at[:, pl.ds(SMALL, HEAD)])


def column_block(w_hbm, w, at):
    return (w_hbm.at[:, pl.ds(at, TILE)], w.at[:, pl.ds(at, TILE)])


def ring_blocks(me, blocks, w):
    pairs = []
    for core in range(2):
        start = me if core == 0 else me + 1 - 2 * (me % 2)
        for block, step in enumerate((0, DP - 2, 2, 4, 4)):
            ref = blocks[core * 5 + block]
            at = (start + step) % DP * SHARD + (SHARD // 2 if block == 4 else 0)
            at = pl.multiple_of(at, SHARD // 2)
            pairs += [(ref, w.at[pl.ds(at, ref.shape[0]), pl.ds(QKV, WIDTH)])]
    return pairs


def attn_forward_kernel(first, ins, outs, scratch):
    (x_hbm, w_hbm, cosine_hbm, sine_hbm, allowed_hbm, take_hbm, give_hbm), ins = ins[:7], ins[7:]
    (columns_hbm, qrot_hbm, krot_hbm, value_hbm, probs_hbm, after_hbm, router_hbm, high_hbm, low_hbm,
     rows_hbm), outs = outs[:10], outs[10:]
    (x_in, w, cosine, sine, allowed, take, give, returned, gates, x, columns, qrot, krot, value, probs,
     after, router, high, low, rows, in_sems, out_sems) = scratch
    acts = columns.at[:, :WIDTH]
    attended = columns.at[:, WIDTH : 2 * WIDTH]
    acts_two = columns.at[:, 2 * WIDTH :]
    pairs = []
    if first:
        out_pairs = ring_blocks(ins[0][0], ins[1:], w)
    else:
        out_pairs = [column_block(w_hbm, w, at) for at in range(QKV, SMALL, TILE)]
        high_below, low_below, returned_hbm = ins
        pairs += [(high_below, gates.at[:ROWS]), (low_below, gates.at[ROWS:])]
        pairs += [(returned_hbm, returned)]
    pairs += [(x_hbm, x_in), small_block(w_hbm, w)]
    pairs += [column_block(w_hbm, w, at) for at in range(0, QKV, TILE)]
    pairs += [(cosine_hbm, cosine), (sine_hbm, sine), (allowed_hbm, allowed)]
    pairs += out_pairs + [(take_hbm, take), (give_hbm, give)]
    reader, writer = Reader(in_sems, pairs), Writer(out_sems)
    if first:
        reader.take()
        x[...] = x_in[...].astype(F32)
    else:
        reader.take(4)
        for tile in tiles(WIDTH):
            both = dot(gates[...], returned[:, tile])
            x[:, tile] = x_in[:, tile] + both[:ROWS] + both[ROWS:]
        writer.send(x, outs[0])
    reader.take()
    small = w[:, SMALL:]
    gain_attn, gain_ffn = gain_rows(small)
    total = x[...]
    acts[...] = (total * unit(total) * gain_attn).astype(BF)
    wide = []
    for tile in tiles(QKV):
        reader.take()
        wide += [dot(acts[...], w[:, tile])]
    reader.take(3)
    for tile in range(QKV // TILE):
        for half in range(TILE // HEAD):
            head = tile * (TILE // HEAD) + half
            part = wide[tile][:, half * HEAD : (half + 1) * HEAD]
            if head < QUERY_HEADS:
                qrot[head] = turn(part, cosine[...], sine[...]).astype(BF)
            elif head < QUERY_HEADS + KEY_VALUE_HEADS:
                krot[head - QUERY_HEADS] = turn(part, cosine[...], sine[...]).astype(BF)
            else:
                value[head - QUERY_HEADS - KEY_VALUE_HEADS] = part.astype(BF)
    writer.send(qrot, qrot_hbm)
    writer.send(krot, krot_hbm)
    writer.send(value, value_hbm)
    open_scores = (allowed[...] > 0.5)[None]
    for k in range(KEY_VALUE_HEADS):
        heads = slice(k * GROUPS, (k + 1) * GROUPS)
        scores = dot(qrot[heads].reshape(GROUPS * ROWS, HEAD), krot[k], 1, 1) * SCALE
        scores = jnp.where(open_scores, scores.reshape(GROUPS, ROWS, ROWS), -1000000000.0)
        powers = jnp.exp(scores - jnp.max(scores, axis=-1, keepdims=True))
        shares = powers / jnp.sum(powers, axis=-1, keepdims=True)
        probs[heads] = shares
        mixed = dot(shares.astype(BF).reshape(GROUPS * ROWS, ROWS), value[k]).astype(BF)
        for group in range(GROUPS):
            at = (k * GROUPS + group) * HEAD
            attended[:, at : at + HEAD] = mixed[group * ROWS : (group + 1) * ROWS]
    writer.send(probs, probs_hbm)
    if first:
        reader.take(len(out_pairs))
    for tile in tiles(WIDTH):
        if not first:
            reader.take()
        after[:, tile] = x[:, tile] + dot(
            attended[...], w[:, QKV + tile.start : QKV + tile.stop]
        )
    writer.send(after, after_hbm)
    total = after[...]
    acts_two[...] = (total * unit(total) * gain_ffn).astype(BF)
    writer.send(columns, columns_hbm)
    reader.take(2)
    for tile in tiles(WIDTH):
        rows[:, tile] = dot(take[...], acts_two[:, tile]).astype(BF)
        writer.send(rows.at[:, tile], rows_hbm.at[:, tile])
    shares = router_probs(acts_two[...], small)
    router[...] = shares
    spread = expert_lanes(in_parts=not first)
    both = dot(jnp.concatenate(split(shares), axis=0), spread).astype(BF)
    high[...] = both[:ROWS] * give[...]
    low[...] = both[ROWS:] * give[...]
    writer.send(router, router_hbm)
    writer.send(high, high_hbm)
    writer.send(low, low_hbm)
    writer.finish()


HEADS = (QUERY_HEADS, ROWS, HEAD)
KEYS = (KEY_VALUE_HEADS, ROWS, HEAD)
TABLE = (ROWS, HEAD)
TOKENS = (ROWS, WIDTH)
WIDE = (SLOTS, WIDTH)


def specs_of(ins):
    return [pl.BlockSpec(memory_space=pltpu.SMEM if a.dtype == jnp.int32 else pl.ANY) for a in ins]


def run_attn(kernel, name, ins, order, outs, scratch, in_copies, out_copies, vmem):
    sd = jax.ShapeDtypeStruct

    def body(*refs):
        first_out = len(ins) + len(order)
        first_scratch = first_out + len(outs)
        kernel(refs[: len(ins)], refs[first_out:first_scratch], refs[first_scratch:])

    return pl.pallas_call(
        body,
        out_shape=[sd(shape, kind) for shape, kind in outs],
        in_specs=specs_of(ins) + [ANY] * len(order),
        out_specs=[ANY] * len(outs),
        scratch_shapes=[pltpu.VMEM(shape, kind) for shape, kind in scratch]
        + [pltpu.SemaphoreType.DMA((in_copies,)), pltpu.SemaphoreType.DMA((out_copies,))],
        compiler_params=pltpu.CompilerParams(vmem_limit_bytes=vmem),
        cost_estimate=pl.CostEstimate(
            flops=2 * ROWS * WIDTH * PACKED, bytes_accessed=20 << 20, transcendentals=200000
        ),
        name=name,
    )(*ins, *order)


def attn_forward(x, combine, w, ring, tables, take, give, order):
    first = combine is None
    outs = [
        ((ROWS, COLUMNS), BF), (HEADS, BF), (KEYS, BF), (KEYS, BF), ((QUERY_HEADS, ROWS, ROWS), F32),
        (TOKENS, F32), (TABLE, F32), ((ROWS, SLOTS), BF), ((ROWS, SLOTS), BF), (WIDE, BF),
    ]
    names = [
        "columns", "qrot", "krot", "value", "probs", "after", "router", "high", "low", "rows"
    ]
    scratch = [(TOKENS, x.dtype), ((WIDTH, PACKED), BF)] + [(TABLE, F32)] * 3
    scratch += [((SLOTS, ROWS), BF), ((ROWS, SLOTS), BF)]
    scratch += [((16, HEAD), BF)] * 2 if first else [(WIDE, BF), ((2 * ROWS, SLOTS), BF)]
    scratch += [(TOKENS, F32)] + outs
    ins = [x, w, *tables, take, give]
    if first:
        ins += ring
    else:
        high, low, returned = combine
        ins += [high, low, returned]
        outs = outs + [(TOKENS, F32)]
        names += ["x"]
    result = run_attn(
        lambda *refs: attn_forward_kernel(first, *refs), "attn_forward", ins, order, outs, scratch,
        20 + QKV // TILE, 20, VMEM_BYTES,
    )
    return dict(zip(names, result))


def norm_back(grad, gain, values):
    scale = unit(values)
    inner = grad * gain
    return scale * inner - values * (scale * scale * scale) * jnp.mean(
        inner * values, axis=-1, keepdims=True
    )


def attn_backward_kernel(last, ins, outs, scratch):
    (dx_hbm, back_hbm, w_hbm, cosine_hbm, sine_hbm, give_hbm, router_hbm, after_hbm, x_hbm, probs_hbm,
     qrot_hbm, krot_hbm, value_hbm), ins = ins[:13], ins[13:]
    (dx_in, back, w, cosine, sine, give, router, after, x_in, probs, qrot, krot, value, wide_in,
     small_in, datt, dx_out, packed), scratch = scratch[:18], scratch[18:]
    if last:
        rows, scratch = scratch[0], scratch[1:]
    else:
        turned, scratch = scratch[0], scratch[1:]
    in_sems, out_sems = scratch
    pairs = [(give_hbm, give), (back_hbm, back), (router_hbm, router), (dx_hbm, dx_in)]
    if not last:
        pairs += [(ins[0], wide_in)]
    pairs += [small_block(w_hbm, w), (after_hbm, after)]
    if last:
        out_pairs, qkv_pairs = [], []
        for at in range(0, WIDTH, TILE):
            block = (pl.ds(at, TILE), pl.ds(QKV, WIDTH))
            out_pairs += [(w_hbm.at[block], w.at[block])]
            block = (pl.ds(at, TILE), pl.ds(0, QKV))
            qkv_pairs += [(w_hbm.at[block], w.at[block])]
    else:
        columns = [(slice(None), pl.ds(at, TILE)) for at in range(0, WIDTH, TILE)]
        out_pairs = [
            (ins[1].at[pl.ds(QKV, WIDTH)].at[c], turned.at[pl.ds(QKV, WIDTH)].at[c])
            for c in columns
        ]
        qkv_pairs = [
            (ins[1].at[pl.ds(0, QKV)].at[c], turned.at[pl.ds(0, QKV)].at[c]) for c in columns
        ]
    pairs += out_pairs + [(probs_hbm, probs), (value_hbm, value), (krot_hbm, krot), (qrot_hbm, qrot)]
    pairs += [(cosine_hbm, cosine), (sine_hbm, sine)] + qkv_pairs + [(x_hbm, x_in)]
    if last:
        pairs += [(ins[0], wide_in), (ins[1], small_in)]
    reader, writer = Reader(in_sems, pairs), Writer(out_sems)
    reader.take(4)
    dx = dx_in[...].astype(F32)
    spread = expert_lanes(True)
    if last:
        dgate = back[:, WIDTH:].astype(F32)
        drouter = dot(give[...], (dgate[:, 0:1] * spread).astype(BF))
        drouter += dot(give[...], (dgate[:, 1:2] * spread).astype(BF))
    else:
        reader.take()
        dgate = dot(dx.astype(BF), wide_in[...], 1, 1) * give[...]
        both = dot(jnp.concatenate(split(dgate), axis=0), spread)
        drouter = both[:ROWS] + both[ROWS:]
    reader.take(2)
    small = w[:, SMALL:]
    gain_attn, gain_ffn = gain_rows(small)
    shares = router[...]
    dlogits = shares * (drouter - jnp.sum(drouter * shares, axis=-1, keepdims=True))
    dlogits = dlogits.astype(BF)
    dacts_two = dot(dlogits, small, 1, 1) + dot(give[...], back[:, :WIDTH])
    total = after[...]
    scale = unit(total)
    dafter = dx + norm_back(dacts_two, gain_ffn, total)
    dx_out[...] = dafter
    packed[:, QKV:SMALL] = dafter.astype(BF)
    dgain = jnp.sum(dacts_two * total * scale, axis=0, keepdims=True)
    dgain_high, dgain_low = split(dgain)
    pieces = [jnp.zeros((GAIN_HIGH, HEAD), F32)]
    for part in (dgain_high.astype(F32), dgain_low.astype(F32)):
        pieces += [part[:, at : at + HEAD] for at in range(0, WIDTH, HEAD)]
        pieces += [jnp.zeros((GAIN_LOW - GAIN_HIGH - PIECES, HEAD), F32)]
    pieces += [jnp.zeros((HEAD - 2 * GAIN_LOW + GAIN_HIGH, HEAD), F32)]
    packed[:, SMALL:] = (dlogits.astype(F32) + jnp.concatenate(pieces, axis=0).T).astype(BF)
    writer.send(packed.at[:, QKV:], outs[1].at[:, QKV:])
    for tile in tiles(WIDTH):
        reader.take()
        if last:
            wide = dot(packed[:, QKV:SMALL], w[tile, QKV:SMALL], 1, 1).astype(BF)
        else:
            wide = dot(packed[:, QKV:SMALL], turned[QKV:SMALL, tile]).astype(BF)
        for half in range(TILE // HEAD):
            datt[tile.start // HEAD + half] = wide[:, half * HEAD : (half + 1) * HEAD]
    reader.take(6)
    for k in range(KEY_VALUE_HEADS):
        heads = slice(k * GROUPS, (k + 1) * GROUPS)
        datt_k = datt[heads].reshape(GROUPS * ROWS, HEAD)
        p = probs[heads].reshape(GROUPS * ROWS, ROWS)
        dprobs = dot(datt_k, value[k], 1, 1)
        dvalue = dot(p.astype(BF), datt_k, 0, 0)
        dscores = (p * (dprobs - jnp.sum(dprobs * p, axis=-1, keepdims=True))).astype(BF)
        dqrot = dot(dscores, krot[k]) * SCALE
        dkrot = dot(dscores, qrot[heads].reshape(GROUPS * ROWS, HEAD), 0, 0) * SCALE
        for group in range(GROUPS):
            at = (k * GROUPS + group) * HEAD
            part = dqrot[group * ROWS : (group + 1) * ROWS]
            packed[:, at : at + HEAD] = turn(part, cosine[...], -sine[...]).astype(BF)
        at = Q_END + k * HEAD
        packed[:, at : at + HEAD] = turn(dkrot, cosine[...], -sine[...]).astype(BF)
        at = K_END + k * HEAD
        packed[:, at : at + HEAD] = dvalue.astype(BF)
    writer.send(packed.at[:, :QKV], outs[1].at[:, :QKV])
    parts = []
    for tile in tiles(WIDTH):
        reader.take()
        if last:
            parts += [dot(packed[:, :QKV], w[tile, :QKV], 1, 1)]
        else:
            parts += [dot(packed[:, :QKV], turned[:QKV, tile])]
    dacts = jnp.concatenate(parts, axis=1)
    reader.take()
    dx = dx_out[...] + norm_back(dacts, gain_attn, x_in[...].astype(F32))
    dx_out[...] = dx
    writer.send(dx_out, outs[0])
    if last:
        reader.take(2)
        dx_low = dx.astype(BF)
        both = dot(spread, jnp.concatenate(split(small_in[...]), axis=0), 1, 1).astype(BF)
        gates = jnp.concatenate([both[:, :ROWS] * wide_in[...], both[:, ROWS:] * wide_in[...]], axis=1)
        twice = jnp.concatenate([dx_low, dx_low], axis=0)
        for tile in tiles(WIDTH):
            rows[:, tile] = dot(gates, twice[:, tile]).astype(BF)
            writer.send(rows.at[:, tile], outs[2].at[:, tile])
    writer.finish()


def attn_backward(dx, back, x, kept, w, turned, tables, give, below, returned, order):
    last = below is not None
    outs = [(TOKENS, F32), ((ROWS, PACKED), BF)]
    if last:
        outs += [(WIDE, BF)]
    ins = [dx, back, w, tables[0], tables[1], give, kept["router"], kept["after"], x]
    ins += [kept[n] for n in ("probs", "qrot", "krot", "value")]
    ins += list(below) if last else [returned, turned]
    scratch = [
        (TOKENS, dx.dtype), (back.shape, BF), ((WIDTH, PACKED), BF),
        (TABLE, F32), (TABLE, F32),
        ((ROWS, SLOTS), BF), (TABLE, F32), (TOKENS, F32), (TOKENS, x.dtype),
        ((QUERY_HEADS, ROWS, ROWS), F32), (HEADS, BF), (KEYS, BF), (KEYS, BF),
        ((SLOTS, ROWS), BF) if last else (WIDE, BF), (TABLE, F32), (HEADS, BF),
    ] + outs
    if not last:
        scratch += [((SMALL, WIDTH), BF)]
    return run_attn(
        lambda *refs: attn_backward_kernel(last, *refs), "attn_backward", ins, order, outs, scratch,
        24 + WIDTH // TILE, 12, VMEM_BYTES,
    )


def gelu_parts(gate):
    square = gate * gate
    bend = jnp.tanh(GELU_A * gate * (1.0 + GELU_B * square))
    return bend, square


def gelu(gate):
    bend, _ = gelu_parts(gate)
    return 0.5 * gate * (1.0 + bend)


def gelu_both(gate):
    bend, square = gelu_parts(gate)
    slope = 0.5 * (1.0 + bend) + 0.5 * gate * (1.0 - bend * bend) * GELU_A * (
        1.0 + 3.0 * GELU_B * square
    )
    return 0.5 * gate * (1.0 + bend), slope


def gate_up_pairs(l, gate_hbm, up_hbm, gate_w, up_w):
    gate_up = []
    for at in range(0, FF, TILE):
        block = (slice(None), pl.ds(at, TILE))
        gate_up += [(gate_hbm.at[l, 0].at[block], gate_w.at[block])]
        gate_up += [(up_hbm.at[l, 0].at[block], up_w.at[block])]
    return gate_up


def run_experts(kernel, name, ins, order, outs, scratch, in_copies, flops):
    sd = jax.ShapeDtypeStruct
    count = len(ins) + len(order)

    def body(*refs):
        kernel(*refs[: len(ins)], *refs[count:])

    return pl.pallas_call(
        body,
        out_shape=[sd(shape, BF) for shape in outs],
        in_specs=specs_of(ins) + [ANY] * len(order),
        out_specs=[ANY] * len(outs),
        scratch_shapes=[pltpu.VMEM(shape, kind) for shape, kind in scratch]
        + [pltpu.SemaphoreType.DMA((in_copies,)), pltpu.SemaphoreType.DMA((40,))],
        compiler_params=pltpu.CompilerParams(vmem_limit_bytes=VMEM_BYTES),
        cost_estimate=pl.CostEstimate(
            flops=flops, bytes_accessed=20 << 20, transcendentals=SLOTS * FF
        ),
        name=name,
    )(*ins, *order)


def experts_forward_kernel(
    received_hbm, gate_hbm, up_hbm, down_hbm, act_hbm, slope_hbm, hidden_hbm, out_hbm,
    received, gate_w, up_w, down_w, act_s, slope_s, hidden, out, in_sems, out_sems,
):
    gate_up = gate_up_pairs(0, gate_hbm, up_hbm, gate_w, up_w)
    pairs = [(received_hbm, received)] + gate_up + [(down_hbm.at[0, 0], down_w)]
    copies = start_all(pairs, in_sems)
    writer = Writer(out_sems)
    copies.pop(0).wait()
    for tile in tiles(FF):
        copies.pop(0).wait()
        copies.pop(0).wait()
        gate = dot(received[...], gate_w[:, tile])
        up = dot(received[...], up_w[:, tile])
        act, slope = gelu_both(gate)
        act_s[:, tile] = act.astype(BF)
        slope_s[:, tile] = (slope * up).astype(BF)
        hidden[:, tile] = (act * up).astype(BF)
    copies.pop(0).wait()
    writer.send(act_s, act_hbm)
    writer.send(slope_s, slope_hbm)
    writer.send(hidden, hidden_hbm)
    for tile in tiles(WIDTH):
        out[:, tile] = dot(hidden[...], down_w[:, tile]).astype(BF)
        writer.send(out.at[:, tile], out_hbm.at[:, tile])
    writer.finish()


EXPERT_SCRATCH = [((WIDTH, FF), BF), ((WIDTH, FF), BF), ((FF, WIDTH), BF)]


def experts_forward(received, weights, order):
    small = (SLOTS, FF)
    wide = (SLOTS, WIDTH)
    return run_experts(
        experts_forward_kernel, "experts_forward", [received, *weights], order,
        [small, small, small, wide],
        [(wide, BF)] + EXPERT_SCRATCH + [(small, BF)] * 3 + [(wide, BF)],
        8, 6 * SLOTS * WIDTH * FF,
    )


def back_tiles(dgate, dup, gate_w, up_w, back, back_hbm, writer):
    for tile in tiles(WIDTH):
        back[:, tile] = (
            dot(dgate[...], gate_w[tile], 1, 1) + dot(dup[...], up_w[tile], 1, 1)
        ).astype(BF)
        writer.send(back.at[:, tile], back_hbm.at[:, tile])


def expert_gate(me, received, small):
    shares = router_probs(received, small)
    lane = lax.broadcasted_iota(jnp.int32, shares.shape, 1)
    return jnp.sum(jnp.where(lane == me, shares, 0.0), axis=-1, keepdims=True)


def experts_both_kernel(
    me, received_hbm, product_hbm, w_hbm, gate_hbm, up_hbm,
    hidden_hbm, dgate_hbm, dup_hbm, back_hbm,
    received, product, small, gate_w, up_w, act_s, slope_s, hidden, dgate, dup, back,
    in_sems, out_sems,
):
    pairs = [(received_hbm, received)] + gate_up_pairs(1, gate_hbm, up_hbm, gate_w, up_w)
    pairs += [small_source(w_hbm, small), (product_hbm, product)]
    reader, writer = Reader(in_sems, pairs), Writer(out_sems)
    reader.take()
    for tile in tiles(FF):
        reader.take(2)
        gate = dot(received[...], gate_w[:, tile])
        up = dot(received[...], up_w[:, tile])
        act, slope = gelu_both(gate)
        act_s[:, tile] = act
        slope_s[:, tile] = slope * up
        hidden[:, tile] = (act * up).astype(BF)
    reader.take(2)
    writer.send(hidden, hidden_hbm)
    weight = expert_gate(me[0], received[...], small[...])
    total = jnp.zeros((SLOTS, 1), F32)
    for tile in tiles(FF):
        dhidden = product[:, tile]
        total += jnp.sum(dhidden * hidden[:, tile].astype(F32), axis=-1, keepdims=True)
        dhidden = weight * dhidden
        dgate[:, tile] = (dhidden * slope_s[:, tile]).astype(BF)
        dup[:, tile] = (dhidden * act_s[:, tile]).astype(BF)
    writer.send(dgate, dgate_hbm)
    writer.send(dup, dup_hbm)
    high, low = split(total)
    lane = lax.broadcasted_iota(jnp.int32, (SLOTS, HEAD), 1)
    back[:, WIDTH:] = jnp.where(
        lane == 0, high.astype(F32), jnp.where(lane == 1, low.astype(F32), 0.0)
    ).astype(BF)
    writer.send(back.at[:, WIDTH:], back_hbm.at[:, WIDTH:])
    back_tiles(dgate, dup, gate_w, up_w, back, back_hbm, writer)
    writer.finish()


def small_source(w_hbm, small):
    return (w_hbm.at[:, pl.ds(SMALL, HEAD)], small)


def experts_both(me, received, product, w, weights, order):
    small = (SLOTS, FF)
    wide = (SLOTS, WIDTH)
    back = (SLOTS, WIDTH + HEAD)
    return run_experts(
        experts_both_kernel, "experts_both", [me, received, product, w, *weights[:2]], order,
        [small, small, small, back],
        [(wide, BF), (small, F32), ((WIDTH, HEAD), BF)] + EXPERT_SCRATCH[:2]
        + [(small, F32), (small, F32), (small, BF), (small, BF), (small, BF), (back, BF)],
        10, 8 * SLOTS * WIDTH * FF,
    )


def experts_out_kernel(
    me, hidden_hbm, received_hbm, dx_hbm, w_hbm, down_hbm,
    part0_hbm, part1_hbm, part2_hbm, dslot_hbm,
    hidden, received, dx, small, down_w, part0, part1, part2, dslot, in_sems, out_sems,
):
    pairs = [(hidden_hbm, hidden), (down_hbm.at[1, 0], down_w), (received_hbm, received)]
    pairs += [small_source(w_hbm, small), (dx_hbm, dx)]
    reader, writer = Reader(in_sems, pairs), Writer(out_sems)
    reader.take(2)
    for tile in tiles(WIDTH):
        out = dot(hidden[...], down_w[:, tile]).astype(BF)
        for expert in range(EXPERTS):
            for p, target in enumerate((part0, part1, part2)):
                at = expert * CAP + p * PART_ROWS
                target[expert, :, tile] = out[at : at + PART_ROWS]
    writer.send(part0, part0_hbm)
    writer.send(part1, part1_hbm)
    writer.send(part2, part2_hbm)
    reader.take(3)
    weight = expert_gate(me[0], received[...], small[...])
    for tile in tiles(WIDTH):
        dslot[:, tile] = (weight * dx[:, tile].astype(F32)).astype(BF)
    writer.send(dslot, dslot_hbm)
    writer.finish()


def experts_out(me, hidden, received, dx, w, down, order):
    small = (SLOTS, FF)
    wide = (SLOTS, WIDTH)
    part = (EXPERTS, PART_ROWS, WIDTH)
    return run_experts(
        experts_out_kernel, "experts_out", [me, hidden, received, dx, w, down], order,
        [part, part, part, wide],
        [(small, BF), (wide, BF), (wide, BF), ((WIDTH, HEAD), BF), ((FF, WIDTH), BF)]
        + [(part, BF)] * 3 + [(wide, BF)],
        5, 2 * SLOTS * WIDTH * FF,
    )


def experts_backward_kernel(
    dslot_hbm, act_hbm, slope_hbm, gate_hbm, up_hbm, down_hbm, dgate_hbm, dup_hbm, back_hbm,
    dslot, act_s, slope_s, gate_w, up_w, down_w, dgate, dup, back, in_sems, out_sems,
):
    pairs = [(dslot_hbm, dslot)]
    for tile in tiles(FF):
        block = pl.ds(tile.start, TILE)
        pairs += [(down_hbm.at[0, 0].at[block], down_w.at[block])]
    pairs += [(slope_hbm, slope_s), (act_hbm, act_s)]
    for tile in tiles(WIDTH):
        block = pl.ds(tile.start, TILE)
        pairs += [(gate_hbm.at[0, 0].at[block], gate_w.at[block])]
        pairs += [(up_hbm.at[0, 0].at[block], up_w.at[block])]
    copies = start_all(pairs, in_sems)
    writer = Writer(out_sems)
    copies.pop(0).wait()
    dhidden = []
    for tile in tiles(FF):
        copies.pop(0).wait()
        dhidden += [dot(dslot[...], down_w[tile], 1, 1)]
    copies.pop(0).wait()
    copies.pop(0).wait()
    for tile, part in zip(tiles(FF), dhidden):
        dgate[:, tile] = (part * slope_s[:, tile].astype(F32)).astype(BF)
        dup[:, tile] = (part * act_s[:, tile].astype(F32)).astype(BF)
    writer.send(dgate, dgate_hbm)
    writer.send(dup, dup_hbm)
    for copy in copies:
        copy.wait()
    back_tiles(dgate, dup, gate_w, up_w, back, back_hbm, writer)
    writer.finish()


def experts_backward(dslot, act, slope, weights, order):
    small = (SLOTS, FF)
    wide = (SLOTS, WIDTH)
    return run_experts(
        experts_backward_kernel, "experts_backward", [dslot, act, slope, *weights], order,
        [small, small, wide],
        [(wide, BF), (small, BF), (small, BF)] + EXPERT_SCRATCH
        + [(small, BF), (small, BF), (wide, BF)],
        6 + 2 * WIDTH // TILE, 6 * SLOTS * WIDTH * FF,
    )


def on_core(core, me, ins, outs, scratch, kernel, name, above, order):
    sd = jax.ShapeDtypeStruct
    held = [] if above is None else list(above)
    first_out = 1 + len(ins) + len(held) + len(order)

    def body(*refs):
        @pl.when(refs[0][0] % 2 == core)
        def _():
            kernel(refs[0][0], refs[1 : 1 + len(ins)], refs[first_out : first_out + len(outs)],
                   refs[first_out + len(outs) :])

    return pl.pallas_call(
        body,
        out_shape=[sd(shape, kind) for shape, kind in outs],
        in_specs=[pl.BlockSpec(memory_space=pltpu.SMEM)]
        + [ANY] * (len(ins) + len(held) + len(order)),
        out_specs=[ANY] * len(outs),
        input_output_aliases={1 + len(ins) + i: i for i in range(len(held))},
        scratch_shapes=[pltpu.VMEM(shape, kind) for shape, kind in scratch]
        + [pltpu.SemaphoreType.DMA((24,)), pltpu.SemaphoreType.DMA((24,))],
        compiler_params=pltpu.CompilerParams(vmem_limit_bytes=VMEM_BYTES),
        name=name,
    )(me, *ins, *held, *order)


def upper_product_kernel(me, ins, outs, scratch):
    rows, down, product, in_sems, out_sems = scratch
    pairs = [(ins[0], rows)]
    for tile in tiles(FF):
        block = pl.ds(tile.start, TILE)
        pairs += [(ins[1].at[1, 0].at[block], down.at[block])]
    reader, writer = Reader(in_sems, pairs), Writer(out_sems)
    reader.take()
    for tile in tiles(FF):
        reader.take()
        product[:, tile] = dot(rows[...], down[tile], 1, 1)
        writer.send(product.at[:, tile], outs[0].at[:, tile])
    writer.finish()


def upper_product(core, me, dx_rows, w_down, above, order):
    small = (SLOTS, FF)
    return on_core(
        core, me, [dx_rows, w_down], [(small, F32)], [(WIDE, BF), ((FF, WIDTH), BF), (small, F32)],
        upper_product_kernel, "upper_product", above, order,
    )


def turn_weights_kernel(me, ins, outs, scratch):
    w, turned, in_sems, out_sems = scratch
    pairs = [column_block(ins[0], w, at) for at in range(0, QKV, TILE)] + ring_blocks(me, ins[1:], w)
    reader, writer = Reader(in_sems, pairs), Writer(out_sems)
    for tile in tiles(QKV):
        reader.take()
        turned[tile] = w[:, tile].T
        writer.send(turned.at[tile], outs[0].at[tile])
    reader.take(len(ins) - 1)
    for tile in tiles(WIDTH):
        at = slice(QKV + tile.start, QKV + tile.stop)
        turned[at] = w[:, at].T
        writer.send(turned.at[at], outs[0].at[at])
    writer.finish()


def turn_weights(core, me, w, blocks, above, order):
    turned = ((SMALL, WIDTH), BF)
    return on_core(
        core, me, [w, *blocks], [turned], [((WIDTH, SMALL), BF), turned], turn_weights_kernel,
        "turn_weights", above, order,
    )


def expert_grads_kernel(received, dgate_pre, dup_pre, hidden, dslot, packed):
    gate = dot(received[...], dgate_pre[...], 0, 0).astype(BF)
    up = dot(received[...], dup_pre[...], 0, 0).astype(BF)
    down = dot(hidden[...], dslot[...], 0, 0).astype(BF)
    for part in range(DP // 2):
        packed[part, :SHARD, :FF] = gate[part * SHARD : (part + 1) * SHARD]
        packed[part, :SHARD, FF:] = up[part * SHARD : (part + 1) * SHARD]
        packed[part, SHARD:] = down[part * FF // DP : (part + 1) * FF // DP]


def expert_grads(received, dgate_pre, dup_pre, hidden, dslot):
    rows = SHARD + FF // DP
    whole = lambda width: pl.BlockSpec((SLOTS, width), lambda i: (0, 0))
    part = lambda width: pl.BlockSpec((SLOTS, width), lambda i: (0, i))
    return pl.pallas_call(
        expert_grads_kernel,
        grid=(2,),
        out_shape=jax.ShapeDtypeStruct((DP, rows, WIDTH), BF),
        in_specs=[part(WIDTH // 2), whole(FF), whole(FF), part(FF // 2), whole(WIDTH)],
        out_specs=pl.BlockSpec((DP // 2, rows, WIDTH), lambda i: (i, 0, 0)),
        compiler_params=pltpu.CompilerParams(vmem_limit_bytes=VMEM_BYTES),
        cost_estimate=pl.CostEstimate(
            flops=6 * SLOTS * WIDTH * FF, bytes_accessed=14 << 20, transcendentals=0
        ),
        name="expert_grads",
    )(received, dgate_pre, dup_pre, hidden, dslot).reshape(DP * rows, WIDTH)


def pack_kernel(
    l, query_hbm, key_hbm, value_hbm, out_hbm, router_hbm, gain_attn, gain_ffn, packed_hbm, *rest
):
    if l == 0:
        out_copy, packed, out, router, sems, out_sems = rest
    else:
        packed, router, sems, out_sems = rest
        out = packed.at[:, pl.ds(QKV, WIDTH)]
    pairs = [
        (router_hbm.at[l], router),
        (query_hbm.at[l], packed.at[:, pl.ds(0, Q_END)]),
        (key_hbm.at[l], packed.at[:, pl.ds(Q_END, K_END - Q_END)]),
        (value_hbm.at[l], packed.at[:, pl.ds(K_END, QKV - K_END)]),
        (out_hbm.at[l], out),
    ]
    reader, writer = Reader(sems, pairs), Writer(out_sems)
    reader.take()
    small = [router[...].astype(F32), gain_attn[l : l + 1].astype(F32)]
    small += [gain_ffn[l : l + 1].astype(F32), jnp.zeros((HEAD - EXPERTS - 2, SHARD), F32)]
    small = jnp.concatenate(small, axis=0)
    small = jnp.concatenate([small, jnp.zeros((HEAD, TILE - SHARD), F32)], axis=1).T
    packed[:, packed.shape[1] - HEAD :] = small[:SHARD].astype(BF)
    reader.take(3)
    if l == 0:
        writer.send(packed, packed_hbm)
        reader.take()
        writer.send(out, out_copy)
    else:
        reader.take()
        writer.send(packed, packed_hbm)
    writer.finish()


def pack(l, query, key, value, out, router, gain_attn, gain_ffn):
    sd = jax.ShapeDtypeStruct
    vmem = pl.BlockSpec(memory_space=pltpu.VMEM)
    packed = (SHARD, QKV + HEAD) if l == 0 else (SHARD, PACKED)
    outs = [packed] + [(SHARD, WIDTH)] * (l == 0)
    return pl.pallas_call(
        lambda *refs: pack_kernel(l, *refs),
        out_shape=[sd(shape, BF) for shape in outs],
        in_specs=[ANY] * 5 + [vmem] * 2,
        out_specs=[ANY] * len(outs),
        scratch_shapes=[pltpu.VMEM(shape, BF) for shape in outs]
        + [pltpu.VMEM((EXPERTS, SHARD), BF)]
        + [pltpu.SemaphoreType.DMA((5,)), pltpu.SemaphoreType.DMA((2,))],
        compiler_params=pltpu.CompilerParams(vmem_limit_bytes=VMEM_BYTES),
        name="pack",
    )(query, key, value, out, router.transpose(0, 2, 1), gain_attn, gain_ffn)


def ring(block):
    def move(values, step):
        return lax.ppermute(values, "dp", [(i, (i + step) % DP) for i in range(DP)])

    half = block.shape[0] // 2
    previous, following = move(block, 2), move(block, -2)
    far = [move(previous[:half], 2), move(following[half:], -2)]
    mine = [block, previous, following, *far]
    swap = [(i, i ^ 1) for i in range(DP)]
    return mine + [lax.ppermute(values, "dp", swap) for values in mine]


def seq_tables(counts):
    ends = jnp.cumsum(counts)
    starts = ends - counts
    place = jnp.arange(ROWS, dtype=jnp.int32)
    member = (place[:, None] >= starts[None, :]) & (place[:, None] < ends[None, :])
    index = jnp.arange(counts.shape[0], dtype=jnp.int32)
    segment = jnp.sum(jnp.where(member, index[None, :], 0), axis=1)
    position = place - jnp.sum(jnp.where(member, starts[None, :], 0), axis=1)
    allowed = (segment[:, None] == segment[None, :]) & (place[:, None] >= place[None, :])
    freqs = ROPE_BASE ** (-2.0 * jnp.arange(HEAD // 2, dtype=F32) / HEAD)
    angle = position.astype(F32)[:, None] * freqs[None, :]
    cosine, sine = jnp.cos(angle), jnp.sin(angle)
    return (
        jnp.concatenate([cosine, cosine], axis=1),
        jnp.concatenate([-sine, sine], axis=1),
        allowed.astype(F32),
    )


def slot_matrix(choices, in_parts=False):
    experts = jnp.arange(EXPERTS, dtype=jnp.int32)
    member = jnp.any(choices[:, :, None] == experts[None, None, :], axis=1).astype(BF)
    row = lax.broadcasted_iota(jnp.int32, (ROWS, ROWS), 0)
    column = lax.broadcasted_iota(jnp.int32, (ROWS, ROWS), 1)
    rank = dot((column < row).astype(BF), member).astype(BF)
    slot = jnp.arange(SLOTS, dtype=jnp.int32)[None, :]
    if in_parts:
        owner, place = slot % PART // PART_ROWS, slot // PART * PART_ROWS + slot % PART_ROWS
    else:
        owner, place = slot // CAP, slot % CAP
    expand = (owner == experts[:, None]).astype(BF)
    return ((dot(member, expand) > 0.5) & (dot(rank, expand) == place.astype(F32))).astype(BF)


def exchange(rows):
    width = rows.shape[-1]
    moved = lax.all_to_all(
        rows.reshape(EXPERTS, -1, width), "expert", split_axis=0, concat_axis=0, tiled=True
    )
    return moved.reshape(-1, width)


def after(values, *order):
    return pl.pallas_call(
        lambda *refs: None,
        out_shape=jax.ShapeDtypeStruct(values.shape, values.dtype),
        in_specs=[ANY] * (1 + len(order)),
        out_specs=ANY,
        input_output_aliases={0: 0},
        name="after",
    )(values, *order)


def turn_columns_kernel(me, columns_hbm, turned_hbm, columns, turned, in_sems, out_sems):
    base = me[0] * SHARD // HEAD * HEAD
    pairs = []
    for i in range(3):
        at = pl.multiple_of(base + i * WIDTH, HEAD)
        pairs += [(columns_hbm.at[:, pl.ds(at, TILE)], columns.at[:, pl.ds(i * TILE, TILE)])]
    reader, writer = Reader(in_sems, pairs), Writer(out_sems)
    for i in range(3):
        reader.take()
        turned[i] = columns[:, i * TILE : (i + 1) * TILE].T
        writer.send(turned.at[i], turned_hbm.at[i])
    writer.finish()


def turn_columns(me, columns):
    tokens = DP * ROWS
    return pl.pallas_call(
        turn_columns_kernel,
        out_shape=jax.ShapeDtypeStruct((3, TILE, tokens), BF),
        in_specs=[pl.BlockSpec(memory_space=pltpu.SMEM), ANY],
        out_specs=ANY,
        scratch_shapes=[
            pltpu.VMEM((tokens, 3 * TILE), BF),
            pltpu.VMEM((3, TILE, tokens), BF),
            pltpu.SemaphoreType.DMA((3,)),
            pltpu.SemaphoreType.DMA((3,)),
        ],
        compiler_params=pltpu.CompilerParams(vmem_limit_bytes=VMEM_BYTES),
        cost_estimate=pl.CostEstimate(flops=0, bytes_accessed=4 << 20, transcendentals=0),
        name="turn_columns",
    )(me, columns)


def dense_grads_kernel(me, turned_hbm, factors_hbm, pieces_hbm, turned, factors, total, pieces,
                       in_sems, out_sems):
    start = me[0] * SHARD
    shift = start % HEAD
    base = start - shift
    copies = Writer(out_sems)
    pairs = [(turned_hbm, turned)]
    for at in range(0, PACKED, CHUNK):
        block = (slice(None), pl.ds(at, min(CHUNK, PACKED - at)))
        pairs += [(factors_hbm.at[block], factors.at[block])]
    reader = Reader(in_sems, pairs)
    reader.take()

    def put(chunk, values):
        pieces[chunk] = values.astype(BF)
        copies.send(pieces.at[chunk], pieces_hbm.at[chunk])

    for chunk in range(SMALL // CHUNK):
        reader.take()
        total[chunk % 2] = dot(
            turned[0 if chunk < QKV // CHUNK else 1],
            factors[:, chunk * CHUNK : (chunk + 1) * CHUNK],
        )
        put(chunk, total[chunk % 2, pl.ds(pl.multiple_of(shift, 64), SHARD), :])
    reader.take()
    ends = jnp.zeros((ROWS, HEAD), F32)
    for source in range(DP):
        ends += factors[source * ROWS : (source + 1) * ROWS, SMALL:].astype(F32)
    lane = lax.broadcasted_iota(jnp.int32, (ROWS, HEAD), 1)

    def gain_piece(piece):
        held = (lane == piece + GAIN_HIGH) | (lane == piece + GAIN_LOW)
        return jnp.sum(jnp.where(held, ends, 0.0), axis=1, keepdims=True)

    first, second = gain_piece(base // HEAD), gain_piece(base // HEAD + 1)
    gain = jnp.where(
        shift == 0,
        jnp.concatenate([first, second[: SHARD - ROWS]], axis=0),
        jnp.concatenate([first[ROWS // 2 :], second], axis=0),
    )
    gain_high, gain_low = split(gain)
    total[0, :, :HEAD] = dot(turned[2], factors[:, SMALL:])
    router = total[0, pl.ds(pl.multiple_of(shift, 64), SHARD), :HEAD]
    lane = lax.broadcasted_iota(jnp.int32, (SHARD, HEAD), 1)
    router = jnp.where(lane < EXPERTS, router, 0.0)
    router = jnp.where(lane == EXPERTS, gain_high.astype(F32), router)
    router = jnp.where(lane == EXPERTS + 1, gain_low.astype(F32), router)
    put(CHUNKS - 2, jnp.concatenate([router, jnp.zeros_like(router)], axis=1))
    put(CHUNKS - 1, jnp.zeros((SHARD, CHUNK), F32))
    copies.finish()


def dense_grads(me, turned, factors, order):
    tokens = DP * ROWS

    def body(*refs):
        dense_grads_kernel(*refs[:3], *refs[3 + len(order) :])

    return pl.pallas_call(
        body,
        out_shape=jax.ShapeDtypeStruct((CHUNKS, SHARD, CHUNK), BF),
        in_specs=[pl.BlockSpec(memory_space=pltpu.SMEM)] + [ANY] * (2 + len(order)),
        out_specs=ANY,
        scratch_shapes=[
            pltpu.VMEM((3, TILE, tokens), BF),
            pltpu.VMEM((tokens, PACKED), BF),
            pltpu.VMEM((2, TILE, CHUNK), F32),
            pltpu.VMEM((CHUNKS, SHARD, CHUNK), BF),
            pltpu.SemaphoreType.DMA((1 + CHUNKS,)),
            pltpu.SemaphoreType.DMA((CHUNKS,)),
        ],
        compiler_params=pltpu.CompilerParams(vmem_limit_bytes=VMEM_BYTES),
        cost_estimate=pl.CostEstimate(
            flops=2 * tokens * TILE * PACKED, bytes_accessed=10 << 20, transcendentals=0
        ),
        name="dense_grads",
    )(me, turned, factors, *order)


def to_expert_peers(pieces):
    return lax.all_to_all(pieces, "expert", split_axis=0, concat_axis=0, tiled=True)


def sum_pieces_kernel(pieces_hbm, out_hbm, pieces, out, in_sems, out_sems):
    half = CHUNKS // 2
    pairs = []
    for at in (0, half):
        block = pl.ds(at, half)
        pairs += [(pieces_hbm.at[block, :, pl.ds(0, CHUNK)], pieces.at[block])]
    reader, writer = Reader(in_sems, pairs), Writer(out_sems)
    reader.take()
    total = pieces[0].astype(F32)
    for i in range(1, half):
        total += pieces[i].astype(F32)
    reader.take()
    for i in range(half, CHUNKS):
        total += pieces[i].astype(F32)
    out[...] = total.astype(BF)
    if len(out_hbm.shape) == 3:
        for i in range(CHUNKS):
            writer.send(out, out_hbm.at[i])
    else:
        writer.send(out, out_hbm)
    writer.finish()


def sum_pieces(pieces, copies):
    return pl.pallas_call(
        sum_pieces_kernel,
        out_shape=jax.ShapeDtypeStruct((copies,) * (copies > 1) + (SHARD, CHUNK), BF),
        in_specs=[ANY],
        out_specs=ANY,
        scratch_shapes=[
            pltpu.VMEM((CHUNKS, SHARD, CHUNK), BF),
            pltpu.VMEM((SHARD, CHUNK), BF),
            pltpu.SemaphoreType.DMA((2,)),
            pltpu.SemaphoreType.DMA((CHUNKS,)),
        ],
        compiler_params=pltpu.CompilerParams(vmem_limit_bytes=VMEM_BYTES),
        name="sum_pieces",
    )(pieces)


def finish_kernel(l, refs):
    (pieces, w_query, key_projection, value_projection, norm_attn), refs = refs[:5], refs[5:]
    if l == 0:
        ends_above, refs = refs[0], refs[5:]
        (query_hbm, key_hbm, value_hbm, out_hbm, gain_attn, gain_ffn, router) = refs[:7]
        query, key, value, out, sems = refs[7:]
    else:
        query_hbm, key_hbm, value_hbm, out_hbm, ends_out, query, key, value, out, sems = refs
    writer = Writer(sems)
    rows = jnp.zeros((SHARD, 1), F32)
    for chunk in range(SMALL // CHUNK):
        part = pieces[chunk].astype(F32)
        lanes = slice(chunk * CHUNK, (chunk + 1) * CHUNK)
        if chunk < Q_END // CHUNK:
            query[:, lanes] = part
            weight = w_query[l, :, lanes]
        elif chunk == Q_END // CHUNK:
            key[...] = part
            weight = key_projection[l]
            writer.send(query, query_hbm.at[l])
            writer.send(key, key_hbm.at[l])
        elif chunk < QKV // CHUNK:
            value[...] = part
            weight = value_projection[l]
            writer.send(value, value_hbm.at[l])
        else:
            out[:, lanes.start - QKV : lanes.stop - QKV] = part
            continue
        rows += jnp.sum(part * weight.astype(F32), axis=1, keepdims=True)
    writer.send(out, out_hbm.at[l])
    ends = pieces[CHUNKS - 2, :, :HEAD].astype(F32)
    ffn = ends[:, EXPERTS : EXPERTS + 1] + ends[:, EXPERTS + 1 : EXPERTS + 2]
    lane = lax.broadcasted_iota(jnp.int32, (SHARD, HEAD), 1)
    ends = jnp.where(lane == EXPERTS, rows, jnp.where(lane == EXPERTS + 1, ffn, ends))
    if l > 0:
        ends_out[...] = ends
    else:
        for layer, part in enumerate((ends, ends_above[...])):
            wide = jnp.concatenate([part, jnp.zeros((TILE - SHARD, HEAD), F32)], axis=0).T
            router[layer] = wide[:EXPERTS, :SHARD]
            gain = norm_attn[layer : layer + 1].astype(F32)
            gain_attn[layer : layer + 1] = wide[EXPERTS : EXPERTS + 1, :SHARD] / gain
            gain_ffn[layer : layer + 1] = wide[EXPERTS + 1 : EXPERTS + 2, :SHARD]
    writer.finish()


def finish(l, pieces, weights, norm_attn, above):
    sd = jax.ShapeDtypeStruct
    vmem = pl.BlockSpec(memory_space=pltpu.VMEM)
    keys = (SHARD, KEY_VALUE_HEADS * HEAD)
    slabs = [(SHARD, Q_END), keys, keys, (SHARD, WIDTH)]
    outs = [sd((LAYERS,) + shape, F32) for shape in slabs]
    if above is None:
        outs += [sd((SHARD, HEAD), F32)]
        ins, in_specs, aliases = [], [], {}
    else:
        outs += [sd((LAYERS, SHARD), F32)] * 2 + [sd((LAYERS, EXPERTS, SHARD), F32)]
        ins, in_specs = [above[4], *above[:4]], [vmem] + [ANY] * 4
        aliases = {6 + i: i for i in range(4)}
    return pl.pallas_call(
        lambda *refs: finish_kernel(l, refs),
        out_shape=outs,
        in_specs=[vmem] * 5 + in_specs,
        out_specs=[ANY] * 4 + [vmem] * (len(outs) - 4),
        input_output_aliases=aliases,
        scratch_shapes=[pltpu.VMEM(shape, F32) for shape in slabs]
        + [pltpu.SemaphoreType.DMA((4,))],
        compiler_params=pltpu.CompilerParams(vmem_limit_bytes=VMEM_BYTES),
        name="finish",
    )(pieces, *weights, norm_attn, *ins)


def finish_experts_kernel(shares0, shares1, gate, up, down):
    for l, shares in enumerate((shares0, shares1)):
        gate[l, 0] = shares[:SHARD, :FF].astype(F32)
        up[l, 0] = shares[:SHARD, FF:].astype(F32)
        down[l, 0] = shares[SHARD:].astype(F32)


def finish_experts(shares0, shares1):
    sd = jax.ShapeDtypeStruct
    vmem = pl.BlockSpec(memory_space=pltpu.VMEM)
    return pl.pallas_call(
        finish_experts_kernel,
        out_shape=[
            sd((LAYERS, 1, SHARD, FF), F32), sd((LAYERS, 1, SHARD, FF), F32),
            sd((LAYERS, 1, FF // DP, WIDTH), F32),
        ],
        in_specs=[vmem] * 2,
        out_specs=[vmem] * 3,
        compiler_params=pltpu.CompilerParams(vmem_limit_bytes=VMEM_BYTES),
        name="finish_experts",
    )(shares0, shares1)


def mixed_kernel(x_hbm, high, low, part0, part1, part2, out, x, gates, returned, sems):
    pairs = [(high, gates.at[:ROWS]), (low, gates.at[ROWS:]), (x_hbm, x)]
    for p, part in enumerate((part0, part1, part2)):
        pairs += [(part, returned.at[pl.ds(p * PART, PART)])]
    Reader(sems, pairs).take(len(pairs))
    for tile in tiles(WIDTH):
        both = dot(gates[...], returned[:, tile])
        out[:, tile] = (x[:, tile] + both[:ROWS] + both[ROWS:]).astype(BF)


def mixed_rows(x, high, low, parts):
    return pl.pallas_call(
        mixed_kernel,
        out_shape=jax.ShapeDtypeStruct(TOKENS, BF),
        in_specs=[ANY] * 6,
        out_specs=pl.BlockSpec(memory_space=pltpu.VMEM),
        scratch_shapes=[
            pltpu.VMEM(TOKENS, F32),
            pltpu.VMEM((2 * ROWS, SLOTS), BF),
            pltpu.VMEM(WIDE, BF),
            pltpu.SemaphoreType.DMA((6,)),
        ],
        compiler_params=pltpu.CompilerParams(vmem_limit_bytes=VMEM_BYTES),
        name="mixed",
    )(x, high, low, *parts)


def local(
    tokens, cotangent, lengths, routes, norm_attn, w_query, key_projection, value_projection,
    w_out, norm_ffn, w_router, w_gate, w_up, w_down,
):
    me_dp = lax.axis_index("dp").astype(jnp.int32).reshape(1)
    me_expert = lax.axis_index("expert").astype(jnp.int32).reshape(1)
    tables = seq_tables(lengths[0])
    give = [slot_matrix(routes[l]) for l in range(LAYERS)]
    take = [g.T for g in give]
    give_parts = slot_matrix(routes[1], True)
    experts = (w_gate, w_up, w_down)

    def gather(values):
        return lax.all_gather(values, "dp", axis=0, tiled=True)

    weights = (w_query, key_projection, value_projection, w_out, w_router, norm_attn, norm_ffn)
    shard0, out_shard0 = pack(0, *weights)
    w = [gather(shard0), gather(pack(1, *weights)[0])]
    out_ring = [me_dp, *ring(out_shard0)]

    dx_rows = exchange(dot(take[1], cotangent).astype(BF))

    product = upper_product(0, me_dp, dx_rows, w_down, None, ())
    turned_w = turn_weights(1, me_dp, w[0], out_ring[1:], None, ())
    product = upper_product(1, me_dp, dx_rows, w_down, product, turned_w)
    kept0 = attn_forward(
        tokens, None, w[0], out_ring, tables, take[0], give[0],
        (*product, give[1], give_parts, me_expert),
    )
    received0 = exchange(kept0["rows"])
    act0, slope0, hidden0, out0 = experts_forward(received0, experts, ())
    returned0 = exchange(out0)
    turned_w = turn_weights(0, me_dp, w[0], out_ring[1:], turned_w, (out0,))
    columns0 = gather(kept0["columns"])

    kept1 = attn_forward(
        kept0["after"], (kept0["high"], kept0["low"], returned0), w[1], None, tables, take[1],
        give_parts, tuple(turned_w),
    )
    received1 = exchange(kept1["rows"])
    columns1 = gather(kept1["columns"])
    hidden1, dgate1, dup1, back1 = experts_both(
        me_expert, received1, product[0], w[1], experts, ()
    )
    back1 = exchange(back1)
    *parts, dslot1 = experts_out(me_expert, hidden1, received1, dx_rows, w[1], w_down, ())
    grads1 = expert_grads(received1, dgate1, dup1, hidden1, dslot1)
    turned0 = turn_columns(me_dp, columns0)
    parts[0] = exchange(after(parts[0], grads1, turned0))

    dx0, packed1, rows0 = attn_backward(
        cotangent, back1, kept1["x"], kept1, w[1], None, tables, give[1],
        (take[0], kept0["router"]), None, (),
    )
    packed1 = after(packed1, parts[0])
    dslot0 = exchange(rows0)
    factors1 = gather(packed1)
    shares1 = lax.psum_scatter(after(grads1, packed1), "dp", scatter_dimension=0, tiled=True)
    dgate0, dup0, back0 = experts_backward(dslot0, act0, slope0, experts, ())
    back0 = exchange(back0)
    grads0 = expert_grads(received0, dgate0, dup0, hidden0, dslot0)
    parts[1] = exchange(parts[1])
    turned1 = turn_columns(me_dp, columns1)
    pieces1 = dense_grads(me_dp, turned1, factors1, (parts[1],))
    parts[2] = exchange(after(parts[2], grads0, pieces1))
    grad_tokens, packed0 = attn_backward(
        dx0, back0, tokens, kept0, w[0], turned_w[0], tables, give[0], None, returned0, ()
    )
    factors0 = gather(after(packed0, parts[2], shares1))
    summed1 = sum_pieces(to_expert_peers(pieces1), CHUNKS)
    shares0 = lax.psum_scatter(after(grads0, summed1), "dp", scatter_dimension=0, tiled=True)
    mixed = mixed_rows(kept1["after"], kept1["high"], kept1["low"], parts)
    pieces1 = to_expert_peers(summed1)
    pieces0 = dense_grads(me_dp, turned0, factors0, ())
    pieces0 = to_expert_peers(after(pieces0, pieces1))
    pieces0 = to_expert_peers(sum_pieces(pieces0, CHUNKS))

    dense = (w_query, key_projection, value_projection)
    above = finish(1, pieces1, dense, norm_attn, None)
    query, key, value, out, gain_attn, gain_ffn, router = finish(
        0, pieces0, dense, norm_attn, above
    )
    gate, up, down = finish_experts(shares0, shares1)
    return (
        mixed, grad_tokens, gain_attn, query, key, value, out, gain_ffn,
        router.transpose(0, 2, 1), gate, up, down,
    )


def solution(mesh):
    placed = (
        P(("dp", "expert"), None),
        P(("dp", "expert"), None),
        P(("dp", "expert"), None),
        P(None, ("dp", "expert"), None),
        P(None, "dp"),
        P(None, "dp", None),
        P(None, "dp", None),
        P(None, "dp", None),
        P(None, "dp", None),
        P(None, "dp"),
        P(None, "dp", None),
        P(None, "expert", None, None),
        P(None, "expert", None, None),
        P(None, "expert", None, None),
    )
    return jax.shard_map(
        local,
        mesh=mesh,
        in_specs=placed,
        out_specs=(
            P(("dp", "expert"), None),
            P(("dp", "expert"), None),
            P(None, "dp"),
            P(None, "dp", None),
            P(None, "dp", None),
            P(None, "dp", None),
            P(None, "dp", None),
            P(None, "dp"),
            P(None, "dp", None),
            P(None, "expert", "dp", None),
            P(None, "expert", "dp", None),
            P(None, "expert", "dp", None),
        ),
        check_vma=False,
    )
```

```python
import jax
import jax.numpy as jnp
from jax import lax
from jax.experimental import pallas as pl
from jax.experimental.pallas import tpu as pltpu
from jax.sharding import PartitionSpec as P

QUERY_HEADS = 12
KEY_VALUE_HEADS = 2
GROUPS = QUERY_HEADS // KEY_VALUE_HEADS
HEAD = 128
LAYERS = 2
WIDTH = 1536
FF = 768
ROWS = 128
EXPERTS = 16
CAP = 48
SLOTS = EXPERTS * CAP
DP = 8
SHARD = WIDTH // DP
Q_END = QUERY_HEADS * HEAD
K_END = Q_END + KEY_VALUE_HEADS * HEAD
QKV = K_END + KEY_VALUE_HEADS * HEAD
SMALL = QKV + WIDTH
PACKED = SMALL + HEAD
GAIN_ATTN, GAIN_FFN = 16, 17
GAIN_HIGH, GAIN_LOW = 16, 32
PIECES = WIDTH // HEAD
TILE = 256
PARTS = 3
PART = SLOTS // PARTS
PART_ROWS = CAP // PARTS
CHUNKS, CHUNK = 16, 256
COLUMNS = 3 * WIDTH
EPSILON = 1e-06
ROPE_BASE = 1000000.0
SCALE = HEAD ** (-0.5)
GELU_A = 0.7978845608028654
GELU_B = 0.044715
VMEM_BYTES = 56 << 20
BF = jnp.bfloat16
F32 = jnp.float32
ANY = pl.BlockSpec(memory_space=pl.ANY)


def dot(left, right, left_dim=1, right_dim=0):
    return lax.dot_general(
        left, right, (((left_dim,), (right_dim,)), ((), ())), preferred_element_type=F32
    )


def split(values):
    high = values.astype(BF)
    return high, (values - high.astype(F32)).astype(BF)


def unit(values):
    return lax.rsqrt(jnp.mean(values * values, axis=-1, keepdims=True) + EPSILON)


def turn(values, cosine, sine):
    return values * cosine + pltpu.roll(values, HEAD // 2, 1) * sine


def expert_lanes(transposed=False, in_parts=False):
    shape = (SLOTS, HEAD) if transposed else (HEAD, SLOTS)
    slot = lax.broadcasted_iota(jnp.int32, shape, 0 if transposed else 1)
    expert = lax.broadcasted_iota(jnp.int32, shape, 1 if transposed else 0)
    if in_parts:
        held = ((slot & (PART - 1)) >> 4) == expert
    else:
        held = (slot >= expert * CAP) & (slot < expert * CAP + CAP)
    return held.astype(F32).astype(BF)


def gain_rows(small):
    row = lax.broadcasted_iota(jnp.int32, (8, HEAD), 0)
    lane = lax.broadcasted_iota(jnp.int32, (8, HEAD), 1)
    pick = ((lane == row + GAIN_ATTN) & (row < 2)).astype(F32).astype(BF)
    rows = dot(pick, small, 1, 1)
    return rows[0:1], rows[1:2]


def router_probs(rows, small):
    logits = dot(rows, small)
    lane = lax.broadcasted_iota(jnp.int32, logits.shape, 1)
    logits = jnp.where(lane < EXPERTS, logits, -1e30)
    powers = jnp.exp(logits - jnp.max(logits, axis=-1, keepdims=True))
    return powers / jnp.sum(powers, axis=-1, keepdims=True)


def start_all(pairs, sems):
    copies = [
        pltpu.make_async_copy(source, target, sems.at[i]) for i, (source, target) in enumerate(pairs)
    ]
    for copy in copies:
        copy.start()
    return copies


class Writer:
    def __init__(self, sems):
        self.sems, self.copies = sems, []

    def send(self, source, target):
        copy = pltpu.make_async_copy(source, target, self.sems.at[len(self.copies)])
        copy.start()
        self.copies.append(copy)

    def finish(self):
        for copy in self.copies:
            copy.wait()


class Reader:
    def __init__(self, sems, pairs):
        self.copies = start_all(pairs, sems)

    def take(self, count=1):
        for _ in range(count):
            self.copies.pop(0).wait()


def tiles(width):
    return [slice(at, at + TILE) for at in range(0, width, TILE)]


def small_block(w_hbm, w):
    last = w_hbm.shape[1] - HEAD
    return (w_hbm.at[:, pl.ds(last, HEAD)], w.at[:, pl.ds(SMALL, HEAD)])


def column_block(w_hbm, w, at):
    return (w_hbm.at[:, pl.ds(at, TILE)], w.at[:, pl.ds(at, TILE)])


def ring_blocks(me, blocks, w):
    pairs = []
    for core in range(2):
        start = me if core == 0 else me + 1 - 2 * (me % 2)
        for block, step in enumerate((0, DP - 2, 2, 4, 4)):
            ref = blocks[core * 5 + block]
            at = (start + step) % DP * SHARD + (SHARD // 2 if block == 4 else 0)
            at = pl.multiple_of(at, SHARD // 2)
            pairs += [(ref, w.at[pl.ds(at, ref.shape[0]), pl.ds(QKV, WIDTH)])]
    return pairs


def attn_forward_kernel(first, ins, outs, scratch):
    (x_hbm, w_hbm, cosine_hbm, sine_hbm, allowed_hbm, take_hbm, give_hbm), ins = ins[:7], ins[7:]
    (columns_hbm, qrot_hbm, krot_hbm, value_hbm, probs_hbm, after_hbm, router_hbm, high_hbm, low_hbm,
     rows_hbm), outs = outs[:10], outs[10:]
    (x_in, w, cosine, sine, allowed, take, give, returned, gates, x, columns, qrot, krot, value, probs,
     after, router, high, low, rows, in_sems, out_sems) = scratch
    acts = columns.at[:, :WIDTH]
    attended = columns.at[:, WIDTH : 2 * WIDTH]
    acts_two = columns.at[:, 2 * WIDTH :]
    pairs = []
    if first:
        out_pairs = ring_blocks(ins[0][0], ins[1:], w)
    else:
        out_pairs = [column_block(w_hbm, w, at) for at in range(QKV, SMALL, TILE)]
        high_below, low_below, returned_hbm = ins
        pairs += [(high_below, gates.at[:ROWS]), (low_below, gates.at[ROWS:])]
        pairs += [(returned_hbm, returned)]
    pairs += [(x_hbm, x_in), small_block(w_hbm, w)]
    pairs += [column_block(w_hbm, w, at) for at in range(0, QKV, TILE)]
    pairs += [(cosine_hbm, cosine), (sine_hbm, sine), (allowed_hbm, allowed)]
    pairs += out_pairs + [(take_hbm, take), (give_hbm, give)]
    reader, writer = Reader(in_sems, pairs), Writer(out_sems)
    if first:
        reader.take()
        x[...] = x_in[...].astype(F32)
    else:
        reader.take(4)
        for tile in tiles(WIDTH):
            both = dot(gates[...], returned[:, tile])
            x[:, tile] = x_in[:, tile] + both[:ROWS] + both[ROWS:]
        writer.send(x, outs[0])
    reader.take()
    small = w[:, SMALL:]
    gain_attn, gain_ffn = gain_rows(small)
    total = x[...]
    acts[...] = (total * unit(total) * gain_attn).astype(BF)
    wide = []
    for tile in tiles(QKV):
        reader.take()
        wide += [dot(acts[...], w[:, tile])]
    reader.take(3)
    for tile in range(QKV // TILE):
        for half in range(TILE // HEAD):
            head = tile * (TILE // HEAD) + half
            part = wide[tile][:, half * HEAD : (half + 1) * HEAD]
            if head < QUERY_HEADS:
                qrot[head] = turn(part, cosine[...], sine[...]).astype(BF)
            elif head < QUERY_HEADS + KEY_VALUE_HEADS:
                krot[head - QUERY_HEADS] = turn(part, cosine[...], sine[...]).astype(BF)
            else:
                value[head - QUERY_HEADS - KEY_VALUE_HEADS] = part.astype(BF)
    writer.send(qrot, qrot_hbm)
    writer.send(krot, krot_hbm)
    writer.send(value, value_hbm)
    open_scores = (allowed[...] > 0.5)[None]
    for k in range(KEY_VALUE_HEADS):
        heads = slice(k * GROUPS, (k + 1) * GROUPS)
        scores = dot(qrot[heads].reshape(GROUPS * ROWS, HEAD), krot[k], 1, 1) * SCALE
        scores = jnp.where(open_scores, scores.reshape(GROUPS, ROWS, ROWS), -1000000000.0)
        powers = jnp.exp(scores - jnp.max(scores, axis=-1, keepdims=True))
        shares = powers / jnp.sum(powers, axis=-1, keepdims=True)
        probs[heads] = shares
        mixed = dot(shares.astype(BF).reshape(GROUPS * ROWS, ROWS), value[k]).astype(BF)
        for group in range(GROUPS):
            at = (k * GROUPS + group) * HEAD
            attended[:, at : at + HEAD] = mixed[group * ROWS : (group + 1) * ROWS]
    writer.send(probs, probs_hbm)
    if first:
        reader.take(len(out_pairs))
    for tile in tiles(WIDTH):
        if not first:
            reader.take()
        after[:, tile] = x[:, tile] + dot(
            attended[...], w[:, QKV + tile.start : QKV + tile.stop]
        )
    writer.send(after, after_hbm)
    total = after[...]
    acts_two[...] = (total * unit(total) * gain_ffn).astype(BF)
    writer.send(columns, columns_hbm)
    reader.take(2)
    for tile in tiles(WIDTH):
        rows[:, tile] = dot(take[...], acts_two[:, tile]).astype(BF)
        writer.send(rows.at[:, tile], rows_hbm.at[:, tile])
    shares = router_probs(acts_two[...], small)
    router[...] = shares
    spread = expert_lanes(in_parts=not first)
    both = dot(jnp.concatenate(split(shares), axis=0), spread).astype(BF)
    high[...] = both[:ROWS] * give[...]
    low[...] = both[ROWS:] * give[...]
    writer.send(router, router_hbm)
    writer.send(high, high_hbm)
    writer.send(low, low_hbm)
    writer.finish()


HEADS = (QUERY_HEADS, ROWS, HEAD)
KEYS = (KEY_VALUE_HEADS, ROWS, HEAD)
TABLE = (ROWS, HEAD)
TOKENS = (ROWS, WIDTH)
WIDE = (SLOTS, WIDTH)


def specs_of(ins):
    return [pl.BlockSpec(memory_space=pltpu.SMEM if a.dtype == jnp.int32 else pl.ANY) for a in ins]


def run_attn(kernel, name, ins, order, outs, scratch, in_copies, out_copies, vmem):
    sd = jax.ShapeDtypeStruct

    def body(*refs):
        first_out = len(ins) + len(order)
        first_scratch = first_out + len(outs)
        kernel(refs[: len(ins)], refs[first_out:first_scratch], refs[first_scratch:])

    return pl.pallas_call(
        body,
        out_shape=[sd(shape, kind) for shape, kind in outs],
        in_specs=specs_of(ins) + [ANY] * len(order),
        out_specs=[ANY] * len(outs),
        scratch_shapes=[pltpu.VMEM(shape, kind) for shape, kind in scratch]
        + [pltpu.SemaphoreType.DMA((in_copies,)), pltpu.SemaphoreType.DMA((out_copies,))],
        compiler_params=pltpu.CompilerParams(vmem_limit_bytes=vmem),
        cost_estimate=pl.CostEstimate(
            flops=2 * ROWS * WIDTH * PACKED, bytes_accessed=20 << 20, transcendentals=200000
        ),
        name=name,
    )(*ins, *order)


def attn_forward(x, combine, w, ring, tables, take, give, order):
    first = combine is None
    outs = [
        ((ROWS, COLUMNS), BF), (HEADS, BF), (KEYS, BF), (KEYS, BF), ((QUERY_HEADS, ROWS, ROWS), F32),
        (TOKENS, F32), (TABLE, F32), ((ROWS, SLOTS), BF), ((ROWS, SLOTS), BF), (WIDE, BF),
    ]
    names = [
        "columns", "qrot", "krot", "value", "probs", "after", "router", "high", "low", "rows"
    ]
    scratch = [(TOKENS, x.dtype), ((WIDTH, PACKED), BF)] + [(TABLE, F32)] * 3
    scratch += [((SLOTS, ROWS), BF), ((ROWS, SLOTS), BF)]
    scratch += [((16, HEAD), BF)] * 2 if first else [(WIDE, BF), ((2 * ROWS, SLOTS), BF)]
    scratch += [(TOKENS, F32)] + outs
    ins = [x, w, *tables, take, give]
    if first:
        ins += ring
    else:
        high, low, returned = combine
        ins += [high, low, returned]
        outs = outs + [(TOKENS, F32)]
        names += ["x"]
    result = run_attn(
        lambda *refs: attn_forward_kernel(first, *refs), "attn_forward", ins, order, outs, scratch,
        20 + QKV // TILE, 20, VMEM_BYTES,
    )
    return dict(zip(names, result))


def norm_back(grad, gain, values):
    scale = unit(values)
    inner = grad * gain
    return scale * inner - values * (scale * scale * scale) * jnp.mean(
        inner * values, axis=-1, keepdims=True
    )


def attn_backward_kernel(last, ins, outs, scratch):
    (dx_hbm, back_hbm, w_hbm, turned_hbm, cosine_hbm, sine_hbm, give_hbm, router_hbm, after_hbm,
     x_hbm, probs_hbm, qrot_hbm, krot_hbm, value_hbm), ins = ins[:14], ins[14:]
    (dx_in, back, small_ref, turned, cosine, sine, give, router, after, x_in, probs, qrot, krot, value, wide_in,
     small_in, datt, dx_out, packed), scratch = scratch[:19], scratch[19:]
    if last:
        rows, scratch = scratch[0], scratch[1:]
    in_sems, out_sems = scratch
    pairs = [(give_hbm, give), (back_hbm, back), (router_hbm, router), (dx_hbm, dx_in)]
    if not last:
        pairs += [(ins[0], wide_in)]
    last_block = pl.ds(w_hbm.shape[1] - HEAD, HEAD)
    pairs += [(w_hbm.at[:, last_block], small_ref), (after_hbm, after)]
    columns = [(slice(None), pl.ds(at, TILE)) for at in range(0, WIDTH, TILE)]
    out_pairs, qkv_pairs = (
        [(turned_hbm.at[rows].at[c], turned.at[rows].at[c]) for c in columns]
        for rows in (pl.ds(QKV, WIDTH), pl.ds(0, QKV))
    )
    pairs += out_pairs + [(probs_hbm, probs), (value_hbm, value), (krot_hbm, krot), (qrot_hbm, qrot)]
    pairs += [(cosine_hbm, cosine), (sine_hbm, sine)] + qkv_pairs + [(x_hbm, x_in)]
    if last:
        pairs += [(ins[0], wide_in), (ins[1], small_in)]
    reader, writer = Reader(in_sems, pairs), Writer(out_sems)
    reader.take(4)
    dx = dx_in[...].astype(F32)
    spread = expert_lanes(True)
    if last:
        dgate = back[:, WIDTH:].astype(F32)
        drouter = dot(give[...], (dgate[:, 0:1] * spread).astype(BF))
        drouter += dot(give[...], (dgate[:, 1:2] * spread).astype(BF))
    else:
        reader.take()
        dgate = dot(dx.astype(BF), wide_in[...], 1, 1) * give[...]
        both = dot(jnp.concatenate(split(dgate), axis=0), spread)
        drouter = both[:ROWS] + both[ROWS:]
    reader.take(2)
    small = small_ref[...]
    gain_attn, gain_ffn = gain_rows(small)
    shares = router[...]
    dlogits = shares * (drouter - jnp.sum(drouter * shares, axis=-1, keepdims=True))
    dlogits = dlogits.astype(BF)
    dacts_two = dot(dlogits, small, 1, 1) + dot(give[...], back[:, :WIDTH])
    total = after[...]
    scale = unit(total)
    dafter = dx + norm_back(dacts_two, gain_ffn, total)
    dx_out[...] = dafter
    packed[:, QKV:SMALL] = dafter.astype(BF)
    dgain = jnp.sum(dacts_two * total * scale, axis=0, keepdims=True)
    dgain_high, dgain_low = split(dgain)
    pieces = [jnp.zeros((GAIN_HIGH, HEAD), F32)]
    for part in (dgain_high.astype(F32), dgain_low.astype(F32)):
        pieces += [part[:, at : at + HEAD] for at in range(0, WIDTH, HEAD)]
        pieces += [jnp.zeros((GAIN_LOW - GAIN_HIGH - PIECES, HEAD), F32)]
    pieces += [jnp.zeros((HEAD - 2 * GAIN_LOW + GAIN_HIGH, HEAD), F32)]
    packed[:, SMALL:] = (dlogits.astype(F32) + jnp.concatenate(pieces, axis=0).T).astype(BF)
    writer.send(packed.at[:, QKV:], outs[1].at[:, QKV:])
    for tile in tiles(WIDTH):
        reader.take()
        wide = dot(packed[:, QKV:SMALL], turned[QKV:SMALL, tile]).astype(BF)
        for half in range(TILE // HEAD):
            datt[tile.start // HEAD + half] = wide[:, half * HEAD : (half + 1) * HEAD]
    reader.take(6)
    for k in range(KEY_VALUE_HEADS):
        heads = slice(k * GROUPS, (k + 1) * GROUPS)
        datt_k = datt[heads].reshape(GROUPS * ROWS, HEAD)
        p = probs[heads].reshape(GROUPS * ROWS, ROWS)
        dprobs = dot(datt_k, value[k], 1, 1)
        dvalue = dot(p.astype(BF), datt_k, 0, 0)
        dscores = (p * (dprobs - jnp.sum(dprobs * p, axis=-1, keepdims=True))).astype(BF)
        dqrot = dot(dscores, krot[k]) * SCALE
        dkrot = dot(dscores, qrot[heads].reshape(GROUPS * ROWS, HEAD), 0, 0) * SCALE
        for group in range(GROUPS):
            at = (k * GROUPS + group) * HEAD
            part = dqrot[group * ROWS : (group + 1) * ROWS]
            packed[:, at : at + HEAD] = turn(part, cosine[...], -sine[...]).astype(BF)
        at = Q_END + k * HEAD
        packed[:, at : at + HEAD] = turn(dkrot, cosine[...], -sine[...]).astype(BF)
        at = K_END + k * HEAD
        packed[:, at : at + HEAD] = dvalue.astype(BF)
    writer.send(packed.at[:, :QKV], outs[1].at[:, :QKV])
    parts = []
    for tile in tiles(WIDTH):
        reader.take()
        parts += [dot(packed[:, :QKV], turned[:QKV, tile])]
    dacts = jnp.concatenate(parts, axis=1)
    reader.take()
    dx = dx_out[...] + norm_back(dacts, gain_attn, x_in[...].astype(F32))
    dx_out[...] = dx
    writer.send(dx_out, outs[0])
    if last:
        reader.take(2)
        dx_low = dx.astype(BF)
        both = dot(spread, jnp.concatenate(split(small_in[...]), axis=0), 1, 1).astype(BF)
        gates = jnp.concatenate([both[:, :ROWS] * wide_in[...], both[:, ROWS:] * wide_in[...]], axis=1)
        twice = jnp.concatenate([dx_low, dx_low], axis=0)
        for tile in tiles(WIDTH):
            rows[:, tile] = dot(gates, twice[:, tile]).astype(BF)
            writer.send(rows.at[:, tile], outs[2].at[:, tile])
    writer.finish()


def attn_backward(dx, back, x, kept, w, turned, tables, give, below, returned, order):
    last = below is not None
    outs = [(TOKENS, F32), ((ROWS, PACKED), BF)]
    if last:
        outs += [(WIDE, BF)]
    ins = [dx, back, w, turned, tables[0], tables[1], give, kept["router"], kept["after"], x]
    ins += [kept[n] for n in ("probs", "qrot", "krot", "value")]
    ins += list(below) if last else [returned]
    scratch = [
        (TOKENS, dx.dtype), (back.shape, BF), ((WIDTH, HEAD), BF), ((SMALL, WIDTH), BF),
        (TABLE, F32), (TABLE, F32),
        ((ROWS, SLOTS), BF), (TABLE, F32), (TOKENS, F32), (TOKENS, x.dtype),
        ((QUERY_HEADS, ROWS, ROWS), F32), (HEADS, BF), (KEYS, BF), (KEYS, BF),
        ((SLOTS, ROWS), BF) if last else (WIDE, BF), (TABLE, F32), (HEADS, BF),
    ] + outs
    return run_attn(
        lambda *refs: attn_backward_kernel(last, *refs), "attn_backward", ins, order, outs, scratch,
        24 + WIDTH // TILE, 12, VMEM_BYTES,
    )


def gelu_parts(gate):
    square = gate * gate
    bend = jnp.tanh(GELU_A * gate * (1.0 + GELU_B * square))
    return bend, square


def gelu(gate):
    bend, _ = gelu_parts(gate)
    return 0.5 * gate * (1.0 + bend)


def gelu_both(gate):
    bend, square = gelu_parts(gate)
    slope = 0.5 * (1.0 + bend) + 0.5 * gate * (1.0 - bend * bend) * GELU_A * (
        1.0 + 3.0 * GELU_B * square
    )
    return 0.5 * gate * (1.0 + bend), slope


def gate_up_pairs(l, gate_hbm, up_hbm, gate_w, up_w):
    gate_up = []
    for at in range(0, FF, TILE):
        block = (slice(None), pl.ds(at, TILE))
        gate_up += [(gate_hbm.at[l, 0].at[block], gate_w.at[block])]
        gate_up += [(up_hbm.at[l, 0].at[block], up_w.at[block])]
    return gate_up


def run_experts(kernel, name, ins, order, outs, scratch, in_copies, flops):
    sd = jax.ShapeDtypeStruct
    count = len(ins) + len(order)

    def body(*refs):
        kernel(*refs[: len(ins)], *refs[count:])

    return pl.pallas_call(
        body,
        out_shape=[sd(shape, BF) for shape in outs],
        in_specs=specs_of(ins) + [ANY] * len(order),
        out_specs=[ANY] * len(outs),
        scratch_shapes=[pltpu.VMEM(shape, kind) for shape, kind in scratch]
        + [pltpu.SemaphoreType.DMA((in_copies,)), pltpu.SemaphoreType.DMA((40,))],
        compiler_params=pltpu.CompilerParams(vmem_limit_bytes=VMEM_BYTES),
        cost_estimate=pl.CostEstimate(
            flops=flops, bytes_accessed=20 << 20, transcendentals=SLOTS * FF
        ),
        name=name,
    )(*ins, *order)


def experts_forward_kernel(
    received_hbm, gate_hbm, up_hbm, down_hbm, act_hbm, slope_hbm, hidden_hbm, out_hbm,
    received, gate_w, up_w, down_w, act_s, slope_s, hidden, out, in_sems, out_sems,
):
    gate_up = gate_up_pairs(0, gate_hbm, up_hbm, gate_w, up_w)
    pairs = [(received_hbm, received)] + gate_up + [(down_hbm.at[0, 0], down_w)]
    copies = start_all(pairs, in_sems)
    writer = Writer(out_sems)
    copies.pop(0).wait()
    for tile in tiles(FF):
        copies.pop(0).wait()
        copies.pop(0).wait()
        gate = dot(received[...], gate_w[:, tile])
        up = dot(received[...], up_w[:, tile])
        act, slope = gelu_both(gate)
        act_s[:, tile] = act.astype(BF)
        slope_s[:, tile] = (slope * up).astype(BF)
        hidden[:, tile] = (act * up).astype(BF)
    copies.pop(0).wait()
    writer.send(act_s, act_hbm)
    writer.send(slope_s, slope_hbm)
    writer.send(hidden, hidden_hbm)
    for tile in tiles(WIDTH):
        out[:, tile] = dot(hidden[...], down_w[:, tile]).astype(BF)
        writer.send(out.at[:, tile], out_hbm.at[:, tile])
    writer.finish()


EXPERT_SCRATCH = [((WIDTH, FF), BF), ((WIDTH, FF), BF), ((FF, WIDTH), BF)]


def experts_forward(received, weights, order):
    small = (SLOTS, FF)
    wide = (SLOTS, WIDTH)
    return run_experts(
        experts_forward_kernel, "experts_forward", [received, *weights], order,
        [small, small, small, wide],
        [(wide, BF)] + EXPERT_SCRATCH + [(small, BF)] * 3 + [(wide, BF)],
        8, 6 * SLOTS * WIDTH * FF,
    )


def back_tiles(dgate, dup, gate_w, up_w, back, back_hbm, writer):
    for tile in tiles(WIDTH):
        back[:, tile] = (
            dot(dgate[...], gate_w[tile], 1, 1) + dot(dup[...], up_w[tile], 1, 1)
        ).astype(BF)
        writer.send(back.at[:, tile], back_hbm.at[:, tile])


def expert_gate(me, received, small):
    shares = router_probs(received, small)
    lane = lax.broadcasted_iota(jnp.int32, shares.shape, 1)
    return jnp.sum(jnp.where(lane == me, shares, 0.0), axis=-1, keepdims=True)


def experts_both_kernel(
    me, received_hbm, product_hbm, w_hbm, gate_hbm, up_hbm,
    hidden_hbm, dgate_hbm, dup_hbm, back_hbm,
    received, product, small, gate_w, up_w, act_s, slope_s, hidden, dgate, dup, back,
    in_sems, out_sems,
):
    pairs = [(received_hbm, received)] + gate_up_pairs(1, gate_hbm, up_hbm, gate_w, up_w)
    pairs += [small_source(w_hbm, small), (product_hbm, product)]
    reader, writer = Reader(in_sems, pairs), Writer(out_sems)
    reader.take()
    for tile in tiles(FF):
        reader.take(2)
        gate = dot(received[...], gate_w[:, tile])
        up = dot(received[...], up_w[:, tile])
        act, slope = gelu_both(gate)
        act_s[:, tile] = act
        slope_s[:, tile] = slope * up
        hidden[:, tile] = (act * up).astype(BF)
    reader.take(2)
    writer.send(hidden, hidden_hbm)
    weight = expert_gate(me[0], received[...], small[...])
    total = jnp.zeros((SLOTS, 1), F32)
    for tile in tiles(FF):
        dhidden = product[:, tile]
        total += jnp.sum(dhidden * hidden[:, tile].astype(F32), axis=-1, keepdims=True)
        dhidden = weight * dhidden
        dgate[:, tile] = (dhidden * slope_s[:, tile]).astype(BF)
        dup[:, tile] = (dhidden * act_s[:, tile]).astype(BF)
    writer.send(dgate, dgate_hbm)
    writer.send(dup, dup_hbm)
    high, low = split(total)
    lane = lax.broadcasted_iota(jnp.int32, (SLOTS, HEAD), 1)
    back[:, WIDTH:] = jnp.where(
        lane == 0, high.astype(F32), jnp.where(lane == 1, low.astype(F32), 0.0)
    ).astype(BF)
    writer.send(back.at[:, WIDTH:], back_hbm.at[:, WIDTH:])
    back_tiles(dgate, dup, gate_w, up_w, back, back_hbm, writer)
    writer.finish()


def small_source(w_hbm, small):
    return (w_hbm.at[:, pl.ds(SMALL, HEAD)], small)


def experts_both(me, received, product, w, weights, order):
    small = (SLOTS, FF)
    wide = (SLOTS, WIDTH)
    back = (SLOTS, WIDTH + HEAD)
    return run_experts(
        experts_both_kernel, "experts_both", [me, received, product, w, *weights[:2]], order,
        [small, small, small, back],
        [(wide, BF), (small, F32), ((WIDTH, HEAD), BF)] + EXPERT_SCRATCH[:2]
        + [(small, F32), (small, F32), (small, BF), (small, BF), (small, BF), (back, BF)],
        10, 8 * SLOTS * WIDTH * FF,
    )


def experts_out_kernel(
    me, hidden_hbm, received_hbm, dx_hbm, w_hbm, down_hbm,
    part0_hbm, part1_hbm, part2_hbm, dslot_hbm,
    hidden, received, dx, small, down_w, part0, part1, part2, dslot, in_sems, out_sems,
):
    pairs = [(hidden_hbm, hidden), (down_hbm.at[1, 0], down_w), (received_hbm, received)]
    pairs += [small_source(w_hbm, small), (dx_hbm, dx)]
    reader, writer = Reader(in_sems, pairs), Writer(out_sems)
    reader.take(2)
    for tile in tiles(WIDTH):
        out = dot(hidden[...], down_w[:, tile]).astype(BF)
        for expert in range(EXPERTS):
            for p, target in enumerate((part0, part1, part2)):
                at = expert * CAP + p * PART_ROWS
                target[expert, :, tile] = out[at : at + PART_ROWS]
    writer.send(part0, part0_hbm)
    writer.send(part1, part1_hbm)
    writer.send(part2, part2_hbm)
    reader.take(3)
    weight = expert_gate(me[0], received[...], small[...])
    for tile in tiles(WIDTH):
        dslot[:, tile] = (weight * dx[:, tile].astype(F32)).astype(BF)
    writer.send(dslot, dslot_hbm)
    writer.finish()


def experts_out(me, hidden, received, dx, w, down, order):
    small = (SLOTS, FF)
    wide = (SLOTS, WIDTH)
    part = (EXPERTS, PART_ROWS, WIDTH)
    return run_experts(
        experts_out_kernel, "experts_out", [me, hidden, received, dx, w, down], order,
        [part, part, part, wide],
        [(small, BF), (wide, BF), (wide, BF), ((WIDTH, HEAD), BF), ((FF, WIDTH), BF)]
        + [(part, BF)] * 3 + [(wide, BF)],
        5, 2 * SLOTS * WIDTH * FF,
    )


def experts_backward_kernel(
    dslot_hbm, act_hbm, slope_hbm, gate_hbm, up_hbm, down_hbm, dgate_hbm, dup_hbm, back_hbm,
    dslot, act_s, slope_s, gate_w, up_w, down_w, dgate, dup, back, in_sems, out_sems,
):
    pairs = [(dslot_hbm, dslot)]
    for tile in tiles(FF):
        block = pl.ds(tile.start, TILE)
        pairs += [(down_hbm.at[0, 0].at[block], down_w.at[block])]
    pairs += [(slope_hbm, slope_s), (act_hbm, act_s)]
    for tile in tiles(WIDTH):
        block = pl.ds(tile.start, TILE)
        pairs += [(gate_hbm.at[0, 0].at[block], gate_w.at[block])]
        pairs += [(up_hbm.at[0, 0].at[block], up_w.at[block])]
    copies = start_all(pairs, in_sems)
    writer = Writer(out_sems)
    copies.pop(0).wait()
    dhidden = []
    for tile in tiles(FF):
        copies.pop(0).wait()
        dhidden += [dot(dslot[...], down_w[tile], 1, 1)]
    copies.pop(0).wait()
    copies.pop(0).wait()
    for tile, part in zip(tiles(FF), dhidden):
        dgate[:, tile] = (part * slope_s[:, tile].astype(F32)).astype(BF)
        dup[:, tile] = (part * act_s[:, tile].astype(F32)).astype(BF)
    writer.send(dgate, dgate_hbm)
    writer.send(dup, dup_hbm)
    for copy in copies:
        copy.wait()
    back_tiles(dgate, dup, gate_w, up_w, back, back_hbm, writer)
    writer.finish()


def experts_backward(dslot, act, slope, weights, order):
    small = (SLOTS, FF)
    wide = (SLOTS, WIDTH)
    return run_experts(
        experts_backward_kernel, "experts_backward", [dslot, act, slope, *weights], order,
        [small, small, wide],
        [(wide, BF), (small, BF), (small, BF)] + EXPERT_SCRATCH
        + [(small, BF), (small, BF), (wide, BF)],
        6 + 2 * WIDTH // TILE, 6 * SLOTS * WIDTH * FF,
    )


def on_core(core, me, ins, outs, scratch, kernel, name, above, order):
    sd = jax.ShapeDtypeStruct
    held = [] if above is None else list(above)
    first_out = 1 + len(ins) + len(held) + len(order)

    def body(*refs):
        @pl.when(refs[0][0] % 2 == core)
        def _():
            kernel(refs[0][0], refs[1 : 1 + len(ins)], refs[first_out : first_out + len(outs)],
                   refs[first_out + len(outs) :])

    return pl.pallas_call(
        body,
        out_shape=[sd(shape, kind) for shape, kind in outs],
        in_specs=[pl.BlockSpec(memory_space=pltpu.SMEM)]
        + [ANY] * (len(ins) + len(held) + len(order)),
        out_specs=[ANY] * len(outs),
        input_output_aliases={1 + len(ins) + i: i for i in range(len(held))},
        scratch_shapes=[pltpu.VMEM(shape, kind) for shape, kind in scratch]
        + [pltpu.SemaphoreType.DMA((24,)), pltpu.SemaphoreType.DMA((24,))],
        compiler_params=pltpu.CompilerParams(vmem_limit_bytes=VMEM_BYTES),
        name=name,
    )(me, *ins, *held, *order)


def upper_product_kernel(me, ins, outs, scratch):
    rows, down, product, in_sems, out_sems = scratch
    pairs = [(ins[0], rows)]
    for tile in tiles(FF):
        block = pl.ds(tile.start, TILE)
        pairs += [(ins[1].at[1, 0].at[block], down.at[block])]
    reader, writer = Reader(in_sems, pairs), Writer(out_sems)
    reader.take()
    for tile in tiles(FF):
        reader.take()
        product[:, tile] = dot(rows[...], down[tile], 1, 1)
        writer.send(product.at[:, tile], outs[0].at[:, tile])
    writer.finish()


def upper_product(core, me, dx_rows, w_down, above, order):
    small = (SLOTS, FF)
    return on_core(
        core, me, [dx_rows, w_down], [(small, F32)], [(WIDE, BF), ((FF, WIDTH), BF), (small, F32)],
        upper_product_kernel, "upper_product", above, order,
    )


def turn_weights_kernel(me, ins, outs, scratch):
    w, turned, in_sems, out_sems = scratch
    ring_out = len(ins) > 1
    pairs = [column_block(ins[0], w, at) for at in range(0, QKV if ring_out else SMALL, TILE)]
    if ring_out:
        pairs += ring_blocks(me, ins[1:], w)
    reader, writer = Reader(in_sems, pairs), Writer(out_sems)
    for tile in tiles(SMALL):
        if ring_out and tile.start == QKV:
            reader.take(len(ins) - 1)
        elif not ring_out or tile.start < QKV:
            reader.take()
        turned[tile] = w[:, tile].T
        writer.send(turned.at[tile], outs[0].at[tile])
    writer.finish()


def turn_weights(core, me, w, blocks, above, order):
    turned = ((SMALL, WIDTH), BF)
    return on_core(
        core, me, [w, *blocks], [turned], [((WIDTH, SMALL), BF), turned], turn_weights_kernel,
        "turn_weights", above, order,
    )


def expert_grads_kernel(received, dgate_pre, dup_pre, hidden, dslot, packed):
    gate = dot(received[...], dgate_pre[...], 0, 0).astype(BF)
    up = dot(received[...], dup_pre[...], 0, 0).astype(BF)
    down = dot(hidden[...], dslot[...], 0, 0).astype(BF)
    for part in range(DP // 2):
        packed[part, :SHARD, :FF] = gate[part * SHARD : (part + 1) * SHARD]
        packed[part, :SHARD, FF:] = up[part * SHARD : (part + 1) * SHARD]
        packed[part, SHARD:] = down[part * FF // DP : (part + 1) * FF // DP]


def expert_grads(received, dgate_pre, dup_pre, hidden, dslot):
    rows = SHARD + FF // DP
    whole = lambda width: pl.BlockSpec((SLOTS, width), lambda i: (0, 0))
    part = lambda width: pl.BlockSpec((SLOTS, width), lambda i: (0, i))
    return pl.pallas_call(
        expert_grads_kernel,
        grid=(2,),
        out_shape=jax.ShapeDtypeStruct((DP, rows, WIDTH), BF),
        in_specs=[part(WIDTH // 2), whole(FF), whole(FF), part(FF // 2), whole(WIDTH)],
        out_specs=pl.BlockSpec((DP // 2, rows, WIDTH), lambda i: (i, 0, 0)),
        compiler_params=pltpu.CompilerParams(vmem_limit_bytes=VMEM_BYTES),
        cost_estimate=pl.CostEstimate(
            flops=6 * SLOTS * WIDTH * FF, bytes_accessed=14 << 20, transcendentals=0
        ),
        name="expert_grads",
    )(received, dgate_pre, dup_pre, hidden, dslot).reshape(DP * rows, WIDTH)


def pack_kernel(
    l, query_hbm, key_hbm, value_hbm, out_hbm, router_hbm, gain_attn, gain_ffn, packed_hbm, *rest
):
    if l == 0:
        out_copy, packed, out, router, sems, out_sems = rest
    else:
        packed, router, sems, out_sems = rest
        out = packed.at[:, pl.ds(QKV, WIDTH)]
    pairs = [
        (router_hbm.at[l], router),
        (query_hbm.at[l], packed.at[:, pl.ds(0, Q_END)]),
        (key_hbm.at[l], packed.at[:, pl.ds(Q_END, K_END - Q_END)]),
        (value_hbm.at[l], packed.at[:, pl.ds(K_END, QKV - K_END)]),
        (out_hbm.at[l], out),
    ]
    reader, writer = Reader(sems, pairs), Writer(out_sems)
    reader.take()
    small = [router[...].astype(F32), gain_attn[l : l + 1].astype(F32)]
    small += [gain_ffn[l : l + 1].astype(F32), jnp.zeros((HEAD - EXPERTS - 2, SHARD), F32)]
    small = jnp.concatenate(small, axis=0)
    small = jnp.concatenate([small, jnp.zeros((HEAD, TILE - SHARD), F32)], axis=1).T
    packed[:, packed.shape[1] - HEAD :] = small[:SHARD].astype(BF)
    reader.take(3)
    if l == 0:
        writer.send(packed, packed_hbm)
        reader.take()
        writer.send(out, out_copy)
    else:
        reader.take()
        writer.send(packed, packed_hbm)
    writer.finish()


def pack(l, query, key, value, out, router, gain_attn, gain_ffn):
    sd = jax.ShapeDtypeStruct
    vmem = pl.BlockSpec(memory_space=pltpu.VMEM)
    packed = (SHARD, QKV + HEAD) if l == 0 else (SHARD, PACKED)
    outs = [packed] + [(SHARD, WIDTH)] * (l == 0)
    return pl.pallas_call(
        lambda *refs: pack_kernel(l, *refs),
        out_shape=[sd(shape, BF) for shape in outs],
        in_specs=[ANY] * 5 + [vmem] * 2,
        out_specs=[ANY] * len(outs),
        scratch_shapes=[pltpu.VMEM(shape, BF) for shape in outs]
        + [pltpu.VMEM((EXPERTS, SHARD), BF)]
        + [pltpu.SemaphoreType.DMA((5,)), pltpu.SemaphoreType.DMA((2,))],
        compiler_params=pltpu.CompilerParams(vmem_limit_bytes=VMEM_BYTES),
        name="pack",
    )(query, key, value, out, router.transpose(0, 2, 1), gain_attn, gain_ffn)


def ring(block):
    def move(values, step):
        return lax.ppermute(values, "dp", [(i, (i + step) % DP) for i in range(DP)])

    half = block.shape[0] // 2
    previous, following = move(block, 2), move(block, -2)
    far = [move(previous[:half], 2), move(following[half:], -2)]
    mine = [block, previous, following, *far]
    swap = [(i, i ^ 1) for i in range(DP)]
    return mine + [lax.ppermute(values, "dp", swap) for values in mine]


def seq_tables(counts):
    ends = jnp.cumsum(counts)
    starts = ends - counts
    place = jnp.arange(ROWS, dtype=jnp.int32)
    member = (place[:, None] >= starts[None, :]) & (place[:, None] < ends[None, :])
    index = jnp.arange(counts.shape[0], dtype=jnp.int32)
    segment = jnp.sum(jnp.where(member, index[None, :], 0), axis=1)
    position = place - jnp.sum(jnp.where(member, starts[None, :], 0), axis=1)
    allowed = (segment[:, None] == segment[None, :]) & (place[:, None] >= place[None, :])
    freqs = ROPE_BASE ** (-2.0 * jnp.arange(HEAD // 2, dtype=F32) / HEAD)
    angle = position.astype(F32)[:, None] * freqs[None, :]
    cosine, sine = jnp.cos(angle), jnp.sin(angle)
    return (
        jnp.concatenate([cosine, cosine], axis=1),
        jnp.concatenate([-sine, sine], axis=1),
        allowed.astype(F32),
    )


def slot_matrix(choices, in_parts=False):
    experts = jnp.arange(EXPERTS, dtype=jnp.int32)
    member = jnp.any(choices[:, :, None] == experts[None, None, :], axis=1).astype(BF)
    row = lax.broadcasted_iota(jnp.int32, (ROWS, ROWS), 0)
    column = lax.broadcasted_iota(jnp.int32, (ROWS, ROWS), 1)
    rank = dot((column < row).astype(BF), member).astype(BF)
    slot = jnp.arange(SLOTS, dtype=jnp.int32)[None, :]
    if in_parts:
        owner, place = slot % PART // PART_ROWS, slot // PART * PART_ROWS + slot % PART_ROWS
    else:
        owner, place = slot // CAP, slot % CAP
    expand = (owner == experts[:, None]).astype(BF)
    return ((dot(member, expand) > 0.5) & (dot(rank, expand) == place.astype(F32))).astype(BF)


def exchange(rows):
    width = rows.shape[-1]
    moved = lax.all_to_all(
        rows.reshape(EXPERTS, -1, width), "expert", split_axis=0, concat_axis=0, tiled=True
    )
    return moved.reshape(-1, width)


def after(values, *order):
    return pl.pallas_call(
        lambda *refs: None,
        out_shape=jax.ShapeDtypeStruct(values.shape, values.dtype),
        in_specs=[ANY] * (1 + len(order)),
        out_specs=ANY,
        input_output_aliases={0: 0},
        name="after",
    )(values, *order)


def turn_columns_kernel(me, columns_hbm, turned_hbm, columns, turned, in_sems, out_sems):
    base = me[0] * SHARD // HEAD * HEAD
    pairs = []
    for i in range(3):
        at = pl.multiple_of(base + i * WIDTH, HEAD)
        pairs += [(columns_hbm.at[:, pl.ds(at, TILE)], columns.at[:, pl.ds(i * TILE, TILE)])]
    reader, writer = Reader(in_sems, pairs), Writer(out_sems)
    for i in range(3):
        reader.take()
        turned[i] = columns[:, i * TILE : (i + 1) * TILE].T
        writer.send(turned.at[i], turned_hbm.at[i])
    writer.finish()


def turn_columns(me, columns):
    tokens = DP * ROWS
    return pl.pallas_call(
        turn_columns_kernel,
        out_shape=jax.ShapeDtypeStruct((3, TILE, tokens), BF),
        in_specs=[pl.BlockSpec(memory_space=pltpu.SMEM), ANY],
        out_specs=ANY,
        scratch_shapes=[
            pltpu.VMEM((tokens, 3 * TILE), BF),
            pltpu.VMEM((3, TILE, tokens), BF),
            pltpu.SemaphoreType.DMA((3,)),
            pltpu.SemaphoreType.DMA((3,)),
        ],
        compiler_params=pltpu.CompilerParams(vmem_limit_bytes=VMEM_BYTES),
        cost_estimate=pl.CostEstimate(flops=0, bytes_accessed=4 << 20, transcendentals=0),
        name="turn_columns",
    )(me, columns)


def dense_grads_kernel(me, turned_hbm, factors_hbm, pieces_hbm, turned, factors, total, pieces,
                       in_sems, out_sems):
    start = me[0] * SHARD
    shift = start % HEAD
    base = start - shift
    copies = Writer(out_sems)
    pairs = [(turned_hbm, turned)]
    for at, width in [(SMALL, HEAD)] + [(at, 2 * CHUNK) for at in range(0, SMALL, 2 * CHUNK)]:
        block = (slice(None), pl.ds(at, width))
        pairs += [(factors_hbm.at[block], factors.at[block])]
    reader = Reader(in_sems, pairs)
    reader.take(2)

    def put(chunk, values):
        pieces[chunk] = values.astype(BF)
        copies.send(pieces.at[chunk], pieces_hbm.at[chunk])

    ends = jnp.zeros((ROWS, HEAD), F32)
    for source in range(DP):
        ends += factors[source * ROWS : (source + 1) * ROWS, SMALL:].astype(F32)
    lane = lax.broadcasted_iota(jnp.int32, (ROWS, HEAD), 1)

    def gain_piece(piece):
        held = (lane == piece + GAIN_HIGH) | (lane == piece + GAIN_LOW)
        return jnp.sum(jnp.where(held, ends, 0.0), axis=1, keepdims=True)

    first, second = gain_piece(base // HEAD), gain_piece(base // HEAD + 1)
    gain = jnp.where(
        shift == 0,
        jnp.concatenate([first, second[: SHARD - ROWS]], axis=0),
        jnp.concatenate([first[ROWS // 2 :], second], axis=0),
    )
    gain_high, gain_low = split(gain)
    rows = pl.ds(pl.multiple_of(shift, 64), SHARD)
    total[1, :, :HEAD] = dot(turned[2], factors[:, SMALL:])
    router = total[1, rows, :HEAD]
    lane = lax.broadcasted_iota(jnp.int32, (SHARD, HEAD), 1)
    router = jnp.where(lane < EXPERTS, router, 0.0)
    router = jnp.where(lane == EXPERTS, gain_high.astype(F32), router)
    router = jnp.where(lane == EXPERTS + 1, gain_low.astype(F32), router)
    put(CHUNKS - 2, jnp.concatenate([router, jnp.zeros_like(router)], axis=1))
    put(CHUNKS - 1, jnp.zeros((SHARD, CHUNK), F32))
    for pair in range(SMALL // CHUNK // 2):
        reader.take()
        at = pair * 2 * CHUNK
        total[pair % 2] = dot(turned[0 if at < QKV else 1], factors[:, at : at + 2 * CHUNK])
        put(2 * pair, total[pair % 2, rows, :CHUNK])
        put(2 * pair + 1, total[pair % 2, rows, CHUNK:])
    copies.finish()


def dense_grads(me, turned, factors, order):
    tokens = DP * ROWS

    def body(*refs):
        dense_grads_kernel(*refs[:3], *refs[3 + len(order) :])

    return pl.pallas_call(
        body,
        out_shape=jax.ShapeDtypeStruct((CHUNKS, SHARD, CHUNK), BF),
        in_specs=[pl.BlockSpec(memory_space=pltpu.SMEM)] + [ANY] * (2 + len(order)),
        out_specs=ANY,
        scratch_shapes=[
            pltpu.VMEM((3, TILE, tokens), BF),
            pltpu.VMEM((tokens, PACKED), BF),
            pltpu.VMEM((2, TILE, 2 * CHUNK), F32),
            pltpu.VMEM((CHUNKS, SHARD, CHUNK), BF),
            pltpu.SemaphoreType.DMA((1 + CHUNKS,)),
            pltpu.SemaphoreType.DMA((CHUNKS,)),
        ],
        compiler_params=pltpu.CompilerParams(vmem_limit_bytes=VMEM_BYTES),
        cost_estimate=pl.CostEstimate(
            flops=2 * tokens * TILE * PACKED, bytes_accessed=10 << 20, transcendentals=0
        ),
        name="dense_grads",
    )(me, turned, factors, *order)


def to_expert_peers(pieces):
    return lax.all_to_all(pieces, "expert", split_axis=0, concat_axis=0, tiled=True)


def sum_pieces_kernel(pieces_hbm, out_hbm, pieces, out, in_sems, out_sems):
    half = CHUNKS // 2
    pairs = []
    for at in (0, half):
        block = pl.ds(at, half)
        pairs += [(pieces_hbm.at[block, :, pl.ds(0, CHUNK)], pieces.at[block])]
    reader, writer = Reader(in_sems, pairs), Writer(out_sems)
    reader.take()
    total = pieces[0].astype(F32)
    for i in range(1, half):
        total += pieces[i].astype(F32)
    reader.take()
    for i in range(half, CHUNKS):
        total += pieces[i].astype(F32)
    out[...] = total.astype(BF)
    if len(out_hbm.shape) == 3:
        for i in range(CHUNKS):
            writer.send(out, out_hbm.at[i])
    else:
        writer.send(out, out_hbm)
    writer.finish()


def sum_pieces(pieces, copies):
    return pl.pallas_call(
        sum_pieces_kernel,
        out_shape=jax.ShapeDtypeStruct((copies,) * (copies > 1) + (SHARD, CHUNK), BF),
        in_specs=[ANY],
        out_specs=ANY,
        scratch_shapes=[
            pltpu.VMEM((CHUNKS, SHARD, CHUNK), BF),
            pltpu.VMEM((SHARD, CHUNK), BF),
            pltpu.SemaphoreType.DMA((2,)),
            pltpu.SemaphoreType.DMA((CHUNKS,)),
        ],
        compiler_params=pltpu.CompilerParams(vmem_limit_bytes=VMEM_BYTES),
        name="sum_pieces",
    )(pieces)


def finish_kernel(l, refs):
    (pieces, w_query, key_projection, value_projection, norm_attn), refs = refs[:5], refs[5:]
    if l == 0:
        ends_above, refs = refs[0], refs[5:]
        (query_hbm, key_hbm, value_hbm, out_hbm, gain_attn, gain_ffn, router) = refs[:7]
        query, key, value, out, sems = refs[7:]
    else:
        query_hbm, key_hbm, value_hbm, out_hbm, ends_out, query, key, value, out, sems = refs
    writer = Writer(sems)
    rows = jnp.zeros((SHARD, 1), F32)
    for chunk in range(SMALL // CHUNK):
        part = pieces[chunk].astype(F32)
        lanes = slice(chunk * CHUNK, (chunk + 1) * CHUNK)
        if chunk < Q_END // CHUNK:
            query[:, lanes] = part
            weight = w_query[l, :, lanes]
        elif chunk == Q_END // CHUNK:
            key[...] = part
            weight = key_projection[l]
            writer.send(query, query_hbm.at[l])
            writer.send(key, key_hbm.at[l])
        elif chunk < QKV // CHUNK:
            value[...] = part
            weight = value_projection[l]
            writer.send(value, value_hbm.at[l])
        else:
            out[:, lanes.start - QKV : lanes.stop - QKV] = part
            continue
        rows += jnp.sum(part * weight.astype(F32), axis=1, keepdims=True)
    writer.send(out, out_hbm.at[l])
    ends = pieces[CHUNKS - 2, :, :HEAD].astype(F32)
    ffn = ends[:, EXPERTS : EXPERTS + 1] + ends[:, EXPERTS + 1 : EXPERTS + 2]
    lane = lax.broadcasted_iota(jnp.int32, (SHARD, HEAD), 1)
    ends = jnp.where(lane == EXPERTS, rows, jnp.where(lane == EXPERTS + 1, ffn, ends))
    if l > 0:
        ends_out[...] = ends
    else:
        for layer, part in enumerate((ends, ends_above[...])):
            wide = jnp.concatenate([part, jnp.zeros((TILE - SHARD, HEAD), F32)], axis=0).T
            router[layer] = wide[:EXPERTS, :SHARD]
            gain = norm_attn[layer : layer + 1].astype(F32)
            gain_attn[layer : layer + 1] = wide[EXPERTS : EXPERTS + 1, :SHARD] / gain
            gain_ffn[layer : layer + 1] = wide[EXPERTS + 1 : EXPERTS + 2, :SHARD]
    writer.finish()


def finish(l, pieces, weights, norm_attn, above):
    sd = jax.ShapeDtypeStruct
    vmem = pl.BlockSpec(memory_space=pltpu.VMEM)
    keys = (SHARD, KEY_VALUE_HEADS * HEAD)
    slabs = [(SHARD, Q_END), keys, keys, (SHARD, WIDTH)]
    outs = [sd((LAYERS,) + shape, F32) for shape in slabs]
    if above is None:
        outs += [sd((SHARD, HEAD), F32)]
        ins, in_specs, aliases = [], [], {}
    else:
        outs += [sd((LAYERS, SHARD), F32)] * 2 + [sd((LAYERS, EXPERTS, SHARD), F32)]
        ins, in_specs = [above[4], *above[:4]], [vmem] + [ANY] * 4
        aliases = {6 + i: i for i in range(4)}
    return pl.pallas_call(
        lambda *refs: finish_kernel(l, refs),
        out_shape=outs,
        in_specs=[vmem] * 5 + in_specs,
        out_specs=[ANY] * 4 + [vmem] * (len(outs) - 4),
        input_output_aliases=aliases,
        scratch_shapes=[pltpu.VMEM(shape, F32) for shape in slabs]
        + [pltpu.SemaphoreType.DMA((4,))],
        compiler_params=pltpu.CompilerParams(vmem_limit_bytes=VMEM_BYTES),
        name="finish",
    )(pieces, *weights, norm_attn, *ins)


def finish_experts_kernel(shares0, shares1, gate, up, down):
    for l, shares in enumerate((shares0, shares1)):
        gate[l, 0] = shares[:SHARD, :FF].astype(F32)
        up[l, 0] = shares[:SHARD, FF:].astype(F32)
        down[l, 0] = shares[SHARD:].astype(F32)


def finish_experts(shares0, shares1):
    sd = jax.ShapeDtypeStruct
    vmem = pl.BlockSpec(memory_space=pltpu.VMEM)
    return pl.pallas_call(
        finish_experts_kernel,
        out_shape=[
            sd((LAYERS, 1, SHARD, FF), F32), sd((LAYERS, 1, SHARD, FF), F32),
            sd((LAYERS, 1, FF // DP, WIDTH), F32),
        ],
        in_specs=[vmem] * 2,
        out_specs=[vmem] * 3,
        compiler_params=pltpu.CompilerParams(vmem_limit_bytes=VMEM_BYTES),
        name="finish_experts",
    )(shares0, shares1)


def mixed_kernel(x_hbm, high, low, part0, part1, part2, out, x, gates, returned, sems):
    pairs = [(high, gates.at[:ROWS]), (low, gates.at[ROWS:]), (x_hbm, x)]
    for p, part in enumerate((part0, part1, part2)):
        pairs += [(part, returned.at[pl.ds(p * PART, PART)])]
    Reader(sems, pairs).take(len(pairs))
    for tile in tiles(WIDTH):
        both = dot(gates[...], returned[:, tile])
        out[:, tile] = (x[:, tile] + both[:ROWS] + both[ROWS:]).astype(BF)


def mixed_rows(x, high, low, parts):
    return pl.pallas_call(
        mixed_kernel,
        out_shape=jax.ShapeDtypeStruct(TOKENS, BF),
        in_specs=[ANY] * 6,
        out_specs=pl.BlockSpec(memory_space=pltpu.VMEM),
        scratch_shapes=[
            pltpu.VMEM(TOKENS, F32),
            pltpu.VMEM((2 * ROWS, SLOTS), BF),
            pltpu.VMEM(WIDE, BF),
            pltpu.SemaphoreType.DMA((6,)),
        ],
        compiler_params=pltpu.CompilerParams(vmem_limit_bytes=VMEM_BYTES),
        name="mixed",
    )(x, high, low, *parts)


def local(
    tokens, cotangent, lengths, routes, norm_attn, w_query, key_projection, value_projection,
    w_out, norm_ffn, w_router, w_gate, w_up, w_down,
):
    me_dp = lax.axis_index("dp").astype(jnp.int32).reshape(1)
    me_expert = lax.axis_index("expert").astype(jnp.int32).reshape(1)
    tables = seq_tables(lengths[0])
    give = [slot_matrix(routes[l]) for l in range(LAYERS)]
    take = [g.T for g in give]
    give_parts = slot_matrix(routes[1], True)
    experts = (w_gate, w_up, w_down)

    def gather(values):
        return lax.all_gather(values, "dp", axis=0, tiled=True)

    weights = (w_query, key_projection, value_projection, w_out, w_router, norm_attn, norm_ffn)
    shard0, out_shard0 = pack(0, *weights)
    w = [gather(shard0), gather(pack(1, *weights)[0])]
    out_ring = [me_dp, *ring(out_shard0)]

    dx_rows = exchange(dot(take[1], cotangent).astype(BF))

    turned_w = turn_weights(1, me_dp, w[0], out_ring[1:], None, ())
    product = upper_product(1, me_dp, dx_rows, w_down, None, turned_w)
    kept0 = attn_forward(
        tokens, None, w[0], out_ring, tables, take[0], give[0],
        (*product, give[1], give_parts, me_expert),
    )
    received0 = exchange(kept0["rows"])
    act0, slope0, hidden0, out0 = experts_forward(received0, experts, ())
    returned0 = exchange(out0)
    turned_w = turn_weights(0, me_dp, w[0], out_ring[1:], turned_w, (out0,))
    product = upper_product(0, me_dp, dx_rows, w_down, product, turned_w)
    turned_w1 = turn_weights(0, me_dp, w[1], [], None, product)
    columns0 = gather(kept0["columns"])

    kept1 = attn_forward(
        kept0["after"], (kept0["high"], kept0["low"], returned0), w[1], None, tables, take[1],
        give_parts, tuple(turned_w1),
    )
    received1 = exchange(kept1["rows"])
    columns1 = gather(kept1["columns"])
    turned_w1 = turn_weights(1, me_dp, w[1], [], turned_w1, (received1,))
    hidden1, dgate1, dup1, back1 = experts_both(
        me_expert, received1, product[0], w[1], experts, tuple(turned_w1)
    )
    back1 = exchange(back1)
    *parts, dslot1 = experts_out(me_expert, hidden1, received1, dx_rows, w[1], w_down, ())
    grads1 = expert_grads(received1, dgate1, dup1, hidden1, dslot1)
    turned0 = turn_columns(me_dp, columns0)
    parts[0] = exchange(after(parts[0], grads1, turned0))

    dx0, packed1, rows0 = attn_backward(
        cotangent, back1, kept1["x"], kept1, w[1], turned_w1[0], tables, give[1],
        (take[0], kept0["router"]), None, (),
    )
    packed1 = after(packed1, parts[0])
    dslot0 = exchange(rows0)
    factors1 = gather(packed1)
    shares1 = lax.psum_scatter(after(grads1, packed1), "dp", scatter_dimension=0, tiled=True)
    dgate0, dup0, back0 = experts_backward(dslot0, act0, slope0, experts, ())
    back0 = exchange(back0)
    grads0 = expert_grads(received0, dgate0, dup0, hidden0, dslot0)
    parts[1] = exchange(parts[1])
    turned1 = turn_columns(me_dp, columns1)
    pieces1 = dense_grads(me_dp, turned1, factors1, (parts[1],))
    parts[2] = exchange(after(parts[2], grads0, pieces1))
    grad_tokens, packed0 = attn_backward(
        dx0, back0, tokens, kept0, w[0], turned_w[0], tables, give[0], None, returned0, ()
    )
    factors0 = gather(after(packed0, parts[2]))
    summed1 = sum_pieces(to_expert_peers(pieces1), CHUNKS)
    shares0 = lax.psum_scatter(after(grads0, summed1, shares1), "dp", scatter_dimension=0, tiled=True)
    mixed = mixed_rows(kept1["after"], kept1["high"], kept1["low"], parts)
    pieces1 = to_expert_peers(summed1)
    pieces0 = dense_grads(me_dp, turned0, factors0, ())
    pieces0 = to_expert_peers(after(pieces0, pieces1))
    pieces0 = to_expert_peers(sum_pieces(pieces0, CHUNKS))

    dense = (w_query, key_projection, value_projection)
    above = finish(1, pieces1, dense, norm_attn, None)
    query, key, value, out, gain_attn, gain_ffn, router = finish(
        0, pieces0, dense, norm_attn, above
    )
    gate, up, down = finish_experts(shares0, shares1)
    return (
        mixed, grad_tokens, gain_attn, query, key, value, out, gain_ffn,
        router.transpose(0, 2, 1), gate, up, down,
    )


def solution(mesh):
    placed = (
        P(("dp", "expert"), None),
        P(("dp", "expert"), None),
        P(("dp", "expert"), None),
        P(None, ("dp", "expert"), None),
        P(None, "dp"),
        P(None, "dp", None),
        P(None, "dp", None),
        P(None, "dp", None),
        P(None, "dp", None),
        P(None, "dp"),
        P(None, "dp", None),
        P(None, "expert", None, None),
        P(None, "expert", None, None),
        P(None, "expert", None, None),
    )
    return jax.shard_map(
        local,
        mesh=mesh,
        in_specs=placed,
        out_specs=(
            P(("dp", "expert"), None),
            P(("dp", "expert"), None),
            P(None, "dp"),
            P(None, "dp", None),
            P(None, "dp", None),
            P(None, "dp", None),
            P(None, "dp", None),
            P(None, "dp"),
            P(None, "dp", None),
            P(None, "expert", "dp", None),
            P(None, "expert", "dp", None),
            P(None, "expert", "dp", None),
        ),
        check_vma=False,
    )
```

```python
import jax
import jax.numpy as jnp
from jax import lax
from jax.experimental import pallas as pl
from jax.experimental.pallas import tpu as pltpu
from jax.sharding import PartitionSpec as P

QUERY_HEADS = 12
KEY_VALUE_HEADS = 2
GROUPS = QUERY_HEADS // KEY_VALUE_HEADS
HEAD = 128
LAYERS = 2
WIDTH = 1536
FF = 768
ROWS = 128
EXPERTS = 16
CAP = 48
SLOTS = EXPERTS * CAP
DP = 8
SHARD = WIDTH // DP
Q_END = QUERY_HEADS * HEAD
K_END = Q_END + KEY_VALUE_HEADS * HEAD
QKV = K_END + KEY_VALUE_HEADS * HEAD
SMALL = QKV + WIDTH
PACKED = SMALL + HEAD
GAIN_ATTN, GAIN_FFN = 16, 17
GAIN_HIGH, GAIN_LOW = 16, 32
PIECES = WIDTH // HEAD
TILE = 256
PARTS = 3
PART = SLOTS // PARTS
PART_ROWS = CAP // PARTS
CHUNKS, CHUNK = 16, 256
COLUMNS = 3 * WIDTH
EPSILON = 1e-06
ROPE_BASE = 1000000.0
SCALE = HEAD ** (-0.5)
GELU_A = 0.7978845608028654
GELU_B = 0.044715
VMEM_BYTES = 56 << 20
BF = jnp.bfloat16
F32 = jnp.float32
ANY = pl.BlockSpec(memory_space=pl.ANY)


def dot(left, right, left_dim=1, right_dim=0):
    return lax.dot_general(
        left, right, (((left_dim,), (right_dim,)), ((), ())), preferred_element_type=F32
    )


def split(values):
    high = values.astype(BF)
    return high, (values - high.astype(F32)).astype(BF)


def unit(values):
    return lax.rsqrt(jnp.mean(values * values, axis=-1, keepdims=True) + EPSILON)


def turn(values, cosine, sine):
    return values * cosine + pltpu.roll(values, HEAD // 2, 1) * sine


def expert_lanes(transposed=False, in_parts=False):
    shape = (SLOTS, HEAD) if transposed else (HEAD, SLOTS)
    slot = lax.broadcasted_iota(jnp.int32, shape, 0 if transposed else 1)
    expert = lax.broadcasted_iota(jnp.int32, shape, 1 if transposed else 0)
    if in_parts:
        held = ((slot & (PART - 1)) >> 4) == expert
    else:
        held = (slot >= expert * CAP) & (slot < expert * CAP + CAP)
    return held.astype(F32).astype(BF)


def gain_rows(small):
    row = lax.broadcasted_iota(jnp.int32, (8, HEAD), 0)
    lane = lax.broadcasted_iota(jnp.int32, (8, HEAD), 1)
    pick = ((lane == row + GAIN_ATTN) & (row < 2)).astype(F32).astype(BF)
    rows = dot(pick, small, 1, 1)
    return rows[0:1], rows[1:2]


def router_probs(rows, small):
    logits = dot(rows, small)
    lane = lax.broadcasted_iota(jnp.int32, logits.shape, 1)
    logits = jnp.where(lane < EXPERTS, logits, -1e30)
    powers = jnp.exp(logits - jnp.max(logits, axis=-1, keepdims=True))
    return powers / jnp.sum(powers, axis=-1, keepdims=True)


def start_all(pairs, sems):
    copies = [
        pltpu.make_async_copy(source, target, sems.at[i]) for i, (source, target) in enumerate(pairs)
    ]
    for copy in copies:
        copy.start()
    return copies


class Writer:
    def __init__(self, sems):
        self.sems, self.copies = sems, []

    def send(self, source, target):
        copy = pltpu.make_async_copy(source, target, self.sems.at[len(self.copies)])
        copy.start()
        self.copies.append(copy)

    def finish(self):
        for copy in self.copies:
            copy.wait()


class Reader:
    def __init__(self, sems, pairs):
        self.copies = start_all(pairs, sems)

    def take(self, count=1):
        for _ in range(count):
            self.copies.pop(0).wait()


def tiles(width):
    return [slice(at, at + TILE) for at in range(0, width, TILE)]


def small_block(w_hbm, w):
    last = w_hbm.shape[1] - HEAD
    return (w_hbm.at[:, pl.ds(last, HEAD)], w.at[:, pl.ds(SMALL, HEAD)])


def column_block(w_hbm, w, at):
    return (w_hbm.at[:, pl.ds(at, TILE)], w.at[:, pl.ds(at, TILE)])


def ring_blocks(me, blocks, w):
    pairs = []
    for core in range(2):
        start = me if core == 0 else me + 1 - 2 * (me % 2)
        for block, step in enumerate((0, DP - 2, 2, 4, 4)):
            ref = blocks[core * 5 + block]
            at = (start + step) % DP * SHARD + (SHARD // 2 if block == 4 else 0)
            at = pl.multiple_of(at, SHARD // 2)
            pairs += [(ref, w.at[pl.ds(at, ref.shape[0]), pl.ds(QKV, WIDTH)])]
    return pairs


def attn_forward_kernel(first, ins, outs, scratch):
    (x_hbm, w_hbm, cosine_hbm, sine_hbm, allowed_hbm, take_hbm, give_hbm), ins = ins[:7], ins[7:]
    (columns_hbm, qrot_hbm, krot_hbm, value_hbm, probs_hbm, after_hbm, router_hbm, high_hbm, low_hbm,
     rows_hbm), outs = outs[:10], outs[10:]
    (x_in, w, cosine, sine, allowed, take, give, returned, gates, x, columns, qrot, krot, value, probs,
     after, router, high, low, rows, in_sems, out_sems) = scratch
    acts = columns.at[:, :WIDTH]
    attended = columns.at[:, WIDTH : 2 * WIDTH]
    acts_two = columns.at[:, 2 * WIDTH :]
    pairs = []
    if first:
        out_pairs = ring_blocks(ins[0][0], ins[1:], w)
    else:
        out_pairs = [column_block(w_hbm, w, at) for at in range(QKV, SMALL, TILE)]
        high_below, low_below, returned_hbm = ins
        pairs += [(high_below, gates.at[:ROWS]), (low_below, gates.at[ROWS:])]
        pairs += [(returned_hbm, returned)]
    pairs += [(x_hbm, x_in), small_block(w_hbm, w)]
    pairs += [column_block(w_hbm, w, at) for at in range(0, QKV, TILE)]
    pairs += [(cosine_hbm, cosine), (sine_hbm, sine), (allowed_hbm, allowed)]
    pairs += out_pairs + [(take_hbm, take), (give_hbm, give)]
    reader, writer = Reader(in_sems, pairs), Writer(out_sems)
    if first:
        reader.take()
        x[...] = x_in[...].astype(F32)
    else:
        reader.take(4)
        for tile in tiles(WIDTH):
            both = dot(gates[...], returned[:, tile])
            x[:, tile] = x_in[:, tile] + both[:ROWS] + both[ROWS:]
        writer.send(x, outs[0])
    reader.take()
    small = w[:, SMALL:]
    gain_attn, gain_ffn = gain_rows(small)
    total = x[...]
    acts[...] = (total * unit(total) * gain_attn).astype(BF)
    wide = []
    for tile in tiles(QKV):
        reader.take()
        wide += [dot(acts[...], w[:, tile])]
    reader.take(3)
    for tile in range(QKV // TILE):
        for half in range(TILE // HEAD):
            head = tile * (TILE // HEAD) + half
            part = wide[tile][:, half * HEAD : (half + 1) * HEAD]
            if head < QUERY_HEADS:
                qrot[head] = turn(part, cosine[...], sine[...]).astype(BF)
            elif head < QUERY_HEADS + KEY_VALUE_HEADS:
                krot[head - QUERY_HEADS] = turn(part, cosine[...], sine[...]).astype(BF)
            else:
                value[head - QUERY_HEADS - KEY_VALUE_HEADS] = part.astype(BF)
    writer.send(qrot, qrot_hbm)
    writer.send(krot, krot_hbm)
    writer.send(value, value_hbm)
    open_scores = (allowed[...] > 0.5)[None]
    for k in range(KEY_VALUE_HEADS):
        heads = slice(k * GROUPS, (k + 1) * GROUPS)
        scores = dot(qrot[heads].reshape(GROUPS * ROWS, HEAD), krot[k], 1, 1) * SCALE
        scores = jnp.where(open_scores, scores.reshape(GROUPS, ROWS, ROWS), -1000000000.0)
        powers = jnp.exp(scores - jnp.max(scores, axis=-1, keepdims=True))
        shares = powers / jnp.sum(powers, axis=-1, keepdims=True)
        probs[heads] = shares
        mixed = dot(shares.astype(BF).reshape(GROUPS * ROWS, ROWS), value[k]).astype(BF)
        for group in range(GROUPS):
            at = (k * GROUPS + group) * HEAD
            attended[:, at : at + HEAD] = mixed[group * ROWS : (group + 1) * ROWS]
    writer.send(probs, probs_hbm)
    if first:
        reader.take(len(out_pairs))
    for tile in tiles(WIDTH):
        if not first:
            reader.take()
        after[:, tile] = x[:, tile] + dot(
            attended[...], w[:, QKV + tile.start : QKV + tile.stop]
        )
    writer.send(after, after_hbm)
    total = after[...]
    acts_two[...] = (total * unit(total) * gain_ffn).astype(BF)
    writer.send(columns, columns_hbm)
    reader.take(2)
    for tile in tiles(WIDTH):
        rows[:, tile] = dot(take[...], acts_two[:, tile]).astype(BF)
        writer.send(rows.at[:, tile], rows_hbm.at[:, tile])
    shares = router_probs(acts_two[...], small)
    router[...] = shares
    spread = expert_lanes(in_parts=not first)
    both = dot(jnp.concatenate(split(shares), axis=0), spread).astype(BF)
    high[...] = both[:ROWS] * give[...]
    low[...] = both[ROWS:] * give[...]
    writer.send(router, router_hbm)
    writer.send(high, high_hbm)
    writer.send(low, low_hbm)
    writer.finish()


HEADS = (QUERY_HEADS, ROWS, HEAD)
KEYS = (KEY_VALUE_HEADS, ROWS, HEAD)
TABLE = (ROWS, HEAD)
TOKENS = (ROWS, WIDTH)
WIDE = (SLOTS, WIDTH)


def specs_of(ins):
    return [pl.BlockSpec(memory_space=pltpu.SMEM if a.dtype == jnp.int32 else pl.ANY) for a in ins]


def run_attn(kernel, name, ins, order, outs, scratch, in_copies, out_copies, vmem):
    sd = jax.ShapeDtypeStruct

    def body(*refs):
        first_out = len(ins) + len(order)
        first_scratch = first_out + len(outs)
        kernel(refs[: len(ins)], refs[first_out:first_scratch], refs[first_scratch:])

    return pl.pallas_call(
        body,
        out_shape=[sd(shape, kind) for shape, kind in outs],
        in_specs=specs_of(ins) + [ANY] * len(order),
        out_specs=[ANY] * len(outs),
        scratch_shapes=[pltpu.VMEM(shape, kind) for shape, kind in scratch]
        + [pltpu.SemaphoreType.DMA((in_copies,)), pltpu.SemaphoreType.DMA((out_copies,))],
        compiler_params=pltpu.CompilerParams(vmem_limit_bytes=vmem),
        cost_estimate=pl.CostEstimate(
            flops=2 * ROWS * WIDTH * PACKED, bytes_accessed=20 << 20, transcendentals=200000
        ),
        name=name,
    )(*ins, *order)


def attn_forward(x, combine, w, ring, tables, take, give, order):
    first = combine is None
    outs = [
        ((ROWS, COLUMNS), BF), (HEADS, BF), (KEYS, BF), (KEYS, BF), ((QUERY_HEADS, ROWS, ROWS), F32),
        (TOKENS, F32), (TABLE, F32), ((ROWS, SLOTS), BF), ((ROWS, SLOTS), BF), (WIDE, BF),
    ]
    names = [
        "columns", "qrot", "krot", "value", "probs", "after", "router", "high", "low", "rows"
    ]
    scratch = [(TOKENS, x.dtype), ((WIDTH, PACKED), BF)] + [(TABLE, F32)] * 3
    scratch += [((SLOTS, ROWS), BF), ((ROWS, SLOTS), BF)]
    scratch += [((16, HEAD), BF)] * 2 if first else [(WIDE, BF), ((2 * ROWS, SLOTS), BF)]
    scratch += [(TOKENS, F32)] + outs
    ins = [x, w, *tables, take, give]
    if first:
        ins += ring
    else:
        high, low, returned = combine
        ins += [high, low, returned]
        outs = outs + [(TOKENS, F32)]
        names += ["x"]
    result = run_attn(
        lambda *refs: attn_forward_kernel(first, *refs), "attn_forward", ins, order, outs, scratch,
        20 + QKV // TILE, 20, VMEM_BYTES,
    )
    return dict(zip(names, result))


def norm_back(grad, gain, values):
    scale = unit(values)
    inner = grad * gain
    return scale * inner - values * (scale * scale * scale) * jnp.mean(
        inner * values, axis=-1, keepdims=True
    )


def attn_backward_kernel(last, ins, outs, scratch):
    (dx_hbm, back_hbm, w_hbm, turned_hbm, cosine_hbm, sine_hbm, give_hbm, router_hbm, after_hbm,
     x_hbm, probs_hbm, qrot_hbm, krot_hbm, value_hbm), ins = ins[:14], ins[14:]
    (dx_in, back, small_ref, turned, cosine, sine, give, router, after, x_in, probs, qrot, krot, value, wide_in,
     small_in, datt, dx_out, packed), scratch = scratch[:19], scratch[19:]
    if last:
        rows, scratch = scratch[0], scratch[1:]
    in_sems, out_sems = scratch
    pairs = [(give_hbm, give), (back_hbm, back), (router_hbm, router), (dx_hbm, dx_in)]
    if not last:
        pairs += [(ins[0], wide_in)]
    last_block = pl.ds(w_hbm.shape[1] - HEAD, HEAD)
    pairs += [(w_hbm.at[:, last_block], small_ref), (after_hbm, after)]
    columns = [(slice(None), pl.ds(at, TILE)) for at in range(0, WIDTH, TILE)]
    out_pairs, qkv_pairs = (
        [(turned_hbm.at[rows].at[c], turned.at[rows].at[c]) for c in columns]
        for rows in (pl.ds(QKV, WIDTH), pl.ds(0, QKV))
    )
    pairs += out_pairs + [(probs_hbm, probs), (value_hbm, value), (krot_hbm, krot), (qrot_hbm, qrot)]
    pairs += [(cosine_hbm, cosine), (sine_hbm, sine)] + qkv_pairs + [(x_hbm, x_in)]
    if last:
        pairs += [(ins[0], wide_in), (ins[1], small_in)]
    reader, writer = Reader(in_sems, pairs), Writer(out_sems)
    reader.take(4)
    dx = dx_in[...].astype(F32)
    spread = expert_lanes(True)
    if last:
        dgate = back[:, WIDTH:].astype(F32)
        drouter = dot(give[...], (dgate[:, 0:1] * spread).astype(BF))
        drouter += dot(give[...], (dgate[:, 1:2] * spread).astype(BF))
    else:
        reader.take()
        dgate = dot(dx.astype(BF), wide_in[...], 1, 1) * give[...]
        both = dot(jnp.concatenate(split(dgate), axis=0), spread)
        drouter = both[:ROWS] + both[ROWS:]
    reader.take(2)
    small = small_ref[...]
    gain_attn, gain_ffn = gain_rows(small)
    shares = router[...]
    dlogits = shares * (drouter - jnp.sum(drouter * shares, axis=-1, keepdims=True))
    dlogits = dlogits.astype(BF)
    dacts_two = dot(dlogits, small, 1, 1) + dot(give[...], back[:, :WIDTH])
    total = after[...]
    scale = unit(total)
    dafter = dx + norm_back(dacts_two, gain_ffn, total)
    dx_out[...] = dafter
    packed[:, QKV:SMALL] = dafter.astype(BF)
    dgain = jnp.sum(dacts_two * total * scale, axis=0, keepdims=True)
    dgain_high, dgain_low = split(dgain)
    pieces = [jnp.zeros((GAIN_HIGH, HEAD), F32)]
    for part in (dgain_high.astype(F32), dgain_low.astype(F32)):
        pieces += [part[:, at : at + HEAD] for at in range(0, WIDTH, HEAD)]
        pieces += [jnp.zeros((GAIN_LOW - GAIN_HIGH - PIECES, HEAD), F32)]
    pieces += [jnp.zeros((HEAD - 2 * GAIN_LOW + GAIN_HIGH, HEAD), F32)]
    packed[:, SMALL:] = (dlogits.astype(F32) + jnp.concatenate(pieces, axis=0).T).astype(BF)
    writer.send(packed.at[:, QKV:], outs[1].at[:, QKV:])
    for tile in tiles(WIDTH):
        reader.take()
        wide = dot(packed[:, QKV:SMALL], turned[QKV:SMALL, tile]).astype(BF)
        for half in range(TILE // HEAD):
            datt[tile.start // HEAD + half] = wide[:, half * HEAD : (half + 1) * HEAD]
    reader.take(6)
    for k in range(KEY_VALUE_HEADS):
        heads = slice(k * GROUPS, (k + 1) * GROUPS)
        datt_k = datt[heads].reshape(GROUPS * ROWS, HEAD)
        p = probs[heads].reshape(GROUPS * ROWS, ROWS)
        dprobs = dot(datt_k, value[k], 1, 1)
        dvalue = dot(p.astype(BF), datt_k, 0, 0)
        dscores = (p * (dprobs - jnp.sum(dprobs * p, axis=-1, keepdims=True))).astype(BF)
        dqrot = dot(dscores, krot[k]) * SCALE
        dkrot = dot(dscores, qrot[heads].reshape(GROUPS * ROWS, HEAD), 0, 0) * SCALE
        for group in range(GROUPS):
            at = (k * GROUPS + group) * HEAD
            part = dqrot[group * ROWS : (group + 1) * ROWS]
            packed[:, at : at + HEAD] = turn(part, cosine[...], -sine[...]).astype(BF)
        at = Q_END + k * HEAD
        packed[:, at : at + HEAD] = turn(dkrot, cosine[...], -sine[...]).astype(BF)
        at = K_END + k * HEAD
        packed[:, at : at + HEAD] = dvalue.astype(BF)
    writer.send(packed.at[:, :QKV], outs[1].at[:, :QKV])
    parts = []
    for tile in tiles(WIDTH):
        reader.take()
        parts += [dot(packed[:, :QKV], turned[:QKV, tile])]
    dacts = jnp.concatenate(parts, axis=1)
    reader.take()
    dx = dx_out[...] + norm_back(dacts, gain_attn, x_in[...].astype(F32))
    dx_out[...] = dx
    writer.send(dx_out, outs[0])
    if last:
        reader.take(2)
        dx_low = dx.astype(BF)
        both = dot(spread, jnp.concatenate(split(small_in[...]), axis=0), 1, 1).astype(BF)
        gates = jnp.concatenate([both[:, :ROWS] * wide_in[...], both[:, ROWS:] * wide_in[...]], axis=1)
        twice = jnp.concatenate([dx_low, dx_low], axis=0)
        for tile in tiles(WIDTH):
            rows[:, tile] = dot(gates, twice[:, tile]).astype(BF)
            writer.send(rows.at[:, tile], outs[2].at[:, tile])
    writer.finish()


def attn_backward(dx, back, x, kept, w, turned, tables, give, below, returned, order):
    last = below is not None
    outs = [(TOKENS, F32), ((ROWS, PACKED), BF)]
    if last:
        outs += [(WIDE, BF)]
    ins = [dx, back, w, turned, tables[0], tables[1], give, kept["router"], kept["after"], x]
    ins += [kept[n] for n in ("probs", "qrot", "krot", "value")]
    ins += list(below) if last else [returned]
    scratch = [
        (TOKENS, dx.dtype), (back.shape, BF), ((WIDTH, HEAD), BF), ((SMALL, WIDTH), BF),
        (TABLE, F32), (TABLE, F32),
        ((ROWS, SLOTS), BF), (TABLE, F32), (TOKENS, F32), (TOKENS, x.dtype),
        ((QUERY_HEADS, ROWS, ROWS), F32), (HEADS, BF), (KEYS, BF), (KEYS, BF),
        ((SLOTS, ROWS), BF) if last else (WIDE, BF), (TABLE, F32), (HEADS, BF),
    ] + outs
    return run_attn(
        lambda *refs: attn_backward_kernel(last, *refs), "attn_backward", ins, order, outs, scratch,
        24 + WIDTH // TILE, 12, VMEM_BYTES,
    )


def gelu_parts(gate):
    square = gate * gate
    bend = jnp.tanh(GELU_A * gate * (1.0 + GELU_B * square))
    return bend, square


def gelu(gate):
    bend, _ = gelu_parts(gate)
    return 0.5 * gate * (1.0 + bend)


def gelu_both(gate):
    bend, square = gelu_parts(gate)
    slope = 0.5 * (1.0 + bend) + 0.5 * gate * (1.0 - bend * bend) * GELU_A * (
        1.0 + 3.0 * GELU_B * square
    )
    return 0.5 * gate * (1.0 + bend), slope


def gate_up_pairs(l, gate_hbm, up_hbm, gate_w, up_w):
    gate_up = []
    for at in range(0, FF, TILE):
        block = (slice(None), pl.ds(at, TILE))
        gate_up += [(gate_hbm.at[l, 0].at[block], gate_w.at[block])]
        gate_up += [(up_hbm.at[l, 0].at[block], up_w.at[block])]
    return gate_up


def run_experts(kernel, name, ins, order, outs, scratch, in_copies, flops):
    sd = jax.ShapeDtypeStruct
    count = len(ins) + len(order)

    def body(*refs):
        kernel(*refs[: len(ins)], *refs[count:])

    return pl.pallas_call(
        body,
        out_shape=[sd(shape, BF) for shape in outs],
        in_specs=specs_of(ins) + [ANY] * len(order),
        out_specs=[ANY] * len(outs),
        scratch_shapes=[pltpu.VMEM(shape, kind) for shape, kind in scratch]
        + [pltpu.SemaphoreType.DMA((in_copies,)), pltpu.SemaphoreType.DMA((40,))],
        compiler_params=pltpu.CompilerParams(vmem_limit_bytes=VMEM_BYTES),
        cost_estimate=pl.CostEstimate(
            flops=flops, bytes_accessed=20 << 20, transcendentals=SLOTS * FF
        ),
        name=name,
    )(*ins, *order)


def experts_forward_kernel(
    received_hbm, gate_hbm, up_hbm, down_hbm, act_hbm, slope_hbm, hidden_hbm, out_hbm,
    received, gate_w, up_w, down_w, act_s, slope_s, hidden, out, in_sems, out_sems,
):
    gate_up = gate_up_pairs(0, gate_hbm, up_hbm, gate_w, up_w)
    pairs = [(received_hbm, received)] + gate_up + [(down_hbm.at[0, 0], down_w)]
    copies = start_all(pairs, in_sems)
    writer = Writer(out_sems)
    copies.pop(0).wait()
    for tile in tiles(FF):
        copies.pop(0).wait()
        copies.pop(0).wait()
        gate = dot(received[...], gate_w[:, tile])
        up = dot(received[...], up_w[:, tile])
        act, slope = gelu_both(gate)
        act_s[:, tile] = act.astype(BF)
        slope_s[:, tile] = (slope * up).astype(BF)
        hidden[:, tile] = (act * up).astype(BF)
    copies.pop(0).wait()
    writer.send(act_s, act_hbm)
    writer.send(slope_s, slope_hbm)
    writer.send(hidden, hidden_hbm)
    for tile in tiles(WIDTH):
        out[:, tile] = dot(hidden[...], down_w[:, tile]).astype(BF)
        writer.send(out.at[:, tile], out_hbm.at[:, tile])
    writer.finish()


EXPERT_SCRATCH = [((WIDTH, FF), BF), ((WIDTH, FF), BF), ((FF, WIDTH), BF)]


def experts_forward(received, weights, order):
    small = (SLOTS, FF)
    wide = (SLOTS, WIDTH)
    return run_experts(
        experts_forward_kernel, "experts_forward", [received, *weights], order,
        [small, small, small, wide],
        [(wide, BF)] + EXPERT_SCRATCH + [(small, BF)] * 3 + [(wide, BF)],
        8, 6 * SLOTS * WIDTH * FF,
    )


def back_tiles(dgate, dup, gate_w, up_w, back, back_hbm, writer):
    for tile in tiles(WIDTH):
        back[:, tile] = (
            dot(dgate[...], gate_w[tile], 1, 1) + dot(dup[...], up_w[tile], 1, 1)
        ).astype(BF)
        writer.send(back.at[:, tile], back_hbm.at[:, tile])


def expert_gate(me, received, small):
    shares = router_probs(received, small)
    lane = lax.broadcasted_iota(jnp.int32, shares.shape, 1)
    return jnp.sum(jnp.where(lane == me, shares, 0.0), axis=-1, keepdims=True)


def experts_both_kernel(
    me, received_hbm, product_hbm, w_hbm, gate_hbm, up_hbm,
    hidden_hbm, dgate_hbm, dup_hbm, back_hbm,
    received, product, small, gate_w, up_w, hidden, dgate, dup, back,
    in_sems, out_sems,
):
    pairs = [(received_hbm, received), small_source(w_hbm, small)]
    gate_up = gate_up_pairs(1, gate_hbm, up_hbm, gate_w, up_w)
    for i, tile in enumerate(tiles(FF)):
        block = (slice(None), pl.ds(tile.start, TILE))
        pairs += gate_up[2 * i : 2 * i + 2] + [(product_hbm.at[block], product.at[block])]
    reader, writer = Reader(in_sems, pairs), Writer(out_sems)
    reader.take(2)
    weight = expert_gate(me[0], received[...], small[...])
    total = jnp.zeros((SLOTS, 1), F32)
    ahead = None
    for tile in tiles(FF) + [None]:
        if tile is not None:
            reader.take(3)
            coming = (tile, dot(received[...], gate_w[:, tile]), dot(received[...], up_w[:, tile]))
        if ahead is not None:
            at, gate, up = ahead
            act, slope = gelu_both(gate)
            low = (act * up).astype(BF)
            hidden[:, at] = low
            dhidden = product[:, at]
            total += jnp.sum(dhidden * low.astype(F32), axis=-1, keepdims=True)
            dhidden = weight * dhidden
            dgate[:, at] = (dhidden * (slope * up)).astype(BF)
            dup[:, at] = (dhidden * act).astype(BF)
        ahead = coming
    writer.send(hidden, hidden_hbm)
    writer.send(dgate, dgate_hbm)
    writer.send(dup, dup_hbm)
    high, low = split(total)
    lane = lax.broadcasted_iota(jnp.int32, (SLOTS, HEAD), 1)
    back[:, WIDTH:] = jnp.where(
        lane == 0, high.astype(F32), jnp.where(lane == 1, low.astype(F32), 0.0)
    ).astype(BF)
    writer.send(back.at[:, WIDTH:], back_hbm.at[:, WIDTH:])
    back_tiles(dgate, dup, gate_w, up_w, back, back_hbm, writer)
    writer.finish()


def small_source(w_hbm, small):
    return (w_hbm.at[:, pl.ds(SMALL, HEAD)], small)


def experts_both(me, received, product, w, weights, order):
    small = (SLOTS, FF)
    wide = (SLOTS, WIDTH)
    back = (SLOTS, WIDTH + HEAD)
    return run_experts(
        experts_both_kernel, "experts_both", [me, received, product, w, *weights[:2]], order,
        [small, small, small, back],
        [(wide, BF), (small, F32), ((WIDTH, HEAD), BF)] + EXPERT_SCRATCH[:2]
        + [(small, BF), (small, BF), (small, BF), (back, BF)],
        11, 8 * SLOTS * WIDTH * FF,
    )


def experts_out_kernel(
    me, hidden_hbm, received_hbm, dx_hbm, w_hbm, down_hbm,
    part0_hbm, part1_hbm, part2_hbm, dslot_hbm,
    hidden, received, dx, small, down_w, part0, part1, part2, dslot, in_sems, out_sems,
):
    pairs = [(hidden_hbm, hidden), (down_hbm.at[1, 0], down_w), (received_hbm, received)]
    pairs += [small_source(w_hbm, small), (dx_hbm, dx)]
    reader, writer = Reader(in_sems, pairs), Writer(out_sems)
    reader.take(2)
    for tile in tiles(WIDTH):
        out = dot(hidden[...], down_w[:, tile]).astype(BF)
        for expert in range(EXPERTS):
            for p, target in enumerate((part0, part1, part2)):
                at = expert * CAP + p * PART_ROWS
                target[expert, :, tile] = out[at : at + PART_ROWS]
    writer.send(part0, part0_hbm)
    writer.send(part1, part1_hbm)
    writer.send(part2, part2_hbm)
    reader.take(3)
    weight = expert_gate(me[0], received[...], small[...])
    for tile in tiles(WIDTH):
        dslot[:, tile] = (weight * dx[:, tile].astype(F32)).astype(BF)
    writer.send(dslot, dslot_hbm)
    writer.finish()


def experts_out(me, hidden, received, dx, w, down, order):
    small = (SLOTS, FF)
    wide = (SLOTS, WIDTH)
    part = (EXPERTS, PART_ROWS, WIDTH)
    return run_experts(
        experts_out_kernel, "experts_out", [me, hidden, received, dx, w, down], order,
        [part, part, part, wide],
        [(small, BF), (wide, BF), (wide, BF), ((WIDTH, HEAD), BF), ((FF, WIDTH), BF)]
        + [(part, BF)] * 3 + [(wide, BF)],
        5, 2 * SLOTS * WIDTH * FF,
    )


def experts_backward_kernel(
    dslot_hbm, act_hbm, slope_hbm, gate_hbm, up_hbm, down_hbm, dgate_hbm, dup_hbm, back_hbm,
    dslot, act_s, slope_s, gate_w, up_w, down_w, dgate, dup, back, in_sems, out_sems,
):
    pairs = [(dslot_hbm, dslot)]
    for tile in tiles(FF):
        block = pl.ds(tile.start, TILE)
        pairs += [(down_hbm.at[0, 0].at[block], down_w.at[block])]
    pairs += [(slope_hbm, slope_s), (act_hbm, act_s)]
    for tile in tiles(WIDTH):
        block = pl.ds(tile.start, TILE)
        pairs += [(gate_hbm.at[0, 0].at[block], gate_w.at[block])]
        pairs += [(up_hbm.at[0, 0].at[block], up_w.at[block])]
    copies = start_all(pairs, in_sems)
    writer = Writer(out_sems)
    copies.pop(0).wait()
    dhidden = []
    for tile in tiles(FF):
        copies.pop(0).wait()
        dhidden += [dot(dslot[...], down_w[tile], 1, 1)]
    copies.pop(0).wait()
    copies.pop(0).wait()
    for tile, part in zip(tiles(FF), dhidden):
        dgate[:, tile] = (part * slope_s[:, tile].astype(F32)).astype(BF)
        dup[:, tile] = (part * act_s[:, tile].astype(F32)).astype(BF)
    writer.send(dgate, dgate_hbm)
    writer.send(dup, dup_hbm)
    for copy in copies:
        copy.wait()
    back_tiles(dgate, dup, gate_w, up_w, back, back_hbm, writer)
    writer.finish()


def experts_backward(dslot, act, slope, weights, order):
    small = (SLOTS, FF)
    wide = (SLOTS, WIDTH)
    return run_experts(
        experts_backward_kernel, "experts_backward", [dslot, act, slope, *weights], order,
        [small, small, wide],
        [(wide, BF), (small, BF), (small, BF)] + EXPERT_SCRATCH
        + [(small, BF), (small, BF), (wide, BF)],
        6 + 2 * WIDTH // TILE, 6 * SLOTS * WIDTH * FF,
    )


def on_core(core, me, ins, outs, scratch, kernel, name, above, order):
    sd = jax.ShapeDtypeStruct
    held = [] if above is None else list(above)
    first_out = 1 + len(ins) + len(held) + len(order)

    def body(*refs):
        @pl.when(refs[0][0] % 2 == core)
        def _():
            kernel(refs[0][0], refs[1 : 1 + len(ins)], refs[first_out : first_out + len(outs)],
                   refs[first_out + len(outs) :])

    return pl.pallas_call(
        body,
        out_shape=[sd(shape, kind) for shape, kind in outs],
        in_specs=[pl.BlockSpec(memory_space=pltpu.SMEM)]
        + [ANY] * (len(ins) + len(held) + len(order)),
        out_specs=[ANY] * len(outs),
        input_output_aliases={1 + len(ins) + i: i for i in range(len(held))},
        scratch_shapes=[pltpu.VMEM(shape, kind) for shape, kind in scratch]
        + [pltpu.SemaphoreType.DMA((24,)), pltpu.SemaphoreType.DMA((24,))],
        compiler_params=pltpu.CompilerParams(vmem_limit_bytes=VMEM_BYTES),
        name=name,
    )(me, *ins, *held, *order)


def upper_product_kernel(me, ins, outs, scratch):
    rows, down, product, in_sems, out_sems = scratch
    pairs = [(ins[0], rows)]
    for tile in tiles(FF):
        block = pl.ds(tile.start, TILE)
        pairs += [(ins[1].at[1, 0].at[block], down.at[block])]
    reader, writer = Reader(in_sems, pairs), Writer(out_sems)
    reader.take()
    for tile in tiles(FF):
        reader.take()
        product[:, tile] = dot(rows[...], down[tile], 1, 1)
        writer.send(product.at[:, tile], outs[0].at[:, tile])
    writer.finish()


def upper_product(core, me, dx_rows, w_down, above, order):
    small = (SLOTS, FF)
    return on_core(
        core, me, [dx_rows, w_down], [(small, F32)], [(WIDE, BF), ((FF, WIDTH), BF), (small, F32)],
        upper_product_kernel, "upper_product", above, order,
    )


def turn_weights_kernel(me, ins, outs, scratch):
    w, turned, in_sems, out_sems = scratch
    ring_out = len(ins) > 1
    pairs = [column_block(ins[0], w, at) for at in range(0, QKV if ring_out else SMALL, TILE)]
    if ring_out:
        pairs += ring_blocks(me, ins[1:], w)
    reader, writer = Reader(in_sems, pairs), Writer(out_sems)
    for tile in tiles(SMALL):
        if ring_out and tile.start == QKV:
            reader.take(len(ins) - 1)
        elif not ring_out or tile.start < QKV:
            reader.take()
        turned[tile] = w[:, tile].T
        writer.send(turned.at[tile], outs[0].at[tile])
    writer.finish()


def turn_weights(core, me, w, blocks, above, order):
    turned = ((SMALL, WIDTH), BF)
    return on_core(
        core, me, [w, *blocks], [turned], [((WIDTH, SMALL), BF), turned], turn_weights_kernel,
        "turn_weights", above, order,
    )


def expert_grads_kernel(received, dgate_pre, dup_pre, hidden, dslot, *rest):
    above = None
    if rest[0].shape[1] == SHARD:
        packed, down_out = rest
    else:
        above, packed = rest
        down_out = packed.at[:, SHARD : SHARD + FF // DP]
    gate = dot(received[...], dgate_pre[...], 0, 0).astype(BF)
    up = dot(received[...], dup_pre[...], 0, 0).astype(BF)
    down = dot(hidden[...], dslot[...], 0, 0).astype(BF)
    for part in range(DP // 2):
        packed[part, :SHARD, :FF] = gate[part * SHARD : (part + 1) * SHARD]
        packed[part, :SHARD, FF:] = up[part * SHARD : (part + 1) * SHARD]
        down_out[part] = down[part * FF // DP : (part + 1) * FF // DP]
    if above is not None:
        packed[:, SHARD + FF // DP :] = above[...]


def expert_grads(received, dgate_pre, dup_pre, hidden, dslot, above):
    down = FF // DP
    shapes = [(SHARD,), (down,)] if above is None else [(SHARD + 2 * down,)]
    whole = lambda width: pl.BlockSpec((SLOTS, width), lambda i: (0, 0))
    part = lambda width: pl.BlockSpec((SLOTS, width), lambda i: (0, i))
    rows = lambda count: pl.BlockSpec((DP // 2, count, WIDTH), lambda i: (i, 0, 0))
    held = [] if above is None else [above]
    return pl.pallas_call(
        expert_grads_kernel,
        grid=(2,),
        out_shape=[jax.ShapeDtypeStruct((DP, count, WIDTH), BF) for count, in shapes],
        in_specs=[part(WIDTH // 2), whole(FF), whole(FF), part(FF // 2), whole(WIDTH)]
        + [rows(down)] * len(held),
        out_specs=[rows(count) for count, in shapes],
        compiler_params=pltpu.CompilerParams(vmem_limit_bytes=VMEM_BYTES),
        cost_estimate=pl.CostEstimate(
            flops=6 * SLOTS * WIDTH * FF, bytes_accessed=14 << 20, transcendentals=0
        ),
        name="expert_grads",
    )(received, dgate_pre, dup_pre, hidden, dslot, *held)


def pack_kernel(
    l, query_hbm, key_hbm, value_hbm, out_hbm, router_hbm, gain_attn, gain_ffn, packed_hbm, *rest
):
    if l == 0:
        out_copy, packed, out, router, sems, out_sems = rest
    else:
        packed, router, sems, out_sems = rest
        out = packed.at[:, pl.ds(QKV, WIDTH)]
    pairs = [
        (router_hbm.at[l], router),
        (query_hbm.at[l], packed.at[:, pl.ds(0, Q_END)]),
        (key_hbm.at[l], packed.at[:, pl.ds(Q_END, K_END - Q_END)]),
        (value_hbm.at[l], packed.at[:, pl.ds(K_END, QKV - K_END)]),
        (out_hbm.at[l], out),
    ]
    reader, writer = Reader(sems, pairs), Writer(out_sems)
    reader.take()
    small = [router[...].astype(F32), gain_attn[l : l + 1].astype(F32)]
    small += [gain_ffn[l : l + 1].astype(F32), jnp.zeros((HEAD - EXPERTS - 2, SHARD), F32)]
    small = jnp.concatenate(small, axis=0)
    small = jnp.concatenate([small, jnp.zeros((HEAD, TILE - SHARD), F32)], axis=1).T
    packed[:, packed.shape[1] - HEAD :] = small[:SHARD].astype(BF)
    reader.take(3)
    if l == 0:
        writer.send(packed, packed_hbm)
        reader.take()
        writer.send(out, out_copy)
    else:
        reader.take()
        writer.send(packed, packed_hbm)
    writer.finish()


def pack(l, query, key, value, out, router, gain_attn, gain_ffn):
    sd = jax.ShapeDtypeStruct
    vmem = pl.BlockSpec(memory_space=pltpu.VMEM)
    packed = (SHARD, QKV + HEAD) if l == 0 else (SHARD, PACKED)
    outs = [packed] + [(SHARD, WIDTH)] * (l == 0)
    return pl.pallas_call(
        lambda *refs: pack_kernel(l, *refs),
        out_shape=[sd(shape, BF) for shape in outs],
        in_specs=[ANY] * 5 + [vmem] * 2,
        out_specs=[ANY] * len(outs),
        scratch_shapes=[pltpu.VMEM(shape, BF) for shape in outs]
        + [pltpu.VMEM((EXPERTS, SHARD), BF)]
        + [pltpu.SemaphoreType.DMA((5,)), pltpu.SemaphoreType.DMA((2,))],
        compiler_params=pltpu.CompilerParams(vmem_limit_bytes=VMEM_BYTES),
        name="pack",
    )(query, key, value, out, router.transpose(0, 2, 1), gain_attn, gain_ffn)


def ring(block):
    def move(values, step):
        return lax.ppermute(values, "dp", [(i, (i + step) % DP) for i in range(DP)])

    half = block.shape[0] // 2
    previous, following = move(block, 2), move(block, -2)
    far = [move(previous[:half], 2), move(following[half:], -2)]
    mine = [block, previous, following, *far]
    swap = [(i, i ^ 1) for i in range(DP)]
    return mine + [lax.ppermute(values, "dp", swap) for values in mine]


def seq_tables(counts):
    ends = jnp.cumsum(counts)
    starts = ends - counts
    place = jnp.arange(ROWS, dtype=jnp.int32)
    member = (place[:, None] >= starts[None, :]) & (place[:, None] < ends[None, :])
    index = jnp.arange(counts.shape[0], dtype=jnp.int32)
    segment = jnp.sum(jnp.where(member, index[None, :], 0), axis=1)
    position = place - jnp.sum(jnp.where(member, starts[None, :], 0), axis=1)
    allowed = (segment[:, None] == segment[None, :]) & (place[:, None] >= place[None, :])
    freqs = ROPE_BASE ** (-2.0 * jnp.arange(HEAD // 2, dtype=F32) / HEAD)
    angle = position.astype(F32)[:, None] * freqs[None, :]
    cosine, sine = jnp.cos(angle), jnp.sin(angle)
    return (
        jnp.concatenate([cosine, cosine], axis=1),
        jnp.concatenate([-sine, sine], axis=1),
        allowed.astype(F32),
    )


def slot_matrix(choices, in_parts=False):
    experts = jnp.arange(EXPERTS, dtype=jnp.int32)
    member = jnp.any(choices[:, :, None] == experts[None, None, :], axis=1).astype(BF)
    row = lax.broadcasted_iota(jnp.int32, (ROWS, ROWS), 0)
    column = lax.broadcasted_iota(jnp.int32, (ROWS, ROWS), 1)
    rank = dot((column < row).astype(BF), member).astype(BF)
    slot = jnp.arange(SLOTS, dtype=jnp.int32)[None, :]
    if in_parts:
        owner, place = slot % PART // PART_ROWS, slot // PART * PART_ROWS + slot % PART_ROWS
    else:
        owner, place = slot // CAP, slot % CAP
    expand = (owner == experts[:, None]).astype(BF)
    return ((dot(member, expand) > 0.5) & (dot(rank, expand) == place.astype(F32))).astype(BF)


def exchange(rows):
    width = rows.shape[-1]
    moved = lax.all_to_all(
        rows.reshape(EXPERTS, -1, width), "expert", split_axis=0, concat_axis=0, tiled=True
    )
    return moved.reshape(-1, width)


def after(values, *order):
    return pl.pallas_call(
        lambda *refs: None,
        out_shape=jax.ShapeDtypeStruct(values.shape, values.dtype),
        in_specs=[ANY] * (1 + len(order)),
        out_specs=ANY,
        input_output_aliases={0: 0},
        name="after",
    )(values, *order)


def turn_columns_kernel(me, columns_hbm, turned_hbm, columns, turned, in_sems, out_sems):
    base = me[0] * SHARD // HEAD * HEAD
    pairs = []
    for i in range(3):
        at = pl.multiple_of(base + i * WIDTH, HEAD)
        pairs += [(columns_hbm.at[:, pl.ds(at, TILE)], columns.at[:, pl.ds(i * TILE, TILE)])]
    reader, writer = Reader(in_sems, pairs), Writer(out_sems)
    for i in range(3):
        reader.take()
        turned[i] = columns[:, i * TILE : (i + 1) * TILE].T
        writer.send(turned.at[i], turned_hbm.at[i])
    writer.finish()


def turn_columns(me, columns):
    tokens = DP * ROWS
    return pl.pallas_call(
        turn_columns_kernel,
        out_shape=jax.ShapeDtypeStruct((3, TILE, tokens), BF),
        in_specs=[pl.BlockSpec(memory_space=pltpu.SMEM), ANY],
        out_specs=ANY,
        scratch_shapes=[
            pltpu.VMEM((tokens, 3 * TILE), BF),
            pltpu.VMEM((3, TILE, tokens), BF),
            pltpu.SemaphoreType.DMA((3,)),
            pltpu.SemaphoreType.DMA((3,)),
        ],
        compiler_params=pltpu.CompilerParams(vmem_limit_bytes=VMEM_BYTES),
        cost_estimate=pl.CostEstimate(flops=0, bytes_accessed=4 << 20, transcendentals=0),
        name="turn_columns",
    )(me, columns)


def dense_grads_kernel(me, turned_hbm, factors_hbm, pieces_hbm, turned, factors, total, pieces,
                       in_sems, out_sems):
    start = me[0] * SHARD
    shift = start % HEAD
    base = start - shift
    copies = Writer(out_sems)
    pairs = [(turned_hbm, turned)]
    for at, width in [(SMALL, HEAD)] + [(at, 2 * CHUNK) for at in range(0, SMALL, 2 * CHUNK)]:
        block = (slice(None), pl.ds(at, width))
        pairs += [(factors_hbm.at[block], factors.at[block])]
    reader = Reader(in_sems, pairs)
    reader.take(2)

    def put(chunk, values):
        pieces[chunk] = values.astype(BF)
        copies.send(pieces.at[chunk], pieces_hbm.at[chunk])

    ends = jnp.zeros((ROWS, HEAD), F32)
    for source in range(DP):
        ends += factors[source * ROWS : (source + 1) * ROWS, SMALL:].astype(F32)
    lane = lax.broadcasted_iota(jnp.int32, (ROWS, HEAD), 1)

    def gain_piece(piece):
        held = (lane == piece + GAIN_HIGH) | (lane == piece + GAIN_LOW)
        return jnp.sum(jnp.where(held, ends, 0.0), axis=1, keepdims=True)

    first, second = gain_piece(base // HEAD), gain_piece(base // HEAD + 1)
    gain = jnp.where(
        shift == 0,
        jnp.concatenate([first, second[: SHARD - ROWS]], axis=0),
        jnp.concatenate([first[ROWS // 2 :], second], axis=0),
    )
    gain_high, gain_low = split(gain)
    rows = pl.ds(pl.multiple_of(shift, 64), SHARD)
    total[1, :, :HEAD] = dot(turned[2], factors[:, SMALL:])
    router = total[1, rows, :HEAD]
    lane = lax.broadcasted_iota(jnp.int32, (SHARD, HEAD), 1)
    router = jnp.where(lane < EXPERTS, router, 0.0)
    router = jnp.where(lane == EXPERTS, gain_high.astype(F32), router)
    router = jnp.where(lane == EXPERTS + 1, gain_low.astype(F32), router)
    put(CHUNKS - 2, jnp.concatenate([router, jnp.zeros_like(router)], axis=1))
    put(CHUNKS - 1, jnp.zeros((SHARD, CHUNK), F32))
    for pair in range(SMALL // CHUNK // 2):
        reader.take()
        at = pair * 2 * CHUNK
        total[pair % 2] = dot(turned[0 if at < QKV else 1], factors[:, at : at + 2 * CHUNK])
        put(2 * pair, total[pair % 2, rows, :CHUNK])
        put(2 * pair + 1, total[pair % 2, rows, CHUNK:])
    copies.finish()


def dense_grads(me, turned, factors, order):
    tokens = DP * ROWS

    def body(*refs):
        dense_grads_kernel(*refs[:3], *refs[3 + len(order) :])

    return pl.pallas_call(
        body,
        out_shape=jax.ShapeDtypeStruct((CHUNKS, SHARD, CHUNK), BF),
        in_specs=[pl.BlockSpec(memory_space=pltpu.SMEM)] + [ANY] * (2 + len(order)),
        out_specs=ANY,
        scratch_shapes=[
            pltpu.VMEM((3, TILE, tokens), BF),
            pltpu.VMEM((tokens, PACKED), BF),
            pltpu.VMEM((2, TILE, 2 * CHUNK), F32),
            pltpu.VMEM((CHUNKS, SHARD, CHUNK), BF),
            pltpu.SemaphoreType.DMA((1 + CHUNKS,)),
            pltpu.SemaphoreType.DMA((CHUNKS,)),
        ],
        compiler_params=pltpu.CompilerParams(vmem_limit_bytes=VMEM_BYTES),
        cost_estimate=pl.CostEstimate(
            flops=2 * tokens * TILE * PACKED, bytes_accessed=10 << 20, transcendentals=0
        ),
        name="dense_grads",
    )(me, turned, factors, *order)


def to_expert_peers(pieces):
    return lax.all_to_all(pieces, "expert", split_axis=0, concat_axis=0, tiled=True)


def sum_pieces_kernel(pieces_hbm, out_hbm, pieces, out, in_sems, out_sems):
    half = CHUNKS // 2
    pairs = []
    for at in (0, half):
        block = pl.ds(at, half)
        pairs += [(pieces_hbm.at[block, :, pl.ds(0, CHUNK)], pieces.at[block])]
    reader, writer = Reader(in_sems, pairs), Writer(out_sems)
    reader.take()
    total = pieces[0].astype(F32)
    for i in range(1, half):
        total += pieces[i].astype(F32)
    reader.take()
    for i in range(half, CHUNKS):
        total += pieces[i].astype(F32)
    out[...] = total.astype(BF)
    if len(out_hbm.shape) == 3:
        for i in range(CHUNKS):
            writer.send(out, out_hbm.at[i])
    else:
        writer.send(out, out_hbm)
    writer.finish()


def sum_pieces(pieces, copies):
    return pl.pallas_call(
        sum_pieces_kernel,
        out_shape=jax.ShapeDtypeStruct((copies,) * (copies > 1) + (SHARD, CHUNK), BF),
        in_specs=[ANY],
        out_specs=ANY,
        scratch_shapes=[
            pltpu.VMEM((CHUNKS, SHARD, CHUNK), BF),
            pltpu.VMEM((SHARD, CHUNK), BF),
            pltpu.SemaphoreType.DMA((2,)),
            pltpu.SemaphoreType.DMA((CHUNKS,)),
        ],
        compiler_params=pltpu.CompilerParams(vmem_limit_bytes=VMEM_BYTES),
        name="sum_pieces",
    )(pieces)


def finish_kernel(l, refs):
    (pieces_hbm, query_w, key_w, value_w, norm_attn), refs = refs[:5], refs[5:]
    if l == 0:
        ends_above, refs = refs[0], refs[5:]
        (query_hbm, key_hbm, value_hbm, out_hbm, gain_attn, gain_ffn, router), refs = refs[:7], refs[7:]
    else:
        (query_hbm, key_hbm, value_hbm, out_hbm, ends_out), refs = refs[:5], refs[5:]
    query, key, value, out, pieces, w_query, w_key, w_value, in_sems, sems = refs
    pairs = [(query_w.at[l], w_query), (key_w.at[l], w_key), (value_w.at[l], w_value)]
    pairs += [(pieces_hbm.at[chunk], pieces.at[chunk]) for chunk in range(CHUNKS - 1)]
    reader, writer = Reader(in_sems, pairs), Writer(sems)
    rows = jnp.zeros((SHARD, 1), F32)
    reader.take(3)
    for chunk in range(SMALL // CHUNK):
        reader.take()
        part = pieces[chunk].astype(F32)
        lanes = slice(chunk * CHUNK, (chunk + 1) * CHUNK)
        if chunk < Q_END // CHUNK:
            query[:, lanes] = part
            weight = w_query[:, lanes]
        elif chunk == Q_END // CHUNK:
            key[...] = part
            weight = w_key[...]
            writer.send(query, query_hbm.at[l])
            writer.send(key, key_hbm.at[l])
        elif chunk < QKV // CHUNK:
            value[...] = part
            weight = w_value[...]
            writer.send(value, value_hbm.at[l])
        else:
            out[:, lanes.start - QKV : lanes.stop - QKV] = part
            continue
        rows += jnp.sum(part * weight.astype(F32), axis=1, keepdims=True)
    writer.send(out, out_hbm.at[l])
    reader.take()
    ends = pieces[CHUNKS - 2, :, :HEAD].astype(F32)
    ffn = ends[:, EXPERTS : EXPERTS + 1] + ends[:, EXPERTS + 1 : EXPERTS + 2]
    lane = lax.broadcasted_iota(jnp.int32, (SHARD, HEAD), 1)
    ends = jnp.where(lane == EXPERTS, rows, jnp.where(lane == EXPERTS + 1, ffn, ends))
    if l > 0:
        ends_out[...] = ends
    else:
        for layer, part in enumerate((ends, ends_above[...])):
            wide = jnp.concatenate([part, jnp.zeros((TILE - SHARD, HEAD), F32)], axis=0).T
            router[layer] = wide[:EXPERTS, :SHARD]
            gain = norm_attn[layer : layer + 1].astype(F32)
            gain_attn[layer : layer + 1] = wide[EXPERTS : EXPERTS + 1, :SHARD] / gain
            gain_ffn[layer : layer + 1] = wide[EXPERTS + 1 : EXPERTS + 2, :SHARD]
    writer.finish()


def finish(l, pieces, weights, norm_attn, above):
    sd = jax.ShapeDtypeStruct
    vmem = pl.BlockSpec(memory_space=pltpu.VMEM)
    keys = (SHARD, KEY_VALUE_HEADS * HEAD)
    slabs = [(SHARD, Q_END), keys, keys, (SHARD, WIDTH)]
    outs = [sd((LAYERS,) + shape, F32) for shape in slabs]
    if above is None:
        outs += [sd((SHARD, HEAD), F32)]
        ins, in_specs, aliases = [], [], {}
    else:
        outs += [sd((LAYERS, SHARD), F32)] * 2 + [sd((LAYERS, EXPERTS, SHARD), F32)]
        ins, in_specs = [above[4], *above[:4]], [vmem] + [ANY] * 4
        aliases = {6 + i: i for i in range(4)}
    return pl.pallas_call(
        lambda *refs: finish_kernel(l, refs),
        out_shape=outs,
        in_specs=[ANY] * 4 + [vmem] + in_specs,
        out_specs=[ANY] * 4 + [vmem] * (len(outs) - 4),
        input_output_aliases=aliases,
        scratch_shapes=[pltpu.VMEM(shape, F32) for shape in slabs]
        + [pltpu.VMEM((CHUNKS, SHARD, CHUNK), BF)]
        + [pltpu.VMEM(shape, BF) for shape in slabs[:3]]
        + [pltpu.SemaphoreType.DMA((2 + CHUNKS,)), pltpu.SemaphoreType.DMA((4,))],
        compiler_params=pltpu.CompilerParams(vmem_limit_bytes=VMEM_BYTES),
        name="finish",
    )(pieces, *weights, norm_attn, *ins)


def finish_experts_kernel(shares0, shares1, gate, up, down):
    rows = FF // DP
    for l, shares in enumerate((shares0, shares1)):
        gate[l, 0] = shares[:SHARD, :FF].astype(F32)
        up[l, 0] = shares[:SHARD, FF:].astype(F32)
        down[l, 0] = shares0[SHARD + l * rows : SHARD + (l + 1) * rows].astype(F32)


def finish_experts(shares0, shares1):
    sd = jax.ShapeDtypeStruct
    vmem = pl.BlockSpec(memory_space=pltpu.VMEM)
    return pl.pallas_call(
        finish_experts_kernel,
        out_shape=[
            sd((LAYERS, 1, SHARD, FF), F32), sd((LAYERS, 1, SHARD, FF), F32),
            sd((LAYERS, 1, FF // DP, WIDTH), F32),
        ],
        in_specs=[vmem] * 2,
        out_specs=[vmem] * 3,
        compiler_params=pltpu.CompilerParams(vmem_limit_bytes=VMEM_BYTES),
        name="finish_experts",
    )(shares0, shares1)


def mixed_kernel(x_hbm, high, low, part0, part1, part2, out, x, gates, returned, sems):
    pairs = [(high, gates.at[:ROWS]), (low, gates.at[ROWS:]), (x_hbm, x)]
    for p, part in enumerate((part0, part1, part2)):
        pairs += [(part, returned.at[pl.ds(p * PART, PART)])]
    Reader(sems, pairs).take(len(pairs))
    for tile in tiles(WIDTH):
        both = dot(gates[...], returned[:, tile])
        out[:, tile] = (x[:, tile] + both[:ROWS] + both[ROWS:]).astype(BF)


def mixed_rows(x, high, low, parts):
    return pl.pallas_call(
        mixed_kernel,
        out_shape=jax.ShapeDtypeStruct(TOKENS, BF),
        in_specs=[ANY] * 6,
        out_specs=pl.BlockSpec(memory_space=pltpu.VMEM),
        scratch_shapes=[
            pltpu.VMEM(TOKENS, F32),
            pltpu.VMEM((2 * ROWS, SLOTS), BF),
            pltpu.VMEM(WIDE, BF),
            pltpu.SemaphoreType.DMA((6,)),
        ],
        compiler_params=pltpu.CompilerParams(vmem_limit_bytes=VMEM_BYTES),
        name="mixed",
    )(x, high, low, *parts)


def local(
    tokens, cotangent, lengths, routes, norm_attn, w_query, key_projection, value_projection,
    w_out, norm_ffn, w_router, w_gate, w_up, w_down,
):
    me_dp = lax.axis_index("dp").astype(jnp.int32).reshape(1)
    me_expert = lax.axis_index("expert").astype(jnp.int32).reshape(1)
    tables = seq_tables(lengths[0])
    give = [slot_matrix(routes[l]) for l in range(LAYERS)]
    take = [g.T for g in give]
    give_parts = slot_matrix(routes[1], True)
    experts = (w_gate, w_up, w_down)

    def gather(values):
        return lax.all_gather(values, "dp", axis=0, tiled=True)

    weights = (w_query, key_projection, value_projection, w_out, w_router, norm_attn, norm_ffn)
    shard0, out_shard0 = pack(0, *weights)
    w = [gather(shard0), gather(pack(1, *weights)[0])]
    out_ring = [me_dp, *ring(out_shard0)]

    dx_rows = exchange(dot(take[1], cotangent).astype(BF))

    turned_w = turn_weights(1, me_dp, w[0], out_ring[1:], None, ())
    product = upper_product(1, me_dp, dx_rows, w_down, None, turned_w)
    kept0 = attn_forward(
        tokens, None, w[0], out_ring, tables, take[0], give[0],
        (*product, give[1], give_parts, me_expert),
    )
    received0 = exchange(kept0["rows"])
    act0, slope0, hidden0, out0 = experts_forward(received0, experts, ())
    returned0 = exchange(out0)
    turned_w = turn_weights(0, me_dp, w[0], out_ring[1:], turned_w, (out0,))
    product = upper_product(0, me_dp, dx_rows, w_down, product, turned_w)
    turned_w1 = turn_weights(0, me_dp, w[1], [], None, product)
    columns0 = gather(kept0["columns"])

    kept1 = attn_forward(
        kept0["after"], (kept0["high"], kept0["low"], returned0), w[1], None, tables, take[1],
        give_parts, tuple(turned_w1),
    )
    received1 = exchange(kept1["rows"])
    columns1 = gather(kept1["columns"])
    turned_w1 = turn_weights(1, me_dp, w[1], [], turned_w1, (received1,))
    hidden1, dgate1, dup1, back1 = experts_both(
        me_expert, received1, product[0], w[1], experts, tuple(turned_w1)
    )
    back1 = exchange(back1)
    *parts, dslot1 = experts_out(me_expert, hidden1, received1, dx_rows, w[1], w_down, ())
    grads1, down1 = expert_grads(received1, dgate1, dup1, hidden1, dslot1, None)
    turned0 = turn_columns(me_dp, columns0)
    parts[0] = exchange(after(parts[0], grads1, turned0))

    dx0, packed1, rows0 = attn_backward(
        cotangent, back1, kept1["x"], kept1, w[1], turned_w1[0], tables, give[1],
        (take[0], kept0["router"]), None, (),
    )
    packed1 = after(packed1, parts[0])
    dslot0 = exchange(rows0)
    factors1 = gather(packed1)
    shares1 = lax.psum_scatter(
        after(grads1, packed1).reshape(-1, WIDTH), "dp", scatter_dimension=0, tiled=True
    )
    dgate0, dup0, back0 = experts_backward(dslot0, act0, slope0, experts, ())
    back0 = exchange(back0)
    (grads0,) = expert_grads(received0, dgate0, dup0, hidden0, dslot0, down1)
    parts[1] = exchange(parts[1])
    turned1 = turn_columns(me_dp, columns1)
    pieces1 = dense_grads(me_dp, turned1, factors1, (parts[1],))
    parts[2] = exchange(after(parts[2], grads0, pieces1))
    grad_tokens, packed0 = attn_backward(
        dx0, back0, tokens, kept0, w[0], turned_w[0], tables, give[0], None, returned0, ()
    )
    factors0 = gather(after(packed0, parts[2]))
    summed1 = sum_pieces(to_expert_peers(pieces1), CHUNKS)
    shares0 = lax.psum_scatter(
        after(grads0, summed1, shares1).reshape(-1, WIDTH), "dp", scatter_dimension=0, tiled=True
    )
    mixed = mixed_rows(kept1["after"], kept1["high"], kept1["low"], parts)
    pieces1 = to_expert_peers(summed1)
    pieces0 = dense_grads(me_dp, turned0, factors0, ())
    pieces0 = to_expert_peers(after(pieces0, pieces1))
    pieces0 = to_expert_peers(sum_pieces(pieces0, CHUNKS))

    dense = (w_query, key_projection, value_projection)
    above = finish(1, pieces1, dense, norm_attn, None)
    gate, up, down = finish_experts(shares0, shares1)
    above = (after(above[0], gate), *above[1:])
    query, key, value, out, gain_attn, gain_ffn, router = finish(
        0, pieces0, dense, norm_attn, above
    )
    return (
        mixed, grad_tokens, gain_attn, query, key, value, out, gain_ffn,
        router.transpose(0, 2, 1), gate, up, down,
    )


def solution(mesh):
    placed = (
        P(("dp", "expert"), None),
        P(("dp", "expert"), None),
        P(("dp", "expert"), None),
        P(None, ("dp", "expert"), None),
        P(None, "dp"),
        P(None, "dp", None),
        P(None, "dp", None),
        P(None, "dp", None),
        P(None, "dp", None),
        P(None, "dp"),
        P(None, "dp", None),
        P(None, "expert", None, None),
        P(None, "expert", None, None),
        P(None, "expert", None, None),
    )
    return jax.shard_map(
        local,
        mesh=mesh,
        in_specs=placed,
        out_specs=(
            P(("dp", "expert"), None),
            P(("dp", "expert"), None),
            P(None, "dp"),
            P(None, "dp", None),
            P(None, "dp", None),
            P(None, "dp", None),
            P(None, "dp", None),
            P(None, "dp"),
            P(None, "dp", None),
            P(None, "expert", "dp", None),
            P(None, "expert", "dp", None),
            P(None, "expert", "dp", None),
        ),
        check_vma=False,
    )
```

```python
import jax
import jax.numpy as jnp
from jax import lax
from jax.experimental import pallas as pl
from jax.experimental.pallas import tpu as pltpu
from jax.sharding import PartitionSpec as P

QUERY_HEADS = 12
KEY_VALUE_HEADS = 2
GROUPS = QUERY_HEADS // KEY_VALUE_HEADS
HEAD = 128
LAYERS = 2
WIDTH = 1536
FF = 768
ROWS = 128
EXPERTS = 16
CAP = 48
SLOTS = EXPERTS * CAP
DP = 8
SHARD = WIDTH // DP
Q_END = QUERY_HEADS * HEAD
K_END = Q_END + KEY_VALUE_HEADS * HEAD
QKV = K_END + KEY_VALUE_HEADS * HEAD
SMALL = QKV + WIDTH
PACKED = SMALL + HEAD
GAIN_ATTN, GAIN_FFN = 16, 17
GAIN_HIGH, GAIN_LOW = 16, 32
PIECES = WIDTH // HEAD
TILE = 256
PARTS = 3
PART = SLOTS // PARTS
PART_ROWS = CAP // PARTS
CHUNKS, CHUNK = 16, 256
COLUMNS = 3 * WIDTH
EPSILON = 1e-06
ROPE_BASE = 1000000.0
SCALE = HEAD ** (-0.5)
GELU_A = 0.7978845608028654
GELU_B = 0.044715
VMEM_BYTES = 56 << 20
BF = jnp.bfloat16
F32 = jnp.float32
ANY = pl.BlockSpec(memory_space=pl.ANY)


def dot(left, right, left_dim=1, right_dim=0):
    return lax.dot_general(
        left, right, (((left_dim,), (right_dim,)), ((), ())), preferred_element_type=F32
    )


def split(values):
    high = values.astype(BF)
    return high, (values - high.astype(F32)).astype(BF)


def unit(values):
    return lax.rsqrt(jnp.mean(values * values, axis=-1, keepdims=True) + EPSILON)


def turn(values, cosine, sine):
    return values * cosine + pltpu.roll(values, HEAD // 2, 1) * sine


def expert_lanes(transposed=False, in_parts=False):
    shape = (SLOTS, HEAD) if transposed else (HEAD, SLOTS)
    slot = lax.broadcasted_iota(jnp.int32, shape, 0 if transposed else 1)
    expert = lax.broadcasted_iota(jnp.int32, shape, 1 if transposed else 0)
    if in_parts:
        held = ((slot & (PART - 1)) >> 4) == expert
    else:
        held = (slot >= expert * CAP) & (slot < expert * CAP + CAP)
    return held.astype(F32).astype(BF)


def gain_rows(small):
    row = lax.broadcasted_iota(jnp.int32, (8, HEAD), 0)
    lane = lax.broadcasted_iota(jnp.int32, (8, HEAD), 1)
    pick = ((lane == row + GAIN_ATTN) & (row < 2)).astype(F32).astype(BF)
    rows = dot(pick, small, 1, 1)
    return rows[0:1], rows[1:2]


def router_probs(rows, small):
    logits = dot(rows, small)
    lane = lax.broadcasted_iota(jnp.int32, logits.shape, 1)
    logits = jnp.where(lane < EXPERTS, logits, -1e30)
    powers = jnp.exp(logits - jnp.max(logits, axis=-1, keepdims=True))
    return powers / jnp.sum(powers, axis=-1, keepdims=True)


def start_all(pairs, sems):
    copies = [
        pltpu.make_async_copy(source, target, sems.at[i]) for i, (source, target) in enumerate(pairs)
    ]
    for copy in copies:
        copy.start()
    return copies


class Writer:
    def __init__(self, sems):
        self.sems, self.copies = sems, []

    def send(self, source, target):
        copy = pltpu.make_async_copy(source, target, self.sems.at[len(self.copies)])
        copy.start()
        self.copies.append(copy)

    def finish(self):
        for copy in self.copies:
            copy.wait()


class Reader:
    def __init__(self, sems, pairs):
        self.copies = start_all(pairs, sems)

    def take(self, count=1):
        for _ in range(count):
            self.copies.pop(0).wait()


def tiles(width):
    return [slice(at, at + TILE) for at in range(0, width, TILE)]


def small_block(w_hbm, w):
    last = w_hbm.shape[1] - HEAD
    return (w_hbm.at[:, pl.ds(last, HEAD)], w.at[:, pl.ds(SMALL, HEAD)])


def column_block(w_hbm, w, at):
    return (w_hbm.at[:, pl.ds(at, TILE)], w.at[:, pl.ds(at, TILE)])


def ring_blocks(me, blocks, w):
    pairs = []
    for core in range(2):
        start = me if core == 0 else me + 1 - 2 * (me % 2)
        for block, step in enumerate((0, DP - 2, 2, 4, 4)):
            ref = blocks[core * 5 + block]
            at = (start + step) % DP * SHARD + (SHARD // 2 if block == 4 else 0)
            at = pl.multiple_of(at, SHARD // 2)
            pairs += [(ref, w.at[pl.ds(at, ref.shape[0]), pl.ds(QKV, WIDTH)])]
    return pairs


def attn_forward_kernel(first, ins, outs, scratch):
    (x_hbm, w_hbm, cosine_hbm, sine_hbm, allowed_hbm, take_hbm, give_hbm), ins = ins[:7], ins[7:]
    (columns_hbm, qrot_hbm, krot_hbm, value_hbm, probs_hbm, after_hbm, router_hbm, high_hbm, low_hbm,
     rows_hbm), outs = outs[:10], outs[10:]
    (x_in, w, cosine, sine, allowed, take, give, returned, gates, x, columns, qrot, krot, value, probs,
     after, router, high, low, rows, in_sems, out_sems) = scratch
    acts = columns.at[:, :WIDTH]
    attended = columns.at[:, WIDTH : 2 * WIDTH]
    acts_two = columns.at[:, 2 * WIDTH :]
    pairs = []
    if first:
        out_pairs = ring_blocks(ins[0][0], ins[1:], w)
    else:
        out_pairs = [column_block(w_hbm, w, at) for at in range(QKV, SMALL, TILE)]
        high_below, low_below, returned_hbm = ins
        pairs += [(high_below, gates.at[:ROWS]), (low_below, gates.at[ROWS:])]
        pairs += [(returned_hbm, returned)]
    pairs += [(x_hbm, x_in), small_block(w_hbm, w)]
    pairs += [column_block(w_hbm, w, at) for at in range(0, QKV, TILE)]
    pairs += [(cosine_hbm, cosine), (sine_hbm, sine), (allowed_hbm, allowed)]
    pairs += out_pairs + [(take_hbm, take), (give_hbm, give)]
    reader, writer = Reader(in_sems, pairs), Writer(out_sems)
    if first:
        reader.take()
        x[...] = x_in[...].astype(F32)
    else:
        reader.take(4)
        for tile in tiles(WIDTH):
            both = dot(gates[...], returned[:, tile])
            x[:, tile] = x_in[:, tile] + both[:ROWS] + both[ROWS:]
        writer.send(x, outs[0])
    reader.take()
    small = w[:, SMALL:]
    gain_attn, gain_ffn = gain_rows(small)
    total = x[...]
    acts[...] = (total * unit(total) * gain_attn).astype(BF)
    wide = []
    for tile in tiles(QKV):
        reader.take()
        wide += [dot(acts[...], w[:, tile])]
    reader.take(3)
    for tile in range(QKV // TILE):
        for half in range(TILE // HEAD):
            head = tile * (TILE // HEAD) + half
            part = wide[tile][:, half * HEAD : (half + 1) * HEAD]
            if head < QUERY_HEADS:
                qrot[head] = turn(part, cosine[...], sine[...]).astype(BF)
            elif head < QUERY_HEADS + KEY_VALUE_HEADS:
                krot[head - QUERY_HEADS] = turn(part, cosine[...], sine[...]).astype(BF)
            else:
                value[head - QUERY_HEADS - KEY_VALUE_HEADS] = part.astype(BF)
    writer.send(qrot, qrot_hbm)
    writer.send(krot, krot_hbm)
    writer.send(value, value_hbm)
    open_scores = (allowed[...] > 0.5)[None]
    for k in range(KEY_VALUE_HEADS):
        heads = slice(k * GROUPS, (k + 1) * GROUPS)
        scores = dot(qrot[heads].reshape(GROUPS * ROWS, HEAD), krot[k], 1, 1) * SCALE
        scores = jnp.where(open_scores, scores.reshape(GROUPS, ROWS, ROWS), -1000000000.0)
        powers = jnp.exp(scores - jnp.max(scores, axis=-1, keepdims=True))
        shares = powers / jnp.sum(powers, axis=-1, keepdims=True)
        probs[heads] = shares
        mixed = dot(shares.astype(BF).reshape(GROUPS * ROWS, ROWS), value[k]).astype(BF)
        for group in range(GROUPS):
            at = (k * GROUPS + group) * HEAD
            attended[:, at : at + HEAD] = mixed[group * ROWS : (group + 1) * ROWS]
    writer.send(probs, probs_hbm)
    if first:
        reader.take(len(out_pairs))
    for tile in tiles(WIDTH):
        if not first:
            reader.take()
        after[:, tile] = x[:, tile] + dot(
            attended[...], w[:, QKV + tile.start : QKV + tile.stop]
        )
    writer.send(after, after_hbm)
    total = after[...]
    acts_two[...] = (total * unit(total) * gain_ffn).astype(BF)
    writer.send(columns, columns_hbm)
    reader.take(2)
    for tile in tiles(WIDTH):
        rows[:, tile] = dot(take[...], acts_two[:, tile]).astype(BF)
        writer.send(rows.at[:, tile], rows_hbm.at[:, tile])
    shares = router_probs(acts_two[...], small)
    router[...] = shares
    spread = expert_lanes(in_parts=not first)
    both = dot(jnp.concatenate(split(shares), axis=0), spread).astype(BF)
    high[...] = both[:ROWS] * give[...]
    low[...] = both[ROWS:] * give[...]
    writer.send(router, router_hbm)
    writer.send(high, high_hbm)
    writer.send(low, low_hbm)
    writer.finish()


HEADS = (QUERY_HEADS, ROWS, HEAD)
KEYS = (KEY_VALUE_HEADS, ROWS, HEAD)
TABLE = (ROWS, HEAD)
TOKENS = (ROWS, WIDTH)
WIDE = (SLOTS, WIDTH)


def specs_of(ins):
    return [pl.BlockSpec(memory_space=pltpu.SMEM if a.dtype == jnp.int32 else pl.ANY) for a in ins]


def run_attn(kernel, name, ins, order, outs, scratch, in_copies, out_copies, vmem):
    sd = jax.ShapeDtypeStruct

    def body(*refs):
        first_out = len(ins) + len(order)
        first_scratch = first_out + len(outs)
        kernel(refs[: len(ins)], refs[first_out:first_scratch], refs[first_scratch:])

    return pl.pallas_call(
        body,
        out_shape=[sd(shape, kind) for shape, kind in outs],
        in_specs=specs_of(ins) + [ANY] * len(order),
        out_specs=[ANY] * len(outs),
        scratch_shapes=[pltpu.VMEM(shape, kind) for shape, kind in scratch]
        + [pltpu.SemaphoreType.DMA((in_copies,)), pltpu.SemaphoreType.DMA((out_copies,))],
        compiler_params=pltpu.CompilerParams(vmem_limit_bytes=vmem),
        cost_estimate=pl.CostEstimate(
            flops=2 * ROWS * WIDTH * PACKED, bytes_accessed=20 << 20, transcendentals=200000
        ),
        name=name,
    )(*ins, *order)


def attn_forward(x, combine, w, ring, tables, take, give, order):
    first = combine is None
    outs = [
        ((ROWS, COLUMNS), BF), (HEADS, BF), (KEYS, BF), (KEYS, BF), ((QUERY_HEADS, ROWS, ROWS), F32),
        (TOKENS, F32), (TABLE, F32), ((ROWS, SLOTS), BF), ((ROWS, SLOTS), BF), (WIDE, BF),
    ]
    names = [
        "columns", "qrot", "krot", "value", "probs", "after", "router", "high", "low", "rows"
    ]
    scratch = [(TOKENS, x.dtype), ((WIDTH, PACKED), BF)] + [(TABLE, F32)] * 3
    scratch += [((SLOTS, ROWS), BF), ((ROWS, SLOTS), BF)]
    scratch += [((16, HEAD), BF)] * 2 if first else [(WIDE, BF), ((2 * ROWS, SLOTS), BF)]
    scratch += [(TOKENS, F32)] + outs
    ins = [x, w, *tables, take, give]
    if first:
        ins += ring
    else:
        high, low, returned = combine
        ins += [high, low, returned]
        outs = outs + [(TOKENS, F32)]
        names += ["x"]
    result = run_attn(
        lambda *refs: attn_forward_kernel(first, *refs), "attn_forward", ins, order, outs, scratch,
        20 + QKV // TILE, 20, VMEM_BYTES,
    )
    return dict(zip(names, result))


def norm_back(grad, gain, values):
    scale = unit(values)
    inner = grad * gain
    return scale * inner - values * (scale * scale * scale) * jnp.mean(
        inner * values, axis=-1, keepdims=True
    )


def attn_backward_kernel(last, ins, outs, scratch):
    (dx_hbm, back_hbm, w_hbm, turned_hbm, cosine_hbm, sine_hbm, give_hbm, router_hbm, after_hbm,
     x_hbm, probs_hbm, qrot_hbm, krot_hbm, value_hbm), ins = ins[:14], ins[14:]
    (dx_in, back, small_ref, turned, cosine, sine, give, router, after, x_in, probs, qrot, krot, value, wide_in,
     small_in, datt, dx_out, packed), scratch = scratch[:19], scratch[19:]
    if last:
        rows, scratch = scratch[0], scratch[1:]
    in_sems, out_sems = scratch
    pairs = [(give_hbm, give), (back_hbm, back), (router_hbm, router), (dx_hbm, dx_in)]
    if not last:
        pairs += [(ins[0], wide_in)]
    last_block = pl.ds(w_hbm.shape[1] - HEAD, HEAD)
    pairs += [(w_hbm.at[:, last_block], small_ref), (after_hbm, after)]
    columns = [(slice(None), pl.ds(at, TILE)) for at in range(0, WIDTH, TILE)]
    out_pairs, qkv_pairs = (
        [(turned_hbm.at[rows].at[c], turned.at[rows].at[c]) for c in columns]
        for rows in (pl.ds(QKV, WIDTH), pl.ds(0, QKV))
    )
    pairs += out_pairs + [(probs_hbm, probs), (value_hbm, value), (krot_hbm, krot), (qrot_hbm, qrot)]
    pairs += [(cosine_hbm, cosine), (sine_hbm, sine)] + qkv_pairs + [(x_hbm, x_in)]
    if last:
        pairs += [(ins[0], wide_in), (ins[1], small_in)]
    reader, writer = Reader(in_sems, pairs), Writer(out_sems)
    reader.take(4)
    dx = dx_in[...].astype(F32)
    spread = expert_lanes(True)
    if last:
        dgate = back[:, WIDTH:].astype(F32)
        drouter = dot(give[...], (dgate[:, 0:1] * spread).astype(BF))
        drouter += dot(give[...], (dgate[:, 1:2] * spread).astype(BF))
    else:
        reader.take()
        dgate = dot(dx.astype(BF), wide_in[...], 1, 1) * give[...]
        both = dot(jnp.concatenate(split(dgate), axis=0), spread)
        drouter = both[:ROWS] + both[ROWS:]
    reader.take(2)
    small = small_ref[...]
    gain_attn, gain_ffn = gain_rows(small)
    shares = router[...]
    dlogits = shares * (drouter - jnp.sum(drouter * shares, axis=-1, keepdims=True))
    dlogits = dlogits.astype(BF)
    dacts_two = dot(dlogits, small, 1, 1) + dot(give[...], back[:, :WIDTH])
    total = after[...]
    scale = unit(total)
    dafter = dx + norm_back(dacts_two, gain_ffn, total)
    dx_out[...] = dafter
    packed[:, QKV:SMALL] = dafter.astype(BF)
    dgain = jnp.sum(dacts_two * total * scale, axis=0, keepdims=True)
    dgain_high, dgain_low = split(dgain)
    pieces = [jnp.zeros((GAIN_HIGH, HEAD), F32)]
    for part in (dgain_high.astype(F32), dgain_low.astype(F32)):
        pieces += [part[:, at : at + HEAD] for at in range(0, WIDTH, HEAD)]
        pieces += [jnp.zeros((GAIN_LOW - GAIN_HIGH - PIECES, HEAD), F32)]
    pieces += [jnp.zeros((HEAD - 2 * GAIN_LOW + GAIN_HIGH, HEAD), F32)]
    packed[:, SMALL:] = (dlogits.astype(F32) + jnp.concatenate(pieces, axis=0).T).astype(BF)
    writer.send(packed.at[:, QKV:], outs[1].at[:, QKV:])
    for tile in tiles(WIDTH):
        reader.take()
        wide = dot(packed[:, QKV:SMALL], turned[QKV:SMALL, tile]).astype(BF)
        for half in range(TILE // HEAD):
            datt[tile.start // HEAD + half] = wide[:, half * HEAD : (half + 1) * HEAD]
    reader.take(6)
    for k in range(KEY_VALUE_HEADS):
        heads = slice(k * GROUPS, (k + 1) * GROUPS)
        datt_k = datt[heads].reshape(GROUPS * ROWS, HEAD)
        p = probs[heads].reshape(GROUPS * ROWS, ROWS)
        dprobs = dot(datt_k, value[k], 1, 1)
        dvalue = dot(p.astype(BF), datt_k, 0, 0)
        dscores = (p * (dprobs - jnp.sum(dprobs * p, axis=-1, keepdims=True))).astype(BF)
        dqrot = dot(dscores, krot[k]) * SCALE
        dkrot = dot(dscores, qrot[heads].reshape(GROUPS * ROWS, HEAD), 0, 0) * SCALE
        for group in range(GROUPS):
            at = (k * GROUPS + group) * HEAD
            part = dqrot[group * ROWS : (group + 1) * ROWS]
            packed[:, at : at + HEAD] = turn(part, cosine[...], -sine[...]).astype(BF)
        at = Q_END + k * HEAD
        packed[:, at : at + HEAD] = turn(dkrot, cosine[...], -sine[...]).astype(BF)
        at = K_END + k * HEAD
        packed[:, at : at + HEAD] = dvalue.astype(BF)
    writer.send(packed.at[:, :QKV], outs[1].at[:, :QKV])
    parts = []
    for tile in tiles(WIDTH):
        reader.take()
        parts += [dot(packed[:, :QKV], turned[:QKV, tile])]
    dacts = jnp.concatenate(parts, axis=1)
    reader.take()
    dx = dx_out[...] + norm_back(dacts, gain_attn, x_in[...].astype(F32))
    dx_out[...] = dx
    writer.send(dx_out, outs[0])
    if last:
        reader.take(2)
        dx_low = dx.astype(BF)
        both = dot(spread, jnp.concatenate(split(small_in[...]), axis=0), 1, 1).astype(BF)
        gates = jnp.concatenate([both[:, :ROWS] * wide_in[...], both[:, ROWS:] * wide_in[...]], axis=1)
        twice = jnp.concatenate([dx_low, dx_low], axis=0)
        for tile in tiles(WIDTH):
            rows[:, tile] = dot(gates, twice[:, tile]).astype(BF)
            writer.send(rows.at[:, tile], outs[2].at[:, tile])
    writer.finish()


def attn_backward(dx, back, x, kept, w, turned, tables, give, below, returned, order):
    last = below is not None
    outs = [(TOKENS, F32), ((ROWS, PACKED), BF)]
    if last:
        outs += [(WIDE, BF)]
    ins = [dx, back, w, turned, tables[0], tables[1], give, kept["router"], kept["after"], x]
    ins += [kept[n] for n in ("probs", "qrot", "krot", "value")]
    ins += list(below) if last else [returned]
    scratch = [
        (TOKENS, dx.dtype), (back.shape, BF), ((WIDTH, HEAD), BF), ((SMALL, WIDTH), BF),
        (TABLE, F32), (TABLE, F32),
        ((ROWS, SLOTS), BF), (TABLE, F32), (TOKENS, F32), (TOKENS, x.dtype),
        ((QUERY_HEADS, ROWS, ROWS), F32), (HEADS, BF), (KEYS, BF), (KEYS, BF),
        ((SLOTS, ROWS), BF) if last else (WIDE, BF), (TABLE, F32), (HEADS, BF),
    ] + outs
    return run_attn(
        lambda *refs: attn_backward_kernel(last, *refs), "attn_backward", ins, order, outs, scratch,
        24 + WIDTH // TILE, 12, VMEM_BYTES,
    )


def gelu_parts(gate):
    square = gate * gate
    bend = jnp.tanh(GELU_A * gate * (1.0 + GELU_B * square))
    return bend, square


def gelu(gate):
    bend, _ = gelu_parts(gate)
    return 0.5 * gate * (1.0 + bend)


def gelu_both(gate):
    bend, square = gelu_parts(gate)
    slope = 0.5 * (1.0 + bend) + 0.5 * gate * (1.0 - bend * bend) * GELU_A * (
        1.0 + 3.0 * GELU_B * square
    )
    return 0.5 * gate * (1.0 + bend), slope


def gate_up_pairs(l, gate_hbm, up_hbm, gate_w, up_w):
    gate_up = []
    for at in range(0, FF, TILE):
        block = (slice(None), pl.ds(at, TILE))
        gate_up += [(gate_hbm.at[l, 0].at[block], gate_w.at[block])]
        gate_up += [(up_hbm.at[l, 0].at[block], up_w.at[block])]
    return gate_up


def run_experts(kernel, name, ins, order, outs, scratch, in_copies, flops):
    sd = jax.ShapeDtypeStruct
    count = len(ins) + len(order)

    def body(*refs):
        kernel(*refs[: len(ins)], *refs[count:])

    return pl.pallas_call(
        body,
        out_shape=[sd(shape, BF) for shape in outs],
        in_specs=specs_of(ins) + [ANY] * len(order),
        out_specs=[ANY] * len(outs),
        scratch_shapes=[pltpu.VMEM(shape, kind) for shape, kind in scratch]
        + [pltpu.SemaphoreType.DMA((in_copies,)), pltpu.SemaphoreType.DMA((40,))],
        compiler_params=pltpu.CompilerParams(vmem_limit_bytes=VMEM_BYTES),
        cost_estimate=pl.CostEstimate(
            flops=flops, bytes_accessed=20 << 20, transcendentals=SLOTS * FF
        ),
        name=name,
    )(*ins, *order)


def experts_forward_kernel(
    received_hbm, gate_hbm, up_hbm, down_hbm, act_hbm, slope_hbm, hidden_hbm, out_hbm,
    received, gate_w, up_w, down_w, act_s, slope_s, hidden, out, in_sems, out_sems,
):
    gate_up = gate_up_pairs(0, gate_hbm, up_hbm, gate_w, up_w)
    pairs = [(received_hbm, received)] + gate_up + [(down_hbm.at[0, 0], down_w)]
    copies = start_all(pairs, in_sems)
    writer = Writer(out_sems)
    copies.pop(0).wait()
    for tile in tiles(FF):
        copies.pop(0).wait()
        copies.pop(0).wait()
        gate = dot(received[...], gate_w[:, tile])
        up = dot(received[...], up_w[:, tile])
        act, slope = gelu_both(gate)
        act_s[:, tile] = act.astype(BF)
        slope_s[:, tile] = (slope * up).astype(BF)
        hidden[:, tile] = (act * up).astype(BF)
    copies.pop(0).wait()
    writer.send(act_s, act_hbm)
    writer.send(slope_s, slope_hbm)
    writer.send(hidden, hidden_hbm)
    for tile in tiles(WIDTH):
        out[:, tile] = dot(hidden[...], down_w[:, tile]).astype(BF)
        writer.send(out.at[:, tile], out_hbm.at[:, tile])
    writer.finish()


EXPERT_SCRATCH = [((WIDTH, FF), BF), ((WIDTH, FF), BF), ((FF, WIDTH), BF)]


def experts_forward(received, weights, order):
    small = (SLOTS, FF)
    wide = (SLOTS, WIDTH)
    return run_experts(
        experts_forward_kernel, "experts_forward", [received, *weights], order,
        [small, small, small, wide],
        [(wide, BF)] + EXPERT_SCRATCH + [(small, BF)] * 3 + [(wide, BF)],
        8, 6 * SLOTS * WIDTH * FF,
    )


def back_tiles(dgate, dup, gate_w, up_w, back, back_hbm, writer):
    for tile in tiles(WIDTH):
        back[:, tile] = (
            dot(dgate[...], gate_w[tile], 1, 1) + dot(dup[...], up_w[tile], 1, 1)
        ).astype(BF)
        writer.send(back.at[:, tile], back_hbm.at[:, tile])


def expert_gate(me, received, small):
    shares = router_probs(received, small)
    lane = lax.broadcasted_iota(jnp.int32, shares.shape, 1)
    return jnp.sum(jnp.where(lane == me, shares, 0.0), axis=-1, keepdims=True)


def experts_both_kernel(
    me, received_hbm, product_hbm, w_hbm, gate_hbm, up_hbm,
    hidden_hbm, dgate_hbm, dup_hbm, back_hbm,
    received, product, small, gate_w, up_w, hidden, dgate, dup, back,
    in_sems, out_sems,
):
    pairs = [(received_hbm, received), small_source(w_hbm, small)]
    gate_up = gate_up_pairs(1, gate_hbm, up_hbm, gate_w, up_w)
    for i, tile in enumerate(tiles(FF)):
        block = (slice(None), pl.ds(tile.start, TILE))
        pairs += gate_up[2 * i : 2 * i + 2] + [(product_hbm.at[block], product.at[block])]
    reader, writer = Reader(in_sems, pairs), Writer(out_sems)
    reader.take(2)
    weight = expert_gate(me[0], received[...], small[...])
    total = jnp.zeros((SLOTS, 1), F32)
    ahead = None
    for tile in tiles(FF) + [None]:
        if tile is not None:
            reader.take(3)
            coming = (tile, dot(received[...], gate_w[:, tile]), dot(received[...], up_w[:, tile]))
        if ahead is not None:
            at, gate, up = ahead
            act, slope = gelu_both(gate)
            low = (act * up).astype(BF)
            hidden[:, at] = low
            dhidden = product[:, at]
            total += jnp.sum(dhidden * low.astype(F32), axis=-1, keepdims=True)
            dhidden = weight * dhidden
            dgate[:, at] = (dhidden * (slope * up)).astype(BF)
            dup[:, at] = (dhidden * act).astype(BF)
        ahead = coming
    writer.send(hidden, hidden_hbm)
    writer.send(dgate, dgate_hbm)
    writer.send(dup, dup_hbm)
    high, low = split(total)
    lane = lax.broadcasted_iota(jnp.int32, (SLOTS, HEAD), 1)
    back[:, WIDTH:] = jnp.where(
        lane == 0, high.astype(F32), jnp.where(lane == 1, low.astype(F32), 0.0)
    ).astype(BF)
    writer.send(back.at[:, WIDTH:], back_hbm.at[:, WIDTH:])
    back_tiles(dgate, dup, gate_w, up_w, back, back_hbm, writer)
    writer.finish()


def small_source(w_hbm, small):
    return (w_hbm.at[:, pl.ds(SMALL, HEAD)], small)


def experts_both(me, received, product, w, weights, order):
    small = (SLOTS, FF)
    wide = (SLOTS, WIDTH)
    back = (SLOTS, WIDTH + HEAD)
    return run_experts(
        experts_both_kernel, "experts_both", [me, received, product, w, *weights[:2]], order,
        [small, small, small, back],
        [(wide, BF), (small, F32), ((WIDTH, HEAD), BF)] + EXPERT_SCRATCH[:2]
        + [(small, BF), (small, BF), (small, BF), (back, BF)],
        11, 8 * SLOTS * WIDTH * FF,
    )


def experts_out_kernel(
    me, hidden_hbm, received_hbm, dx_hbm, w_hbm, down_hbm,
    part0_hbm, part1_hbm, part2_hbm, dslot_hbm,
    hidden, received, dx, small, down_w, part0, part1, part2, dslot, in_sems, out_sems,
):
    pairs = [(hidden_hbm, hidden), (down_hbm.at[1, 0], down_w), (received_hbm, received)]
    pairs += [small_source(w_hbm, small), (dx_hbm, dx)]
    reader, writer = Reader(in_sems, pairs), Writer(out_sems)
    reader.take(2)
    for tile in tiles(WIDTH):
        out = dot(hidden[...], down_w[:, tile]).astype(BF)
        for expert in range(EXPERTS):
            for p, target in enumerate((part0, part1, part2)):
                at = expert * CAP + p * PART_ROWS
                target[expert, :, tile] = out[at : at + PART_ROWS]
    writer.send(part0, part0_hbm)
    writer.send(part1, part1_hbm)
    writer.send(part2, part2_hbm)
    reader.take(3)
    weight = expert_gate(me[0], received[...], small[...])
    for tile in tiles(WIDTH):
        dslot[:, tile] = (weight * dx[:, tile].astype(F32)).astype(BF)
    writer.send(dslot, dslot_hbm)
    writer.finish()


def experts_out(me, hidden, received, dx, w, down, order):
    small = (SLOTS, FF)
    wide = (SLOTS, WIDTH)
    part = (EXPERTS, PART_ROWS, WIDTH)
    return run_experts(
        experts_out_kernel, "experts_out", [me, hidden, received, dx, w, down], order,
        [part, part, part, wide],
        [(small, BF), (wide, BF), (wide, BF), ((WIDTH, HEAD), BF), ((FF, WIDTH), BF)]
        + [(part, BF)] * 3 + [(wide, BF)],
        5, 2 * SLOTS * WIDTH * FF,
    )


def experts_backward_kernel(
    dslot_hbm, act_hbm, slope_hbm, gate_hbm, up_hbm, down_hbm, dgate_hbm, dup_hbm, back_hbm,
    dslot, act_s, slope_s, gate_w, up_w, down_w, dgate, dup, back, in_sems, out_sems,
):
    pairs = [(dslot_hbm, dslot)]
    for tile in tiles(FF):
        block = pl.ds(tile.start, TILE)
        pairs += [(down_hbm.at[0, 0].at[block], down_w.at[block])]
    pairs += [(slope_hbm, slope_s), (act_hbm, act_s)]
    for tile in tiles(WIDTH):
        block = pl.ds(tile.start, TILE)
        pairs += [(gate_hbm.at[0, 0].at[block], gate_w.at[block])]
        pairs += [(up_hbm.at[0, 0].at[block], up_w.at[block])]
    copies = start_all(pairs, in_sems)
    writer = Writer(out_sems)
    copies.pop(0).wait()
    dhidden = []
    for tile in tiles(FF):
        copies.pop(0).wait()
        dhidden += [dot(dslot[...], down_w[tile], 1, 1)]
    copies.pop(0).wait()
    copies.pop(0).wait()
    for tile, part in zip(tiles(FF), dhidden):
        dgate[:, tile] = (part * slope_s[:, tile].astype(F32)).astype(BF)
        dup[:, tile] = (part * act_s[:, tile].astype(F32)).astype(BF)
    writer.send(dgate, dgate_hbm)
    writer.send(dup, dup_hbm)
    for copy in copies:
        copy.wait()
    back_tiles(dgate, dup, gate_w, up_w, back, back_hbm, writer)
    writer.finish()


def experts_backward(dslot, act, slope, weights, order):
    small = (SLOTS, FF)
    wide = (SLOTS, WIDTH)
    return run_experts(
        experts_backward_kernel, "experts_backward", [dslot, act, slope, *weights], order,
        [small, small, wide],
        [(wide, BF), (small, BF), (small, BF)] + EXPERT_SCRATCH
        + [(small, BF), (small, BF), (wide, BF)],
        6 + 2 * WIDTH // TILE, 6 * SLOTS * WIDTH * FF,
    )


def on_core(core, me, ins, outs, scratch, kernel, name, above, order):
    sd = jax.ShapeDtypeStruct
    held = [] if above is None else list(above)
    first_out = 1 + len(ins) + len(held) + len(order)

    def body(*refs):
        @pl.when(refs[0][0] % 2 == core)
        def _():
            kernel(refs[0][0], refs[1 : 1 + len(ins)], refs[first_out : first_out + len(outs)],
                   refs[first_out + len(outs) :])

    return pl.pallas_call(
        body,
        out_shape=[sd(shape, kind) for shape, kind in outs],
        in_specs=[pl.BlockSpec(memory_space=pltpu.SMEM)]
        + [ANY] * (len(ins) + len(held) + len(order)),
        out_specs=[ANY] * len(outs),
        input_output_aliases={1 + len(ins) + i: i for i in range(len(held))},
        scratch_shapes=[pltpu.VMEM(shape, kind) for shape, kind in scratch]
        + [pltpu.SemaphoreType.DMA((24,)), pltpu.SemaphoreType.DMA((24,))],
        compiler_params=pltpu.CompilerParams(vmem_limit_bytes=VMEM_BYTES),
        name=name,
    )(me, *ins, *held, *order)


def upper_product_kernel(me, ins, outs, scratch):
    rows, down, product, in_sems, out_sems = scratch
    pairs = [(ins[0], rows)]
    for tile in tiles(FF):
        block = pl.ds(tile.start, TILE)
        pairs += [(ins[1].at[1, 0].at[block], down.at[block])]
    reader, writer = Reader(in_sems, pairs), Writer(out_sems)
    reader.take()
    for tile in tiles(FF):
        reader.take()
        product[:, tile] = dot(rows[...], down[tile], 1, 1)
        writer.send(product.at[:, tile], outs[0].at[:, tile])
    writer.finish()


def upper_product(core, me, dx_rows, w_down, above, order):
    small = (SLOTS, FF)
    return on_core(
        core, me, [dx_rows, w_down], [(small, F32)], [(WIDE, BF), ((FF, WIDTH), BF), (small, F32)],
        upper_product_kernel, "upper_product", above, order,
    )


def turn_weights_kernel(me, ins, outs, scratch):
    w, turned, in_sems, out_sems = scratch
    ring_out = len(ins) > 1
    pairs = [column_block(ins[0], w, at) for at in range(0, QKV if ring_out else SMALL, TILE)]
    if ring_out:
        pairs += ring_blocks(me, ins[1:], w)
    reader, writer = Reader(in_sems, pairs), Writer(out_sems)
    for tile in tiles(SMALL):
        if ring_out and tile.start == QKV:
            reader.take(len(ins) - 1)
        elif not ring_out or tile.start < QKV:
            reader.take()
        turned[tile] = w[:, tile].T
        writer.send(turned.at[tile], outs[0].at[tile])
    writer.finish()


def turn_weights(core, me, w, blocks, above, order):
    turned = ((SMALL, WIDTH), BF)
    return on_core(
        core, me, [w, *blocks], [turned], [((WIDTH, SMALL), BF), turned], turn_weights_kernel,
        "turn_weights", above, order,
    )


def expert_grads_kernel(received, dgate_pre, dup_pre, hidden, dslot, *rest):
    above = None
    if rest[0].shape[1] == SHARD:
        packed, down_out = rest
    else:
        above, packed = rest
        down_out = packed.at[:, SHARD : SHARD + FF // DP]
    gate = dot(received[...], dgate_pre[...], 0, 0).astype(BF)
    up = dot(received[...], dup_pre[...], 0, 0).astype(BF)
    down = dot(hidden[...], dslot[...], 0, 0).astype(BF)
    for part in range(DP // 2):
        packed[part, :SHARD, :FF] = gate[part * SHARD : (part + 1) * SHARD]
        packed[part, :SHARD, FF:] = up[part * SHARD : (part + 1) * SHARD]
        down_out[part] = down[part * FF // DP : (part + 1) * FF // DP]
    if above is not None:
        packed[:, SHARD + FF // DP :] = above[...]


def expert_grads(received, dgate_pre, dup_pre, hidden, dslot, above):
    down = FF // DP
    shapes = [(SHARD,), (down,)] if above is None else [(SHARD + 2 * down,)]
    whole = lambda width: pl.BlockSpec((SLOTS, width), lambda i: (0, 0))
    part = lambda width: pl.BlockSpec((SLOTS, width), lambda i: (0, i))
    rows = lambda count: pl.BlockSpec((DP // 2, count, WIDTH), lambda i: (i, 0, 0))
    held = [] if above is None else [above]
    return pl.pallas_call(
        expert_grads_kernel,
        grid=(2,),
        out_shape=[jax.ShapeDtypeStruct((DP, count, WIDTH), BF) for count, in shapes],
        in_specs=[part(WIDTH // 2), whole(FF), whole(FF), part(FF // 2), whole(WIDTH)]
        + [rows(down)] * len(held),
        out_specs=[rows(count) for count, in shapes],
        compiler_params=pltpu.CompilerParams(vmem_limit_bytes=VMEM_BYTES),
        cost_estimate=pl.CostEstimate(
            flops=6 * SLOTS * WIDTH * FF, bytes_accessed=14 << 20, transcendentals=0
        ),
        name="expert_grads",
    )(received, dgate_pre, dup_pre, hidden, dslot, *held)


def pack_kernel(
    l, query_hbm, key_hbm, value_hbm, out_hbm, router_hbm, gain_attn, gain_ffn, packed_hbm, *rest
):
    if l == 0:
        out_copy, packed, out, router, sems, out_sems = rest
    else:
        packed, router, sems, out_sems = rest
        out = packed.at[:, pl.ds(QKV, WIDTH)]
    pairs = [
        (router_hbm.at[l], router),
        (query_hbm.at[l], packed.at[:, pl.ds(0, Q_END)]),
        (key_hbm.at[l], packed.at[:, pl.ds(Q_END, K_END - Q_END)]),
        (value_hbm.at[l], packed.at[:, pl.ds(K_END, QKV - K_END)]),
        (out_hbm.at[l], out),
    ]
    reader, writer = Reader(sems, pairs), Writer(out_sems)
    reader.take()
    small = [router[...].astype(F32), gain_attn[l : l + 1].astype(F32)]
    small += [gain_ffn[l : l + 1].astype(F32), jnp.zeros((HEAD - EXPERTS - 2, SHARD), F32)]
    small = jnp.concatenate(small, axis=0)
    small = jnp.concatenate([small, jnp.zeros((HEAD, TILE - SHARD), F32)], axis=1).T
    packed[:, packed.shape[1] - HEAD :] = small[:SHARD].astype(BF)
    reader.take(3)
    if l == 0:
        writer.send(packed, packed_hbm)
        reader.take()
        writer.send(out, out_copy)
    else:
        reader.take()
        writer.send(packed, packed_hbm)
    writer.finish()


def pack(l, query, key, value, out, router, gain_attn, gain_ffn):
    sd = jax.ShapeDtypeStruct
    vmem = pl.BlockSpec(memory_space=pltpu.VMEM)
    packed = (SHARD, QKV + HEAD) if l == 0 else (SHARD, PACKED)
    outs = [packed] + [(SHARD, WIDTH)] * (l == 0)
    return pl.pallas_call(
        lambda *refs: pack_kernel(l, *refs),
        out_shape=[sd(shape, BF) for shape in outs],
        in_specs=[ANY] * 5 + [vmem] * 2,
        out_specs=[ANY] * len(outs),
        scratch_shapes=[pltpu.VMEM(shape, BF) for shape in outs]
        + [pltpu.VMEM((EXPERTS, SHARD), BF)]
        + [pltpu.SemaphoreType.DMA((5,)), pltpu.SemaphoreType.DMA((2,))],
        compiler_params=pltpu.CompilerParams(vmem_limit_bytes=VMEM_BYTES),
        name="pack",
    )(query, key, value, out, router.transpose(0, 2, 1), gain_attn, gain_ffn)


def ring(block):
    def move(values, step):
        return lax.ppermute(values, "dp", [(i, (i + step) % DP) for i in range(DP)])

    half = block.shape[0] // 2
    previous, following = move(block, 2), move(block, -2)
    far = [move(previous[:half], 2), move(following[half:], -2)]
    mine = [block, previous, following, *far]
    swap = [(i, i ^ 1) for i in range(DP)]
    return mine + [lax.ppermute(values, "dp", swap) for values in mine]


def seq_tables(counts):
    ends = jnp.cumsum(counts)
    starts = ends - counts
    place = jnp.arange(ROWS, dtype=jnp.int32)
    member = (place[:, None] >= starts[None, :]) & (place[:, None] < ends[None, :])
    index = jnp.arange(counts.shape[0], dtype=jnp.int32)
    segment = jnp.sum(jnp.where(member, index[None, :], 0), axis=1)
    position = place - jnp.sum(jnp.where(member, starts[None, :], 0), axis=1)
    allowed = (segment[:, None] == segment[None, :]) & (place[:, None] >= place[None, :])
    freqs = ROPE_BASE ** (-2.0 * jnp.arange(HEAD // 2, dtype=F32) / HEAD)
    angle = position.astype(F32)[:, None] * freqs[None, :]
    cosine, sine = jnp.cos(angle), jnp.sin(angle)
    return (
        jnp.concatenate([cosine, cosine], axis=1),
        jnp.concatenate([-sine, sine], axis=1),
        allowed.astype(F32),
    )


def slot_matrix(choices, in_parts=False):
    experts = jnp.arange(EXPERTS, dtype=jnp.int32)
    member = jnp.any(choices[:, :, None] == experts[None, None, :], axis=1).astype(BF)
    row = lax.broadcasted_iota(jnp.int32, (ROWS, ROWS), 0)
    column = lax.broadcasted_iota(jnp.int32, (ROWS, ROWS), 1)
    rank = dot((column < row).astype(BF), member).astype(BF)
    slot = jnp.arange(SLOTS, dtype=jnp.int32)[None, :]
    if in_parts:
        owner, place = slot % PART // PART_ROWS, slot // PART * PART_ROWS + slot % PART_ROWS
    else:
        owner, place = slot // CAP, slot % CAP
    expand = (owner == experts[:, None]).astype(BF)
    return ((dot(member, expand) > 0.5) & (dot(rank, expand) == place.astype(F32))).astype(BF)


def exchange(rows):
    width = rows.shape[-1]
    moved = lax.all_to_all(
        rows.reshape(EXPERTS, -1, width), "expert", split_axis=0, concat_axis=0, tiled=True
    )
    return moved.reshape(-1, width)


def after(values, *order):
    return pl.pallas_call(
        lambda *refs: None,
        out_shape=jax.ShapeDtypeStruct(values.shape, values.dtype),
        in_specs=[ANY] * (1 + len(order)),
        out_specs=ANY,
        input_output_aliases={0: 0},
        name="after",
    )(values, *order)


def turn_columns_kernel(me, columns_hbm, turned_hbm, columns, turned, in_sems, out_sems):
    base = me[0] * SHARD // HEAD * HEAD
    pairs = []
    for i in range(3):
        at = pl.multiple_of(base + i * WIDTH, HEAD)
        pairs += [(columns_hbm.at[:, pl.ds(at, TILE)], columns.at[:, pl.ds(i * TILE, TILE)])]
    reader, writer = Reader(in_sems, pairs), Writer(out_sems)
    for i in range(3):
        reader.take()
        turned[i] = columns[:, i * TILE : (i + 1) * TILE].T
        writer.send(turned.at[i], turned_hbm.at[i])
    writer.finish()


def turn_columns(me, columns):
    tokens = DP * ROWS
    return pl.pallas_call(
        turn_columns_kernel,
        out_shape=jax.ShapeDtypeStruct((3, TILE, tokens), BF),
        in_specs=[pl.BlockSpec(memory_space=pltpu.SMEM), ANY],
        out_specs=ANY,
        scratch_shapes=[
            pltpu.VMEM((tokens, 3 * TILE), BF),
            pltpu.VMEM((3, TILE, tokens), BF),
            pltpu.SemaphoreType.DMA((3,)),
            pltpu.SemaphoreType.DMA((3,)),
        ],
        compiler_params=pltpu.CompilerParams(vmem_limit_bytes=VMEM_BYTES),
        cost_estimate=pl.CostEstimate(flops=0, bytes_accessed=4 << 20, transcendentals=0),
        name="turn_columns",
    )(me, columns)


def dense_grads_kernel(me, turned_hbm, factors_hbm, pieces_hbm, turned, factors, total, pieces,
                       in_sems, out_sems):
    start = me[0] * SHARD
    shift = start % HEAD
    base = start - shift
    copies = Writer(out_sems)
    pairs = [(turned_hbm, turned)]
    for at, width in [(SMALL, HEAD)] + [(at, 2 * CHUNK) for at in range(0, SMALL, 2 * CHUNK)]:
        block = (slice(None), pl.ds(at, width))
        pairs += [(factors_hbm.at[block], factors.at[block])]
    reader = Reader(in_sems, pairs)
    reader.take(2)

    def put(chunk, values):
        pieces[chunk] = values.astype(BF)
        copies.send(pieces.at[chunk], pieces_hbm.at[chunk])

    ends = jnp.zeros((ROWS, HEAD), F32)
    for source in range(DP):
        ends += factors[source * ROWS : (source + 1) * ROWS, SMALL:].astype(F32)
    lane = lax.broadcasted_iota(jnp.int32, (ROWS, HEAD), 1)

    def gain_piece(piece):
        held = (lane == piece + GAIN_HIGH) | (lane == piece + GAIN_LOW)
        return jnp.sum(jnp.where(held, ends, 0.0), axis=1, keepdims=True)

    first, second = gain_piece(base // HEAD), gain_piece(base // HEAD + 1)
    gain = jnp.where(
        shift == 0,
        jnp.concatenate([first, second[: SHARD - ROWS]], axis=0),
        jnp.concatenate([first[ROWS // 2 :], second], axis=0),
    )
    gain_high, gain_low = split(gain)
    rows = pl.ds(pl.multiple_of(shift, 64), SHARD)
    total[1, :, :HEAD] = dot(turned[2], factors[:, SMALL:])
    router = total[1, rows, :HEAD]
    lane = lax.broadcasted_iota(jnp.int32, (SHARD, HEAD), 1)
    router = jnp.where(lane < EXPERTS, router, 0.0)
    router = jnp.where(lane == EXPERTS, gain_high.astype(F32), router)
    router = jnp.where(lane == EXPERTS + 1, gain_low.astype(F32), router)
    put(CHUNKS - 2, jnp.concatenate([router, jnp.zeros_like(router)], axis=1))
    put(CHUNKS - 1, jnp.zeros((SHARD, CHUNK), F32))
    for pair in range(SMALL // CHUNK // 2):
        reader.take()
        at = pair * 2 * CHUNK
        total[pair % 2] = dot(turned[0 if at < QKV else 1], factors[:, at : at + 2 * CHUNK])
        put(2 * pair, total[pair % 2, rows, :CHUNK])
        put(2 * pair + 1, total[pair % 2, rows, CHUNK:])
    copies.finish()


def dense_grads(me, turned, factors, order):
    tokens = DP * ROWS

    def body(*refs):
        dense_grads_kernel(*refs[:3], *refs[3 + len(order) :])

    return pl.pallas_call(
        body,
        out_shape=jax.ShapeDtypeStruct((CHUNKS, SHARD, CHUNK), BF),
        in_specs=[pl.BlockSpec(memory_space=pltpu.SMEM)] + [ANY] * (2 + len(order)),
        out_specs=ANY,
        scratch_shapes=[
            pltpu.VMEM((3, TILE, tokens), BF),
            pltpu.VMEM((tokens, PACKED), BF),
            pltpu.VMEM((2, TILE, 2 * CHUNK), F32),
            pltpu.VMEM((CHUNKS, SHARD, CHUNK), BF),
            pltpu.SemaphoreType.DMA((1 + CHUNKS,)),
            pltpu.SemaphoreType.DMA((CHUNKS,)),
        ],
        compiler_params=pltpu.CompilerParams(vmem_limit_bytes=VMEM_BYTES),
        cost_estimate=pl.CostEstimate(
            flops=2 * tokens * TILE * PACKED, bytes_accessed=10 << 20, transcendentals=0
        ),
        name="dense_grads",
    )(me, turned, factors, *order)


def to_expert_peers(pieces):
    return lax.all_to_all(pieces, "expert", split_axis=0, concat_axis=0, tiled=True)


def sum_pieces_kernel(pieces_hbm, out_hbm, pieces, out, in_sems, out_sems):
    half = CHUNKS // 2
    pairs = []
    for at in (0, half):
        block = pl.ds(at, half)
        pairs += [(pieces_hbm.at[block, :, pl.ds(0, CHUNK)], pieces.at[block])]
    reader, writer = Reader(in_sems, pairs), Writer(out_sems)
    reader.take()
    total = pieces[0].astype(F32)
    for i in range(1, half):
        total += pieces[i].astype(F32)
    reader.take()
    for i in range(half, CHUNKS):
        total += pieces[i].astype(F32)
    out[...] = total.astype(BF)
    if len(out_hbm.shape) == 3:
        for i in range(CHUNKS):
            writer.send(out, out_hbm.at[i])
    else:
        writer.send(out, out_hbm)
    writer.finish()


def sum_pieces(pieces, copies):
    return pl.pallas_call(
        sum_pieces_kernel,
        out_shape=jax.ShapeDtypeStruct((copies,) * (copies > 1) + (SHARD, CHUNK), BF),
        in_specs=[ANY],
        out_specs=ANY,
        scratch_shapes=[
            pltpu.VMEM((CHUNKS, SHARD, CHUNK), BF),
            pltpu.VMEM((SHARD, CHUNK), BF),
            pltpu.SemaphoreType.DMA((2,)),
            pltpu.SemaphoreType.DMA((CHUNKS,)),
        ],
        compiler_params=pltpu.CompilerParams(vmem_limit_bytes=VMEM_BYTES),
        name="sum_pieces",
    )(pieces)


def finish_kernel(l, refs):
    (pieces, w_query, key_projection, value_projection, norm_attn), refs = refs[:5], refs[5:]
    if l == 0:
        ends_above, refs = refs[0], refs[5:]
        (query_hbm, key_hbm, value_hbm, out_hbm, gain_attn, gain_ffn, router) = refs[:7]
        query, key, value, out, sems = refs[7:]
    else:
        query_hbm, key_hbm, value_hbm, out_hbm, ends_out, query, key, value, out, sems = refs
    writer = Writer(sems)
    rows = jnp.zeros((SHARD, 1), F32)
    for chunk in range(SMALL // CHUNK):
        part = pieces[chunk].astype(F32)
        lanes = slice(chunk * CHUNK, (chunk + 1) * CHUNK)
        if chunk < Q_END // CHUNK:
            query[:, lanes] = part
            weight = w_query[l, :, lanes]
        elif chunk == Q_END // CHUNK:
            key[...] = part
            weight = key_projection[l]
            writer.send(query, query_hbm.at[l])
            writer.send(key, key_hbm.at[l])
        elif chunk < QKV // CHUNK:
            value[...] = part
            weight = value_projection[l]
            writer.send(value, value_hbm.at[l])
        else:
            out[:, lanes.start - QKV : lanes.stop - QKV] = part
            continue
        rows += jnp.sum(part * weight.astype(F32), axis=1, keepdims=True)
    writer.send(out, out_hbm.at[l])
    ends = pieces[CHUNKS - 2, :, :HEAD].astype(F32)
    ffn = ends[:, EXPERTS : EXPERTS + 1] + ends[:, EXPERTS + 1 : EXPERTS + 2]
    lane = lax.broadcasted_iota(jnp.int32, (SHARD, HEAD), 1)
    ends = jnp.where(lane == EXPERTS, rows, jnp.where(lane == EXPERTS + 1, ffn, ends))
    if l > 0:
        ends_out[...] = ends
    else:
        for layer, part in enumerate((ends, ends_above[...])):
            wide = jnp.concatenate([part, jnp.zeros((TILE - SHARD, HEAD), F32)], axis=0).T
            router[layer] = wide[:EXPERTS, :SHARD]
            gain = norm_attn[layer : layer + 1].astype(F32)
            gain_attn[layer : layer + 1] = wide[EXPERTS : EXPERTS + 1, :SHARD] / gain
            gain_ffn[layer : layer + 1] = wide[EXPERTS + 1 : EXPERTS + 2, :SHARD]
    writer.finish()


def finish(l, pieces, weights, norm_attn, above):
    sd = jax.ShapeDtypeStruct
    vmem = pl.BlockSpec(memory_space=pltpu.VMEM)
    keys = (SHARD, KEY_VALUE_HEADS * HEAD)
    slabs = [(SHARD, Q_END), keys, keys, (SHARD, WIDTH)]
    outs = [sd((LAYERS,) + shape, F32) for shape in slabs]
    if above is None:
        outs += [sd((SHARD, HEAD), F32)]
        ins, in_specs, aliases = [], [], {}
    else:
        outs += [sd((LAYERS, SHARD), F32)] * 2 + [sd((LAYERS, EXPERTS, SHARD), F32)]
        ins, in_specs = [above[4], *above[:4]], [vmem] + [ANY] * 4
        aliases = {6 + i: i for i in range(4)}
    return pl.pallas_call(
        lambda *refs: finish_kernel(l, refs),
        out_shape=outs,
        in_specs=[vmem] * 5 + in_specs,
        out_specs=[ANY] * 4 + [vmem] * (len(outs) - 4),
        input_output_aliases=aliases,
        scratch_shapes=[pltpu.VMEM(shape, F32) for shape in slabs]
        + [pltpu.SemaphoreType.DMA((4,))],
        compiler_params=pltpu.CompilerParams(vmem_limit_bytes=VMEM_BYTES),
        name="finish",
    )(pieces, *weights, norm_attn, *ins)


def finish_experts_kernel(shares0, shares1, gate, up, down):
    rows = FF // DP
    for l, shares in enumerate((shares0, shares1)):
        gate[l, 0] = shares[:SHARD, :FF].astype(F32)
        up[l, 0] = shares[:SHARD, FF:].astype(F32)
        down[l, 0] = shares0[SHARD + l * rows : SHARD + (l + 1) * rows].astype(F32)


def finish_experts(shares0, shares1):
    sd = jax.ShapeDtypeStruct
    vmem = pl.BlockSpec(memory_space=pltpu.VMEM)
    return pl.pallas_call(
        finish_experts_kernel,
        out_shape=[
            sd((LAYERS, 1, SHARD, FF), F32), sd((LAYERS, 1, SHARD, FF), F32),
            sd((LAYERS, 1, FF // DP, WIDTH), F32),
        ],
        in_specs=[vmem] * 2,
        out_specs=[vmem] * 3,
        compiler_params=pltpu.CompilerParams(vmem_limit_bytes=VMEM_BYTES),
        name="finish_experts",
    )(shares0, shares1)


def mixed_kernel(x_hbm, high, low, part0, part1, part2, out, x, gates, returned, sems):
    pairs = [(high, gates.at[:ROWS]), (low, gates.at[ROWS:]), (x_hbm, x)]
    for p, part in enumerate((part0, part1, part2)):
        pairs += [(part, returned.at[pl.ds(p * PART, PART)])]
    Reader(sems, pairs).take(len(pairs))
    for tile in tiles(WIDTH):
        both = dot(gates[...], returned[:, tile])
        out[:, tile] = (x[:, tile] + both[:ROWS] + both[ROWS:]).astype(BF)


def mixed_rows(x, high, low, parts):
    return pl.pallas_call(
        mixed_kernel,
        out_shape=jax.ShapeDtypeStruct(TOKENS, BF),
        in_specs=[ANY] * 6,
        out_specs=pl.BlockSpec(memory_space=pltpu.VMEM),
        scratch_shapes=[
            pltpu.VMEM(TOKENS, F32),
            pltpu.VMEM((2 * ROWS, SLOTS), BF),
            pltpu.VMEM(WIDE, BF),
            pltpu.SemaphoreType.DMA((6,)),
        ],
        compiler_params=pltpu.CompilerParams(vmem_limit_bytes=VMEM_BYTES),
        name="mixed",
    )(x, high, low, *parts)


def local(
    tokens, cotangent, lengths, routes, norm_attn, w_query, key_projection, value_projection,
    w_out, norm_ffn, w_router, w_gate, w_up, w_down,
):
    me_dp = lax.axis_index("dp").astype(jnp.int32).reshape(1)
    me_expert = lax.axis_index("expert").astype(jnp.int32).reshape(1)
    tables = seq_tables(lengths[0])
    give = [slot_matrix(routes[l]) for l in range(LAYERS)]
    take = [g.T for g in give]
    give_parts = slot_matrix(routes[1], True)
    experts = (w_gate, w_up, w_down)

    def gather(values):
        return lax.all_gather(values, "dp", axis=0, tiled=True)

    weights = (w_query, key_projection, value_projection, w_out, w_router, norm_attn, norm_ffn)
    shard0, out_shard0 = pack(0, *weights)
    w = [gather(shard0), gather(pack(1, *weights)[0])]
    out_ring = [me_dp, *ring(out_shard0)]

    dx_rows = exchange(dot(take[1], cotangent).astype(BF))

    turned_w = turn_weights(1, me_dp, w[0], out_ring[1:], None, ())
    product = upper_product(1, me_dp, dx_rows, w_down, None, turned_w)
    kept0 = attn_forward(
        tokens, None, w[0], out_ring, tables, take[0], give[0],
        (*product, give[1], give_parts, me_expert),
    )
    received0 = exchange(kept0["rows"])
    act0, slope0, hidden0, out0 = experts_forward(received0, experts, ())
    returned0 = exchange(out0)
    turned_w = turn_weights(0, me_dp, w[0], out_ring[1:], turned_w, (out0,))
    product = upper_product(0, me_dp, dx_rows, w_down, product, turned_w)
    turned_w1 = turn_weights(0, me_dp, w[1], [], None, product)
    turned_w1 = turn_weights(1, me_dp, w[1], [], turned_w1, (returned0,))
    columns0 = gather(kept0["columns"])

    kept1 = attn_forward(
        kept0["after"], (kept0["high"], kept0["low"], returned0), w[1], None, tables, take[1],
        give_parts, tuple(turned_w1),
    )
    received1 = exchange(kept1["rows"])
    columns1 = gather(kept1["columns"])
    hidden1, dgate1, dup1, back1 = experts_both(
        me_expert, received1, product[0], w[1], experts, ()
    )
    back1 = exchange(back1)
    *parts, dslot1 = experts_out(me_expert, hidden1, received1, dx_rows, w[1], w_down, ())
    grads1, down1 = expert_grads(received1, dgate1, dup1, hidden1, dslot1, None)
    turned0 = turn_columns(me_dp, columns0)
    parts[0] = exchange(after(parts[0], grads1, turned0))

    dx0, packed1, rows0 = attn_backward(
        cotangent, back1, kept1["x"], kept1, w[1], turned_w1[0], tables, give[1],
        (take[0], kept0["router"]), None, (),
    )
    packed1 = after(packed1, parts[0])
    dslot0 = exchange(rows0)
    factors1 = gather(packed1)
    shares1 = lax.psum_scatter(
        after(grads1, packed1).reshape(-1, WIDTH), "dp", scatter_dimension=0, tiled=True
    )
    dgate0, dup0, back0 = experts_backward(dslot0, act0, slope0, experts, ())
    back0 = exchange(back0)
    (grads0,) = expert_grads(received0, dgate0, dup0, hidden0, dslot0, down1)
    parts[1] = exchange(parts[1])
    turned1 = turn_columns(me_dp, columns1)
    pieces1 = dense_grads(me_dp, turned1, factors1, (parts[1],))
    parts[2] = exchange(after(parts[2], grads0, pieces1))
    grad_tokens, packed0 = attn_backward(
        dx0, back0, tokens, kept0, w[0], turned_w[0], tables, give[0], None, returned0, ()
    )
    factors0 = gather(after(packed0, parts[2]))
    summed1 = sum_pieces(to_expert_peers(pieces1), CHUNKS)
    shares0 = lax.psum_scatter(
        after(grads0, summed1, shares1).reshape(-1, WIDTH), "dp", scatter_dimension=0, tiled=True
    )
    mixed = mixed_rows(kept1["after"], kept1["high"], kept1["low"], parts)
    pieces1 = to_expert_peers(summed1)
    pieces0 = dense_grads(me_dp, turned0, factors0, ())
    pieces0 = to_expert_peers(after(pieces0, pieces1))
    pieces0 = to_expert_peers(sum_pieces(pieces0, CHUNKS))

    dense = (w_query, key_projection, value_projection)
    above = finish(1, pieces1, dense, norm_attn, None)
    gate, up, down = finish_experts(shares0, shares1)
    above = (after(above[0], gate), *above[1:])
    query, key, value, out, gain_attn, gain_ffn, router = finish(
        0, pieces0, dense, norm_attn, above
    )
    return (
        mixed, grad_tokens, gain_attn, query, key, value, out, gain_ffn,
        router.transpose(0, 2, 1), gate, up, down,
    )


def solution(mesh):
    placed = (
        P(("dp", "expert"), None),
        P(("dp", "expert"), None),
        P(("dp", "expert"), None),
        P(None, ("dp", "expert"), None),
        P(None, "dp"),
        P(None, "dp", None),
        P(None, "dp", None),
        P(None, "dp", None),
        P(None, "dp", None),
        P(None, "dp"),
        P(None, "dp", None),
        P(None, "expert", None, None),
        P(None, "expert", None, None),
        P(None, "expert", None, None),
    )
    return jax.shard_map(
        local,
        mesh=mesh,
        in_specs=placed,
        out_specs=(
            P(("dp", "expert"), None),
            P(("dp", "expert"), None),
            P(None, "dp"),
            P(None, "dp", None),
            P(None, "dp", None),
            P(None, "dp", None),
            P(None, "dp", None),
            P(None, "dp"),
            P(None, "dp", None),
            P(None, "expert", "dp", None),
            P(None, "expert", "dp", None),
            P(None, "expert", "dp", None),
        ),
        check_vma=False,
    )
```

```python
import jax
import jax.numpy as jnp
from jax import lax
from jax.experimental import pallas as pl
from jax.experimental.pallas import tpu as pltpu
from jax.sharding import PartitionSpec as P

QUERY_HEADS = 12
KEY_VALUE_HEADS = 2
GROUPS = QUERY_HEADS // KEY_VALUE_HEADS
HEAD = 128
LAYERS = 2
WIDTH = 1536
FF = 768
ROWS = 128
EXPERTS = 16
CAP = 48
SLOTS = EXPERTS * CAP
DP = 8
SHARD = WIDTH // DP
Q_END = QUERY_HEADS * HEAD
K_END = Q_END + KEY_VALUE_HEADS * HEAD
QKV = K_END + KEY_VALUE_HEADS * HEAD
SMALL = QKV + WIDTH
PACKED = SMALL + HEAD
GAIN_ATTN, GAIN_FFN = 16, 17
GAIN_HIGH, GAIN_LOW = 16, 32
PIECES = WIDTH // HEAD
TILE = 256
PARTS = 3
PART = SLOTS // PARTS
PART_ROWS = CAP // PARTS
CHUNKS, CHUNK = 16, 256
COLUMNS = 3 * WIDTH
EPSILON = 1e-06
ROPE_BASE = 1000000.0
SCALE = HEAD ** (-0.5)
GELU_A = 0.7978845608028654
GELU_B = 0.044715
VMEM_BYTES = 56 << 20
BF = jnp.bfloat16
F32 = jnp.float32
ANY = pl.BlockSpec(memory_space=pl.ANY)


def dot(left, right, left_dim=1, right_dim=0):
    return lax.dot_general(
        left, right, (((left_dim,), (right_dim,)), ((), ())), preferred_element_type=F32
    )


def split(values):
    high = values.astype(BF)
    return high, (values - high.astype(F32)).astype(BF)


def unit(values):
    return lax.rsqrt(jnp.mean(values * values, axis=-1, keepdims=True) + EPSILON)


def turn(values, cosine, sine):
    return values * cosine + pltpu.roll(values, HEAD // 2, 1) * sine


def expert_lanes(transposed=False, in_parts=False):
    shape = (SLOTS, HEAD) if transposed else (HEAD, SLOTS)
    slot = lax.broadcasted_iota(jnp.int32, shape, 0 if transposed else 1)
    expert = lax.broadcasted_iota(jnp.int32, shape, 1 if transposed else 0)
    if in_parts:
        held = ((slot & (PART - 1)) >> 4) == expert
    else:
        held = (slot >= expert * CAP) & (slot < expert * CAP + CAP)
    return held.astype(F32).astype(BF)


def gain_rows(small):
    row = lax.broadcasted_iota(jnp.int32, (8, HEAD), 0)
    lane = lax.broadcasted_iota(jnp.int32, (8, HEAD), 1)
    pick = ((lane == row + GAIN_ATTN) & (row < 2)).astype(F32).astype(BF)
    rows = dot(pick, small, 1, 1)
    return rows[0:1], rows[1:2]


def router_probs(rows, small):
    logits = dot(rows, small)
    lane = lax.broadcasted_iota(jnp.int32, logits.shape, 1)
    logits = jnp.where(lane < EXPERTS, logits, -1e30)
    powers = jnp.exp(logits - jnp.max(logits, axis=-1, keepdims=True))
    return powers / jnp.sum(powers, axis=-1, keepdims=True)


def start_all(pairs, sems):
    copies = [
        pltpu.make_async_copy(source, target, sems.at[i]) for i, (source, target) in enumerate(pairs)
    ]
    for copy in copies:
        copy.start()
    return copies


class Writer:
    def __init__(self, sems):
        self.sems, self.copies = sems, []

    def send(self, source, target):
        copy = pltpu.make_async_copy(source, target, self.sems.at[len(self.copies)])
        copy.start()
        self.copies.append(copy)

    def finish(self):
        for copy in self.copies:
            copy.wait()


class Reader:
    def __init__(self, sems, pairs):
        self.copies = start_all(pairs, sems)

    def take(self, count=1):
        for _ in range(count):
            self.copies.pop(0).wait()


def tiles(width):
    return [slice(at, at + TILE) for at in range(0, width, TILE)]


def small_block(w_hbm, w):
    last = w_hbm.shape[1] - HEAD
    return (w_hbm.at[:, pl.ds(last, HEAD)], w.at[:, pl.ds(SMALL, HEAD)])


def column_block(w_hbm, w, at):
    return (w_hbm.at[:, pl.ds(at, TILE)], w.at[:, pl.ds(at, TILE)])


def ring_blocks(me, blocks, w):
    pairs = []
    for core in range(2):
        start = me if core == 0 else me + 1 - 2 * (me % 2)
        for block, step in enumerate((0, DP - 2, 2, 4, 4)):
            ref = blocks[core * 5 + block]
            at = (start + step) % DP * SHARD + (SHARD // 2 if block == 4 else 0)
            at = pl.multiple_of(at, SHARD // 2)
            pairs += [(ref, w.at[pl.ds(at, ref.shape[0]), pl.ds(QKV, WIDTH)])]
    return pairs


def attn_forward_kernel(first, ins, outs, scratch):
    (x_hbm, w_hbm, cosine_hbm, sine_hbm, allowed_hbm, take_hbm, give_hbm), ins = ins[:7], ins[7:]
    (columns_hbm, qrot_hbm, krot_hbm, value_hbm, probs_hbm, after_hbm, router_hbm, high_hbm, low_hbm,
     rows_hbm), outs = outs[:10], outs[10:]
    (x_in, w, cosine, sine, allowed, take, give, returned, gates, x, columns, qrot, krot, value, probs,
     after, router, high, low, rows, in_sems, out_sems) = scratch
    acts = columns.at[:, :WIDTH]
    attended = columns.at[:, WIDTH : 2 * WIDTH]
    acts_two = columns.at[:, 2 * WIDTH :]
    pairs = []
    if first:
        out_pairs = ring_blocks(ins[0][0], ins[1:], w)
    else:
        out_pairs = [column_block(w_hbm, w, at) for at in range(QKV, SMALL, TILE)]
        high_below, low_below, returned_hbm = ins
        pairs += [(high_below, gates.at[:ROWS]), (low_below, gates.at[ROWS:])]
        pairs += [(returned_hbm, returned)]
    pairs += [(x_hbm, x_in), small_block(w_hbm, w)]
    pairs += [column_block(w_hbm, w, at) for at in range(0, QKV, TILE)]
    pairs += [(cosine_hbm, cosine), (sine_hbm, sine), (allowed_hbm, allowed)]
    pairs += out_pairs + [(take_hbm, take), (give_hbm, give)]
    reader, writer = Reader(in_sems, pairs), Writer(out_sems)
    if first:
        reader.take()
        x[...] = x_in[...].astype(F32)
    else:
        reader.take(4)
        for tile in tiles(WIDTH):
            both = dot(gates[...], returned[:, tile])
            x[:, tile] = x_in[:, tile] + both[:ROWS] + both[ROWS:]
        writer.send(x, outs[0])
    reader.take()
    small = w[:, SMALL:]
    gain_attn, gain_ffn = gain_rows(small)
    total = x[...]
    acts[...] = (total * unit(total) * gain_attn).astype(BF)
    wide = []
    for tile in tiles(QKV):
        reader.take()
        wide += [dot(acts[...], w[:, tile])]
    reader.take(3)
    for tile in range(QKV // TILE):
        for half in range(TILE // HEAD):
            head = tile * (TILE // HEAD) + half
            part = wide[tile][:, half * HEAD : (half + 1) * HEAD]
            if head < QUERY_HEADS:
                qrot[head] = turn(part, cosine[...], sine[...]).astype(BF)
            elif head < QUERY_HEADS + KEY_VALUE_HEADS:
                krot[head - QUERY_HEADS] = turn(part, cosine[...], sine[...]).astype(BF)
            else:
                value[head - QUERY_HEADS - KEY_VALUE_HEADS] = part.astype(BF)
    writer.send(qrot, qrot_hbm)
    writer.send(krot, krot_hbm)
    writer.send(value, value_hbm)
    open_scores = (allowed[...] > 0.5)[None]
    for k in range(KEY_VALUE_HEADS):
        heads = slice(k * GROUPS, (k + 1) * GROUPS)
        scores = dot(qrot[heads].reshape(GROUPS * ROWS, HEAD), krot[k], 1, 1) * SCALE
        scores = jnp.where(open_scores, scores.reshape(GROUPS, ROWS, ROWS), -1000000000.0)
        powers = jnp.exp(scores - jnp.max(scores, axis=-1, keepdims=True))
        shares = powers / jnp.sum(powers, axis=-1, keepdims=True)
        probs[heads] = shares
        mixed = dot(shares.astype(BF).reshape(GROUPS * ROWS, ROWS), value[k]).astype(BF)
        for group in range(GROUPS):
            at = (k * GROUPS + group) * HEAD
            attended[:, at : at + HEAD] = mixed[group * ROWS : (group + 1) * ROWS]
    writer.send(probs, probs_hbm)
    if first:
        reader.take(len(out_pairs))
    for tile in tiles(WIDTH):
        if not first:
            reader.take()
        after[:, tile] = x[:, tile] + dot(
            attended[...], w[:, QKV + tile.start : QKV + tile.stop]
        )
    writer.send(after, after_hbm)
    total = after[...]
    acts_two[...] = (total * unit(total) * gain_ffn).astype(BF)
    writer.send(columns, columns_hbm)
    reader.take(2)
    for tile in tiles(WIDTH):
        rows[:, tile] = dot(take[...], acts_two[:, tile]).astype(BF)
        writer.send(rows.at[:, tile], rows_hbm.at[:, tile])
    shares = router_probs(acts_two[...], small)
    router[...] = shares
    spread = expert_lanes(in_parts=not first)
    both = dot(jnp.concatenate(split(shares), axis=0), spread).astype(BF)
    high[...] = both[:ROWS] * give[...]
    low[...] = both[ROWS:] * give[...]
    writer.send(router, router_hbm)
    writer.send(high, high_hbm)
    writer.send(low, low_hbm)
    writer.finish()


HEADS = (QUERY_HEADS, ROWS, HEAD)
KEYS = (KEY_VALUE_HEADS, ROWS, HEAD)
TABLE = (ROWS, HEAD)
TOKENS = (ROWS, WIDTH)
WIDE = (SLOTS, WIDTH)


def specs_of(ins):
    return [pl.BlockSpec(memory_space=pltpu.SMEM if a.dtype == jnp.int32 else pl.ANY) for a in ins]


def run_attn(kernel, name, ins, order, outs, scratch, in_copies, out_copies, vmem):
    sd = jax.ShapeDtypeStruct

    def body(*refs):
        first_out = len(ins) + len(order)
        first_scratch = first_out + len(outs)
        kernel(refs[: len(ins)], refs[first_out:first_scratch], refs[first_scratch:])

    return pl.pallas_call(
        body,
        out_shape=[sd(shape, kind) for shape, kind in outs],
        in_specs=specs_of(ins) + [ANY] * len(order),
        out_specs=[ANY] * len(outs),
        scratch_shapes=[pltpu.VMEM(shape, kind) for shape, kind in scratch]
        + [pltpu.SemaphoreType.DMA((in_copies,)), pltpu.SemaphoreType.DMA((out_copies,))],
        compiler_params=pltpu.CompilerParams(vmem_limit_bytes=vmem),
        cost_estimate=pl.CostEstimate(
            flops=2 * ROWS * WIDTH * PACKED, bytes_accessed=20 << 20, transcendentals=200000
        ),
        name=name,
    )(*ins, *order)


def attn_forward(x, combine, w, ring, tables, take, give, order):
    first = combine is None
    outs = [
        ((ROWS, COLUMNS), BF), (HEADS, BF), (KEYS, BF), (KEYS, BF), ((QUERY_HEADS, ROWS, ROWS), F32),
        (TOKENS, F32), (TABLE, F32), ((ROWS, SLOTS), BF), ((ROWS, SLOTS), BF), (WIDE, BF),
    ]
    names = [
        "columns", "qrot", "krot", "value", "probs", "after", "router", "high", "low", "rows"
    ]
    scratch = [(TOKENS, x.dtype), ((WIDTH, PACKED), BF)] + [(TABLE, F32)] * 3
    scratch += [((SLOTS, ROWS), BF), ((ROWS, SLOTS), BF)]
    scratch += [((16, HEAD), BF)] * 2 if first else [(WIDE, BF), ((2 * ROWS, SLOTS), BF)]
    scratch += [(TOKENS, F32)] + outs
    ins = [x, w, *tables, take, give]
    if first:
        ins += ring
    else:
        high, low, returned = combine
        ins += [high, low, returned]
        outs = outs + [(TOKENS, F32)]
        names += ["x"]
    result = run_attn(
        lambda *refs: attn_forward_kernel(first, *refs), "attn_forward", ins, order, outs, scratch,
        20 + QKV // TILE, 20, VMEM_BYTES,
    )
    return dict(zip(names, result))


def norm_back(grad, gain, values):
    scale = unit(values)
    inner = grad * gain
    return scale * inner - values * (scale * scale * scale) * jnp.mean(
        inner * values, axis=-1, keepdims=True
    )


def attn_backward_kernel(last, ins, outs, scratch):
    (dx_hbm, back_hbm, w_hbm, turned_hbm, cosine_hbm, sine_hbm, give_hbm, router_hbm, after_hbm,
     x_hbm, probs_hbm, qrot_hbm, krot_hbm, value_hbm), ins = ins[:14], ins[14:]
    (dx_in, back, small_ref, turned, cosine, sine, give, router, after, x_in, probs, qrot, krot, value, wide_in,
     small_in, datt, dx_out, packed), scratch = scratch[:19], scratch[19:]
    if last:
        rows, scratch = scratch[0], scratch[1:]
    in_sems, out_sems = scratch
    pairs = [(give_hbm, give), (back_hbm, back), (router_hbm, router), (dx_hbm, dx_in)]
    if not last:
        pairs += [(ins[0], wide_in)]
    last_block = pl.ds(w_hbm.shape[1] - HEAD, HEAD)
    pairs += [(w_hbm.at[:, last_block], small_ref), (after_hbm, after)]
    columns = [(slice(None), pl.ds(at, TILE)) for at in range(0, WIDTH, TILE)]
    out_pairs, qkv_pairs = (
        [(turned_hbm.at[rows].at[c], turned.at[rows].at[c]) for c in columns]
        for rows in (pl.ds(QKV, WIDTH), pl.ds(0, QKV))
    )
    pairs += out_pairs + [(probs_hbm, probs), (value_hbm, value), (krot_hbm, krot), (qrot_hbm, qrot)]
    pairs += [(cosine_hbm, cosine), (sine_hbm, sine)] + qkv_pairs + [(x_hbm, x_in)]
    if last:
        pairs += [(ins[0], wide_in), (ins[1], small_in)]
    reader, writer = Reader(in_sems, pairs), Writer(out_sems)
    reader.take(4)
    dx = dx_in[...].astype(F32)
    spread = expert_lanes(True)
    if last:
        dgate = back[:, WIDTH:].astype(F32)
        drouter = dot(give[...], (dgate[:, 0:1] * spread).astype(BF))
        drouter += dot(give[...], (dgate[:, 1:2] * spread).astype(BF))
    else:
        reader.take()
        dgate = dot(dx.astype(BF), wide_in[...], 1, 1) * give[...]
        both = dot(jnp.concatenate(split(dgate), axis=0), spread)
        drouter = both[:ROWS] + both[ROWS:]
    reader.take(2)
    small = small_ref[...]
    gain_attn, gain_ffn = gain_rows(small)
    shares = router[...]
    dlogits = shares * (drouter - jnp.sum(drouter * shares, axis=-1, keepdims=True))
    dlogits = dlogits.astype(BF)
    dacts_two = dot(dlogits, small, 1, 1) + dot(give[...], back[:, :WIDTH])
    total = after[...]
    scale = unit(total)
    dafter = dx + norm_back(dacts_two, gain_ffn, total)
    dx_out[...] = dafter
    packed[:, QKV:SMALL] = dafter.astype(BF)
    dgain = jnp.sum(dacts_two * total * scale, axis=0, keepdims=True)
    dgain_high, dgain_low = split(dgain)
    pieces = [jnp.zeros((GAIN_HIGH, HEAD), F32)]
    for part in (dgain_high.astype(F32), dgain_low.astype(F32)):
        pieces += [part[:, at : at + HEAD] for at in range(0, WIDTH, HEAD)]
        pieces += [jnp.zeros((GAIN_LOW - GAIN_HIGH - PIECES, HEAD), F32)]
    pieces += [jnp.zeros((HEAD - 2 * GAIN_LOW + GAIN_HIGH, HEAD), F32)]
    packed[:, SMALL:] = (dlogits.astype(F32) + jnp.concatenate(pieces, axis=0).T).astype(BF)
    writer.send(packed.at[:, QKV:], outs[1].at[:, QKV:])
    for tile in tiles(WIDTH):
        reader.take()
        wide = dot(packed[:, QKV:SMALL], turned[QKV:SMALL, tile]).astype(BF)
        for half in range(TILE // HEAD):
            datt[tile.start // HEAD + half] = wide[:, half * HEAD : (half + 1) * HEAD]
    reader.take(6)
    for k in range(KEY_VALUE_HEADS):
        heads = slice(k * GROUPS, (k + 1) * GROUPS)
        datt_k = datt[heads].reshape(GROUPS * ROWS, HEAD)
        p = probs[heads].reshape(GROUPS * ROWS, ROWS)
        dprobs = dot(datt_k, value[k], 1, 1)
        dvalue = dot(p.astype(BF), datt_k, 0, 0)
        dscores = (p * (dprobs - jnp.sum(dprobs * p, axis=-1, keepdims=True))).astype(BF)
        dqrot = dot(dscores, krot[k]) * SCALE
        dkrot = dot(dscores, qrot[heads].reshape(GROUPS * ROWS, HEAD), 0, 0) * SCALE
        for group in range(GROUPS):
            at = (k * GROUPS + group) * HEAD
            part = dqrot[group * ROWS : (group + 1) * ROWS]
            packed[:, at : at + HEAD] = turn(part, cosine[...], -sine[...]).astype(BF)
        at = Q_END + k * HEAD
        packed[:, at : at + HEAD] = turn(dkrot, cosine[...], -sine[...]).astype(BF)
        at = K_END + k * HEAD
        packed[:, at : at + HEAD] = dvalue.astype(BF)
    writer.send(packed.at[:, :QKV], outs[1].at[:, :QKV])
    parts = []
    for tile in tiles(WIDTH):
        reader.take()
        parts += [dot(packed[:, :QKV], turned[:QKV, tile])]
    dacts = jnp.concatenate(parts, axis=1)
    reader.take()
    dx = dx_out[...] + norm_back(dacts, gain_attn, x_in[...].astype(F32))
    dx_out[...] = dx
    writer.send(dx_out, outs[0])
    if last:
        reader.take(2)
        dx_low = dx.astype(BF)
        both = dot(spread, jnp.concatenate(split(small_in[...]), axis=0), 1, 1).astype(BF)
        gates = jnp.concatenate([both[:, :ROWS] * wide_in[...], both[:, ROWS:] * wide_in[...]], axis=1)
        twice = jnp.concatenate([dx_low, dx_low], axis=0)
        for tile in tiles(WIDTH):
            rows[:, tile] = dot(gates, twice[:, tile]).astype(BF)
            writer.send(rows.at[:, tile], outs[2].at[:, tile])
    writer.finish()


def attn_backward(dx, back, x, kept, w, turned, tables, give, below, returned, order):
    last = below is not None
    outs = [(TOKENS, F32), ((ROWS, PACKED), BF)]
    if last:
        outs += [(WIDE, BF)]
    ins = [dx, back, w, turned, tables[0], tables[1], give, kept["router"], kept["after"], x]
    ins += [kept[n] for n in ("probs", "qrot", "krot", "value")]
    ins += list(below) if last else [returned]
    scratch = [
        (TOKENS, dx.dtype), (back.shape, BF), ((WIDTH, HEAD), BF), ((SMALL, WIDTH), BF),
        (TABLE, F32), (TABLE, F32),
        ((ROWS, SLOTS), BF), (TABLE, F32), (TOKENS, F32), (TOKENS, x.dtype),
        ((QUERY_HEADS, ROWS, ROWS), F32), (HEADS, BF), (KEYS, BF), (KEYS, BF),
        ((SLOTS, ROWS), BF) if last else (WIDE, BF), (TABLE, F32), (HEADS, BF),
    ] + outs
    return run_attn(
        lambda *refs: attn_backward_kernel(last, *refs), "attn_backward", ins, order, outs, scratch,
        24 + WIDTH // TILE, 12, VMEM_BYTES,
    )


def gelu_parts(gate):
    square = gate * gate
    bend = jnp.tanh(GELU_A * gate * (1.0 + GELU_B * square))
    return bend, square


def gelu(gate):
    bend, _ = gelu_parts(gate)
    return 0.5 * gate * (1.0 + bend)


def gelu_both(gate):
    bend, square = gelu_parts(gate)
    slope = 0.5 * (1.0 + bend) + 0.5 * gate * (1.0 - bend * bend) * GELU_A * (
        1.0 + 3.0 * GELU_B * square
    )
    return 0.5 * gate * (1.0 + bend), slope


def gate_up_pairs(l, gate_hbm, up_hbm, gate_w, up_w):
    gate_up = []
    for at in range(0, FF, TILE):
        block = (slice(None), pl.ds(at, TILE))
        gate_up += [(gate_hbm.at[l, 0].at[block], gate_w.at[block])]
        gate_up += [(up_hbm.at[l, 0].at[block], up_w.at[block])]
    return gate_up


def run_experts(kernel, name, ins, order, outs, scratch, in_copies, flops):
    sd = jax.ShapeDtypeStruct
    count = len(ins) + len(order)

    def body(*refs):
        kernel(*refs[: len(ins)], *refs[count:])

    return pl.pallas_call(
        body,
        out_shape=[sd(shape, BF) for shape in outs],
        in_specs=specs_of(ins) + [ANY] * len(order),
        out_specs=[ANY] * len(outs),
        scratch_shapes=[pltpu.VMEM(shape, kind) for shape, kind in scratch]
        + [pltpu.SemaphoreType.DMA((in_copies,)), pltpu.SemaphoreType.DMA((40,))],
        compiler_params=pltpu.CompilerParams(vmem_limit_bytes=VMEM_BYTES),
        cost_estimate=pl.CostEstimate(
            flops=flops, bytes_accessed=20 << 20, transcendentals=SLOTS * FF
        ),
        name=name,
    )(*ins, *order)


def experts_forward_kernel(
    received_hbm, gate_hbm, up_hbm, down_hbm, act_hbm, slope_hbm, hidden_hbm, out_hbm,
    received, gate_w, up_w, down_w, act_s, slope_s, hidden, out, in_sems, out_sems,
):
    gate_up = gate_up_pairs(0, gate_hbm, up_hbm, gate_w, up_w)
    pairs = [(received_hbm, received)] + gate_up + [(down_hbm.at[0, 0], down_w)]
    copies = start_all(pairs, in_sems)
    writer = Writer(out_sems)
    copies.pop(0).wait()
    for tile in tiles(FF):
        copies.pop(0).wait()
        copies.pop(0).wait()
        gate = dot(received[...], gate_w[:, tile])
        up = dot(received[...], up_w[:, tile])
        act, slope = gelu_both(gate)
        act_s[:, tile] = act.astype(BF)
        slope_s[:, tile] = (slope * up).astype(BF)
        hidden[:, tile] = (act * up).astype(BF)
    copies.pop(0).wait()
    writer.send(act_s, act_hbm)
    writer.send(slope_s, slope_hbm)
    writer.send(hidden, hidden_hbm)
    for tile in tiles(WIDTH):
        out[:, tile] = dot(hidden[...], down_w[:, tile]).astype(BF)
        writer.send(out.at[:, tile], out_hbm.at[:, tile])
    writer.finish()


EXPERT_SCRATCH = [((WIDTH, FF), BF), ((WIDTH, FF), BF), ((FF, WIDTH), BF)]


def experts_forward(received, weights, order):
    small = (SLOTS, FF)
    wide = (SLOTS, WIDTH)
    return run_experts(
        experts_forward_kernel, "experts_forward", [received, *weights], order,
        [small, small, small, wide],
        [(wide, BF)] + EXPERT_SCRATCH + [(small, BF)] * 3 + [(wide, BF)],
        8, 6 * SLOTS * WIDTH * FF,
    )


def back_tiles(dgate, dup, gate_w, up_w, back, back_hbm, writer):
    for tile in tiles(WIDTH):
        back[:, tile] = (
            dot(dgate[...], gate_w[tile], 1, 1) + dot(dup[...], up_w[tile], 1, 1)
        ).astype(BF)
        writer.send(back.at[:, tile], back_hbm.at[:, tile])


def expert_gate(me, received, small):
    shares = router_probs(received, small)
    lane = lax.broadcasted_iota(jnp.int32, shares.shape, 1)
    return jnp.sum(jnp.where(lane == me, shares, 0.0), axis=-1, keepdims=True)


def experts_both_kernel(
    me, received_hbm, product_hbm, w_hbm, gate_hbm, up_hbm,
    hidden_hbm, dgate_hbm, dup_hbm, back_hbm,
    received, product, small, gate_w, up_w, hidden, dgate, dup, back,
    in_sems, out_sems,
):
    pairs = [(received_hbm, received), small_source(w_hbm, small)]
    gate_up = gate_up_pairs(1, gate_hbm, up_hbm, gate_w, up_w)
    for i, tile in enumerate(tiles(FF)):
        block = (slice(None), pl.ds(tile.start, TILE))
        pairs += gate_up[2 * i : 2 * i + 2] + [(product_hbm.at[block], product.at[block])]
    reader, writer = Reader(in_sems, pairs), Writer(out_sems)
    reader.take(2)
    weight = expert_gate(me[0], received[...], small[...])
    total = jnp.zeros((SLOTS, 1), F32)
    ahead = None
    for tile in tiles(FF) + [None]:
        if tile is not None:
            reader.take(3)
            coming = (tile, dot(received[...], gate_w[:, tile]), dot(received[...], up_w[:, tile]))
        if ahead is not None:
            at, gate, up = ahead
            act, slope = gelu_both(gate)
            low = (act * up).astype(BF)
            hidden[:, at] = low
            dhidden = product[:, at]
            total += jnp.sum(dhidden * low.astype(F32), axis=-1, keepdims=True)
            dhidden = weight * dhidden
            dgate[:, at] = (dhidden * (slope * up)).astype(BF)
            dup[:, at] = (dhidden * act).astype(BF)
        ahead = coming
    writer.send(hidden, hidden_hbm)
    writer.send(dgate, dgate_hbm)
    writer.send(dup, dup_hbm)
    high, low = split(total)
    lane = lax.broadcasted_iota(jnp.int32, (SLOTS, HEAD), 1)
    back[:, WIDTH:] = jnp.where(
        lane == 0, high.astype(F32), jnp.where(lane == 1, low.astype(F32), 0.0)
    ).astype(BF)
    writer.send(back.at[:, WIDTH:], back_hbm.at[:, WIDTH:])
    back_tiles(dgate, dup, gate_w, up_w, back, back_hbm, writer)
    writer.finish()


def small_source(w_hbm, small):
    return (w_hbm.at[:, pl.ds(SMALL, HEAD)], small)


def experts_both(me, received, product, w, weights, order):
    small = (SLOTS, FF)
    wide = (SLOTS, WIDTH)
    back = (SLOTS, WIDTH + HEAD)
    return run_experts(
        experts_both_kernel, "experts_both", [me, received, product, w, *weights[:2]], order,
        [small, small, small, back],
        [(wide, BF), (small, F32), ((WIDTH, HEAD), BF)] + EXPERT_SCRATCH[:2]
        + [(small, BF), (small, BF), (small, BF), (back, BF)],
        11, 8 * SLOTS * WIDTH * FF,
    )


def experts_out_kernel(
    me, hidden_hbm, received_hbm, dx_hbm, w_hbm, down_hbm,
    part0_hbm, part1_hbm, part2_hbm, dslot_hbm,
    hidden, received, dx, small, down_w, part0, part1, part2, dslot, in_sems, out_sems,
):
    pairs = [(hidden_hbm, hidden), (down_hbm.at[1, 0], down_w), (received_hbm, received)]
    pairs += [small_source(w_hbm, small), (dx_hbm, dx)]
    reader, writer = Reader(in_sems, pairs), Writer(out_sems)
    reader.take(2)
    for tile in tiles(WIDTH):
        out = dot(hidden[...], down_w[:, tile]).astype(BF)
        for expert in range(EXPERTS):
            for p, target in enumerate((part0, part1, part2)):
                at = expert * CAP + p * PART_ROWS
                target[expert, :, tile] = out[at : at + PART_ROWS]
    writer.send(part0, part0_hbm)
    writer.send(part1, part1_hbm)
    writer.send(part2, part2_hbm)
    reader.take(3)
    weight = expert_gate(me[0], received[...], small[...])
    for tile in tiles(WIDTH):
        dslot[:, tile] = (weight * dx[:, tile].astype(F32)).astype(BF)
    writer.send(dslot, dslot_hbm)
    writer.finish()


def experts_out(me, hidden, received, dx, w, down, order):
    small = (SLOTS, FF)
    wide = (SLOTS, WIDTH)
    part = (EXPERTS, PART_ROWS, WIDTH)
    return run_experts(
        experts_out_kernel, "experts_out", [me, hidden, received, dx, w, down], order,
        [part, part, part, wide],
        [(small, BF), (wide, BF), (wide, BF), ((WIDTH, HEAD), BF), ((FF, WIDTH), BF)]
        + [(part, BF)] * 3 + [(wide, BF)],
        5, 2 * SLOTS * WIDTH * FF,
    )


def experts_backward_kernel(
    dslot_hbm, act_hbm, slope_hbm, gate_hbm, up_hbm, down_hbm, dgate_hbm, dup_hbm, back_hbm,
    dslot, act_s, slope_s, gate_w, up_w, down_w, dgate, dup, back, in_sems, out_sems,
):
    pairs = [(dslot_hbm, dslot)]
    for tile in tiles(FF):
        block = pl.ds(tile.start, TILE)
        pairs += [(down_hbm.at[0, 0].at[block], down_w.at[block])]
    pairs += [(slope_hbm, slope_s), (act_hbm, act_s)]
    for tile in tiles(WIDTH):
        block = pl.ds(tile.start, TILE)
        pairs += [(gate_hbm.at[0, 0].at[block], gate_w.at[block])]
        pairs += [(up_hbm.at[0, 0].at[block], up_w.at[block])]
    copies = start_all(pairs, in_sems)
    writer = Writer(out_sems)
    copies.pop(0).wait()
    dhidden = []
    for tile in tiles(FF):
        copies.pop(0).wait()
        dhidden += [dot(dslot[...], down_w[tile], 1, 1)]
    copies.pop(0).wait()
    copies.pop(0).wait()
    for tile, part in zip(tiles(FF), dhidden):
        dgate[:, tile] = (part * slope_s[:, tile].astype(F32)).astype(BF)
        dup[:, tile] = (part * act_s[:, tile].astype(F32)).astype(BF)
    writer.send(dgate, dgate_hbm)
    writer.send(dup, dup_hbm)
    for copy in copies:
        copy.wait()
    back_tiles(dgate, dup, gate_w, up_w, back, back_hbm, writer)
    writer.finish()


def experts_backward(dslot, act, slope, weights, order):
    small = (SLOTS, FF)
    wide = (SLOTS, WIDTH)
    return run_experts(
        experts_backward_kernel, "experts_backward", [dslot, act, slope, *weights], order,
        [small, small, wide],
        [(wide, BF), (small, BF), (small, BF)] + EXPERT_SCRATCH
        + [(small, BF), (small, BF), (wide, BF)],
        6 + 2 * WIDTH // TILE, 6 * SLOTS * WIDTH * FF,
    )


def on_core(core, me, ins, outs, scratch, kernel, name, above, order):
    sd = jax.ShapeDtypeStruct
    held = [] if above is None else list(above)
    first_out = 1 + len(ins) + len(held) + len(order)

    def body(*refs):
        @pl.when(refs[0][0] % 2 == core)
        def _():
            kernel(refs[0][0], refs[1 : 1 + len(ins)], refs[first_out : first_out + len(outs)],
                   refs[first_out + len(outs) :])

    return pl.pallas_call(
        body,
        out_shape=[sd(shape, kind) for shape, kind in outs],
        in_specs=[pl.BlockSpec(memory_space=pltpu.SMEM)]
        + [ANY] * (len(ins) + len(held) + len(order)),
        out_specs=[ANY] * len(outs),
        input_output_aliases={1 + len(ins) + i: i for i in range(len(held))},
        scratch_shapes=[pltpu.VMEM(shape, kind) for shape, kind in scratch]
        + [pltpu.SemaphoreType.DMA((24,)), pltpu.SemaphoreType.DMA((24,))],
        compiler_params=pltpu.CompilerParams(vmem_limit_bytes=VMEM_BYTES),
        name=name,
    )(me, *ins, *held, *order)


def upper_product_kernel(me, ins, outs, scratch):
    rows, down, product, in_sems, out_sems = scratch
    pairs = [(ins[0], rows)]
    for tile in tiles(FF):
        block = pl.ds(tile.start, TILE)
        pairs += [(ins[1].at[1, 0].at[block], down.at[block])]
    reader, writer = Reader(in_sems, pairs), Writer(out_sems)
    reader.take()
    for tile in tiles(FF):
        reader.take()
        product[:, tile] = dot(rows[...], down[tile], 1, 1)
        writer.send(product.at[:, tile], outs[0].at[:, tile])
    writer.finish()


def upper_product(core, me, dx_rows, w_down, above, order):
    small = (SLOTS, FF)
    return on_core(
        core, me, [dx_rows, w_down], [(small, F32)], [(WIDE, BF), ((FF, WIDTH), BF), (small, F32)],
        upper_product_kernel, "upper_product", above, order,
    )


def turn_weights_kernel(me, ins, outs, scratch):
    w, turned, in_sems, out_sems = scratch
    ring_out = len(ins) > 1
    pairs = [column_block(ins[0], w, at) for at in range(0, QKV if ring_out else SMALL, TILE)]
    if ring_out:
        pairs += ring_blocks(me, ins[1:], w)
    reader, writer = Reader(in_sems, pairs), Writer(out_sems)
    for tile in tiles(SMALL):
        if ring_out and tile.start == QKV:
            reader.take(len(ins) - 1)
        elif not ring_out or tile.start < QKV:
            reader.take()
        turned[tile] = w[:, tile].T
        writer.send(turned.at[tile], outs[0].at[tile])
    writer.finish()


def turn_weights(core, me, w, blocks, above, order):
    turned = ((SMALL, WIDTH), BF)
    return on_core(
        core, me, [w, *blocks], [turned], [((WIDTH, SMALL), BF), turned], turn_weights_kernel,
        "turn_weights", above, order,
    )


def expert_grads_kernel(received, dgate_pre, dup_pre, hidden, dslot, *rest):
    above = None
    if rest[0].shape[1] == SHARD:
        packed, down_out = rest
    else:
        above, packed = rest
        down_out = packed.at[:, SHARD : SHARD + FF // DP]
    gate = dot(received[...], dgate_pre[...], 0, 0).astype(BF)
    up = dot(received[...], dup_pre[...], 0, 0).astype(BF)
    down = dot(hidden[...], dslot[...], 0, 0).astype(BF)
    for part in range(DP // 2):
        packed[part, :SHARD, :FF] = gate[part * SHARD : (part + 1) * SHARD]
        packed[part, :SHARD, FF:] = up[part * SHARD : (part + 1) * SHARD]
        down_out[part] = down[part * FF // DP : (part + 1) * FF // DP]
    if above is not None:
        packed[:, SHARD + FF // DP :] = above[...]


def expert_grads(received, dgate_pre, dup_pre, hidden, dslot, above):
    down = FF // DP
    shapes = [(SHARD,), (down,)] if above is None else [(SHARD + 2 * down,)]
    whole = lambda width: pl.BlockSpec((SLOTS, width), lambda i: (0, 0))
    part = lambda width: pl.BlockSpec((SLOTS, width), lambda i: (0, i))
    rows = lambda count: pl.BlockSpec((DP // 2, count, WIDTH), lambda i: (i, 0, 0))
    held = [] if above is None else [above]
    return pl.pallas_call(
        expert_grads_kernel,
        grid=(2,),
        out_shape=[jax.ShapeDtypeStruct((DP, count, WIDTH), BF) for count, in shapes],
        in_specs=[part(WIDTH // 2), whole(FF), whole(FF), part(FF // 2), whole(WIDTH)]
        + [rows(down)] * len(held),
        out_specs=[rows(count) for count, in shapes],
        compiler_params=pltpu.CompilerParams(vmem_limit_bytes=VMEM_BYTES),
        cost_estimate=pl.CostEstimate(
            flops=6 * SLOTS * WIDTH * FF, bytes_accessed=14 << 20, transcendentals=0
        ),
        name="expert_grads",
    )(received, dgate_pre, dup_pre, hidden, dslot, *held)


def pack_kernel(
    l, query_hbm, key_hbm, value_hbm, out_hbm, router_hbm, gain_attn, gain_ffn, packed_hbm, *rest
):
    if l == 0:
        out_copy, packed, out, router, sems, out_sems = rest
    else:
        packed, router, sems, out_sems = rest
        out = packed.at[:, pl.ds(QKV, WIDTH)]
    pairs = [
        (router_hbm.at[l], router),
        (query_hbm.at[l], packed.at[:, pl.ds(0, Q_END)]),
        (key_hbm.at[l], packed.at[:, pl.ds(Q_END, K_END - Q_END)]),
        (value_hbm.at[l], packed.at[:, pl.ds(K_END, QKV - K_END)]),
        (out_hbm.at[l], out),
    ]
    reader, writer = Reader(sems, pairs), Writer(out_sems)
    reader.take()
    small = [router[...].astype(F32), gain_attn[l : l + 1].astype(F32)]
    small += [gain_ffn[l : l + 1].astype(F32), jnp.zeros((HEAD - EXPERTS - 2, SHARD), F32)]
    small = jnp.concatenate(small, axis=0)
    small = jnp.concatenate([small, jnp.zeros((HEAD, TILE - SHARD), F32)], axis=1).T
    packed[:, packed.shape[1] - HEAD :] = small[:SHARD].astype(BF)
    reader.take(3)
    if l == 0:
        writer.send(packed, packed_hbm)
        reader.take()
        writer.send(out, out_copy)
    else:
        reader.take()
        writer.send(packed, packed_hbm)
    writer.finish()


def pack(l, query, key, value, out, router, gain_attn, gain_ffn):
    sd = jax.ShapeDtypeStruct
    vmem = pl.BlockSpec(memory_space=pltpu.VMEM)
    packed = (SHARD, QKV + HEAD) if l == 0 else (SHARD, PACKED)
    outs = [packed] + [(SHARD, WIDTH)] * (l == 0)
    return pl.pallas_call(
        lambda *refs: pack_kernel(l, *refs),
        out_shape=[sd(shape, BF) for shape in outs],
        in_specs=[ANY] * 5 + [vmem] * 2,
        out_specs=[ANY] * len(outs),
        scratch_shapes=[pltpu.VMEM(shape, BF) for shape in outs]
        + [pltpu.VMEM((EXPERTS, SHARD), BF)]
        + [pltpu.SemaphoreType.DMA((5,)), pltpu.SemaphoreType.DMA((2,))],
        compiler_params=pltpu.CompilerParams(vmem_limit_bytes=VMEM_BYTES),
        name="pack",
    )(query, key, value, out, router.transpose(0, 2, 1), gain_attn, gain_ffn)


def ring(block):
    def move(values, step):
        return lax.ppermute(values, "dp", [(i, (i + step) % DP) for i in range(DP)])

    half = block.shape[0] // 2
    previous, following = move(block, 2), move(block, -2)
    far = [move(previous[:half], 2), move(following[half:], -2)]
    mine = [block, previous, following, *far]
    swap = [(i, i ^ 1) for i in range(DP)]
    return mine + [lax.ppermute(values, "dp", swap) for values in mine]


def seq_tables(counts):
    ends = jnp.cumsum(counts)
    starts = ends - counts
    place = jnp.arange(ROWS, dtype=jnp.int32)
    member = (place[:, None] >= starts[None, :]) & (place[:, None] < ends[None, :])
    index = jnp.arange(counts.shape[0], dtype=jnp.int32)
    segment = jnp.sum(jnp.where(member, index[None, :], 0), axis=1)
    position = place - jnp.sum(jnp.where(member, starts[None, :], 0), axis=1)
    allowed = (segment[:, None] == segment[None, :]) & (place[:, None] >= place[None, :])
    freqs = ROPE_BASE ** (-2.0 * jnp.arange(HEAD // 2, dtype=F32) / HEAD)
    angle = position.astype(F32)[:, None] * freqs[None, :]
    cosine, sine = jnp.cos(angle), jnp.sin(angle)
    return (
        jnp.concatenate([cosine, cosine], axis=1),
        jnp.concatenate([-sine, sine], axis=1),
        allowed.astype(F32),
    )


def slot_matrix(choices, in_parts=False):
    experts = jnp.arange(EXPERTS, dtype=jnp.int32)
    member = jnp.any(choices[:, :, None] == experts[None, None, :], axis=1).astype(BF)
    row = lax.broadcasted_iota(jnp.int32, (ROWS, ROWS), 0)
    column = lax.broadcasted_iota(jnp.int32, (ROWS, ROWS), 1)
    rank = dot((column < row).astype(BF), member).astype(BF)
    slot = jnp.arange(SLOTS, dtype=jnp.int32)[None, :]
    if in_parts:
        owner, place = slot % PART // PART_ROWS, slot // PART * PART_ROWS + slot % PART_ROWS
    else:
        owner, place = slot // CAP, slot % CAP
    expand = (owner == experts[:, None]).astype(BF)
    return ((dot(member, expand) > 0.5) & (dot(rank, expand) == place.astype(F32))).astype(BF)


def exchange(rows):
    width = rows.shape[-1]
    moved = lax.all_to_all(
        rows.reshape(EXPERTS, -1, width), "expert", split_axis=0, concat_axis=0, tiled=True
    )
    return moved.reshape(-1, width)


def after(values, *order):
    return pl.pallas_call(
        lambda *refs: None,
        out_shape=jax.ShapeDtypeStruct(values.shape, values.dtype),
        in_specs=[ANY] * (1 + len(order)),
        out_specs=ANY,
        input_output_aliases={0: 0},
        name="after",
    )(values, *order)


def turn_columns_kernel(me, columns_hbm, turned_hbm, columns, turned, in_sems, out_sems):
    base = me[0] * SHARD // HEAD * HEAD
    pairs = []
    for i in range(3):
        at = pl.multiple_of(base + i * WIDTH, HEAD)
        pairs += [(columns_hbm.at[:, pl.ds(at, TILE)], columns.at[:, pl.ds(i * TILE, TILE)])]
    reader, writer = Reader(in_sems, pairs), Writer(out_sems)
    for i in range(3):
        reader.take()
        turned[i] = columns[:, i * TILE : (i + 1) * TILE].T
        writer.send(turned.at[i], turned_hbm.at[i])
    writer.finish()


def turn_columns(me, columns):
    tokens = DP * ROWS
    return pl.pallas_call(
        turn_columns_kernel,
        out_shape=jax.ShapeDtypeStruct((3, TILE, tokens), BF),
        in_specs=[pl.BlockSpec(memory_space=pltpu.SMEM), ANY],
        out_specs=ANY,
        scratch_shapes=[
            pltpu.VMEM((tokens, 3 * TILE), BF),
            pltpu.VMEM((3, TILE, tokens), BF),
            pltpu.SemaphoreType.DMA((3,)),
            pltpu.SemaphoreType.DMA((3,)),
        ],
        compiler_params=pltpu.CompilerParams(vmem_limit_bytes=VMEM_BYTES),
        cost_estimate=pl.CostEstimate(flops=0, bytes_accessed=4 << 20, transcendentals=0),
        name="turn_columns",
    )(me, columns)


def dense_grads_kernel(me, turned_hbm, factors_hbm, pieces_hbm, turned, factors, total, pieces,
                       in_sems, out_sems):
    start = me[0] * SHARD
    shift = start % HEAD
    base = start - shift
    copies = Writer(out_sems)
    pairs = [(turned_hbm, turned)]
    for at, width in [(SMALL, HEAD)] + [(at, 2 * CHUNK) for at in range(0, SMALL, 2 * CHUNK)]:
        block = (slice(None), pl.ds(at, width))
        pairs += [(factors_hbm.at[block], factors.at[block])]
    reader = Reader(in_sems, pairs)
    reader.take(2)

    def put(chunk, values):
        pieces[chunk] = values.astype(BF)
        copies.send(pieces.at[chunk], pieces_hbm.at[chunk])

    ends = jnp.zeros((ROWS, HEAD), F32)
    for source in range(DP):
        ends += factors[source * ROWS : (source + 1) * ROWS, SMALL:].astype(F32)
    lane = lax.broadcasted_iota(jnp.int32, (ROWS, HEAD), 1)

    def gain_piece(piece):
        held = (lane == piece + GAIN_HIGH) | (lane == piece + GAIN_LOW)
        return jnp.sum(jnp.where(held, ends, 0.0), axis=1, keepdims=True)

    first, second = gain_piece(base // HEAD), gain_piece(base // HEAD + 1)
    gain = jnp.where(
        shift == 0,
        jnp.concatenate([first, second[: SHARD - ROWS]], axis=0),
        jnp.concatenate([first[ROWS // 2 :], second], axis=0),
    )
    gain_high, gain_low = split(gain)
    rows = pl.ds(pl.multiple_of(shift, 64), SHARD)
    total[1, :, :HEAD] = dot(turned[2], factors[:, SMALL:])
    router = total[1, rows, :HEAD]
    lane = lax.broadcasted_iota(jnp.int32, (SHARD, HEAD), 1)
    router = jnp.where(lane < EXPERTS, router, 0.0)
    router = jnp.where(lane == EXPERTS, gain_high.astype(F32), router)
    router = jnp.where(lane == EXPERTS + 1, gain_low.astype(F32), router)
    put(CHUNKS - 2, jnp.concatenate([router, jnp.zeros_like(router)], axis=1))
    put(CHUNKS - 1, jnp.zeros((SHARD, CHUNK), F32))
    for pair in range(SMALL // CHUNK // 2):
        reader.take()
        at = pair * 2 * CHUNK
        total[pair % 2] = dot(turned[0 if at < QKV else 1], factors[:, at : at + 2 * CHUNK])
        put(2 * pair, total[pair % 2, rows, :CHUNK])
        put(2 * pair + 1, total[pair % 2, rows, CHUNK:])
    copies.finish()


def dense_grads(me, turned, factors, order):
    tokens = DP * ROWS

    def body(*refs):
        dense_grads_kernel(*refs[:3], *refs[3 + len(order) :])

    return pl.pallas_call(
        body,
        out_shape=jax.ShapeDtypeStruct((CHUNKS, SHARD, CHUNK), BF),
        in_specs=[pl.BlockSpec(memory_space=pltpu.SMEM)] + [ANY] * (2 + len(order)),
        out_specs=ANY,
        scratch_shapes=[
            pltpu.VMEM((3, TILE, tokens), BF),
            pltpu.VMEM((tokens, PACKED), BF),
            pltpu.VMEM((2, TILE, 2 * CHUNK), F32),
            pltpu.VMEM((CHUNKS, SHARD, CHUNK), BF),
            pltpu.SemaphoreType.DMA((1 + CHUNKS,)),
            pltpu.SemaphoreType.DMA((CHUNKS,)),
        ],
        compiler_params=pltpu.CompilerParams(vmem_limit_bytes=VMEM_BYTES),
        cost_estimate=pl.CostEstimate(
            flops=2 * tokens * TILE * PACKED, bytes_accessed=10 << 20, transcendentals=0
        ),
        name="dense_grads",
    )(me, turned, factors, *order)


def to_expert_peers(pieces):
    return lax.all_to_all(pieces, "expert", split_axis=0, concat_axis=0, tiled=True)


def sum_pieces_kernel(pieces_hbm, out_hbm, pieces, out, in_sems, out_sems):
    half = CHUNKS // 2
    pairs = []
    for at in (0, half):
        block = pl.ds(at, half)
        pairs += [(pieces_hbm.at[block, :, pl.ds(0, CHUNK)], pieces.at[block])]
    reader, writer = Reader(in_sems, pairs), Writer(out_sems)
    reader.take()
    total = pieces[0].astype(F32)
    for i in range(1, half):
        total += pieces[i].astype(F32)
    reader.take()
    for i in range(half, CHUNKS):
        total += pieces[i].astype(F32)
    out[...] = total.astype(BF)
    if len(out_hbm.shape) == 3:
        for i in range(CHUNKS):
            writer.send(out, out_hbm.at[i])
    else:
        writer.send(out, out_hbm)
    writer.finish()


def sum_pieces(pieces, copies):
    return pl.pallas_call(
        sum_pieces_kernel,
        out_shape=jax.ShapeDtypeStruct((copies,) * (copies > 1) + (SHARD, CHUNK), BF),
        in_specs=[ANY],
        out_specs=ANY,
        scratch_shapes=[
            pltpu.VMEM((CHUNKS, SHARD, CHUNK), BF),
            pltpu.VMEM((SHARD, CHUNK), BF),
            pltpu.SemaphoreType.DMA((2,)),
            pltpu.SemaphoreType.DMA((CHUNKS,)),
        ],
        compiler_params=pltpu.CompilerParams(vmem_limit_bytes=VMEM_BYTES),
        name="sum_pieces",
    )(pieces)


def finish_kernel(l, refs):
    (pieces, w_query, key_projection, value_projection, norm_attn), refs = refs[:5], refs[5:]
    if l == 0:
        ends_above, refs = refs[0], refs[5:]
        (query_hbm, key_hbm, value_hbm, out_hbm, gain_attn, gain_ffn, router) = refs[:7]
        query, key, value, out, sems = refs[7:]
    else:
        query_hbm, key_hbm, value_hbm, out_hbm, ends_out, query, key, value, out, sems = refs
    writer = Writer(sems)
    rows = jnp.zeros((SHARD, 1), F32)
    for chunk in range(SMALL // CHUNK):
        part = pieces[chunk].astype(F32)
        lanes = slice(chunk * CHUNK, (chunk + 1) * CHUNK)
        if chunk < Q_END // CHUNK:
            query[:, lanes] = part
            weight = w_query[l, :, lanes]
        elif chunk == Q_END // CHUNK:
            key[...] = part
            weight = key_projection[l]
            writer.send(query, query_hbm.at[l])
            writer.send(key, key_hbm.at[l])
        elif chunk < QKV // CHUNK:
            value[...] = part
            weight = value_projection[l]
            writer.send(value, value_hbm.at[l])
        else:
            out[:, lanes.start - QKV : lanes.stop - QKV] = part
            continue
        rows += jnp.sum(part * weight.astype(F32), axis=1, keepdims=True)
    writer.send(out, out_hbm.at[l])
    ends = pieces[CHUNKS - 2, :, :HEAD].astype(F32)
    ffn = ends[:, EXPERTS : EXPERTS + 1] + ends[:, EXPERTS + 1 : EXPERTS + 2]
    lane = lax.broadcasted_iota(jnp.int32, (SHARD, HEAD), 1)
    ends = jnp.where(lane == EXPERTS, rows, jnp.where(lane == EXPERTS + 1, ffn, ends))
    if l > 0:
        ends_out[...] = ends
    else:
        for layer, part in enumerate((ends, ends_above[...])):
            wide = jnp.concatenate([part, jnp.zeros((TILE - SHARD, HEAD), F32)], axis=0).T
            router[layer] = wide[:EXPERTS, :SHARD]
            gain = norm_attn[layer : layer + 1].astype(F32)
            gain_attn[layer : layer + 1] = wide[EXPERTS : EXPERTS + 1, :SHARD] / gain
            gain_ffn[layer : layer + 1] = wide[EXPERTS + 1 : EXPERTS + 2, :SHARD]
    writer.finish()


def finish(l, pieces, weights, norm_attn, above):
    sd = jax.ShapeDtypeStruct
    vmem = pl.BlockSpec(memory_space=pltpu.VMEM)
    keys = (SHARD, KEY_VALUE_HEADS * HEAD)
    slabs = [(SHARD, Q_END), keys, keys, (SHARD, WIDTH)]
    outs = [sd((LAYERS,) + shape, F32) for shape in slabs]
    if above is None:
        outs += [sd((SHARD, HEAD), F32)]
        ins, in_specs, aliases = [], [], {}
    else:
        outs += [sd((LAYERS, SHARD), F32)] * 2 + [sd((LAYERS, EXPERTS, SHARD), F32)]
        ins, in_specs = [above[4], *above[:4]], [vmem] + [ANY] * 4
        aliases = {6 + i: i for i in range(4)}
    return pl.pallas_call(
        lambda *refs: finish_kernel(l, refs),
        out_shape=outs,
        in_specs=[vmem] * 5 + in_specs,
        out_specs=[ANY] * 4 + [vmem] * (len(outs) - 4),
        input_output_aliases=aliases,
        scratch_shapes=[pltpu.VMEM(shape, F32) for shape in slabs]
        + [pltpu.SemaphoreType.DMA((4,))],
        compiler_params=pltpu.CompilerParams(vmem_limit_bytes=VMEM_BYTES),
        name="finish",
    )(pieces, *weights, norm_attn, *ins)


def finish_experts_kernel(shares0, shares1, gate, up, down):
    rows = FF // DP
    for l, shares in enumerate((shares0, shares1)):
        gate[l, 0] = shares[:SHARD, :FF].astype(F32)
        up[l, 0] = shares[:SHARD, FF:].astype(F32)
        down[l, 0] = shares0[SHARD + l * rows : SHARD + (l + 1) * rows].astype(F32)


def finish_experts(shares0, shares1):
    sd = jax.ShapeDtypeStruct
    vmem = pl.BlockSpec(memory_space=pltpu.VMEM)
    return pl.pallas_call(
        finish_experts_kernel,
        out_shape=[
            sd((LAYERS, 1, SHARD, FF), F32), sd((LAYERS, 1, SHARD, FF), F32),
            sd((LAYERS, 1, FF // DP, WIDTH), F32),
        ],
        in_specs=[vmem] * 2,
        out_specs=[vmem] * 3,
        compiler_params=pltpu.CompilerParams(vmem_limit_bytes=VMEM_BYTES),
        name="finish_experts",
    )(shares0, shares1)


def mixed_kernel(x_hbm, high, low, part0, part1, part2, out, x, gates, returned, sems):
    pairs = [(high, gates.at[:ROWS]), (low, gates.at[ROWS:]), (x_hbm, x)]
    for p, part in enumerate((part0, part1, part2)):
        pairs += [(part, returned.at[pl.ds(p * PART, PART)])]
    Reader(sems, pairs).take(len(pairs))
    for tile in tiles(WIDTH):
        both = dot(gates[...], returned[:, tile])
        out[:, tile] = (x[:, tile] + both[:ROWS] + both[ROWS:]).astype(BF)


def mixed_rows(x, high, low, parts):
    return pl.pallas_call(
        mixed_kernel,
        out_shape=jax.ShapeDtypeStruct(TOKENS, BF),
        in_specs=[ANY] * 6,
        out_specs=pl.BlockSpec(memory_space=pltpu.VMEM),
        scratch_shapes=[
            pltpu.VMEM(TOKENS, F32),
            pltpu.VMEM((2 * ROWS, SLOTS), BF),
            pltpu.VMEM(WIDE, BF),
            pltpu.SemaphoreType.DMA((6,)),
        ],
        compiler_params=pltpu.CompilerParams(vmem_limit_bytes=VMEM_BYTES),
        name="mixed",
    )(x, high, low, *parts)


def local(
    tokens, cotangent, lengths, routes, norm_attn, w_query, key_projection, value_projection,
    w_out, norm_ffn, w_router, w_gate, w_up, w_down,
):
    me_dp = lax.axis_index("dp").astype(jnp.int32).reshape(1)
    me_expert = lax.axis_index("expert").astype(jnp.int32).reshape(1)
    tables = seq_tables(lengths[0])
    give = [slot_matrix(routes[l]) for l in range(LAYERS)]
    take = [g.T for g in give]
    give_parts = slot_matrix(routes[1], True)
    experts = (w_gate, w_up, w_down)

    def gather(values):
        return lax.all_gather(values, "dp", axis=0, tiled=True)

    weights = (w_query, key_projection, value_projection, w_out, w_router, norm_attn, norm_ffn)
    shard0, out_shard0 = pack(0, *weights)
    w = [gather(shard0), gather(pack(1, *weights)[0])]
    out_ring = [me_dp, *ring(out_shard0)]

    dx_rows = exchange(dot(take[1], cotangent).astype(BF))

    turned_w = turn_weights(1, me_dp, w[0], out_ring[1:], None, ())
    kept0 = attn_forward(
        tokens, None, w[0], out_ring, tables, take[0], give[0],
        (dx_rows, *turned_w, give[1], give_parts, me_expert),
    )
    received0 = exchange(kept0["rows"])
    act0, slope0, hidden0, out0 = experts_forward(received0, experts, ())
    returned0 = exchange(out0)
    turned_w = turn_weights(0, me_dp, w[0], out_ring[1:], turned_w, (out0,))
    product = upper_product(0, me_dp, dx_rows, w_down, None, turned_w)
    product = upper_product(1, me_dp, dx_rows, w_down, product, turned_w)
    turned_w1 = turn_weights(0, me_dp, w[1], [], None, product)
    turned_w1 = turn_weights(1, me_dp, w[1], [], turned_w1, (returned0,))
    columns0 = gather(kept0["columns"])

    kept1 = attn_forward(
        kept0["after"], (kept0["high"], kept0["low"], returned0), w[1], None, tables, take[1],
        give_parts, tuple(turned_w1),
    )
    received1 = exchange(kept1["rows"])
    columns1 = gather(kept1["columns"])
    hidden1, dgate1, dup1, back1 = experts_both(
        me_expert, received1, product[0], w[1], experts, ()
    )
    back1 = exchange(back1)
    *parts, dslot1 = experts_out(me_expert, hidden1, received1, dx_rows, w[1], w_down, ())
    grads1, down1 = expert_grads(received1, dgate1, dup1, hidden1, dslot1, None)
    turned0 = turn_columns(me_dp, columns0)
    parts[0] = exchange(after(parts[0], grads1, turned0))

    dx0, packed1, rows0 = attn_backward(
        cotangent, back1, kept1["x"], kept1, w[1], turned_w1[0], tables, give[1],
        (take[0], kept0["router"]), None, (),
    )
    packed1 = after(packed1, parts[0])
    dslot0 = exchange(rows0)
    factors1 = gather(packed1)
    shares1 = lax.psum_scatter(
        after(grads1, packed1).reshape(-1, WIDTH), "dp", scatter_dimension=0, tiled=True
    )
    dgate0, dup0, back0 = experts_backward(dslot0, act0, slope0, experts, ())
    back0 = exchange(back0)
    (grads0,) = expert_grads(received0, dgate0, dup0, hidden0, dslot0, down1)
    parts[1] = exchange(parts[1])
    turned1 = turn_columns(me_dp, columns1)
    pieces1 = dense_grads(me_dp, turned1, factors1, (parts[1],))
    parts[2] = exchange(after(parts[2], grads0, pieces1))
    grad_tokens, packed0 = attn_backward(
        dx0, back0, tokens, kept0, w[0], turned_w[0], tables, give[0], None, returned0, ()
    )
    factors0 = gather(after(packed0, parts[2]))
    summed1 = sum_pieces(to_expert_peers(pieces1), CHUNKS)
    shares0 = lax.psum_scatter(
        after(grads0, summed1, shares1).reshape(-1, WIDTH), "dp", scatter_dimension=0, tiled=True
    )
    mixed = mixed_rows(kept1["after"], kept1["high"], kept1["low"], parts)
    pieces1 = to_expert_peers(summed1)
    pieces0 = dense_grads(me_dp, turned0, factors0, ())
    pieces0 = to_expert_peers(after(pieces0, pieces1))
    pieces0 = to_expert_peers(sum_pieces(pieces0, CHUNKS))

    dense = (w_query, key_projection, value_projection)
    above = finish(1, pieces1, dense, norm_attn, None)
    gate, up, down = finish_experts(shares0, shares1)
    above = (after(above[0], gate), *above[1:])
    query, key, value, out, gain_attn, gain_ffn, router = finish(
        0, pieces0, dense, norm_attn, above
    )
    return (
        mixed, grad_tokens, gain_attn, query, key, value, out, gain_ffn,
        router.transpose(0, 2, 1), gate, up, down,
    )


def solution(mesh):
    placed = (
        P(("dp", "expert"), None),
        P(("dp", "expert"), None),
        P(("dp", "expert"), None),
        P(None, ("dp", "expert"), None),
        P(None, "dp"),
        P(None, "dp", None),
        P(None, "dp", None),
        P(None, "dp", None),
        P(None, "dp", None),
        P(None, "dp"),
        P(None, "dp", None),
        P(None, "expert", None, None),
        P(None, "expert", None, None),
        P(None, "expert", None, None),
    )
    return jax.shard_map(
        local,
        mesh=mesh,
        in_specs=placed,
        out_specs=(
            P(("dp", "expert"), None),
            P(("dp", "expert"), None),
            P(None, "dp"),
            P(None, "dp", None),
            P(None, "dp", None),
            P(None, "dp", None),
            P(None, "dp", None),
            P(None, "dp"),
            P(None, "dp", None),
            P(None, "expert", "dp", None),
            P(None, "expert", "dp", None),
            P(None, "expert", "dp", None),
        ),
        check_vma=False,
    )
```
